32 devices in a mesh: tm: 8 (over z, y), chan: 4 (over x, core).
Axes of the slice: x: 2, y: 2, z: 4, core: 2. Of those that a mesh axis runs over, the one named last changes fastest.
Arguments:
- raw_strain: bfloat16 [512, 40960], P('chan', 'tm'), may hold values from -48 to 48
- fir_taps: float32 [128], replicated, may hold values from -0.5 to 0.5
- source_channels: int32 [32], replicated, may hold values from 0 to 511, as said below
- live_counts: int32 [32], P(('chan', 'tm')), may hold values from 8 to 16, as said below
Outputs:
- correlations: float32 [32, 512, 384], P(None, ('chan', 'tm'))
The draws below stay inside these ranges and needn't reach their ends.
Inputs may be any that keep to these rules, and one draw needn't show every extreme that they name: `source_channels`: the virtual sources are distinct live channels; at most 2 of them lie in one aligned block of 16 channels, and some block holds exactly 2. `live_counts`: some block has all 16 channels live and some has exactly half of them.
All inputs are finite; a program needn't handle non-finite values.
Results may differ from the reference program's by a relative error of at most 0.015.
Values may be sent and summed in bfloat16 or wider, within the bound.
No kernel may reach another device: no remote copies, remote signals or barrier semaphores. Data moves between devices by JAX's collectives and lax.ppermute only.
A program may use at most 128 MiB of HBM per device.

```python
import math
import jax
import jax.numpy as jnp
from jax import lax

TAPS = 128
DECIM = 10
SEG = 1024
BAND = 64
LAGH = 192
SRC_DEV = 1
CH_DEV = 16
NCH = 512
NBLK = 32
NTR = 40960
NSEG = 4
SRC = 32


def draw_raw_strain(key, part):
    noise_key, chan_key, env_key = jax.random.split(key, 3)
    env_count = NTR // 64
    noise_field = jnp.clip(jax.random.normal(noise_key, (NCH, NTR), jnp.float32), -6.0, 6.0)
    chan_scale = jnp.exp(jax.random.uniform(chan_key, (NCH, 1), jnp.float32, math.log(0.3), math.log(3.0)))
    envelope = jnp.exp(jax.random.uniform(env_key, (1, env_count), jnp.float32, math.log(0.5), math.log(2.0)))
    envelope = jnp.repeat(envelope, 64, axis=1)
    return (noise_field * chan_scale * envelope).astype(jnp.bfloat16)


def layout_draw(key):
    base = jax.random.fold_in(key, 7)
    count_key, order_key, pair_key, score_key, shuffle_key = jax.random.split(base, 5)
    counts = jax.random.randint(count_key, (NBLK,), CH_DEV // 2, CH_DEV + 1)
    block_order = jax.random.permutation(order_key, NBLK)
    counts = counts.at[block_order[0]].set(CH_DEV).at[block_order[1]].set(CH_DEV // 2)
    pair_shift = jax.random.randint(pair_key, (NBLK // 2,), 0, SRC_DEV + 1)
    pair_shift = pair_shift.at[0].set(SRC_DEV)
    first_half = block_order[0::2]
    second_half = block_order[1::2]
    per_block = jnp.zeros((NBLK,), jnp.int32)
    per_block = per_block.at[first_half].set(SRC_DEV + pair_shift).at[second_half].set(SRC_DEV - pair_shift)
    positions = jnp.arange(CH_DEV, dtype=jnp.int32)
    scores = jax.random.randint(score_key, (NBLK, CH_DEV), 0, 1 << 16) * CH_DEV + positions[None, :]
    is_live = positions[None, :] < counts[:, None]
    scores = jnp.where(is_live, scores, (1 << 24) + positions[None, :])
    chosen_spots = jnp.argsort(scores, axis=1, stable=True)[:, :2 * SRC_DEV].astype(jnp.int32)
    block_index = jnp.arange(NBLK, dtype=jnp.int32)
    candidate = (block_index[:, None] * CH_DEV + chosen_spots).reshape(-1)
    is_valid = (jnp.arange(2 * SRC_DEV, dtype=jnp.int32)[None, :] < per_block[:, None]).reshape(-1)
    keep_order = jnp.argsort(jnp.where(is_valid, 0, 1), stable=True)[:SRC]
    selected = candidate[keep_order]
    shuffle = jax.random.permutation(shuffle_key, SRC)
    return (counts.astype(jnp.int32), selected[shuffle].astype(jnp.int32))


def draw_source_channels(key, part):
    return layout_draw(key)[1]


def draw_live_counts(key, part):
    return layout_draw(key)[0]


def gaussian(own_key, shape, width, reach, kind=jnp.bfloat16):
    result = width * jax.random.normal(own_key, shape, jnp.float32)
    return jnp.clip(result, min=-reach, max=reach).astype(kind)


def setup_inputs(seed: int = 0) -> dict:
    key_of = jax.random.split(jax.random.key(seed), 5)
    raw_strain = draw_raw_strain(jax.random.fold_in(key_of[4], 71), 0)
    fir_taps = gaussian(key_of[1], (TAPS,), TAPS ** -0.5, 0.5, jnp.float32)
    source_channels = draw_source_channels(jax.random.fold_in(key_of[4], 71), 0)
    live_counts = draw_live_counts(jax.random.fold_in(key_of[4], 71), 0)
    return dict(raw_strain=raw_strain, fir_taps=fir_taps, source_channels=source_channels, live_counts=live_counts)


whiten_eps = 1e-06

def whiten_rows(traces):
    rows = traces.shape[0]
    half_len = SEG // 2
    segments = traces.astype(jnp.float32).reshape(rows, NSEG, SEG)
    spectrum = jnp.fft.rfft(segments, axis=-1)[..., :half_len]
    real_part = jnp.real(spectrum)
    imag_part = jnp.imag(spectrum)
    band_power = (real_part * real_part + imag_part * imag_part).reshape(rows, NSEG, half_len // BAND, BAND)
    band_scale = 1.0 / jnp.sqrt(lax.optimization_barrier(jnp.mean(band_power, axis=-1)) + whiten_eps)
    band_scale = jnp.repeat(band_scale, BAND, axis=-1)
    return jnp.concatenate([real_part * band_scale, imag_part * band_scale], axis=-1).astype(jnp.bfloat16)

def reference(raw_strain, fir_taps, source_channels, live_counts):
    block_ids = jnp.arange(NBLK, dtype=jnp.int32)
    half_len = SEG // 2

    def prepare(block_id):
        rows = lax.dynamic_slice_in_dim(raw_strain, block_id * CH_DEV, CH_DEV, 0).astype(jnp.float32)
        kernel = jnp.flip(fir_taps).astype(rows.dtype)[None, None, :]
        filtered = lax.conv_general_dilated(rows[:, None, :], kernel, (DECIM,), [(TAPS - 1, 0)], precision=lax.Precision.HIGHEST)[:, 0, :]
        decimated = filtered.astype(jnp.bfloat16)
        is_live = jnp.arange(CH_DEV, dtype=jnp.int32) < live_counts[block_id]
        traces = jnp.where(is_live[:, None], decimated, jnp.zeros_like(decimated))
        return whiten_rows(traces)
    whitened = lax.map(prepare, block_ids).reshape(NCH, NSEG, SEG)
    sources = jnp.take(whitened, source_channels, axis=0).astype(jnp.float32)
    src_re = sources[..., :half_len]
    src_im = sources[..., half_len:]
    lag_index = jnp.mod(jnp.arange(-LAGH, LAGH, dtype=jnp.int32), SEG)
    factor = math.sqrt(SEG / NSEG)
    highest = lax.Precision.HIGHEST

    def correlate(block_id):
        local = lax.dynamic_slice_in_dim(whitened, block_id * CH_DEV, CH_DEV, 0).astype(jnp.float32)
        loc_re = local[..., :half_len]
        loc_im = local[..., half_len:]
        cross_re = jnp.einsum('csk,nsk->nck', loc_re, src_re, precision=highest) + jnp.einsum('csk,nsk->nck', loc_im, src_im, precision=highest)
        cross_im = jnp.einsum('csk,nsk->nck', loc_im, src_re, precision=highest) - jnp.einsum('csk,nsk->nck', loc_re, src_im, precision=highest)
        spectrum = cross_re + 1j * cross_im
        spectrum = jnp.pad(spectrum, ((0, 0), (0, 0), (0, 1)))
        full_lags = jnp.fft.irfft(spectrum, n=SEG, axis=-1)
        return jnp.take(full_lags, lag_index, axis=-1) * factor
    blocks = lax.map(correlate, block_ids)
    return jnp.transpose(blocks, (1, 0, 2, 3)).reshape(SRC, NCH, 2 * LAGH).astype(jnp.float32)
```

```python
import functools
import math

import jax
import jax.numpy as jnp
import ml_dtypes
import numpy as np
from jax import lax
from jax.experimental import pallas as pl
from jax.experimental.pallas import tpu as pltpu
from jax.sharding import PartitionSpec as P

DECIM = 10
SEG = 1024
BAND = 64
LAGH = 192
SRC_DEV = 1
LANES = 128
HALF = SEG // 2
CHUNKS = HALF // LANES
VMEM_BYTES = 56 * 1024 * 1024

whiten_eps = 1e-06

NT = (((1,), (1,)), ((), ()))


def split_table(table):
    hi = table.astype(ml_dtypes.bfloat16)
    lo = (table - hi.astype(np.float64)).astype(ml_dtypes.bfloat16)
    return hi, lo


def dft_table(rows):
    phase = (np.arange(rows)[:, None] * np.arange(HALF)[None, :] % SEG) * (2.0 * np.pi / SEG)
    parts = []
    for j in range(CHUNKS):
        cut = slice(j * LANES, (j + 1) * LANES)
        hi, lo = split_table(np.concatenate([np.cos(phase[:, cut]), -np.sin(phase[:, cut])], 1))
        parts += [hi, lo]
    return np.concatenate(parts, axis=1)


def lag_table(seg_count):
    freq = np.arange(HALF)[:, None]
    phase = (freq * np.arange(-LAGH, LAGH)[None, :] % SEG) * (2.0 * np.pi / SEG)
    weight = np.where(freq == 0, 1.0, 2.0) * (math.sqrt(SEG / seg_count) / SEG)
    re = (weight * np.cos(phase)).reshape(CHUNKS, LANES, 2 * LAGH)
    im = (-weight * np.sin(phase)).reshape(CHUNKS, LANES, 2 * LAGH)
    return np.concatenate([re, im], axis=1).reshape(SEG, 2 * LAGH).astype(ml_dtypes.bfloat16)


def iota(shape, dim):
    return lax.broadcasted_iota(jnp.int32, shape, dim)


def one_hot(mask):
    return jnp.where(mask, 1.0, 0.0).astype(jnp.bfloat16)


def column(row):
    n = row.shape[1]
    return jnp.sum(jnp.where(iota((n, n), 0) == iota((n, n), 1), row, 0), axis=1, keepdims=True)


def tap_rows(taps):
    tap_count = taps.shape[1]
    width = 3 * LANES
    flip = one_hot(iota((tap_count, width), 0) + iota((tap_count, width), 1) == tap_count)
    hi = taps.astype(jnp.bfloat16)
    lo = (taps - hi.astype(jnp.float32)).astype(jnp.bfloat16)
    out = []
    for part in (hi, lo):
        base = jnp.dot(
            jnp.broadcast_to(part.astype(jnp.float32), (8, tap_count)).astype(jnp.bfloat16),
            flip,
            preferred_element_type=jnp.float32,
        )
        upper = pltpu.roll(base, 0, 1, stride=DECIM, stride_axis=0)
        out.append(jnp.concatenate([upper, pltpu.roll(upper, 8 * DECIM, 1)], axis=0))
    return out


def filter_kernel(blocks, src_ref, taps_ref, raw_ref, chan_ref, slot_ref, ext, weight, sems):
    rows, raw_len = raw_ref.shape
    span = raw_len // blocks
    wide = span + LANES
    copies = []
    for b in range(blocks):
        if b == 0:
            copy = pltpu.make_async_copy(
                raw_ref.at[:, pl.ds(0, span)],
                ext.at[pl.ds(0, rows), pl.ds(LANES, span)],
                sems.at[b],
            )
        else:
            copy = pltpu.make_async_copy(
                raw_ref.at[:, pl.ds(b * span - LANES, wide)],
                ext.at[pl.ds(b * rows, rows), :],
                sems.at[b],
            )
        copy.start()
        copies.append(copy)
    ext[:rows, :LANES] = jnp.zeros((rows, LANES), ext.dtype)
    weight[...] = jnp.zeros_like(weight)
    for p, base in enumerate(tap_rows(taps_ref[...])):
        for i in range(LANES // 16):
            tile, lane = divmod(16 * DECIM * i, LANES)
            piece = pltpu.roll(base, lane, 1) if lane else base
            weight[p * LANES + 16 * i : p * LANES + 16 * (i + 1), tile * LANES : (tile + 3) * LANES] = (
                piece.astype(jnp.bfloat16)
            )
    src = src_ref[...]
    src_count = src.shape[1]
    slots = slot_ref.shape[0]
    group = src // rows
    group_col = column(group)
    src_col = column(src)
    rank = jnp.sum(
        jnp.where(
            (group_col == group)
            & (iota((src_count, src_count), 0) < iota((src_count, src_count), 1)),
            1,
            0,
        ),
        axis=0,
        keepdims=True,
    )
    mine = lax.axis_index("chan")
    to_slot = one_hot((iota((slots, src_count), 0) == rank) & (group == mine))
    to_row = one_hot(src_col - mine * rows == iota((src_count, rows), 1))
    pick = jnp.dot(to_slot, to_row, preferred_element_type=jnp.float32).astype(jnp.bfloat16)
    for copy in copies:
        copy.wait()
    acc = lax.dot_general(ext[...], weight[...], NT, preferred_element_type=jnp.float32)
    y = (acc[:, :LANES] + acc[:, LANES:]).astype(jnp.bfloat16)
    dec = blocks * LANES
    for b in range(blocks):
        chan_ref[:, b * LANES : (b + 1) * LANES] = y[b * rows : (b + 1) * rows]
    chan_ref[:, dec : dec + LANES] = ext[:rows, LANES : 2 * LANES]
    chan_ref[:, dec + LANES :] = ext[(blocks - 1) * rows :, wide - LANES :]
    slot_ref[...] = jnp.dot(pick, chan_ref[...], preferred_element_type=jnp.float32).astype(jnp.bfloat16)


def correlate_kernel(
    seg_count, chan_count, part_rows,
    src_ref, live_ref, taps_ref, x_ref, g_ref, d_ref, l_ref, out_ref,
    trace, own, other, cross,
):
    steps, ch, width = x_ref.shape
    dec = width - 2 * LANES
    src_count = src_ref.shape[1]
    rows = ch + src_count
    per_seg = SEG // dec

    @pl.when(pl.program_id(0) == 0)
    def _():
        src = src_ref[...]
        slots = g_ref.shape[1] // chan_count
        group = src // (steps * ch)
        group_col = column(group)
        rank = jnp.sum(
            jnp.where(
                (group_col == group)
                & (iota((src_count, src_count), 1) < iota((src_count, src_count), 0)),
                1,
                0,
            ),
            axis=1,
            keepdims=True,
        )
        place = group_col * slots + rank
        pick = one_hot(place == iota((src_count, chan_count * slots), 1))
        base = [v[:, : 2 * LANES].astype(jnp.bfloat16) for v in tap_rows(taps_ref[...])]
        empty = jnp.zeros((LANES - 16, 2 * LANES), jnp.bfloat16)
        weight = jnp.concatenate([base[0], empty, base[1], empty], axis=0)
        live = iota((ch, width), 0) < live_ref[0]
        before = jnp.zeros((rows, LANES), jnp.bfloat16)
        head_len = -(-(taps_ref.shape[1] - 1) // DECIM)
        is_head = iota((rows, LANES), 1) < head_len
        for t in range(steps):
            mine = jnp.where(live, x_ref[t], jnp.zeros((ch, width), jnp.bfloat16))
            theirs = jnp.dot(pick, g_ref[t], preferred_element_type=jnp.float32).astype(jnp.bfloat16)
            both = jnp.concatenate([mine, theirs], axis=0)
            edge = jnp.concatenate([before, both[:, dec : dec + LANES]], axis=1)
            fix = lax.dot_general(edge, weight, NT, preferred_element_type=jnp.float32)
            fix = (fix[:, :LANES] + fix[:, LANES:]).astype(jnp.bfloat16)
            trace[t * rows : (t + 1) * rows, :LANES] = jnp.where(is_head, fix, both[:, :LANES])
            trace[t * rows : (t + 1) * rows, LANES:] = both[:, LANES:dec]
            before = both[:, dec + LANES :]
        odd = (iota((rows, 2 * LANES), 1) & 1) == 1
        sign = jnp.where(odd, -1.0, 1.0)
        same = one_hot(
            iota((2 * LANES, LANES), 0) % LANES // BAND == iota((2 * LANES, LANES), 1) // BAND
        )
        group_segs = max(1, min(seg_count, part_rows // (per_seg * rows)))
        for first in range(0, seg_count, group_segs):
            segs = min(group_segs, seg_count - first)
            lhs = trace[first * per_seg * rows : (first + segs) * per_seg * rows, :]
            for j in range(CHUNKS):
                acc = jnp.dot(
                    lhs, d_ref[:, 4 * j * LANES : 4 * (j + 1) * LANES],
                    preferred_element_type=jnp.float32,
                )
                half = acc[:, : 2 * LANES] + acc[:, 2 * LANES :]
                spec = []
                for g in range(segs):
                    a = half[g * per_seg * rows : (g * per_seg + 1) * rows]
                    b = half[(g * per_seg + 1) * rows : (g * per_seg + 2) * rows]
                    spec.append(a + sign * b)
                spec = jnp.concatenate(spec, axis=0)
                re, im = spec[:, :LANES], spec[:, LANES:]
                power = re * re + im * im
                hi = power.astype(jnp.bfloat16)
                lo = (power - hi.astype(jnp.float32)).astype(jnp.bfloat16)
                total = jnp.dot(
                    jnp.concatenate([hi, lo], axis=1), same, preferred_element_type=jnp.float32
                )
                scale = lax.rsqrt(total * (1.0 / BAND) + whiten_eps)
                w_re = (re * scale).astype(jnp.bfloat16).astype(jnp.float32)
                w_im = (im * scale).astype(jnp.bfloat16).astype(jnp.float32)
                at = 2 * j * LANES
                for g in range(segs):
                    r, o = g * rows, (first + g) * ch
                    own[o : o + ch, at : at + LANES] = w_re[r : r + ch]
                    own[o : o + ch, at + LANES : at + 2 * LANES] = w_im[r : r + ch]
                    o = (first + g) * src_count
                    other[o : o + src_count, at : at + LANES] = w_re[r + ch : r + rows]
                    other[o : o + src_count, at + LANES : at + 2 * LANES] = w_im[r + ch : r + rows]

    block = out_ref.shape[0]
    start = pl.multiple_of(pl.program_id(0) * block, 8)
    for j in range(CHUNKS):
        at = 2 * j * LANES
        a_re = [own[g * ch : (g + 1) * ch, at : at + LANES] for g in range(seg_count)]
        a_im = [own[g * ch : (g + 1) * ch, at + LANES : at + 2 * LANES] for g in range(seg_count)]
        for s in range(block):
            if s % 8 == 0:
                tiles = [
                    other[pl.ds(pl.multiple_of(g * src_count + start + s, 8), 8), at : at + 2 * LANES]
                    for g in range(seg_count)
                ]
            re = im = None
            for g in range(seg_count):
                b_re = tiles[g][s % 8 : s % 8 + 1, :LANES]
                b_im = tiles[g][s % 8 : s % 8 + 1, LANES:]
                p = a_re[g] * b_re + a_im[g] * b_im
                q = a_im[g] * b_re - a_re[g] * b_im
                re, im = (p, q) if re is None else (re + p, im + q)
            cross[s * ch : (s + 1) * ch, at : at + LANES] = re.astype(jnp.bfloat16)
            cross[s * ch : (s + 1) * ch, at + LANES : at + 2 * LANES] = im.astype(jnp.bfloat16)
    lags = jnp.dot(cross[...], l_ref[...], preferred_element_type=jnp.float32)
    out_ref[...] = lags.reshape(out_ref.shape)


def whole(space=pltpu.VMEM):
    return pl.BlockSpec(memory_space=space)


def local(raw_strain, fir_taps, source_channels, live_counts):
    rows, raw_len = raw_strain.shape
    steps = lax.axis_size("tm")
    chan_count = lax.axis_size("chan")
    dec = raw_len // DECIM
    blocks = dec // LANES
    ch = rows // steps
    seg_count = steps * dec // SEG
    src_count = source_channels.shape[0]
    slots = 2 * SRC_DEV * steps
    width = dec + 2 * LANES
    span = raw_len // blocks
    src = source_channels.reshape(1, src_count)
    taps = fir_taps.reshape(1, fir_taps.shape[0])
    params = pltpu.CompilerParams(vmem_limit_bytes=VMEM_BYTES)
    packed, picked = pl.pallas_call(
        functools.partial(filter_kernel, blocks),
        out_shape=[
            jax.ShapeDtypeStruct((rows, width), jnp.bfloat16),
            jax.ShapeDtypeStruct((slots, width), jnp.bfloat16),
        ],
        in_specs=[whole(), whole(), whole(pl.ANY)],
        out_specs=[whole(), whole()],
        scratch_shapes=[
            pltpu.VMEM((blocks * rows, span + LANES), jnp.bfloat16),
            pltpu.VMEM((2 * LANES, span + LANES), jnp.bfloat16),
            pltpu.SemaphoreType.DMA((blocks,)),
        ],
        compiler_params=params,
        name="fir",
    )(src, taps, raw_strain)
    gathered = lax.all_gather(picked, ("tm", "chan"), axis=0, tiled=True)
    relaid = lax.all_to_all(packed, "tm", split_axis=0, concat_axis=0, tiled=True)
    block = math.gcd(src_count, 16)
    total_rows = ch + src_count
    return pl.pallas_call(
        functools.partial(correlate_kernel, seg_count, chan_count, 1024),
        grid=(src_count // block,),
        out_shape=jax.ShapeDtypeStruct((src_count, ch, 2 * LAGH), jnp.float32),
        in_specs=[whole(), whole(pltpu.SMEM)] + [whole()] * 5,
        out_specs=pl.BlockSpec((block, ch, 2 * LAGH), lambda i: (i, 0, 0)),
        scratch_shapes=[
            pltpu.VMEM((steps * total_rows, dec), jnp.bfloat16),
            pltpu.VMEM((seg_count * ch, SEG), jnp.float32),
            pltpu.VMEM((seg_count * src_count, SEG), jnp.float32),
            pltpu.VMEM((block * ch, SEG), jnp.bfloat16),
        ],
        compiler_params=params,
        name="correlate",
    )(
        src,
        live_counts,
        taps,
        relaid.reshape(steps, ch, width),
        gathered.reshape(steps, chan_count * slots, width),
        jnp.asarray(dft_table(dec)),
        jnp.asarray(lag_table(seg_count)),
    )


def solution(mesh):
    placed = (P("chan", "tm"), P(), P(), P(("chan", "tm")))
    return jax.shard_map(
        local, mesh=mesh, in_specs=placed, out_specs=P(None, ("chan", "tm"), None), check_vma=False
    )
```

```python
import functools
import math

import jax
import jax.numpy as jnp
import ml_dtypes
import numpy as np
from jax import lax
from jax.experimental import pallas as pl
from jax.experimental.pallas import tpu as pltpu
from jax.sharding import PartitionSpec as P

DECIM = 10
SEG = 1024
BAND = 64
LAGH = 192
SRC_DEV = 1
LANES = 128
HALF = SEG // 2
CHUNKS = HALF // LANES
VMEM_BYTES = 56 * 1024 * 1024

whiten_eps = 1e-06

NT = (((1,), (1,)), ((), ()))


def split_table(table):
    hi = table.astype(ml_dtypes.bfloat16)
    lo = (table - hi.astype(np.float64)).astype(ml_dtypes.bfloat16)
    return hi, lo


def dft_table(rows):
    phase = (np.arange(rows)[:, None] * np.arange(HALF)[None, :] % SEG) * (2.0 * np.pi / SEG)
    parts = []
    for j in range(CHUNKS):
        cut = slice(j * LANES, (j + 1) * LANES)
        hi, lo = split_table(np.concatenate([np.cos(phase[:, cut]), -np.sin(phase[:, cut])], 1))
        parts += [hi, lo]
    return np.concatenate(parts, axis=1)


def lag_table(seg_count):
    freq = np.arange(HALF)[:, None]
    phase = (freq * np.arange(-LAGH, LAGH)[None, :] % SEG) * (2.0 * np.pi / SEG)
    weight = np.where(freq == 0, 1.0, 2.0) * (math.sqrt(SEG / seg_count) / SEG)
    re = (weight * np.cos(phase)).reshape(CHUNKS, LANES, 2 * LAGH)
    im = (-weight * np.sin(phase)).reshape(CHUNKS, LANES, 2 * LAGH)
    return np.concatenate([re, im], axis=1).reshape(SEG, 2 * LAGH).astype(ml_dtypes.bfloat16)


def iota(shape, dim):
    return lax.broadcasted_iota(jnp.int32, shape, dim)


def one_hot(mask):
    return jnp.where(mask, 1.0, 0.0).astype(jnp.bfloat16)


def column(row):
    n = row.shape[1]
    return jnp.sum(jnp.where(iota((n, n), 0) == iota((n, n), 1), row, 0), axis=1, keepdims=True)


def tap_rows(taps):
    tap_count = taps.shape[1]
    width = 3 * LANES
    flip = one_hot(iota((tap_count, width), 0) + iota((tap_count, width), 1) == tap_count)
    hi = taps.astype(jnp.bfloat16)
    lo = (taps - hi.astype(jnp.float32)).astype(jnp.bfloat16)
    out = []
    for part in (hi, lo):
        base = jnp.dot(
            jnp.broadcast_to(part.astype(jnp.float32), (8, tap_count)).astype(jnp.bfloat16),
            flip,
            preferred_element_type=jnp.float32,
        )
        upper = pltpu.roll(base, 0, 1, stride=DECIM, stride_axis=0)
        out.append(jnp.concatenate([upper, pltpu.roll(upper, 8 * DECIM, 1)], axis=0))
    return out


def filter_kernel(blocks, src_ref, taps_ref, raw_ref, chan_ref, slot_ref, ext, weight, sems):
    rows, raw_len = raw_ref.shape
    span = raw_len // blocks
    wide = span + LANES
    copies = []
    for b in range(blocks):
        if b == 0:
            copy = pltpu.make_async_copy(
                raw_ref.at[:, pl.ds(0, span)],
                ext.at[pl.ds(0, rows), pl.ds(LANES, span)],
                sems.at[b],
            )
        else:
            copy = pltpu.make_async_copy(
                raw_ref.at[:, pl.ds(b * span - LANES, wide)],
                ext.at[pl.ds(b * rows, rows), :],
                sems.at[b],
            )
        copy.start()
        copies.append(copy)
    ext[:rows, :LANES] = jnp.zeros((rows, LANES), ext.dtype)
    weight[...] = jnp.zeros_like(weight)
    for p, base in enumerate(tap_rows(taps_ref[...])):
        for i in range(LANES // 16):
            tile, lane = divmod(16 * DECIM * i, LANES)
            piece = pltpu.roll(base, lane, 1) if lane else base
            weight[p * LANES + 16 * i : p * LANES + 16 * (i + 1), tile * LANES : (tile + 3) * LANES] = (
                piece.astype(jnp.bfloat16)
            )
    src = src_ref[...]
    src_count = src.shape[1]
    slots = slot_ref.shape[0]
    group = src // rows
    group_col = column(group)
    src_col = column(src)
    rank = jnp.sum(
        jnp.where(
            (group_col == group)
            & (iota((src_count, src_count), 0) < iota((src_count, src_count), 1)),
            1,
            0,
        ),
        axis=0,
        keepdims=True,
    )
    mine = lax.axis_index("chan")
    to_slot = one_hot((iota((slots, src_count), 0) == rank) & (group == mine))
    to_row = one_hot(src_col - mine * rows == iota((src_count, rows), 1))
    pick = jnp.dot(to_slot, to_row, preferred_element_type=jnp.float32).astype(jnp.bfloat16)
    for copy in copies:
        copy.wait()
    acc = lax.dot_general(ext[...], weight[...], NT, preferred_element_type=jnp.float32)
    y = (acc[:, :LANES] + acc[:, LANES:]).astype(jnp.bfloat16)
    dec = blocks * LANES
    for b in range(blocks):
        chan_ref[:, b * LANES : (b + 1) * LANES] = y[b * rows : (b + 1) * rows]
    chan_ref[:, dec : dec + LANES] = ext[:rows, LANES : 2 * LANES]
    chan_ref[:, dec + LANES :] = ext[(blocks - 1) * rows :, wide - LANES :]
    slot_ref[...] = jnp.dot(pick, chan_ref[...], preferred_element_type=jnp.float32).astype(jnp.bfloat16)


def arrange_kernel(chan_count, src_ref, chan_ref, slots_ref, out_ref):
    steps = out_ref.shape[0]
    ch = chan_ref.shape[0] // steps
    src = src_ref[...]
    src_count = src.shape[1]
    total = slots_ref.shape[0]
    group = src // (steps * ch)
    group_col = column(group)
    rank = jnp.sum(
        jnp.where(
            (group_col == group)
            & (iota((src_count, src_count), 1) < iota((src_count, src_count), 0)),
            1,
            0,
        ),
        axis=1,
        keepdims=True,
    )
    pick = one_hot(group_col * (total // chan_count) + rank == iota((src_count, total), 1))
    found = jnp.dot(pick, slots_ref[...], preferred_element_type=jnp.float32).astype(jnp.bfloat16)
    for t in range(steps):
        out_ref[t, :ch] = chan_ref[t * ch : (t + 1) * ch]
        out_ref[t, ch:] = found


def correlate_kernel(
    seg_count, part_rows,
    live_ref, taps_ref, x_ref, d_ref, l_ref, out_ref,
    trace, own, other, cross,
):
    steps, rows, width = x_ref.shape
    ch = out_ref.shape[1]
    src_count = rows - ch
    dec = width - 2 * LANES
    per_seg = SEG // dec

    @pl.when(pl.program_id(0) == 0)
    def _():
        base = [v[:, : 2 * LANES].astype(jnp.bfloat16) for v in tap_rows(taps_ref[...])]
        empty = jnp.zeros((LANES - 16, 2 * LANES), jnp.bfloat16)
        weight = jnp.concatenate([base[0], empty, base[1], empty], axis=0)
        row_id = iota((rows, width), 0)
        live = (row_id < live_ref[0]) | (row_id >= ch)
        before = jnp.zeros((rows, LANES), jnp.bfloat16)
        head_len = -(-(taps_ref.shape[1] - 1) // DECIM)
        is_head = iota((rows, LANES), 1) < head_len
        for t in range(steps):
            both = jnp.where(live, x_ref[t], jnp.zeros((rows, width), jnp.bfloat16))
            edge = jnp.concatenate([before, both[:, dec : dec + LANES]], axis=1)
            fix = lax.dot_general(edge, weight, NT, preferred_element_type=jnp.float32)
            fix = (fix[:, :LANES] + fix[:, LANES:]).astype(jnp.bfloat16)
            trace[t * rows : (t + 1) * rows, :LANES] = jnp.where(is_head, fix, both[:, :LANES])
            trace[t * rows : (t + 1) * rows, LANES:] = both[:, LANES:dec]
            before = both[:, dec + LANES :]
        odd = (iota((rows, 2 * LANES), 1) & 1) == 1
        sign = jnp.where(odd, -1.0, 1.0)
        same = one_hot(
            iota((2 * LANES, LANES), 0) % LANES // BAND == iota((2 * LANES, LANES), 1) // BAND
        )
        group_segs = max(1, min(seg_count, part_rows // (per_seg * rows)))
        for first in range(0, seg_count, group_segs):
            segs = min(group_segs, seg_count - first)
            lhs = trace[first * per_seg * rows : (first + segs) * per_seg * rows, :]
            for j in range(CHUNKS):
                acc = jnp.dot(
                    lhs, d_ref[:, 4 * j * LANES : 4 * (j + 1) * LANES],
                    preferred_element_type=jnp.float32,
                )
                half = acc[:, : 2 * LANES] + acc[:, 2 * LANES :]
                spec = []
                for g in range(segs):
                    a = half[g * per_seg * rows : (g * per_seg + 1) * rows]
                    b = half[(g * per_seg + 1) * rows : (g * per_seg + 2) * rows]
                    spec.append(a + sign * b)
                spec = jnp.concatenate(spec, axis=0)
                re, im = spec[:, :LANES], spec[:, LANES:]
                power = re * re + im * im
                hi = power.astype(jnp.bfloat16)
                lo = (power - hi.astype(jnp.float32)).astype(jnp.bfloat16)
                total = jnp.dot(
                    jnp.concatenate([hi, lo], axis=1), same, preferred_element_type=jnp.float32
                )
                scale = lax.rsqrt(total * (1.0 / BAND) + whiten_eps)
                w_re = (re * scale).astype(jnp.bfloat16).astype(jnp.float32)
                w_im = (im * scale).astype(jnp.bfloat16).astype(jnp.float32)
                at = 2 * j * LANES
                for g in range(segs):
                    r, o = g * rows, (first + g) * ch
                    own[o : o + ch, at : at + LANES] = w_re[r : r + ch]
                    own[o : o + ch, at + LANES : at + 2 * LANES] = w_im[r : r + ch]
                    o = (first + g) * src_count
                    other[o : o + src_count, at : at + LANES] = w_re[r + ch : r + rows]
                    other[o : o + src_count, at + LANES : at + 2 * LANES] = w_im[r + ch : r + rows]

    block = out_ref.shape[0]
    start = pl.multiple_of(pl.program_id(0) * block, 8)
    for j in range(CHUNKS):
        at = 2 * j * LANES
        a_re = [own[g * ch : (g + 1) * ch, at : at + LANES] for g in range(seg_count)]
        a_im = [own[g * ch : (g + 1) * ch, at + LANES : at + 2 * LANES] for g in range(seg_count)]
        for s in range(block):
            if s % 8 == 0:
                tiles = [
                    other[pl.ds(pl.multiple_of(g * src_count + start + s, 8), 8), at : at + 2 * LANES]
                    for g in range(seg_count)
                ]
            re = im = None
            for g in range(seg_count):
                b_re = tiles[g][s % 8 : s % 8 + 1, :LANES]
                b_im = tiles[g][s % 8 : s % 8 + 1, LANES:]
                p = a_re[g] * b_re + a_im[g] * b_im
                q = a_im[g] * b_re - a_re[g] * b_im
                re, im = (p, q) if re is None else (re + p, im + q)
            cross[s * ch : (s + 1) * ch, at : at + LANES] = re.astype(jnp.bfloat16)
            cross[s * ch : (s + 1) * ch, at + LANES : at + 2 * LANES] = im.astype(jnp.bfloat16)
    lags = jnp.dot(cross[...], l_ref[...], preferred_element_type=jnp.float32)
    out_ref[...] = lags.reshape(out_ref.shape)


def whole(space=pltpu.VMEM):
    return pl.BlockSpec(memory_space=space)


def local(raw_strain, fir_taps, source_channels, live_counts):
    rows, raw_len = raw_strain.shape
    steps = lax.axis_size("tm")
    chan_count = lax.axis_size("chan")
    dec = raw_len // DECIM
    blocks = dec // LANES
    ch = rows // steps
    seg_count = steps * dec // SEG
    src_count = source_channels.shape[0]
    slots = 2 * SRC_DEV * steps
    width = dec + 2 * LANES
    span = raw_len // blocks
    src = source_channels.reshape(1, src_count)
    taps = fir_taps.reshape(1, fir_taps.shape[0])
    params = pltpu.CompilerParams(vmem_limit_bytes=VMEM_BYTES)
    packed, picked = pl.pallas_call(
        functools.partial(filter_kernel, blocks),
        out_shape=[
            jax.ShapeDtypeStruct((rows, width), jnp.bfloat16),
            jax.ShapeDtypeStruct((slots, width), jnp.bfloat16),
        ],
        in_specs=[whole(), whole(), whole(pl.ANY)],
        out_specs=[whole(), whole()],
        scratch_shapes=[
            pltpu.VMEM((blocks * rows, span + LANES), jnp.bfloat16),
            pltpu.VMEM((2 * LANES, span + LANES), jnp.bfloat16),
            pltpu.SemaphoreType.DMA((blocks,)),
        ],
        compiler_params=params,
        name="fir",
    )(src, taps, raw_strain)
    gathered = lax.all_gather(picked, "chan", axis=0, tiled=True)
    total_rows = ch + src_count
    outgoing = pl.pallas_call(
        functools.partial(arrange_kernel, chan_count),
        out_shape=jax.ShapeDtypeStruct((steps, total_rows, width), jnp.bfloat16),
        in_specs=[whole()] * 3,
        out_specs=whole(),
        compiler_params=params,
        name="arrange",
    )(src, packed, gathered)
    relaid = lax.all_to_all(outgoing, "tm", split_axis=0, concat_axis=0)
    block = math.gcd(src_count, 16)
    return pl.pallas_call(
        functools.partial(correlate_kernel, seg_count, 1024),
        grid=(src_count // block,),
        out_shape=jax.ShapeDtypeStruct((src_count, ch, 2 * LAGH), jnp.float32),
        in_specs=[whole(pltpu.SMEM)] + [whole()] * 4,
        out_specs=pl.BlockSpec((block, ch, 2 * LAGH), lambda i: (i, 0, 0)),
        scratch_shapes=[
            pltpu.VMEM((steps * total_rows, dec), jnp.bfloat16),
            pltpu.VMEM((seg_count * ch, SEG), jnp.float32),
            pltpu.VMEM((seg_count * src_count, SEG), jnp.float32),
            pltpu.VMEM((block * ch, SEG), jnp.bfloat16),
        ],
        compiler_params=params,
        name="correlate",
    )(
        live_counts,
        taps,
        relaid,
        jnp.asarray(dft_table(dec)),
        jnp.asarray(lag_table(seg_count)),
    )


def solution(mesh):
    placed = (P("chan", "tm"), P(), P(), P(("chan", "tm")))
    return jax.shard_map(
        local, mesh=mesh, in_specs=placed, out_specs=P(None, ("chan", "tm"), None), check_vma=False
    )
```

```python
import functools
import math

import jax
import jax.numpy as jnp
import ml_dtypes
import numpy as np
from jax import lax
from jax.experimental import pallas as pl
from jax.experimental.pallas import tpu as pltpu
from jax.sharding import PartitionSpec as P

DECIM = 10
SEG = 1024
BAND = 64
LAGH = 192
SRC_DEV = 1
LANES = 128
HALF = SEG // 2
CHUNKS = HALF // LANES
EDGE = 16
MIB = 1024 * 1024

whiten_eps = 1e-06

NT = (((1,), (1,)), ((), ()))


def split_table(table):
    hi = table.astype(ml_dtypes.bfloat16)
    lo = (table - hi.astype(np.float64)).astype(ml_dtypes.bfloat16)
    return hi, lo


def dft_table(rows):
    phase = (np.arange(rows)[:, None] * np.arange(HALF)[None, :] % SEG) * (2.0 * np.pi / SEG)
    parts = []
    for j in range(CHUNKS):
        cut = slice(j * LANES, (j + 1) * LANES)
        hi, lo = split_table(np.concatenate([np.cos(phase[:, cut]), -np.sin(phase[:, cut])], 1))
        parts += [hi, lo]
    return np.concatenate(parts, axis=1)


def lag_table(seg_count):
    freq = np.arange(HALF)[:, None]
    phase = (freq * np.arange(-LAGH, LAGH)[None, :] % SEG) * (2.0 * np.pi / SEG)
    weight = np.where(freq == 0, 1.0, 2.0) * (math.sqrt(SEG / seg_count) / SEG)
    re = (weight * np.cos(phase)).reshape(CHUNKS, LANES, 2 * LAGH)
    im = (-weight * np.sin(phase)).reshape(CHUNKS, LANES, 2 * LAGH)
    return np.concatenate([re, im], axis=1).reshape(SEG, 2 * LAGH).astype(ml_dtypes.bfloat16)


def iota(shape, dim):
    return lax.broadcasted_iota(jnp.int32, shape, dim)


def one_hot(mask):
    return jnp.where(mask, 1.0, 0.0).astype(jnp.bfloat16)


def column(row):
    n = row.shape[1]
    return jnp.sum(jnp.where(iota((n, n), 0) == iota((n, n), 1), row, 0), axis=1, keepdims=True)


def tap_rows(taps):
    tap_count = taps.shape[1]
    width = 3 * LANES
    flip = one_hot(iota((tap_count, width), 0) + iota((tap_count, width), 1) == tap_count)
    hi = taps.astype(jnp.bfloat16)
    lo = (taps - hi.astype(jnp.float32)).astype(jnp.bfloat16)
    out = []
    for part in (hi, lo):
        base = jnp.dot(
            jnp.broadcast_to(part.astype(jnp.float32), (8, tap_count)).astype(jnp.bfloat16),
            flip,
            preferred_element_type=jnp.float32,
        )
        upper = pltpu.roll(base, 0, 1, stride=DECIM, stride_axis=0)
        out.append(jnp.concatenate([upper, pltpu.roll(upper, 8 * DECIM, 1)], axis=0))
    return out


def filter_kernel(blocks, src_ref, taps_ref, raw_ref, chan_ref, slot_ref, ext, weight, sems):
    rows, raw_len = raw_ref.shape
    span = raw_len // blocks
    wide = span + LANES
    copies = []
    for b in range(blocks):
        if b == 0:
            copy = pltpu.make_async_copy(
                raw_ref.at[:, pl.ds(0, span)],
                ext.at[pl.ds(0, rows), pl.ds(LANES, span)],
                sems.at[b],
            )
        else:
            copy = pltpu.make_async_copy(
                raw_ref.at[:, pl.ds(b * span - LANES, wide)],
                ext.at[pl.ds(b * rows, rows), :],
                sems.at[b],
            )
        copy.start()
        copies.append(copy)
    ext[:rows, :LANES] = jnp.zeros((rows, LANES), ext.dtype)
    weight[...] = jnp.zeros_like(weight)
    for p, base in enumerate(tap_rows(taps_ref[...])):
        for i in range(LANES // 16):
            tile, lane = divmod(16 * DECIM * i, LANES)
            piece = pltpu.roll(base, lane, 1) if lane else base
            weight[p * LANES + 16 * i : p * LANES + 16 * (i + 1), tile * LANES : (tile + 3) * LANES] = (
                piece.astype(jnp.bfloat16)
            )
    src = src_ref[...]
    src_count = src.shape[1]
    slots = slot_ref.shape[0]
    group = src // rows
    group_col = column(group)
    src_col = column(src)
    rank = jnp.sum(
        jnp.where(
            (group_col == group)
            & (iota((src_count, src_count), 0) < iota((src_count, src_count), 1)),
            1,
            0,
        ),
        axis=0,
        keepdims=True,
    )
    mine = lax.axis_index("chan")
    to_slot = one_hot((iota((slots, src_count), 0) == rank) & (group == mine))
    to_row = one_hot(src_col - mine * rows == iota((src_count, rows), 1))
    pick = jnp.dot(to_slot, to_row, preferred_element_type=jnp.float32).astype(jnp.bfloat16)
    for copy in copies:
        copy.wait()
    acc = lax.dot_general(ext[...], weight[...], NT, preferred_element_type=jnp.float32)
    y = (acc[:, :LANES] + acc[:, LANES:]).astype(jnp.bfloat16)
    dec = blocks * LANES
    for b in range(blocks):
        chan_ref[:, b * LANES : (b + 1) * LANES] = y[b * rows : (b + 1) * rows]
    head = acc[:rows, :LANES] + acc[:rows, LANES:]
    head_lo = head - head.astype(jnp.bfloat16).astype(jnp.float32)
    tail = lax.dot_general(
        ext[(blocks - 1) * rows :, wide - LANES :], weight[:, :LANES], NT,
        preferred_element_type=jnp.float32,
    )
    tail = tail[:, :LANES] + tail[:, LANES:]
    tail_hi = tail.astype(jnp.bfloat16).astype(jnp.float32)
    lane = iota((rows, LANES), 1)
    edge = jnp.where(
        lane < EDGE,
        head_lo,
        jnp.where(
            lane < 2 * EDGE,
            pltpu.roll(tail_hi, EDGE, 1),
            pltpu.roll(tail - tail_hi, 2 * EDGE, 1),
        ),
    )
    chan_ref[:, dec:] = edge.astype(jnp.bfloat16)
    slot_ref[...] = jnp.dot(pick, chan_ref[...], preferred_element_type=jnp.float32).astype(jnp.bfloat16)


def arrange_kernel(chan_count, src_ref, chan_ref, slots_ref, out_ref):
    steps = out_ref.shape[0]
    ch = chan_ref.shape[0] // steps
    src = src_ref[...]
    src_count = src.shape[1]
    total = slots_ref.shape[0]
    group = src // (steps * ch)
    group_col = column(group)
    rank = jnp.sum(
        jnp.where(
            (group_col == group)
            & (iota((src_count, src_count), 1) < iota((src_count, src_count), 0)),
            1,
            0,
        ),
        axis=1,
        keepdims=True,
    )
    pick = one_hot(group_col * (total // chan_count) + rank == iota((src_count, total), 1))
    found = jnp.dot(pick, slots_ref[...], preferred_element_type=jnp.float32).astype(jnp.bfloat16)
    for t in range(steps):
        out_ref[t, :ch] = chan_ref[t * ch : (t + 1) * ch]
        out_ref[t, ch:] = found


def correlate_kernel(
    seg_count, head_len, part_rows,
    live_ref, x_ref, d_ref, l_ref, out_ref,
    trace, own, other, cross,
):
    steps, rows, width = x_ref.shape
    ch = out_ref.shape[1]
    src_count = rows - ch
    dec = width - LANES
    per_seg = SEG // dec

    @pl.when(pl.program_id(0) == 0)
    def _():
        row_id = iota((rows, width), 0)
        live = (row_id < live_ref[0]) | (row_id >= ch)
        before = jnp.zeros((rows, LANES), jnp.float32)
        is_head = iota((rows, LANES), 1) < head_len
        for t in range(steps):
            both = jnp.where(live, x_ref[t], jnp.zeros((rows, width), jnp.bfloat16))
            first = both[:, :LANES].astype(jnp.float32)
            edge = both[:, dec:].astype(jnp.float32)
            tail = pltpu.roll(before, LANES - EDGE, 1) + pltpu.roll(before, LANES - 2 * EDGE, 1)
            first = jnp.where(is_head, first + edge + tail, first)
            trace[t * rows : (t + 1) * rows, :LANES] = first.astype(jnp.bfloat16)
            trace[t * rows : (t + 1) * rows, LANES:] = both[:, LANES:dec]
            before = edge
        odd = (iota((rows, 2 * LANES), 1) & 1) == 1
        sign = jnp.where(odd, -1.0, 1.0)
        same = one_hot(
            iota((2 * LANES, LANES), 0) % LANES // BAND == iota((2 * LANES, LANES), 1) // BAND
        )
        group_segs = max(1, min(seg_count, part_rows // (per_seg * rows)))
        for first in range(0, seg_count, group_segs):
            segs = min(group_segs, seg_count - first)
            lhs = trace[first * per_seg * rows : (first + segs) * per_seg * rows, :]
            for j in range(CHUNKS):
                acc = jnp.dot(
                    lhs, d_ref[:, 4 * j * LANES : 4 * (j + 1) * LANES],
                    preferred_element_type=jnp.float32,
                )
                half = acc[:, : 2 * LANES] + acc[:, 2 * LANES :]
                spec = []
                for g in range(segs):
                    a = half[g * per_seg * rows : (g * per_seg + 1) * rows]
                    b = half[(g * per_seg + 1) * rows : (g * per_seg + 2) * rows]
                    spec.append(a + sign * b)
                spec = jnp.concatenate(spec, axis=0)
                re, im = spec[:, :LANES], spec[:, LANES:]
                power = re * re + im * im
                hi = power.astype(jnp.bfloat16)
                lo = (power - hi.astype(jnp.float32)).astype(jnp.bfloat16)
                total = jnp.dot(
                    jnp.concatenate([hi, lo], axis=1), same, preferred_element_type=jnp.float32
                )
                scale = lax.rsqrt(total * (1.0 / BAND) + whiten_eps)
                w_re = (re * scale).astype(jnp.bfloat16).astype(jnp.float32)
                w_im = (im * scale).astype(jnp.bfloat16).astype(jnp.float32)
                at = 2 * j * LANES
                for g in range(segs):
                    r, o = g * rows, (first + g) * ch
                    own[o : o + ch, at : at + LANES] = w_re[r : r + ch]
                    own[o : o + ch, at + LANES : at + 2 * LANES] = w_im[r : r + ch]
                    o = (first + g) * src_count
                    other[o : o + src_count, at : at + LANES] = w_re[r + ch : r + rows]
                    other[o : o + src_count, at + LANES : at + 2 * LANES] = w_im[r + ch : r + rows]

    block = out_ref.shape[0]
    start = pl.multiple_of(pl.program_id(0) * block, 8)
    for j in range(CHUNKS):
        at = 2 * j * LANES
        a_re = [own[g * ch : (g + 1) * ch, at : at + LANES] for g in range(seg_count)]
        a_im = [own[g * ch : (g + 1) * ch, at + LANES : at + 2 * LANES] for g in range(seg_count)]
        for s in range(block):
            if s % 8 == 0:
                tiles = [
                    other[pl.ds(pl.multiple_of(g * src_count + start + s, 8), 8), at : at + 2 * LANES]
                    for g in range(seg_count)
                ]
            re = im = None
            for g in range(seg_count):
                b_re = tiles[g][s % 8 : s % 8 + 1, :LANES]
                b_im = tiles[g][s % 8 : s % 8 + 1, LANES:]
                p = a_re[g] * b_re + a_im[g] * b_im
                q = a_im[g] * b_re - a_re[g] * b_im
                re, im = (p, q) if re is None else (re + p, im + q)
            cross[s * ch : (s + 1) * ch, at : at + LANES] = re.astype(jnp.bfloat16)
            cross[s * ch : (s + 1) * ch, at + LANES : at + 2 * LANES] = im.astype(jnp.bfloat16)
    lags = jnp.dot(cross[...], l_ref[...], preferred_element_type=jnp.float32)
    out_ref[...] = lags.reshape(out_ref.shape)


def whole(space=pltpu.VMEM):
    return pl.BlockSpec(memory_space=space)


def local(raw_strain, fir_taps, source_channels, live_counts):
    rows, raw_len = raw_strain.shape
    steps = lax.axis_size("tm")
    chan_count = lax.axis_size("chan")
    dec = raw_len // DECIM
    blocks = dec // LANES
    ch = rows // steps
    seg_count = steps * dec // SEG
    src_count = source_channels.shape[0]
    slots = 2 * SRC_DEV * steps
    width = dec + LANES
    span = raw_len // blocks
    src = source_channels.reshape(1, src_count)
    taps = fir_taps.reshape(1, fir_taps.shape[0])
    params = pltpu.CompilerParams(vmem_limit_bytes=12 * MIB)
    packed, picked = pl.pallas_call(
        functools.partial(filter_kernel, blocks),
        out_shape=[
            jax.ShapeDtypeStruct((rows, width), jnp.bfloat16),
            jax.ShapeDtypeStruct((slots, width), jnp.bfloat16),
        ],
        in_specs=[whole(), whole(), whole(pl.ANY)],
        out_specs=[whole(), whole()],
        scratch_shapes=[
            pltpu.VMEM((blocks * rows, span + LANES), jnp.bfloat16),
            pltpu.VMEM((2 * LANES, span + LANES), jnp.bfloat16),
            pltpu.SemaphoreType.DMA((blocks,)),
        ],
        compiler_params=pltpu.CompilerParams(vmem_limit_bytes=60 * MIB),
        name="fir",
    )(src, taps, raw_strain)
    gathered = lax.all_gather(picked, "chan", axis=0, tiled=True)
    total_rows = ch + src_count
    outgoing = pl.pallas_call(
        functools.partial(arrange_kernel, chan_count),
        out_shape=jax.ShapeDtypeStruct((steps, total_rows, width), jnp.bfloat16),
        in_specs=[whole()] * 3,
        out_specs=whole(),
        compiler_params=params,
        name="arrange",
    )(src, packed, gathered)
    relaid = lax.all_to_all(outgoing, "tm", split_axis=0, concat_axis=0)
    block = math.gcd(src_count, 16)
    head_len = -(-(fir_taps.shape[0] - 1) // DECIM)
    assert head_len <= EDGE
    state = seg_count * total_rows * SEG * 4
    return pl.pallas_call(
        functools.partial(correlate_kernel, seg_count, head_len, 1024),
        grid=(src_count // block,),
        out_shape=jax.ShapeDtypeStruct((src_count, ch, 2 * LAGH), jnp.float32),
        in_specs=[whole(pltpu.SMEM)] + [whole()] * 3,
        out_specs=pl.BlockSpec((block, ch, 2 * LAGH), lambda i: (i, 0, 0)),
        scratch_shapes=[
            pltpu.VMEM((steps * total_rows, dec), jnp.bfloat16),
            pltpu.VMEM((seg_count * ch, SEG), jnp.float32),
            pltpu.VMEM((seg_count * src_count, SEG), jnp.float32),
            pltpu.VMEM((block * ch, SEG), jnp.bfloat16),
        ],
        compiler_params=pltpu.CompilerParams(vmem_limit_bytes=16 * MIB + 2 * state),
        name="correlate",
    )(
        live_counts,
        relaid,
        jnp.asarray(dft_table(dec)),
        jnp.asarray(lag_table(seg_count)),
    )


def solution(mesh):
    placed = (P("chan", "tm"), P(), P(), P(("chan", "tm")))
    return jax.shard_map(
        local, mesh=mesh, in_specs=placed, out_specs=P(None, ("chan", "tm"), None), check_vma=False
    )
```

```python
import functools
import math

import jax
import jax.numpy as jnp
import ml_dtypes
import numpy as np
from jax import lax
from jax.experimental import pallas as pl
from jax.experimental.pallas import tpu as pltpu
from jax.sharding import PartitionSpec as P

DECIM = 10
SEG = 1024
BAND = 64
LAGH = 192
SRC_DEV = 1
LANES = 128
HALF = SEG // 2
CHUNKS = HALF // LANES
EDGE = 16
CORES = 2
MIB = 1024 * 1024

whiten_eps = 1e-06

NT = (((1,), (1,)), ((), ()))


def split_table(table):
    hi = table.astype(ml_dtypes.bfloat16)
    lo = (table - hi.astype(np.float64)).astype(ml_dtypes.bfloat16)
    return hi, lo


def dft_table(rows):
    phase = (np.arange(rows)[:, None] * np.arange(HALF)[None, :] % SEG) * (2.0 * np.pi / SEG)
    parts = []
    for j in range(CHUNKS):
        cut = slice(j * LANES, (j + 1) * LANES)
        hi, lo = split_table(np.concatenate([np.cos(phase[:, cut]), -np.sin(phase[:, cut])], 1))
        parts += [hi, lo]
    return np.concatenate(parts, axis=1)


def lag_table(seg_count):
    freq = np.arange(HALF)[:, None]
    phase = (freq * np.arange(-LAGH, LAGH)[None, :] % SEG) * (2.0 * np.pi / SEG)
    weight = np.where(freq == 0, 1.0, 2.0) * (math.sqrt(SEG / seg_count) / SEG)
    re = (weight * np.cos(phase)).reshape(CHUNKS, LANES, 2 * LAGH)
    im = (-weight * np.sin(phase)).reshape(CHUNKS, LANES, 2 * LAGH)
    return np.concatenate([re, im], axis=1).reshape(SEG, 2 * LAGH).astype(ml_dtypes.bfloat16)


def iota(shape, dim):
    return lax.broadcasted_iota(jnp.int32, shape, dim)


def one_hot(mask):
    return jnp.where(mask, 1.0, 0.0).astype(jnp.bfloat16)


def column(row):
    n = row.shape[1]
    return jnp.sum(jnp.where(iota((n, n), 0) == iota((n, n), 1), row, 0), axis=1, keepdims=True)


def tap_rows(taps):
    tap_count = taps.shape[1]
    width = 3 * LANES
    flip = one_hot(iota((tap_count, width), 0) + iota((tap_count, width), 1) == tap_count)
    hi = taps.astype(jnp.bfloat16)
    lo = (taps - hi.astype(jnp.float32)).astype(jnp.bfloat16)
    out = []
    for part in (hi, lo):
        base = jnp.dot(
            jnp.broadcast_to(part.astype(jnp.float32), (8, tap_count)).astype(jnp.bfloat16),
            flip,
            preferred_element_type=jnp.float32,
        )
        upper = pltpu.roll(base, 0, 1, stride=DECIM, stride_axis=0)
        out.append(jnp.concatenate([upper, pltpu.roll(upper, 8 * DECIM, 1)], axis=0))
    return out


def filter_kernel(blocks, src_ref, taps_ref, raw_ref, chan_ref, slot_ref, ext, weight, sems):
    rows, raw_len = raw_ref.shape
    span = raw_len // blocks
    wide = span + LANES
    copies = []
    for b in range(blocks):
        if b == 0:
            copy = pltpu.make_async_copy(
                raw_ref.at[:, pl.ds(0, span)],
                ext.at[pl.ds(0, rows), pl.ds(LANES, span)],
                sems.at[b],
            )
        else:
            copy = pltpu.make_async_copy(
                raw_ref.at[:, pl.ds(b * span - LANES, wide)],
                ext.at[pl.ds(b * rows, rows), :],
                sems.at[b],
            )
        copy.start()
        copies.append(copy)
    ext[:rows, :LANES] = jnp.zeros((rows, LANES), ext.dtype)
    weight[...] = jnp.zeros_like(weight)
    for p, base in enumerate(tap_rows(taps_ref[...])):
        for i in range(LANES // 16):
            tile, lane = divmod(16 * DECIM * i, LANES)
            piece = pltpu.roll(base, lane, 1) if lane else base
            weight[p * LANES + 16 * i : p * LANES + 16 * (i + 1), tile * LANES : (tile + 3) * LANES] = (
                piece.astype(jnp.bfloat16)
            )
    src = src_ref[...]
    src_count = src.shape[1]
    slots = slot_ref.shape[1]
    group = src // rows
    group_col = column(group)
    src_col = column(src)
    rank = jnp.sum(
        jnp.where(
            (group_col == group)
            & (iota((src_count, src_count), 0) < iota((src_count, src_count), 1)),
            1,
            0,
        ),
        axis=0,
        keepdims=True,
    )
    mine = lax.axis_index("chan")
    to_slot = one_hot((iota((slots, src_count), 0) == rank) & (group == mine))
    to_row = one_hot(src_col - mine * rows == iota((src_count, rows), 1))
    pick = jnp.dot(to_slot, to_row, preferred_element_type=jnp.float32).astype(jnp.bfloat16)
    for copy in copies:
        copy.wait()
    acc = lax.dot_general(ext[...], weight[...], NT, preferred_element_type=jnp.float32)
    y = (acc[:, :LANES] + acc[:, LANES:]).astype(jnp.bfloat16)
    dec = blocks * LANES
    for b in range(blocks):
        chan_ref[:, b * LANES : (b + 1) * LANES] = y[b * rows : (b + 1) * rows]
    head = acc[:rows, :LANES] + acc[:rows, LANES:]
    head_lo = head - head.astype(jnp.bfloat16).astype(jnp.float32)
    tail = lax.dot_general(
        ext[(blocks - 1) * rows :, wide - LANES :], weight[:, :LANES], NT,
        preferred_element_type=jnp.float32,
    )
    tail = tail[:, :LANES] + tail[:, LANES:]
    tail_hi = tail.astype(jnp.bfloat16).astype(jnp.float32)
    lane = iota((rows, LANES), 1)
    edge = jnp.where(
        lane < EDGE,
        head_lo,
        jnp.where(
            lane < 2 * EDGE,
            pltpu.roll(tail_hi, EDGE, 1),
            pltpu.roll(tail - tail_hi, 2 * EDGE, 1),
        ),
    )
    chan_ref[:, dec:] = edge.astype(jnp.bfloat16)
    found = jnp.dot(pick, chan_ref[...], preferred_element_type=jnp.float32).astype(jnp.bfloat16)
    for peer in range(slot_ref.shape[0]):
        slot_ref[peer] = found


def correlate_kernel(
    seg_count, chan_count, head_len, part_rows,
    src_ref, live_ref, x_ref, near_ref, far_ref, d_ref, l_ref, out_ref,
    trace, own, other, cross,
):
    steps, ch, width = x_ref.shape
    src_count = src_ref.shape[1]
    rows = ch + src_count
    dec = width - LANES
    per_seg = SEG // dec

    @pl.when(pl.program_id(0) == 0)
    def _():
        src = src_ref[...]
        held = near_ref.shape[1]
        group = src // (steps * ch)
        group_col = column(group)
        rank = jnp.sum(
            jnp.where(
                (group_col == group)
                & (iota((src_count, src_count), 1) < iota((src_count, src_count), 0)),
                1,
                0,
            ),
            axis=1,
            keepdims=True,
        )
        slots = held * CORES // chan_count
        place = group_col // CORES * slots + rank
        place += jnp.where(group_col % CORES == lax.axis_index("chan") % CORES, 0, held)
        pick = one_hot(place == iota((src_count, 2 * held), 1))
        live = iota((ch, width), 0) < live_ref[0]
        before = jnp.zeros((rows, LANES), jnp.float32)
        is_head = iota((rows, LANES), 1) < head_len
        for t in range(steps):
            mine = jnp.where(live, x_ref[t], jnp.zeros((ch, width), jnp.bfloat16))
            theirs = jnp.dot(
                pick, jnp.concatenate([near_ref[t], far_ref[t]], axis=0),
                preferred_element_type=jnp.float32,
            ).astype(jnp.bfloat16)
            both = jnp.concatenate([mine, theirs], axis=0)
            first = both[:, :LANES].astype(jnp.float32)
            edge = both[:, dec:].astype(jnp.float32)
            tail = pltpu.roll(before, LANES - EDGE, 1) + pltpu.roll(before, LANES - 2 * EDGE, 1)
            first = jnp.where(is_head, first + edge + tail, first)
            trace[t * rows : (t + 1) * rows, :LANES] = first.astype(jnp.bfloat16)
            trace[t * rows : (t + 1) * rows, LANES:] = both[:, LANES:dec]
            before = edge
        odd = (iota((rows, 2 * LANES), 1) & 1) == 1
        sign = jnp.where(odd, -1.0, 1.0)
        same = one_hot(
            iota((2 * LANES, LANES), 0) % LANES // BAND == iota((2 * LANES, LANES), 1) // BAND
        )
        group_segs = max(1, min(seg_count, part_rows // (per_seg * rows)))
        for first in range(0, seg_count, group_segs):
            segs = min(group_segs, seg_count - first)
            lhs = trace[first * per_seg * rows : (first + segs) * per_seg * rows, :]
            for j in range(CHUNKS):
                acc = jnp.dot(
                    lhs, d_ref[:, 4 * j * LANES : 4 * (j + 1) * LANES],
                    preferred_element_type=jnp.float32,
                )
                half = acc[:, : 2 * LANES] + acc[:, 2 * LANES :]
                spec = []
                for g in range(segs):
                    a = half[g * per_seg * rows : (g * per_seg + 1) * rows]
                    b = half[(g * per_seg + 1) * rows : (g * per_seg + 2) * rows]
                    spec.append(a + sign * b)
                spec = jnp.concatenate(spec, axis=0)
                re, im = spec[:, :LANES], spec[:, LANES:]
                power = re * re + im * im
                hi = power.astype(jnp.bfloat16)
                lo = (power - hi.astype(jnp.float32)).astype(jnp.bfloat16)
                total = jnp.dot(
                    jnp.concatenate([hi, lo], axis=1), same, preferred_element_type=jnp.float32
                )
                scale = lax.rsqrt(total * (1.0 / BAND) + whiten_eps)
                w_re = (re * scale).astype(jnp.bfloat16).astype(jnp.float32)
                w_im = (im * scale).astype(jnp.bfloat16).astype(jnp.float32)
                at = 2 * j * LANES
                for g in range(segs):
                    r, o = g * rows, (first + g) * ch
                    own[o : o + ch, at : at + LANES] = w_re[r : r + ch]
                    own[o : o + ch, at + LANES : at + 2 * LANES] = w_im[r : r + ch]
                    o = (first + g) * src_count
                    other[o : o + src_count, at : at + LANES] = w_re[r + ch : r + rows]
                    other[o : o + src_count, at + LANES : at + 2 * LANES] = w_im[r + ch : r + rows]

    block = out_ref.shape[0]
    start = pl.multiple_of(pl.program_id(0) * block, 8)
    for j in range(CHUNKS):
        at = 2 * j * LANES
        a_re = [own[g * ch : (g + 1) * ch, at : at + LANES] for g in range(seg_count)]
        a_im = [own[g * ch : (g + 1) * ch, at + LANES : at + 2 * LANES] for g in range(seg_count)]
        for s in range(block):
            if s % 8 == 0:
                tiles = [
                    other[pl.ds(pl.multiple_of(g * src_count + start + s, 8), 8), at : at + 2 * LANES]
                    for g in range(seg_count)
                ]
            re = im = None
            for g in range(seg_count):
                b_re = tiles[g][s % 8 : s % 8 + 1, :LANES]
                b_im = tiles[g][s % 8 : s % 8 + 1, LANES:]
                p = a_re[g] * b_re + a_im[g] * b_im
                q = a_im[g] * b_re - a_re[g] * b_im
                re, im = (p, q) if re is None else (re + p, im + q)
            cross[s * ch : (s + 1) * ch, at : at + LANES] = re.astype(jnp.bfloat16)
            cross[s * ch : (s + 1) * ch, at + LANES : at + 2 * LANES] = im.astype(jnp.bfloat16)
    lags = jnp.dot(cross[...], l_ref[...], preferred_element_type=jnp.float32)
    out_ref[...] = lags.reshape(out_ref.shape)


def whole(space=pltpu.VMEM):
    return pl.BlockSpec(memory_space=space)


def local(raw_strain, fir_taps, source_channels, live_counts):
    rows, raw_len = raw_strain.shape
    steps = lax.axis_size("tm")
    chan_count = lax.axis_size("chan")
    dec = raw_len // DECIM
    blocks = dec // LANES
    ch = rows // steps
    seg_count = steps * dec // SEG
    src_count = source_channels.shape[0]
    slots = 2 * SRC_DEV * steps
    peers = steps * chan_count // CORES
    width = dec + LANES
    span = raw_len // blocks
    src = source_channels.reshape(1, src_count)
    taps = fir_taps.reshape(1, fir_taps.shape[0])
    packed, picked = pl.pallas_call(
        functools.partial(filter_kernel, blocks),
        out_shape=[
            jax.ShapeDtypeStruct((rows, width), jnp.bfloat16),
            jax.ShapeDtypeStruct((peers, slots, width), jnp.bfloat16),
        ],
        in_specs=[whole(), whole(), whole(pl.ANY)],
        out_specs=[whole(), whole()],
        scratch_shapes=[
            pltpu.VMEM((blocks * rows, span + LANES), jnp.bfloat16),
            pltpu.VMEM((2 * LANES, span + LANES), jnp.bfloat16),
            pltpu.SemaphoreType.DMA((blocks,)),
        ],
        compiler_params=pltpu.CompilerParams(vmem_limit_bytes=60 * MIB),
        name="fir",
    )(src, taps, raw_strain)
    alike = [
        [t * chan_count + c for t in range(steps) for c in range(core, chan_count, CORES)]
        for core in range(CORES)
    ]
    near = lax.all_to_all(picked, ("tm", "chan"), 0, 0, axis_index_groups=alike, tiled=True)
    far = lax.ppermute(near, "chan", [(c, c ^ 1) for c in range(chan_count)])
    held = (steps, peers // steps * slots, width)
    relaid = lax.all_to_all(packed.reshape(steps, ch, width), "tm", 0, 0, tiled=True)
    total_rows = ch + src_count
    block = math.gcd(src_count, 16)
    head_len = -(-(fir_taps.shape[0] - 1) // DECIM)
    assert head_len <= EDGE
    state = seg_count * total_rows * SEG * 4
    return pl.pallas_call(
        functools.partial(correlate_kernel, seg_count, chan_count, head_len, 1024),
        grid=(src_count // block,),
        out_shape=jax.ShapeDtypeStruct((src_count, ch, 2 * LAGH), jnp.float32),
        in_specs=[whole(), whole(pltpu.SMEM)] + [whole()] * 5,
        out_specs=pl.BlockSpec((block, ch, 2 * LAGH), lambda i: (i, 0, 0)),
        scratch_shapes=[
            pltpu.VMEM((steps * total_rows, dec), jnp.bfloat16),
            pltpu.VMEM((seg_count * ch, SEG), jnp.float32),
            pltpu.VMEM((seg_count * src_count, SEG), jnp.float32),
            pltpu.VMEM((block * ch, SEG), jnp.bfloat16),
        ],
        compiler_params=pltpu.CompilerParams(vmem_limit_bytes=16 * MIB + 2 * state),
        name="correlate",
    )(
        src,
        live_counts,
        relaid,
        near.reshape(held),
        far.reshape(held),
        jnp.asarray(dft_table(dec)),
        jnp.asarray(lag_table(seg_count)),
    )


def solution(mesh):
    placed = (P("chan", "tm"), P(), P(), P(("chan", "tm")))
    return jax.shard_map(
        local, mesh=mesh, in_specs=placed, out_specs=P(None, ("chan", "tm"), None), check_vma=False
    )
```

```python
import functools
import math

import jax
import jax.numpy as jnp
import ml_dtypes
import numpy as np
from jax import lax
from jax.experimental import pallas as pl
from jax.experimental.pallas import tpu as pltpu
from jax.sharding import Mesh
from jax.sharding import PartitionSpec as P

DECIM = 10
SEG = 1024
BAND = 64
LAGH = 192
SRC_DEV = 1
LANES = 128
HALF = SEG // 2
CHUNKS = HALF // LANES
EDGE = 16
CORES = 2
MIB = 1024 * 1024

whiten_eps = 1e-06

NT = (((1,), (1,)), ((), ()))


def split_table(table):
    hi = table.astype(ml_dtypes.bfloat16)
    lo = (table - hi.astype(np.float64)).astype(ml_dtypes.bfloat16)
    return hi, lo


def dft_table(rows):
    phase = (np.arange(rows)[:, None] * np.arange(HALF)[None, :] % SEG) * (2.0 * np.pi / SEG)
    parts = []
    for j in range(CHUNKS):
        cut = slice(j * LANES, (j + 1) * LANES)
        hi, lo = split_table(np.concatenate([np.cos(phase[:, cut]), -np.sin(phase[:, cut])], 1))
        parts += [hi, lo]
    return np.concatenate(parts, axis=1)


def lag_table(seg_count):
    freq = np.arange(HALF)[:, None]
    phase = (freq * np.arange(-LAGH, LAGH)[None, :] % SEG) * (2.0 * np.pi / SEG)
    weight = np.where(freq == 0, 1.0, 2.0) * (math.sqrt(SEG / seg_count) / SEG)
    re = (weight * np.cos(phase)).reshape(CHUNKS, LANES, 2 * LAGH)
    im = (-weight * np.sin(phase)).reshape(CHUNKS, LANES, 2 * LAGH)
    return np.concatenate([re, im], axis=1).reshape(SEG, 2 * LAGH).astype(ml_dtypes.bfloat16)


def iota(shape, dim):
    return lax.broadcasted_iota(jnp.int32, shape, dim)


def one_hot(mask):
    return jnp.where(mask, 1.0, 0.0).astype(jnp.bfloat16)


def column(row):
    n = row.shape[1]
    return jnp.sum(jnp.where(iota((n, n), 0) == iota((n, n), 1), row, 0), axis=1, keepdims=True)


def tap_rows(taps):
    tap_count = taps.shape[1]
    width = 3 * LANES
    flip = one_hot(iota((tap_count, width), 0) + iota((tap_count, width), 1) == tap_count)
    hi = taps.astype(jnp.bfloat16)
    lo = (taps - hi.astype(jnp.float32)).astype(jnp.bfloat16)
    out = []
    for part in (hi, lo):
        base = jnp.dot(
            jnp.broadcast_to(part.astype(jnp.float32), (8, tap_count)).astype(jnp.bfloat16),
            flip,
            preferred_element_type=jnp.float32,
        )
        upper = pltpu.roll(base, 0, 1, stride=DECIM, stride_axis=0)
        out.append(jnp.concatenate([upper, pltpu.roll(upper, 8 * DECIM, 1)], axis=0))
    return out


def filter_kernel(blocks, src_ref, taps_ref, raw_ref, chan_ref, slot_ref, ext, weight, sems):
    rows, raw_len = raw_ref.shape
    span = raw_len // blocks
    wide = span + LANES
    copies = []
    for b in range(blocks):
        if b == 0:
            copy = pltpu.make_async_copy(
                raw_ref.at[:, pl.ds(0, span)],
                ext.at[pl.ds(0, rows), pl.ds(LANES, span)],
                sems.at[b],
            )
        else:
            copy = pltpu.make_async_copy(
                raw_ref.at[:, pl.ds(b * span - LANES, wide)],
                ext.at[pl.ds(b * rows, rows), :],
                sems.at[b],
            )
        copy.start()
        copies.append(copy)
    ext[:rows, :LANES] = jnp.zeros((rows, LANES), ext.dtype)
    weight[...] = jnp.zeros_like(weight)
    for p, base in enumerate(tap_rows(taps_ref[...])):
        for i in range(LANES // 16):
            tile, lane = divmod(16 * DECIM * i, LANES)
            piece = pltpu.roll(base, lane, 1) if lane else base
            weight[p * LANES + 16 * i : p * LANES + 16 * (i + 1), tile * LANES : (tile + 3) * LANES] = (
                piece.astype(jnp.bfloat16)
            )
    src = src_ref[...]
    src_count = src.shape[1]
    slots = slot_ref.shape[1]
    group = src // rows
    group_col = column(group)
    src_col = column(src)
    rank = jnp.sum(
        jnp.where(
            (group_col == group)
            & (iota((src_count, src_count), 0) < iota((src_count, src_count), 1)),
            1,
            0,
        ),
        axis=0,
        keepdims=True,
    )
    mine = lax.axis_index("cx") * CORES + lax.axis_index("core")
    to_slot = one_hot((iota((slots, src_count), 0) == rank) & (group == mine))
    to_row = one_hot(src_col - mine * rows == iota((src_count, rows), 1))
    pick = jnp.dot(to_slot, to_row, preferred_element_type=jnp.float32).astype(jnp.bfloat16)
    for copy in copies:
        copy.wait()
    acc = lax.dot_general(ext[...], weight[...], NT, preferred_element_type=jnp.float32)
    y = (acc[:, :LANES] + acc[:, LANES:]).astype(jnp.bfloat16)
    dec = blocks * LANES
    for b in range(blocks):
        chan_ref[:, b * LANES : (b + 1) * LANES] = y[b * rows : (b + 1) * rows]
    head = acc[:rows, :LANES] + acc[:rows, LANES:]
    head_lo = head - head.astype(jnp.bfloat16).astype(jnp.float32)
    tail = lax.dot_general(
        ext[(blocks - 1) * rows :, wide - LANES :], weight[:, :LANES], NT,
        preferred_element_type=jnp.float32,
    )
    tail = tail[:, :LANES] + tail[:, LANES:]
    tail_hi = tail.astype(jnp.bfloat16).astype(jnp.float32)
    lane = iota((rows, LANES), 1)
    edge = jnp.where(
        lane < EDGE,
        head_lo,
        jnp.where(
            lane < 2 * EDGE,
            pltpu.roll(tail_hi, EDGE, 1),
            pltpu.roll(tail - tail_hi, 2 * EDGE, 1),
        ),
    )
    chan_ref[:, dec:] = edge.astype(jnp.bfloat16)
    found = jnp.dot(pick, chan_ref[...], preferred_element_type=jnp.float32).astype(jnp.bfloat16)
    for peer in range(slot_ref.shape[0]):
        slot_ref[peer] = found


def correlate_kernel(
    seg_count, chan_count, head_len, part_rows,
    src_ref, live_ref, x_ref, near_ref, far_ref, d_ref, l_ref, out_ref,
    trace, own, other, cross, lag, lag_sem,
):
    steps, ch, width = x_ref.shape
    src_count = src_ref.shape[1]
    rows = ch + src_count
    dec = width - LANES
    per_seg = SEG // dec

    @pl.when(pl.program_id(0) == 0)
    def _():
        fetch = pltpu.make_async_copy(l_ref, lag, lag_sem)
        fetch.start()
        src = src_ref[...]
        held = near_ref.shape[1]
        group = src // (steps * ch)
        group_col = column(group)
        rank = jnp.sum(
            jnp.where(
                (group_col == group)
                & (iota((src_count, src_count), 1) < iota((src_count, src_count), 0)),
                1,
                0,
            ),
            axis=1,
            keepdims=True,
        )
        slots = held * CORES // chan_count
        place = group_col // CORES * slots + rank
        place += jnp.where(group_col % CORES == lax.axis_index("core"), 0, held)
        pick = one_hot(place == iota((src_count, 2 * held), 1))
        live = iota((ch, width), 0) < live_ref[0]
        before = jnp.zeros((rows, LANES), jnp.float32)
        is_head = iota((rows, LANES), 1) < head_len
        for t in range(steps):
            mine = jnp.where(live, x_ref[t], jnp.zeros((ch, width), jnp.bfloat16))
            theirs = jnp.dot(
                pick, jnp.concatenate([near_ref[t], far_ref[t]], axis=0),
                preferred_element_type=jnp.float32,
            ).astype(jnp.bfloat16)
            both = jnp.concatenate([mine, theirs], axis=0)
            first = both[:, :LANES].astype(jnp.float32)
            edge = both[:, dec:].astype(jnp.float32)
            tail = pltpu.roll(before, LANES - EDGE, 1) + pltpu.roll(before, LANES - 2 * EDGE, 1)
            first = jnp.where(is_head, first + edge + tail, first)
            trace[t * rows : (t + 1) * rows, :LANES] = first.astype(jnp.bfloat16)
            trace[t * rows : (t + 1) * rows, LANES:] = both[:, LANES:dec]
            before = edge
        odd = (iota((rows, 2 * LANES), 1) & 1) == 1
        sign = jnp.where(odd, -1.0, 1.0)
        same = one_hot(
            iota((2 * LANES, LANES), 0) % LANES // BAND == iota((2 * LANES, LANES), 1) // BAND
        )
        group_segs = max(1, min(seg_count, part_rows // (per_seg * rows)))
        for first in range(0, seg_count, group_segs):
            segs = min(group_segs, seg_count - first)
            lhs = trace[first * per_seg * rows : (first + segs) * per_seg * rows, :]
            for j in range(CHUNKS):
                acc = jnp.dot(
                    lhs, d_ref[:, 4 * j * LANES : 4 * (j + 1) * LANES],
                    preferred_element_type=jnp.float32,
                )
                half = acc[:, : 2 * LANES] + acc[:, 2 * LANES :]
                spec = []
                for g in range(segs):
                    a = half[g * per_seg * rows : (g * per_seg + 1) * rows]
                    b = half[(g * per_seg + 1) * rows : (g * per_seg + 2) * rows]
                    spec.append(a + sign * b)
                spec = jnp.concatenate(spec, axis=0)
                re, im = spec[:, :LANES], spec[:, LANES:]
                power = re * re + im * im
                hi = power.astype(jnp.bfloat16)
                lo = (power - hi.astype(jnp.float32)).astype(jnp.bfloat16)
                total = jnp.dot(
                    jnp.concatenate([hi, lo], axis=1), same, preferred_element_type=jnp.float32
                )
                scale = lax.rsqrt(total * (1.0 / BAND) + whiten_eps)
                w_re = (re * scale).astype(jnp.bfloat16).astype(jnp.float32)
                w_im = (im * scale).astype(jnp.bfloat16).astype(jnp.float32)
                at = 2 * j * LANES
                for g in range(segs):
                    r, o = g * rows, (first + g) * ch
                    own[o : o + ch, at : at + LANES] = w_re[r : r + ch]
                    own[o : o + ch, at + LANES : at + 2 * LANES] = w_im[r : r + ch]
                    o = (first + g) * src_count
                    other[o : o + src_count, at : at + LANES] = w_re[r + ch : r + rows]
                    other[o : o + src_count, at + LANES : at + 2 * LANES] = w_im[r + ch : r + rows]

        fetch.wait()

    block = out_ref.shape[0]
    start = pl.multiple_of(pl.program_id(0) * block, 8)
    for j in range(CHUNKS):
        at = 2 * j * LANES
        a_re = [own[g * ch : (g + 1) * ch, at : at + LANES] for g in range(seg_count)]
        a_im = [own[g * ch : (g + 1) * ch, at + LANES : at + 2 * LANES] for g in range(seg_count)]
        for s in range(block):
            if s % 8 == 0:
                tiles = [
                    other[pl.ds(pl.multiple_of(g * src_count + start + s, 8), 8), at : at + 2 * LANES]
                    for g in range(seg_count)
                ]
            re = im = None
            for g in range(seg_count):
                b_re = tiles[g][s % 8 : s % 8 + 1, :LANES]
                b_im = tiles[g][s % 8 : s % 8 + 1, LANES:]
                p = a_re[g] * b_re + a_im[g] * b_im
                q = a_im[g] * b_re - a_re[g] * b_im
                re, im = (p, q) if re is None else (re + p, im + q)
            cross[s * ch : (s + 1) * ch, at : at + LANES] = re.astype(jnp.bfloat16)
            cross[s * ch : (s + 1) * ch, at + LANES : at + 2 * LANES] = im.astype(jnp.bfloat16)
    lags = jnp.dot(cross[...], lag[...], preferred_element_type=jnp.float32)
    out_ref[...] = lags.reshape(out_ref.shape)


def whole(space=pltpu.VMEM):
    return pl.BlockSpec(memory_space=space)


def local(raw_strain, fir_taps, source_channels, live_counts):
    rows, raw_len = raw_strain.shape
    steps = lax.axis_size("tm")
    chan_count = lax.axis_size("cx") * CORES
    dec = raw_len // DECIM
    blocks = dec // LANES
    ch = rows // steps
    seg_count = steps * dec // SEG
    src_count = source_channels.shape[0]
    slots = 2 * SRC_DEV * steps
    peers = steps * chan_count // CORES
    width = dec + LANES
    span = raw_len // blocks
    src = source_channels.reshape(1, src_count)
    taps = fir_taps.reshape(1, fir_taps.shape[0])
    packed, picked = pl.pallas_call(
        functools.partial(filter_kernel, blocks),
        out_shape=[
            jax.ShapeDtypeStruct((rows, width), jnp.bfloat16),
            jax.ShapeDtypeStruct((peers, slots, width), jnp.bfloat16),
        ],
        in_specs=[whole(), whole(), whole(pl.ANY)],
        out_specs=[whole(), whole()],
        scratch_shapes=[
            pltpu.VMEM((blocks * rows, span + LANES), jnp.bfloat16),
            pltpu.VMEM((2 * LANES, span + LANES), jnp.bfloat16),
            pltpu.SemaphoreType.DMA((blocks,)),
        ],
        compiler_params=pltpu.CompilerParams(vmem_limit_bytes=60 * MIB),
        name="fir",
    )(src, taps, raw_strain)
    near = lax.all_to_all(picked, ("tm", "cx"), 0, 0, tiled=True)
    far = lax.ppermute(near, "core", [(c, c ^ 1) for c in range(CORES)])
    held = (steps, peers // steps * slots, width)
    relaid = lax.all_to_all(packed.reshape(steps, ch, width), "tm", 0, 0, tiled=True)
    total_rows = ch + src_count
    block = math.gcd(src_count, 16)
    head_len = -(-(fir_taps.shape[0] - 1) // DECIM)
    assert head_len <= EDGE
    state = seg_count * total_rows * SEG * 4
    return pl.pallas_call(
        functools.partial(correlate_kernel, seg_count, chan_count, head_len, 1024),
        grid=(src_count // block,),
        out_shape=jax.ShapeDtypeStruct((src_count, ch, 2 * LAGH), jnp.float32),
        in_specs=[whole(), whole(pltpu.SMEM)] + [whole()] * 4 + [whole(pl.ANY)],
        out_specs=pl.BlockSpec((block, ch, 2 * LAGH), lambda i: (i, 0, 0)),
        scratch_shapes=[
            pltpu.VMEM((steps * total_rows, dec), jnp.bfloat16),
            pltpu.VMEM((seg_count * ch, SEG), jnp.float32),
            pltpu.VMEM((seg_count * src_count, SEG), jnp.float32),
            pltpu.VMEM((block * ch, SEG), jnp.bfloat16),
            pltpu.VMEM((SEG, 2 * LAGH), jnp.bfloat16),
            pltpu.SemaphoreType.DMA,
        ],
        compiler_params=pltpu.CompilerParams(vmem_limit_bytes=16 * MIB + 2 * state),
        name="correlate",
    )(
        src,
        live_counts,
        relaid,
        near.reshape(held),
        far.reshape(held),
        jnp.asarray(dft_table(dec)),
        jnp.asarray(lag_table(seg_count)),
    )


def solution(mesh):
    steps, chan_count = mesh.shape["tm"], mesh.shape["chan"]
    view = Mesh(
        mesh.devices.reshape(steps, chan_count // CORES, CORES), ("tm", "cx", "core")
    )
    chan = ("cx", "core")
    return jax.shard_map(
        local,
        mesh=view,
        in_specs=(P(chan, "tm"), P(), P(), P((*chan, "tm"))),
        out_specs=P(None, (*chan, "tm"), None),
        check_vma=False,
    )
```

```python
import functools
import math

import jax
import jax.numpy as jnp
import ml_dtypes
import numpy as np
from jax import lax
from jax.experimental import pallas as pl
from jax.experimental.pallas import tpu as pltpu
from jax.sharding import PartitionSpec as P

DECIM = 10
SEG = 1024
BAND = 64
LAGH = 192
LANES = 128
HALF = SEG // 2
CHUNKS = HALF // LANES
EDGE = 16
MIB = 1024 * 1024

whiten_eps = 1e-06

NT = (((1,), (1,)), ((), ()))


def split_table(table):
    hi = table.astype(ml_dtypes.bfloat16)
    lo = (table - hi.astype(np.float64)).astype(ml_dtypes.bfloat16)
    return hi, lo


def dft_table(rows):
    phase = (np.arange(rows)[:, None] * np.arange(HALF)[None, :] % SEG) * (2.0 * np.pi / SEG)
    parts = []
    for j in range(CHUNKS):
        cut = slice(j * LANES, (j + 1) * LANES)
        hi, lo = split_table(np.concatenate([np.cos(phase[:, cut]), -np.sin(phase[:, cut])], 1))
        parts += [hi, lo]
    return np.concatenate(parts, axis=1)


def lag_table(seg_count):
    freq = np.arange(HALF)[:, None]
    phase = (freq * np.arange(-LAGH, LAGH)[None, :] % SEG) * (2.0 * np.pi / SEG)
    weight = np.where(freq == 0, 1.0, 2.0) * (math.sqrt(SEG / seg_count) / SEG)
    re = (weight * np.cos(phase)).reshape(CHUNKS, LANES, 2 * LAGH)
    im = (-weight * np.sin(phase)).reshape(CHUNKS, LANES, 2 * LAGH)
    return np.concatenate([re, im], axis=1).reshape(SEG, 2 * LAGH).astype(ml_dtypes.bfloat16)


def iota(shape, dim):
    return lax.broadcasted_iota(jnp.int32, shape, dim)


def one_hot(mask):
    return jnp.where(mask, 1.0, 0.0).astype(jnp.bfloat16)


def column(row):
    n = row.shape[1]
    return jnp.sum(jnp.where(iota((n, n), 0) == iota((n, n), 1), row, 0), axis=1, keepdims=True)


def tap_rows(taps):
    tap_count = taps.shape[1]
    width = 3 * LANES
    flip = one_hot(iota((tap_count, width), 0) + iota((tap_count, width), 1) == tap_count)
    hi = taps.astype(jnp.bfloat16)
    lo = (taps - hi.astype(jnp.float32)).astype(jnp.bfloat16)
    out = []
    for part in (hi, lo):
        base = jnp.dot(
            jnp.broadcast_to(part.astype(jnp.float32), (8, tap_count)).astype(jnp.bfloat16),
            flip,
            preferred_element_type=jnp.float32,
        )
        upper = pltpu.roll(base, 0, 1, stride=DECIM, stride_axis=0)
        out.append(jnp.concatenate([upper, pltpu.roll(upper, 8 * DECIM, 1)], axis=0))
    return out


def filter_kernel(blocks, src_ref, taps_ref, raw_ref, chan_ref, slot_ref, ext, weight, sems):
    rows, raw_len = raw_ref.shape
    span = raw_len // blocks
    wide = span + LANES
    copies = []
    for b in range(blocks):
        if b == 0:
            copy = pltpu.make_async_copy(
                raw_ref.at[:, pl.ds(0, span)],
                ext.at[pl.ds(0, rows), pl.ds(LANES, span)],
                sems.at[b],
            )
        else:
            copy = pltpu.make_async_copy(
                raw_ref.at[:, pl.ds(b * span - LANES, wide)],
                ext.at[pl.ds(b * rows, rows), :],
                sems.at[b],
            )
        copy.start()
        copies.append(copy)
    ext[:rows, :LANES] = jnp.zeros((rows, LANES), ext.dtype)
    weight[...] = jnp.zeros_like(weight)
    for p, base in enumerate(tap_rows(taps_ref[...])):
        for i in range(LANES // 16):
            tile, lane = divmod(16 * DECIM * i, LANES)
            piece = pltpu.roll(base, lane, 1) if lane else base
            weight[p * LANES + 16 * i : p * LANES + 16 * (i + 1), tile * LANES : (tile + 3) * LANES] = (
                piece.astype(jnp.bfloat16)
            )
    src = src_ref[...]
    src_count = src.shape[1]
    mine = lax.axis_index("chan")
    pick = one_hot(column(src) - mine * rows == iota((src_count, rows), 1))
    slot_ref[...] = jnp.zeros_like(slot_ref)
    for copy in copies:
        copy.wait()
    acc = lax.dot_general(ext[...], weight[...], NT, preferred_element_type=jnp.float32)
    y = (acc[:, :LANES] + acc[:, LANES:]).astype(jnp.bfloat16)
    dec = blocks * LANES
    for b in range(blocks):
        chan_ref[:, b * LANES : (b + 1) * LANES] = y[b * rows : (b + 1) * rows]
    head = acc[:rows, :LANES] + acc[:rows, LANES:]
    head_lo = head - head.astype(jnp.bfloat16).astype(jnp.float32)
    tail = lax.dot_general(
        ext[(blocks - 1) * rows :, wide - LANES :], weight[:, :LANES], NT,
        preferred_element_type=jnp.float32,
    )
    tail = tail[:, :LANES] + tail[:, LANES:]
    tail_hi = tail.astype(jnp.bfloat16).astype(jnp.float32)
    lane = iota((rows, LANES), 1)
    edge = jnp.where(
        lane < EDGE,
        head_lo,
        jnp.where(
            lane < 2 * EDGE,
            pltpu.roll(tail_hi, EDGE, 1),
            pltpu.roll(tail - tail_hi, 2 * EDGE, 1),
        ),
    )
    chan_ref[:, dec:] = edge.astype(jnp.bfloat16)
    found = jnp.dot(pick, chan_ref[...], preferred_element_type=jnp.float32)
    slot_ref[lax.axis_index("tm")] = found.astype(jnp.bfloat16)


def correlate_kernel(
    seg_count, head_len, part_rows,
    live_ref, x_ref, y_ref, d_ref, l_ref, out_ref,
    trace, own, other, cross, lag, lag_sem,
):
    steps, ch, width = x_ref.shape
    src_count = y_ref.shape[1]
    rows = ch + src_count
    dec = width - LANES
    per_seg = SEG // dec

    @pl.when(pl.program_id(0) == 0)
    def _():
        fetch = pltpu.make_async_copy(l_ref, lag, lag_sem)
        fetch.start()
        live = iota((ch, width), 0) < live_ref[0]
        before = jnp.zeros((rows, LANES), jnp.float32)
        is_head = iota((rows, LANES), 1) < head_len
        for t in range(steps):
            mine = jnp.where(live, x_ref[t], jnp.zeros((ch, width), jnp.bfloat16))
            both = jnp.concatenate([mine, y_ref[t]], axis=0)
            first = both[:, :LANES].astype(jnp.float32)
            edge = both[:, dec:].astype(jnp.float32)
            tail = pltpu.roll(before, LANES - EDGE, 1) + pltpu.roll(before, LANES - 2 * EDGE, 1)
            first = jnp.where(is_head, first + edge + tail, first)
            trace[t * rows : (t + 1) * rows, :LANES] = first.astype(jnp.bfloat16)
            trace[t * rows : (t + 1) * rows, LANES:] = both[:, LANES:dec]
            before = edge
        odd = (iota((rows, 2 * LANES), 1) & 1) == 1
        sign = jnp.where(odd, -1.0, 1.0)
        same = one_hot(
            iota((2 * LANES, LANES), 0) % LANES // BAND == iota((2 * LANES, LANES), 1) // BAND
        )
        group_segs = max(1, min(seg_count, part_rows // (per_seg * rows)))
        for first in range(0, seg_count, group_segs):
            segs = min(group_segs, seg_count - first)
            lhs = trace[first * per_seg * rows : (first + segs) * per_seg * rows, :]
            for j in range(CHUNKS):
                acc = jnp.dot(
                    lhs, d_ref[:, 4 * j * LANES : 4 * (j + 1) * LANES],
                    preferred_element_type=jnp.float32,
                )
                half = acc[:, : 2 * LANES] + acc[:, 2 * LANES :]
                spec = []
                for g in range(segs):
                    a = half[g * per_seg * rows : (g * per_seg + 1) * rows]
                    b = half[(g * per_seg + 1) * rows : (g * per_seg + 2) * rows]
                    spec.append(a + sign * b)
                spec = jnp.concatenate(spec, axis=0)
                re, im = spec[:, :LANES], spec[:, LANES:]
                power = re * re + im * im
                hi = power.astype(jnp.bfloat16)
                lo = (power - hi.astype(jnp.float32)).astype(jnp.bfloat16)
                total = jnp.dot(
                    jnp.concatenate([hi, lo], axis=1), same, preferred_element_type=jnp.float32
                )
                scale = lax.rsqrt(total * (1.0 / BAND) + whiten_eps)
                w_re = (re * scale).astype(jnp.bfloat16).astype(jnp.float32)
                w_im = (im * scale).astype(jnp.bfloat16).astype(jnp.float32)
                at = 2 * j * LANES
                for g in range(segs):
                    r, o = g * rows, (first + g) * ch
                    own[o : o + ch, at : at + LANES] = w_re[r : r + ch]
                    own[o : o + ch, at + LANES : at + 2 * LANES] = w_im[r : r + ch]
                    o = (first + g) * src_count
                    other[o : o + src_count, at : at + LANES] = w_re[r + ch : r + rows]
                    other[o : o + src_count, at + LANES : at + 2 * LANES] = w_im[r + ch : r + rows]

        fetch.wait()

    block = out_ref.shape[0]
    start = pl.multiple_of(pl.program_id(0) * block, 8)
    for j in range(CHUNKS):
        at = 2 * j * LANES
        a_re = [own[g * ch : (g + 1) * ch, at : at + LANES] for g in range(seg_count)]
        a_im = [own[g * ch : (g + 1) * ch, at + LANES : at + 2 * LANES] for g in range(seg_count)]
        for s in range(block):
            if s % 8 == 0:
                tiles = [
                    other[pl.ds(pl.multiple_of(g * src_count + start + s, 8), 8), at : at + 2 * LANES]
                    for g in range(seg_count)
                ]
            re = im = None
            for g in range(seg_count):
                b_re = tiles[g][s % 8 : s % 8 + 1, :LANES]
                b_im = tiles[g][s % 8 : s % 8 + 1, LANES:]
                p = a_re[g] * b_re + a_im[g] * b_im
                q = a_im[g] * b_re - a_re[g] * b_im
                re, im = (p, q) if re is None else (re + p, im + q)
            cross[s * ch : (s + 1) * ch, at : at + LANES] = re.astype(jnp.bfloat16)
            cross[s * ch : (s + 1) * ch, at + LANES : at + 2 * LANES] = im.astype(jnp.bfloat16)
    lags = jnp.dot(cross[...], lag[...], preferred_element_type=jnp.float32)
    out_ref[...] = lags.reshape(out_ref.shape)


def whole(space=pltpu.VMEM):
    return pl.BlockSpec(memory_space=space)


def local(raw_strain, fir_taps, source_channels, live_counts):
    rows, raw_len = raw_strain.shape
    steps = lax.axis_size("tm")
    dec = raw_len // DECIM
    blocks = dec // LANES
    ch = rows // steps
    seg_count = steps * dec // SEG
    src_count = source_channels.shape[0]
    width = dec + LANES
    span = raw_len // blocks
    src = source_channels.reshape(1, src_count)
    taps = fir_taps.reshape(1, fir_taps.shape[0])
    packed, picked = pl.pallas_call(
        functools.partial(filter_kernel, blocks),
        out_shape=[
            jax.ShapeDtypeStruct((rows, width), jnp.bfloat16),
            jax.ShapeDtypeStruct((steps, src_count, width), jnp.bfloat16),
        ],
        in_specs=[whole(), whole(), whole(pl.ANY)],
        out_specs=[whole(), whole()],
        scratch_shapes=[
            pltpu.VMEM((blocks * rows, span + LANES), jnp.bfloat16),
            pltpu.VMEM((2 * LANES, span + LANES), jnp.bfloat16),
            pltpu.SemaphoreType.DMA((blocks,)),
        ],
        compiler_params=pltpu.CompilerParams(vmem_limit_bytes=60 * MIB),
        name="fir",
    )(src, taps, raw_strain)
    sources = lax.psum(picked, ("tm", "chan"))
    relaid = lax.all_to_all(packed.reshape(steps, ch, width), "tm", 0, 0, tiled=True)
    total_rows = ch + src_count
    block = math.gcd(src_count, 16)
    head_len = -(-(fir_taps.shape[0] - 1) // DECIM)
    assert head_len <= EDGE
    state = seg_count * total_rows * SEG * 4
    return pl.pallas_call(
        functools.partial(correlate_kernel, seg_count, head_len, 1024),
        grid=(src_count // block,),
        out_shape=jax.ShapeDtypeStruct((src_count, ch, 2 * LAGH), jnp.float32),
        in_specs=[whole(pltpu.SMEM)] + [whole()] * 3 + [whole(pl.ANY)],
        out_specs=pl.BlockSpec((block, ch, 2 * LAGH), lambda i: (i, 0, 0)),
        scratch_shapes=[
            pltpu.VMEM((steps * total_rows, dec), jnp.bfloat16),
            pltpu.VMEM((seg_count * ch, SEG), jnp.float32),
            pltpu.VMEM((seg_count * src_count, SEG), jnp.float32),
            pltpu.VMEM((block * ch, SEG), jnp.bfloat16),
            pltpu.VMEM((SEG, 2 * LAGH), jnp.bfloat16),
            pltpu.SemaphoreType.DMA,
        ],
        compiler_params=pltpu.CompilerParams(vmem_limit_bytes=16 * MIB + 2 * state),
        name="correlate",
    )(
        live_counts,
        relaid,
        sources,
        jnp.asarray(dft_table(dec)),
        jnp.asarray(lag_table(seg_count)),
    )


def solution(mesh):
    placed = (P("chan", "tm"), P(), P(), P(("chan", "tm")))
    return jax.shard_map(
        local, mesh=mesh, in_specs=placed, out_specs=P(None, ("chan", "tm"), None), check_vma=False
    )
```

```python
import functools
import math

import jax
import jax.numpy as jnp
import ml_dtypes
import numpy as np
from jax import lax
from jax.experimental import pallas as pl
from jax.experimental.pallas import tpu as pltpu
from jax.sharding import PartitionSpec as P

DECIM = 10
SEG = 1024
BAND = 64
LAGH = 192
SRC_DEV = 1
LANES = 128
HALF = SEG // 2
CHUNKS = HALF // LANES
EDGE = 14
PER_TILE = LANES // (3 * EDGE)
ROWS = 16
MIB = 1024 * 1024

whiten_eps = 1e-06

NT = (((1,), (1,)), ((), ()))


def split_table(table):
    hi = table.astype(ml_dtypes.bfloat16)
    lo = (table - hi.astype(np.float64)).astype(ml_dtypes.bfloat16)
    return hi, lo


def dft_table(rows):
    phase = (np.arange(rows)[:, None] * np.arange(HALF)[None, :] % SEG) * (2.0 * np.pi / SEG)
    parts = []
    for j in range(CHUNKS):
        cut = slice(j * LANES, (j + 1) * LANES)
        hi, lo = split_table(np.concatenate([np.cos(phase[:, cut]), -np.sin(phase[:, cut])], 1))
        parts += [hi, lo]
    return np.concatenate(parts, axis=1)


def lag_table(seg_count):
    freq = np.arange(HALF)[:, None]
    phase = (freq * np.arange(-LAGH, LAGH)[None, :] % SEG) * (2.0 * np.pi / SEG)
    weight = np.where(freq == 0, 1.0, 2.0) * (math.sqrt(SEG / seg_count) / SEG)
    re = (weight * np.cos(phase)).reshape(CHUNKS, LANES, 2 * LAGH)
    im = (-weight * np.sin(phase)).reshape(CHUNKS, LANES, 2 * LAGH)
    return np.concatenate([re, im], axis=1).reshape(SEG, 2 * LAGH).astype(ml_dtypes.bfloat16)


def iota(shape, dim):
    return lax.broadcasted_iota(jnp.int32, shape, dim)


def one_hot(mask):
    return jnp.where(mask, 1.0, 0.0).astype(jnp.bfloat16)


def column(row):
    n = row.shape[1]
    return jnp.sum(jnp.where(iota((n, n), 0) == iota((n, n), 1), row, 0), axis=1, keepdims=True)


def tap_rows(taps):
    tap_count = taps.shape[1]
    width = 3 * LANES
    flip = one_hot(iota((tap_count, width), 0) + iota((tap_count, width), 1) == tap_count)
    hi = taps.astype(jnp.bfloat16)
    lo = (taps - hi.astype(jnp.float32)).astype(jnp.bfloat16)
    out = []
    for part in (hi, lo):
        base = jnp.dot(
            jnp.broadcast_to(part.astype(jnp.float32), (8, tap_count)).astype(jnp.bfloat16),
            flip,
            preferred_element_type=jnp.float32,
        )
        upper = pltpu.roll(base, 0, 1, stride=DECIM, stride_axis=0)
        out.append(jnp.concatenate([upper, pltpu.roll(upper, 8 * DECIM, 1)], axis=0))
    return out


def edge_tiles(count):
    return -(-count // (PER_TILE * ROWS))


def filter_kernel(blocks, src_ref, taps_ref, raw_ref, out_ref, slot_ref, ext, weight, sems):
    rows, raw_len = raw_ref.shape
    steps = out_ref.shape[0]
    ch = rows // steps
    span = raw_len // blocks
    wide = span + LANES
    copies = []
    for b in range(blocks):
        if b == 0:
            copy = pltpu.make_async_copy(
                raw_ref.at[:, pl.ds(0, span)],
                ext.at[pl.ds(0, rows), pl.ds(LANES, span)],
                sems.at[b],
            )
        else:
            copy = pltpu.make_async_copy(
                raw_ref.at[:, pl.ds(b * span - LANES, wide)],
                ext.at[pl.ds(b * rows, rows), :],
                sems.at[b],
            )
        copy.start()
        copies.append(copy)
    ext[:rows, :LANES] = jnp.zeros((rows, LANES), ext.dtype)
    weight[...] = jnp.zeros_like(weight)
    for p, base in enumerate(tap_rows(taps_ref[...])):
        for i in range(LANES // 16):
            tile, lane = divmod(16 * DECIM * i, LANES)
            piece = pltpu.roll(base, lane, 1) if lane else base
            weight[p * LANES + 16 * i : p * LANES + 16 * (i + 1), tile * LANES : (tile + 3) * LANES] = (
                piece.astype(jnp.bfloat16)
            )
    src = src_ref[...]
    src_count = src.shape[1]
    slots = slot_ref.shape[0]
    group = src // rows
    group_col = column(group)
    src_col = column(src)
    rank = jnp.sum(
        jnp.where(
            (group_col == group)
            & (iota((src_count, src_count), 0) < iota((src_count, src_count), 1)),
            1,
            0,
        ),
        axis=0,
        keepdims=True,
    )
    mine = lax.axis_index("chan")
    to_slot = one_hot((iota((slots, src_count), 0) == rank) & (group == mine))
    to_row = one_hot(src_col - mine * rows == iota((src_count, rows), 1))
    pick = jnp.dot(to_slot, to_row, preferred_element_type=jnp.float32).astype(jnp.bfloat16)
    number = jnp.where(
        iota((src_count, LANES), 1) == LANES - 1, iota((src_count, LANES), 0) + 1, 0
    ).astype(jnp.float32).astype(jnp.bfloat16)
    number = jnp.dot(to_slot, number, preferred_element_type=jnp.float32)
    for copy in copies:
        copy.wait()
    acc = lax.dot_general(ext[...], weight[...], NT, preferred_element_type=jnp.float32)
    acc = acc[:, :LANES] + acc[:, LANES:]
    y = acc.astype(jnp.bfloat16)
    head = acc[:rows]
    head_lo = head - head.astype(jnp.bfloat16).astype(jnp.float32)
    tail = lax.dot_general(
        ext[(blocks - 1) * rows :, wide - LANES :], weight[:, :LANES], NT,
        preferred_element_type=jnp.float32,
    )
    tail = tail[:, :LANES] + tail[:, LANES:]
    tail_hi = tail.astype(jnp.bfloat16).astype(jnp.float32)
    lane = iota((rows, LANES), 1)
    edge = jnp.where(
        lane < EDGE,
        head_lo,
        jnp.where(
            lane < 2 * EDGE,
            pltpu.roll(tail_hi, EDGE, 1),
            jnp.where(lane < 3 * EDGE, pltpu.roll(tail - tail_hi, 2 * EDGE, 1), 0.0),
        ),
    ).astype(jnp.bfloat16)
    parts = [y[b * rows : (b + 1) * rows] for b in range(blocks)] + [edge]
    last = out_ref.shape[1] - edge_tiles(ch + src_count) * ROWS
    for t in range(steps):
        for b in range(blocks):
            out_ref[t, b * ch : (b + 1) * ch] = parts[b][t * ch : (t + 1) * ch]
        out_ref[t, last : last + ch] = edge[t * ch : (t + 1) * ch]
    for b, part in enumerate(parts):
        found = jnp.dot(pick, part, preferred_element_type=jnp.float32)
        if b == blocks:
            found += number
        slot_ref[:, b * LANES : (b + 1) * LANES] = found.astype(jnp.bfloat16)


def arrange_kernel(src_count, blocks, slots_ref, part_ref, out_ref, fill, packs, in_sem, sems):
    steps, height, _ = part_ref.shape
    tile_rows = packs.shape[1]
    start = height - tile_rows - fill.shape[0]
    fetch = pltpu.make_async_copy(
        part_ref.at[:, pl.ds(height - tile_rows, tile_rows)], packs, in_sem
    )
    fetch.start()
    numbers = slots_ref[:, blocks * LANES :].astype(jnp.float32)
    total = numbers.shape[0]
    numbers = jnp.sum(
        jnp.where(iota((total, LANES), 1) == LANES - 1, numbers, 0.0), axis=1, keepdims=True
    ).astype(jnp.int32)
    pick = one_hot(numbers == iota((total, src_count), 1) + 1)
    found = lax.dot_general(
        pick, slots_ref[...], (((0,), (0,)), ((), ())), preferred_element_type=jnp.float32
    )
    for b in range(blocks):
        fill[b * src_count : (b + 1) * src_count] = found[:, b * LANES : (b + 1) * LANES].astype(
            jnp.bfloat16
        )
    copies = [
        pltpu.make_async_copy(fill, out_ref.at[t, pl.ds(start, fill.shape[0])], sems.at[t])
        for t in range(steps)
    ]
    for copy in copies:
        copy.start()
    edges = jnp.where(
        iota((src_count, LANES), 1) < 3 * EDGE, found[:, blocks * LANES :], 0.0
    )
    added = [jnp.zeros((ROWS, LANES), jnp.float32) for _ in range(tile_rows // ROWS)]
    for i in range(src_count // ROWS):
        tile, place = divmod(i + 1, PER_TILE)
        piece = edges[i * ROWS : (i + 1) * ROWS]
        added[tile] += pltpu.roll(piece, 3 * EDGE * place, 1) if place else piece
    fetch.wait()
    added = jnp.concatenate(added, axis=0)
    for t in range(steps):
        own = packs[t].astype(jnp.float32)
        own = jnp.where(
            (iota(own.shape, 0) < ROWS) & (iota(own.shape, 1) < 3 * EDGE), own, 0.0
        )
        packs[t] = (own + added).astype(jnp.bfloat16)
    store = pltpu.make_async_copy(
        packs, out_ref.at[:, pl.ds(height - tile_rows, tile_rows)], in_sem
    )
    store.start()
    for copy in copies:
        copy.wait()
    store.wait()


def correlate_kernel(
    seg_count, src_count, dec, head_len, part_rows,
    live_ref, x_ref, tab_ref, out_ref,
    trace, own, other, cross,
):
    steps, height, _ = x_ref.shape
    ch = out_ref.shape[1]
    rows = ch + src_count
    per_seg = SEG // dec
    blocks = dec // LANES
    d_cols = 4 * HALF

    @pl.when(pl.program_id(0) == 0)
    def _():
        live = iota((ch, LANES), 0) < live_ref[0]
        before = jnp.zeros((rows, LANES), jnp.float32)
        is_head = iota((rows, LANES), 1) < head_len
        last = height - edge_tiles(rows) * ROWS
        for t in range(steps):
            edge = []
            for i in range(rows // ROWS):
                tile, place = divmod(i, PER_TILE)
                if place == 0:
                    pack = x_ref[t, last + tile * ROWS : last + (tile + 1) * ROWS].astype(jnp.float32)
                    edge.append(pack)
                else:
                    edge.append(pltpu.roll(pack, LANES - 3 * EDGE * place, 1))
            edge[0] = jnp.where(live, edge[0], 0.0)
            edge = jnp.concatenate(edge, axis=0)
            for b in range(blocks):
                mine = x_ref[t, b * ch : (b + 1) * ch]
                mine = jnp.where(live, mine, jnp.zeros_like(mine))
                at = blocks * ch + b * src_count
                both = jnp.concatenate([mine, x_ref[t, at : at + src_count]], axis=0)
                if b == 0:
                    tail = pltpu.roll(before, LANES - EDGE, 1) + pltpu.roll(before, LANES - 2 * EDGE, 1)
                    both = both.astype(jnp.float32)
                    both = jnp.where(is_head, both + edge + tail, both).astype(jnp.bfloat16)
                trace[t * rows : (t + 1) * rows, b * LANES : (b + 1) * LANES] = both
            before = edge
        odd = (iota((rows, 2 * LANES), 1) & 1) == 1
        sign = jnp.where(odd, -1.0, 1.0)
        same = one_hot(
            iota((2 * LANES, LANES), 0) % LANES // BAND == iota((2 * LANES, LANES), 1) // BAND
        )
        group_segs = max(1, min(seg_count, part_rows // (per_seg * rows)))
        for first in range(0, seg_count, group_segs):
            segs = min(group_segs, seg_count - first)
            lhs = trace[first * per_seg * rows : (first + segs) * per_seg * rows, :]
            for j in range(CHUNKS):
                acc = jnp.dot(
                    lhs, tab_ref[:, 4 * j * LANES : 4 * (j + 1) * LANES],
                    preferred_element_type=jnp.float32,
                )
                half = acc[:, : 2 * LANES] + acc[:, 2 * LANES :]
                spec = []
                for g in range(segs):
                    a = half[g * per_seg * rows : (g * per_seg + 1) * rows]
                    b = half[(g * per_seg + 1) * rows : (g * per_seg + 2) * rows]
                    spec.append(a + sign * b)
                spec = jnp.concatenate(spec, axis=0)
                re, im = spec[:, :LANES], spec[:, LANES:]
                power = re * re + im * im
                hi = power.astype(jnp.bfloat16)
                lo = (power - hi.astype(jnp.float32)).astype(jnp.bfloat16)
                total = jnp.dot(
                    jnp.concatenate([hi, lo], axis=1), same, preferred_element_type=jnp.float32
                )
                scale = lax.rsqrt(total * (1.0 / BAND) + whiten_eps)
                w_re = (re * scale).astype(jnp.bfloat16).astype(jnp.float32)
                w_im = (im * scale).astype(jnp.bfloat16).astype(jnp.float32)
                at = 2 * j * LANES
                for g in range(segs):
                    r, o = g * rows, (first + g) * ch
                    own[o : o + ch, at : at + LANES] = w_re[r : r + ch]
                    own[o : o + ch, at + LANES : at + 2 * LANES] = w_im[r : r + ch]
                    o = (first + g) * src_count
                    other[o : o + src_count, at : at + LANES] = w_re[r + ch : r + rows]
                    other[o : o + src_count, at + LANES : at + 2 * LANES] = w_im[r + ch : r + rows]

    block = out_ref.shape[0]
    start = pl.multiple_of(pl.program_id(0) * block, 8)
    for j in range(CHUNKS):
        at = 2 * j * LANES
        a_re = [own[g * ch : (g + 1) * ch, at : at + LANES] for g in range(seg_count)]
        a_im = [own[g * ch : (g + 1) * ch, at + LANES : at + 2 * LANES] for g in range(seg_count)]
        for s in range(block):
            if s % 8 == 0:
                tiles = [
                    other[pl.ds(pl.multiple_of(g * src_count + start + s, 8), 8), at : at + 2 * LANES]
                    for g in range(seg_count)
                ]
            re = im = None
            for g in range(seg_count):
                b_re = tiles[g][s % 8 : s % 8 + 1, :LANES]
                b_im = tiles[g][s % 8 : s % 8 + 1, LANES:]
                p = a_re[g] * b_re + a_im[g] * b_im
                q = a_im[g] * b_re - a_re[g] * b_im
                re, im = (p, q) if re is None else (re + p, im + q)
            cross[s * ch : (s + 1) * ch, at : at + LANES] = re.astype(jnp.bfloat16)
            cross[s * ch : (s + 1) * ch, at + LANES : at + 2 * LANES] = im.astype(jnp.bfloat16)
    lags = sum(
        jnp.dot(
            cross[:, h * dec : (h + 1) * dec],
            tab_ref[:, d_cols + 2 * LAGH * h : d_cols + 2 * LAGH * (h + 1)],
            preferred_element_type=jnp.float32,
        )
        for h in range(per_seg)
    )
    out_ref[...] = lags.reshape(out_ref.shape)


def whole(space=pltpu.VMEM):
    return pl.BlockSpec(memory_space=space)


def local(raw_strain, fir_taps, source_channels, live_counts):
    rows, raw_len = raw_strain.shape
    steps = lax.axis_size("tm")
    chan_count = lax.axis_size("chan")
    dec = raw_len // DECIM
    blocks = dec // LANES
    ch = rows // steps
    seg_count = steps * dec // SEG
    src_count = source_channels.shape[0]
    slots = 2 * SRC_DEV * steps
    span = raw_len // blocks
    total_rows = ch + src_count
    tile_rows = edge_tiles(total_rows) * ROWS
    height = blocks * total_rows + tile_rows
    head_len = -(-(fir_taps.shape[0] - 1) // DECIM)
    assert head_len < EDGE and ch == ROWS and src_count <= 256
    src = source_channels.reshape(1, src_count)
    taps = fir_taps.reshape(1, fir_taps.shape[0])
    part, picked = pl.pallas_call(
        functools.partial(filter_kernel, blocks),
        out_shape=[
            jax.ShapeDtypeStruct((steps, height, LANES), jnp.bfloat16),
            jax.ShapeDtypeStruct((slots, dec + LANES), jnp.bfloat16),
        ],
        in_specs=[whole(), whole(), whole(pl.ANY)],
        out_specs=[whole(), whole()],
        scratch_shapes=[
            pltpu.VMEM((blocks * rows, span + LANES), jnp.bfloat16),
            pltpu.VMEM((2 * LANES, span + LANES), jnp.bfloat16),
            pltpu.SemaphoreType.DMA((blocks,)),
        ],
        compiler_params=pltpu.CompilerParams(vmem_limit_bytes=60 * MIB),
        name="fir",
    )(src, taps, raw_strain)
    gathered = lax.all_gather(picked, "chan", axis=0, tiled=True)
    outgoing = pl.pallas_call(
        functools.partial(arrange_kernel, src_count, blocks),
        out_shape=jax.ShapeDtypeStruct(part.shape, part.dtype),
        in_specs=[whole(), whole(pl.ANY)],
        out_specs=whole(pl.ANY),
        scratch_shapes=[
            pltpu.VMEM((blocks * src_count, LANES), jnp.bfloat16),
            pltpu.VMEM((steps, tile_rows, LANES), jnp.bfloat16),
            pltpu.SemaphoreType.DMA,
            pltpu.SemaphoreType.DMA((steps,)),
        ],
        input_output_aliases={1: 0},
        compiler_params=pltpu.CompilerParams(vmem_limit_bytes=60 * MIB),
        name="arrange",
    )(gathered, part)
    relaid = lax.all_to_all(outgoing, "tm", split_axis=0, concat_axis=0)
    block = math.gcd(src_count, 16)
    state = seg_count * total_rows * SEG * 4
    table = np.concatenate([dft_table(dec), *lag_table(seg_count).reshape(SEG // dec, dec, -1)], axis=1)
    return pl.pallas_call(
        functools.partial(correlate_kernel, seg_count, src_count, dec, head_len, 1024),
        grid=(src_count // block,),
        out_shape=jax.ShapeDtypeStruct((src_count, ch, 2 * LAGH), jnp.float32),
        in_specs=[whole(pltpu.SMEM), whole(), whole()],
        out_specs=pl.BlockSpec((block, ch, 2 * LAGH), lambda i: (i, 0, 0)),
        scratch_shapes=[
            pltpu.VMEM((steps * total_rows, dec), jnp.bfloat16),
            pltpu.VMEM((seg_count * ch, SEG), jnp.float32),
            pltpu.VMEM((seg_count * src_count, SEG), jnp.float32),
            pltpu.VMEM((block * ch, SEG), jnp.bfloat16),
        ],
        compiler_params=pltpu.CompilerParams(vmem_limit_bytes=16 * MIB + 2 * state),
        name="correlate",
    )(live_counts, relaid, jnp.asarray(table))


def solution(mesh):
    placed = (P("chan", "tm"), P(), P(), P(("chan", "tm")))
    return jax.shard_map(
        local, mesh=mesh, in_specs=placed, out_specs=P(None, ("chan", "tm"), None), check_vma=False
    )
```

```python
import functools
import math

import jax
import jax.numpy as jnp
import ml_dtypes
import numpy as np
from jax import lax
from jax.experimental import pallas as pl
from jax.experimental.pallas import tpu as pltpu
from jax.sharding import PartitionSpec as P

DECIM = 10
SEG = 1024
BAND = 64
LAGH = 192
SRC_DEV = 1
LANES = 128
HALF = SEG // 2
CHUNKS = HALF // LANES
EDGE = 14
PER_TILE = LANES // (3 * EDGE)
ROWS = 16
MIB = 1024 * 1024

whiten_eps = 1e-06

NT = (((1,), (1,)), ((), ()))


def split_table(table):
    hi = table.astype(ml_dtypes.bfloat16)
    lo = (table - hi.astype(np.float64)).astype(ml_dtypes.bfloat16)
    return hi, lo


def dft_table(rows):
    phase = (np.arange(rows)[:, None] * np.arange(HALF)[None, :] % SEG) * (2.0 * np.pi / SEG)
    parts = []
    for j in range(CHUNKS):
        cut = slice(j * LANES, (j + 1) * LANES)
        hi, lo = split_table(np.concatenate([np.cos(phase[:, cut]), -np.sin(phase[:, cut])], 1))
        parts += [hi, lo]
    return np.concatenate(parts, axis=1)


def lag_table(seg_count):
    freq = np.arange(HALF)[:, None]
    phase = (freq * np.arange(-LAGH, LAGH)[None, :] % SEG) * (2.0 * np.pi / SEG)
    weight = np.where(freq == 0, 1.0, 2.0) * (math.sqrt(SEG / seg_count) / SEG)
    re = (weight * np.cos(phase)).reshape(CHUNKS, LANES, 2 * LAGH)
    im = (-weight * np.sin(phase)).reshape(CHUNKS, LANES, 2 * LAGH)
    return np.concatenate([re, im], axis=1).reshape(SEG, 2 * LAGH).astype(ml_dtypes.bfloat16)


def iota(shape, dim):
    return lax.broadcasted_iota(jnp.int32, shape, dim)


def one_hot(mask):
    return jnp.where(mask, 1.0, 0.0).astype(jnp.bfloat16)


def column(row):
    n = row.shape[1]
    return jnp.sum(jnp.where(iota((n, n), 0) == iota((n, n), 1), row, 0), axis=1, keepdims=True)


def tap_rows(taps):
    tap_count = taps.shape[1]
    width = 3 * LANES
    flip = one_hot(iota((tap_count, width), 0) + iota((tap_count, width), 1) == tap_count)
    hi = taps.astype(jnp.bfloat16)
    lo = (taps - hi.astype(jnp.float32)).astype(jnp.bfloat16)
    out = []
    for part in (hi, lo):
        base = jnp.dot(
            jnp.broadcast_to(part.astype(jnp.float32), (8, tap_count)).astype(jnp.bfloat16),
            flip,
            preferred_element_type=jnp.float32,
        )
        upper = pltpu.roll(base, 0, 1, stride=DECIM, stride_axis=0)
        out.append(jnp.concatenate([upper, pltpu.roll(upper, 8 * DECIM, 1)], axis=0))
    return out


def edge_tiles(count):
    return -(-count // (PER_TILE * ROWS))


def filter_kernel(
    blocks, src_hbm, taps_hbm, raw_ref, out_ref, slot_ref, ext, weight, src_ref, taps_ref, sems
):
    rows, raw_len = raw_ref.shape
    steps = out_ref.shape[0]
    ch = rows // steps
    span = raw_len // blocks
    wide = span + LANES
    copies = []
    for b in range(blocks):
        if b == 0:
            copy = pltpu.make_async_copy(
                raw_ref.at[:, pl.ds(0, span)],
                ext.at[pl.ds(0, rows), pl.ds(LANES, span)],
                sems.at[b],
            )
        else:
            copy = pltpu.make_async_copy(
                raw_ref.at[:, pl.ds(b * span - LANES, wide)],
                ext.at[pl.ds(b * rows, rows), :],
                sems.at[b],
            )
        copy.start()
        copies.append(copy)
    small = [
        pltpu.make_async_copy(taps_hbm, taps_ref, sems.at[blocks]),
        pltpu.make_async_copy(src_hbm, src_ref, sems.at[blocks + 1]),
    ]
    for copy in small:
        copy.start()
    ext[:rows, :LANES] = jnp.zeros((rows, LANES), ext.dtype)
    weight[...] = jnp.zeros_like(weight)
    for copy in small:
        copy.wait()
    for p, base in enumerate(tap_rows(taps_ref[...])):
        for i in range(LANES // 16):
            tile, lane = divmod(16 * DECIM * i, LANES)
            piece = pltpu.roll(base, lane, 1) if lane else base
            weight[p * LANES + 16 * i : p * LANES + 16 * (i + 1), tile * LANES : (tile + 3) * LANES] = (
                piece.astype(jnp.bfloat16)
            )
    src = src_ref[...]
    src_count = src.shape[1]
    slots = slot_ref.shape[0]
    group = src // rows
    group_col = column(group)
    src_col = column(src)
    rank = jnp.sum(
        jnp.where(
            (group_col == group)
            & (iota((src_count, src_count), 0) < iota((src_count, src_count), 1)),
            1,
            0,
        ),
        axis=0,
        keepdims=True,
    )
    mine = lax.axis_index("chan")
    to_slot = one_hot((iota((slots, src_count), 0) == rank) & (group == mine))
    to_row = one_hot(src_col - mine * rows == iota((src_count, rows), 1))
    pick = jnp.dot(to_slot, to_row, preferred_element_type=jnp.float32).astype(jnp.bfloat16)
    number = jnp.where(
        iota((src_count, LANES), 1) == LANES - 1, iota((src_count, LANES), 0) + 1, 0
    ).astype(jnp.float32).astype(jnp.bfloat16)
    number = jnp.dot(to_slot, number, preferred_element_type=jnp.float32)
    for copy in copies:
        copy.wait()
    acc = lax.dot_general(ext[...], weight[...], NT, preferred_element_type=jnp.float32)
    acc = acc[:, :LANES] + acc[:, LANES:]
    y = acc.astype(jnp.bfloat16)
    head = acc[:rows]
    head_lo = head - head.astype(jnp.bfloat16).astype(jnp.float32)
    tail = lax.dot_general(
        ext[(blocks - 1) * rows :, wide - LANES :], weight[:, :LANES], NT,
        preferred_element_type=jnp.float32,
    )
    tail = tail[:, :LANES] + tail[:, LANES:]
    tail_hi = tail.astype(jnp.bfloat16).astype(jnp.float32)
    lane = iota((rows, LANES), 1)
    edge = jnp.where(
        lane < EDGE,
        head_lo,
        jnp.where(
            lane < 2 * EDGE,
            pltpu.roll(tail_hi, EDGE, 1),
            jnp.where(lane < 3 * EDGE, pltpu.roll(tail - tail_hi, 2 * EDGE, 1), 0.0),
        ),
    ).astype(jnp.bfloat16)
    parts = [y[b * rows : (b + 1) * rows] for b in range(blocks)] + [edge]
    last = out_ref.shape[1] - edge_tiles(ch + src_count) * ROWS
    for t in range(steps):
        for b in range(blocks):
            out_ref[t, b * ch : (b + 1) * ch] = parts[b][t * ch : (t + 1) * ch]
        out_ref[t, last : last + ch] = edge[t * ch : (t + 1) * ch]
    for b, part in enumerate(parts):
        found = jnp.dot(pick, part, preferred_element_type=jnp.float32)
        if b == blocks:
            found += number
        slot_ref[:, b * LANES : (b + 1) * LANES] = found.astype(jnp.bfloat16)


def arrange_kernel(src_count, blocks, slots_ref, part_ref, out_ref, fill, packs, in_sem, sems):
    steps, height, _ = part_ref.shape
    tile_rows = packs.shape[1]
    start = height - tile_rows - fill.shape[0]
    fetch = pltpu.make_async_copy(
        part_ref.at[:, pl.ds(height - tile_rows, tile_rows)], packs, in_sem
    )
    fetch.start()
    numbers = slots_ref[:, blocks * LANES :].astype(jnp.float32)
    total = numbers.shape[0]
    numbers = jnp.sum(
        jnp.where(iota((total, LANES), 1) == LANES - 1, numbers, 0.0), axis=1, keepdims=True
    ).astype(jnp.int32)
    pick = one_hot(numbers == iota((total, src_count), 1) + 1)
    found = lax.dot_general(
        pick, slots_ref[...], (((0,), (0,)), ((), ())), preferred_element_type=jnp.float32
    )
    for b in range(blocks):
        fill[b * src_count : (b + 1) * src_count] = found[:, b * LANES : (b + 1) * LANES].astype(
            jnp.bfloat16
        )
    copies = [
        pltpu.make_async_copy(fill, out_ref.at[t, pl.ds(start, fill.shape[0])], sems.at[t])
        for t in range(steps)
    ]
    for copy in copies:
        copy.start()
    edges = jnp.where(
        iota((src_count, LANES), 1) < 3 * EDGE, found[:, blocks * LANES :], 0.0
    )
    added = [jnp.zeros((ROWS, LANES), jnp.float32) for _ in range(tile_rows // ROWS)]
    for i in range(src_count // ROWS):
        tile, place = divmod(i + 1, PER_TILE)
        piece = edges[i * ROWS : (i + 1) * ROWS]
        added[tile] += pltpu.roll(piece, 3 * EDGE * place, 1) if place else piece
    fetch.wait()
    added = jnp.concatenate(added, axis=0)
    for t in range(steps):
        own = packs[t].astype(jnp.float32)
        own = jnp.where(
            (iota(own.shape, 0) < ROWS) & (iota(own.shape, 1) < 3 * EDGE), own, 0.0
        )
        packs[t] = (own + added).astype(jnp.bfloat16)
    store = pltpu.make_async_copy(
        packs, out_ref.at[:, pl.ds(height - tile_rows, tile_rows)], in_sem
    )
    store.start()
    for copy in copies:
        copy.wait()
    store.wait()


def correlate_kernel(
    seg_count, src_count, dec, head_len, part_rows,
    live_ref, x_ref, tab_ref, out_ref,
    trace, own, other, cross,
):
    steps, height, _ = x_ref.shape
    ch = out_ref.shape[1]
    rows = ch + src_count
    per_seg = SEG // dec
    blocks = dec // LANES
    d_cols = 4 * HALF

    @pl.when(pl.program_id(0) == 0)
    def _():
        live = iota((ch, LANES), 0) < live_ref[0]
        before = jnp.zeros((rows, LANES), jnp.float32)
        is_head = iota((rows, LANES), 1) < head_len
        last = height - edge_tiles(rows) * ROWS
        for t in range(steps):
            edge = []
            for i in range(rows // ROWS):
                tile, place = divmod(i, PER_TILE)
                if place == 0:
                    pack = x_ref[t, last + tile * ROWS : last + (tile + 1) * ROWS].astype(jnp.float32)
                    edge.append(pack)
                else:
                    edge.append(pltpu.roll(pack, LANES - 3 * EDGE * place, 1))
            edge[0] = jnp.where(live, edge[0], 0.0)
            edge = jnp.concatenate(edge, axis=0)
            for b in range(blocks):
                mine = x_ref[t, b * ch : (b + 1) * ch]
                mine = jnp.where(live, mine, jnp.zeros_like(mine))
                at = blocks * ch + b * src_count
                both = jnp.concatenate([mine, x_ref[t, at : at + src_count]], axis=0)
                if b == 0:
                    tail = pltpu.roll(before, LANES - EDGE, 1) + pltpu.roll(before, LANES - 2 * EDGE, 1)
                    both = both.astype(jnp.float32)
                    both = jnp.where(is_head, both + edge + tail, both).astype(jnp.bfloat16)
                trace[t * rows : (t + 1) * rows, b * LANES : (b + 1) * LANES] = both
            before = edge
        odd = (iota((rows, 2 * LANES), 1) & 1) == 1
        sign = jnp.where(odd, -1.0, 1.0)
        same = one_hot(
            iota((2 * LANES, LANES), 0) % LANES // BAND == iota((2 * LANES, LANES), 1) // BAND
        )
        group_segs = max(1, min(seg_count, part_rows // (per_seg * rows)))
        for first in range(0, seg_count, group_segs):
            segs = min(group_segs, seg_count - first)
            lhs = trace[first * per_seg * rows : (first + segs) * per_seg * rows, :]
            for j in range(CHUNKS):
                acc = jnp.dot(
                    lhs, tab_ref[:, 4 * j * LANES : 4 * (j + 1) * LANES],
                    preferred_element_type=jnp.float32,
                )
                half = acc[:, : 2 * LANES] + acc[:, 2 * LANES :]
                spec = []
                for g in range(segs):
                    a = half[g * per_seg * rows : (g * per_seg + 1) * rows]
                    b = half[(g * per_seg + 1) * rows : (g * per_seg + 2) * rows]
                    spec.append(a + sign * b)
                spec = jnp.concatenate(spec, axis=0)
                re, im = spec[:, :LANES], spec[:, LANES:]
                power = re * re + im * im
                hi = power.astype(jnp.bfloat16)
                lo = (power - hi.astype(jnp.float32)).astype(jnp.bfloat16)
                total = jnp.dot(
                    jnp.concatenate([hi, lo], axis=1), same, preferred_element_type=jnp.float32
                )
                scale = lax.rsqrt(total * (1.0 / BAND) + whiten_eps)
                w_re = (re * scale).astype(jnp.bfloat16).astype(jnp.float32)
                w_im = (im * scale).astype(jnp.bfloat16).astype(jnp.float32)
                at = 2 * j * LANES
                for g in range(segs):
                    r, o = g * rows, (first + g) * ch
                    own[o : o + ch, at : at + LANES] = w_re[r : r + ch]
                    own[o : o + ch, at + LANES : at + 2 * LANES] = w_im[r : r + ch]
                    o = (first + g) * src_count
                    other[o : o + src_count, at : at + LANES] = w_re[r + ch : r + rows]
                    other[o : o + src_count, at + LANES : at + 2 * LANES] = w_im[r + ch : r + rows]

    block = out_ref.shape[0]
    start = pl.multiple_of(pl.program_id(0) * block, 8)
    for j in range(CHUNKS):
        at = 2 * j * LANES
        a_re = [own[g * ch : (g + 1) * ch, at : at + LANES] for g in range(seg_count)]
        a_im = [own[g * ch : (g + 1) * ch, at + LANES : at + 2 * LANES] for g in range(seg_count)]
        for s in range(block):
            if s % 8 == 0:
                tiles = [
                    other[pl.ds(pl.multiple_of(g * src_count + start + s, 8), 8), at : at + 2 * LANES]
                    for g in range(seg_count)
                ]
            re = im = None
            for g in range(seg_count):
                b_re = tiles[g][s % 8 : s % 8 + 1, :LANES]
                b_im = tiles[g][s % 8 : s % 8 + 1, LANES:]
                p = a_re[g] * b_re + a_im[g] * b_im
                q = a_im[g] * b_re - a_re[g] * b_im
                re, im = (p, q) if re is None else (re + p, im + q)
            cross[s * ch : (s + 1) * ch, at : at + LANES] = re.astype(jnp.bfloat16)
            cross[s * ch : (s + 1) * ch, at + LANES : at + 2 * LANES] = im.astype(jnp.bfloat16)
    lags = sum(
        jnp.dot(
            cross[:, h * dec : (h + 1) * dec],
            tab_ref[:, d_cols + 2 * LAGH * h : d_cols + 2 * LAGH * (h + 1)],
            preferred_element_type=jnp.float32,
        )
        for h in range(per_seg)
    )
    out_ref[...] = lags.reshape(out_ref.shape)


def whole(space=pltpu.VMEM):
    return pl.BlockSpec(memory_space=space)


def local(raw_strain, fir_taps, source_channels, live_counts):
    rows, raw_len = raw_strain.shape
    steps = lax.axis_size("tm")
    chan_count = lax.axis_size("chan")
    dec = raw_len // DECIM
    blocks = dec // LANES
    ch = rows // steps
    seg_count = steps * dec // SEG
    src_count = source_channels.shape[0]
    slots = 2 * SRC_DEV * steps
    span = raw_len // blocks
    total_rows = ch + src_count
    tile_rows = edge_tiles(total_rows) * ROWS
    height = blocks * total_rows + tile_rows
    head_len = -(-(fir_taps.shape[0] - 1) // DECIM)
    assert head_len < EDGE and ch == ROWS and src_count <= 256
    src = source_channels.reshape(1, src_count)
    taps = fir_taps.reshape(1, fir_taps.shape[0])
    part, picked = pl.pallas_call(
        functools.partial(filter_kernel, blocks),
        out_shape=[
            pltpu.VMEM((steps, height, LANES), jnp.bfloat16),
            pltpu.VMEM((slots, dec + LANES), jnp.bfloat16),
        ],
        in_specs=[whole(pl.ANY)] * 3,
        out_specs=[whole(), whole()],
        scratch_shapes=[
            pltpu.VMEM((blocks * rows, span + LANES), jnp.bfloat16),
            pltpu.VMEM((2 * LANES, span + LANES), jnp.bfloat16),
            pltpu.VMEM(src.shape, src.dtype),
            pltpu.VMEM(taps.shape, taps.dtype),
            pltpu.SemaphoreType.DMA((blocks + 2,)),
        ],
        compiler_params=pltpu.CompilerParams(vmem_limit_bytes=16 * MIB),
        name="fir",
    )(*(pltpu.with_memory_space_constraint(a, pltpu.HBM) for a in (src, taps, raw_strain)))
    gathered = lax.all_gather(picked, "chan", axis=0, tiled=True)
    outgoing = pl.pallas_call(
        functools.partial(arrange_kernel, src_count, blocks),
        out_shape=pltpu.VMEM(part.shape, part.dtype),
        in_specs=[whole(), whole(pl.ANY)],
        out_specs=whole(pl.ANY),
        scratch_shapes=[
            pltpu.VMEM((blocks * src_count, LANES), jnp.bfloat16),
            pltpu.VMEM((steps, tile_rows, LANES), jnp.bfloat16),
            pltpu.SemaphoreType.DMA,
            pltpu.SemaphoreType.DMA((steps,)),
        ],
        input_output_aliases={1: 0},
        compiler_params=pltpu.CompilerParams(vmem_limit_bytes=8 * MIB),
        name="arrange",
    )(pltpu.with_memory_space_constraint(gathered, pltpu.VMEM), part)
    relaid = lax.all_to_all(outgoing, "tm", split_axis=0, concat_axis=0)
    block = math.gcd(src_count, 16)
    state = seg_count * total_rows * SEG * 4
    table = np.concatenate([dft_table(dec), *lag_table(seg_count).reshape(SEG // dec, dec, -1)], axis=1)
    return pl.pallas_call(
        functools.partial(correlate_kernel, seg_count, src_count, dec, head_len, 1024),
        grid=(src_count // block,),
        out_shape=jax.ShapeDtypeStruct((src_count, ch, 2 * LAGH), jnp.float32),
        in_specs=[whole(pltpu.SMEM), whole(), whole()],
        out_specs=pl.BlockSpec((block, ch, 2 * LAGH), lambda i: (i, 0, 0)),
        scratch_shapes=[
            pltpu.VMEM((steps * total_rows, dec), jnp.bfloat16),
            pltpu.VMEM((seg_count * ch, SEG), jnp.float32),
            pltpu.VMEM((seg_count * src_count, SEG), jnp.float32),
            pltpu.VMEM((block * ch, SEG), jnp.bfloat16),
        ],
        compiler_params=pltpu.CompilerParams(vmem_limit_bytes=16 * MIB + 2 * state),
        name="correlate",
    )(live_counts, relaid, jnp.asarray(table))


def solution(mesh):
    placed = (P("chan", "tm"), P(), P(), P(("chan", "tm")))
    return jax.shard_map(
        local, mesh=mesh, in_specs=placed, out_specs=P(None, ("chan", "tm"), None), check_vma=False
    )
```

```python
import functools
import math

import jax
import jax.numpy as jnp
import ml_dtypes
import numpy as np
from jax import lax
from jax.experimental import pallas as pl
from jax.experimental.pallas import tpu as pltpu
from jax.sharding import PartitionSpec as P

DECIM = 10
SEG = 1024
BAND = 64
LAGH = 192
SRC_DEV = 1
LANES = 128
HALF = SEG // 2
CHUNKS = HALF // LANES
EDGE = 14
PER_TILE = LANES // (3 * EDGE)
ROWS = 16
MIB = 1024 * 1024

whiten_eps = 1e-06

NT = (((1,), (1,)), ((), ()))


def split_table(table):
    hi = table.astype(ml_dtypes.bfloat16)
    lo = (table - hi.astype(np.float64)).astype(ml_dtypes.bfloat16)
    return hi, lo


def dft_table(rows):
    phase = (np.arange(rows)[:, None] * np.arange(HALF)[None, :] % SEG) * (2.0 * np.pi / SEG)
    parts = []
    for j in range(CHUNKS):
        cut = slice(j * LANES, (j + 1) * LANES)
        hi, lo = split_table(np.concatenate([np.cos(phase[:, cut]), -np.sin(phase[:, cut])], 1))
        parts += [hi, lo]
    return np.concatenate(parts, axis=1)


def lag_table(seg_count):
    freq = np.arange(HALF)[:, None]
    phase = (freq * np.arange(-LAGH, LAGH)[None, :] % SEG) * (2.0 * np.pi / SEG)
    weight = np.where(freq == 0, 1.0, 2.0) * (math.sqrt(SEG / seg_count) / SEG)
    re = (weight * np.cos(phase)).reshape(CHUNKS, LANES, 2 * LAGH)
    im = (-weight * np.sin(phase)).reshape(CHUNKS, LANES, 2 * LAGH)
    return np.concatenate([re, im], axis=1).reshape(SEG, 2 * LAGH).astype(ml_dtypes.bfloat16)


def iota(shape, dim):
    return lax.broadcasted_iota(jnp.int32, shape, dim)


def one_hot(mask):
    return jnp.where(mask, 1.0, 0.0).astype(jnp.bfloat16)


def column(row):
    n = row.shape[1]
    return jnp.sum(jnp.where(iota((n, n), 0) == iota((n, n), 1), row, 0), axis=1, keepdims=True)


def tap_rows(taps):
    tap_count = taps.shape[1]
    width = 3 * LANES
    flip = one_hot(iota((tap_count, width), 0) + iota((tap_count, width), 1) == tap_count)
    hi = taps.astype(jnp.bfloat16)
    lo = (taps - hi.astype(jnp.float32)).astype(jnp.bfloat16)
    out = []
    for part in (hi, lo):
        base = jnp.dot(
            jnp.broadcast_to(part.astype(jnp.float32), (8, tap_count)).astype(jnp.bfloat16),
            flip,
            preferred_element_type=jnp.float32,
        )
        upper = pltpu.roll(base, 0, 1, stride=DECIM, stride_axis=0)
        out.append(jnp.concatenate([upper, pltpu.roll(upper, 8 * DECIM, 1)], axis=0))
    return out


def edge_tiles(count):
    return -(-count // (PER_TILE * ROWS))


def filter_kernel(
    blocks, src_hbm, taps_hbm, raw_ref, out_ref, slot_ref, ext, weight, src_ref, taps_ref, sems
):
    rows, raw_len = raw_ref.shape
    steps = out_ref.shape[0]
    ch = rows // steps
    span = raw_len // blocks
    wide = span + LANES
    copies = []
    for b in range(blocks):
        if b == 0:
            copy = pltpu.make_async_copy(
                raw_ref.at[:, pl.ds(0, span)],
                ext.at[pl.ds(0, rows), pl.ds(LANES, span)],
                sems.at[b],
            )
        else:
            copy = pltpu.make_async_copy(
                raw_ref.at[:, pl.ds(b * span - LANES, wide)],
                ext.at[pl.ds(b * rows, rows), :],
                sems.at[b],
            )
        copy.start()
        copies.append(copy)
    small = [
        pltpu.make_async_copy(taps_hbm, taps_ref, sems.at[blocks]),
        pltpu.make_async_copy(src_hbm, src_ref, sems.at[blocks + 1]),
    ]
    for copy in small:
        copy.start()
    ext[:rows, :LANES] = jnp.zeros((rows, LANES), ext.dtype)
    weight[...] = jnp.zeros_like(weight)
    for copy in small:
        copy.wait()
    for p, base in enumerate(tap_rows(taps_ref[...])):
        for i in range(LANES // 16):
            tile, lane = divmod(16 * DECIM * i, LANES)
            piece = pltpu.roll(base, lane, 1) if lane else base
            weight[p * LANES + 16 * i : p * LANES + 16 * (i + 1), tile * LANES : (tile + 3) * LANES] = (
                piece.astype(jnp.bfloat16)
            )
    src = src_ref[...]
    src_count = src.shape[1]
    slots = slot_ref.shape[0]
    group = src // rows
    group_col = column(group)
    src_col = column(src)
    rank = jnp.sum(
        jnp.where(
            (group_col == group)
            & (iota((src_count, src_count), 0) < iota((src_count, src_count), 1)),
            1,
            0,
        ),
        axis=0,
        keepdims=True,
    )
    mine = lax.axis_index("chan")
    to_slot = one_hot((iota((slots, src_count), 0) == rank) & (group == mine))
    to_row = one_hot(src_col - mine * rows == iota((src_count, rows), 1))
    pick = jnp.dot(to_slot, to_row, preferred_element_type=jnp.float32).astype(jnp.bfloat16)
    number = jnp.where(
        iota((src_count, LANES), 1) == LANES - 1, iota((src_count, LANES), 0) + 1, 0
    ).astype(jnp.float32).astype(jnp.bfloat16)
    number = jnp.dot(to_slot, number, preferred_element_type=jnp.float32)
    for copy in copies:
        copy.wait()
    acc = lax.dot_general(ext[...], weight[...], NT, preferred_element_type=jnp.float32)
    acc = acc[:, :LANES] + acc[:, LANES:]
    y = acc.astype(jnp.bfloat16)
    head = acc[:rows]
    head_lo = head - head.astype(jnp.bfloat16).astype(jnp.float32)
    tail = lax.dot_general(
        ext[(blocks - 1) * rows :, wide - LANES :], weight[:, :LANES], NT,
        preferred_element_type=jnp.float32,
    )
    tail = tail[:, :LANES] + tail[:, LANES:]
    tail_hi = tail.astype(jnp.bfloat16).astype(jnp.float32)
    lane = iota((rows, LANES), 1)
    edge = jnp.where(
        lane < EDGE,
        head_lo,
        jnp.where(
            lane < 2 * EDGE,
            pltpu.roll(tail_hi, EDGE, 1),
            jnp.where(lane < 3 * EDGE, pltpu.roll(tail - tail_hi, 2 * EDGE, 1), 0.0),
        ),
    ).astype(jnp.bfloat16)
    parts = [y[b * rows : (b + 1) * rows] for b in range(blocks)] + [edge]
    last = blocks * ch
    for t in range(steps):
        for b in range(blocks):
            out_ref[t, b * ch : (b + 1) * ch] = parts[b][t * ch : (t + 1) * ch]
        out_ref[t, last : last + ch] = edge[t * ch : (t + 1) * ch]
    for b, part in enumerate(parts):
        found = jnp.dot(pick, part, preferred_element_type=jnp.float32)
        if b == blocks:
            found += number
        slot_ref[:, b * LANES : (b + 1) * LANES] = found.astype(jnp.bfloat16)


def arrange_kernel(src_count, blocks, order, slots_ref, part_ref, out_ref, fill, packs, sems):
    steps, height, _ = out_ref.shape
    tile_rows = packs.shape[1]
    own_rows = part_ref.shape[1] - ROWS
    copies = [
        pltpu.make_async_copy(
            part_ref.at[t, pl.ds(0, own_rows)], out_ref.at[p, pl.ds(0, own_rows)], sems.at[p]
        )
        for p, t in enumerate(order)
    ]
    for copy in copies:
        copy.start()
    numbers = slots_ref[:, blocks * LANES :].astype(jnp.float32)
    total = numbers.shape[0]
    numbers = jnp.sum(
        jnp.where(iota((total, LANES), 1) == LANES - 1, numbers, 0.0), axis=1, keepdims=True
    ).astype(jnp.int32)
    pick = one_hot(numbers == iota((total, src_count), 1) + 1)
    found = lax.dot_general(
        pick, slots_ref[...], (((0,), (0,)), ((), ())), preferred_element_type=jnp.float32
    )
    for b in range(blocks):
        fill[b * src_count : (b + 1) * src_count] = found[:, b * LANES : (b + 1) * LANES].astype(
            jnp.bfloat16
        )
    fills = [
        pltpu.make_async_copy(
            fill, out_ref.at[p, pl.ds(own_rows, fill.shape[0])], sems.at[steps + p]
        )
        for p in range(steps)
    ]
    for copy in fills:
        copy.start()
    edges = jnp.where(
        iota((src_count, LANES), 1) < 3 * EDGE, found[:, blocks * LANES :], 0.0
    )
    added = [jnp.zeros((ROWS, LANES), jnp.float32) for _ in range(tile_rows // ROWS)]
    for i in range(src_count // ROWS):
        tile, place = divmod(i + 1, PER_TILE)
        piece = edges[i * ROWS : (i + 1) * ROWS]
        added[tile] += pltpu.roll(piece, 3 * EDGE * place, 1) if place else piece
    for p, t in enumerate(order):
        own = part_ref[t, own_rows:].astype(jnp.float32)
        packs[p, :ROWS] = (own + added[0]).astype(jnp.bfloat16)
        for tile in range(1, tile_rows // ROWS):
            packs[p, tile * ROWS : (tile + 1) * ROWS] = added[tile].astype(jnp.bfloat16)
    store = pltpu.make_async_copy(
        packs, out_ref.at[:, pl.ds(height - tile_rows, tile_rows)], sems.at[2 * steps]
    )
    store.start()
    for copy in [*copies, *fills, store]:
        copy.wait()


def correlate_kernel(
    seg_count, src_count, dec, head_len, part_rows, order, count,
    live_ref, x_ref, tab_ref, out_ref,
    trace, own, other, cross, result, sems,
):
    steps, height, _ = x_ref.shape
    ch = out_ref.shape[1]
    rows = ch + src_count
    per_seg = SEG // dec
    blocks = dec // LANES
    d_cols = 4 * HALF

    @pl.when(pl.program_id(0) == 0)
    def _():
        live = iota((ch, LANES), 0) < live_ref[0]
        before = jnp.zeros((rows, LANES), jnp.float32)
        is_head = iota((rows, LANES), 1) < head_len
        last = height - edge_tiles(rows) * ROWS
        for t in range(steps):
            p = order.index(t)
            edge = []
            for i in range(rows // ROWS):
                tile, place = divmod(i, PER_TILE)
                if place == 0:
                    pack = x_ref[p, last + tile * ROWS : last + (tile + 1) * ROWS].astype(jnp.float32)
                    edge.append(pack)
                else:
                    edge.append(pltpu.roll(pack, LANES - 3 * EDGE * place, 1))
            edge[0] = jnp.where(live, edge[0], 0.0)
            edge = jnp.concatenate(edge, axis=0)
            for b in range(blocks):
                mine = x_ref[p, b * ch : (b + 1) * ch]
                mine = jnp.where(live, mine, jnp.zeros_like(mine))
                at = blocks * ch + b * src_count
                both = jnp.concatenate([mine, x_ref[p, at : at + src_count]], axis=0)
                if b == 0:
                    tail = pltpu.roll(before, LANES - EDGE, 1) + pltpu.roll(before, LANES - 2 * EDGE, 1)
                    both = both.astype(jnp.float32)
                    both = jnp.where(is_head, both + edge + tail, both).astype(jnp.bfloat16)
                trace[t * rows : (t + 1) * rows, b * LANES : (b + 1) * LANES] = both
            before = edge
        odd = (iota((rows, 2 * LANES), 1) & 1) == 1
        sign = jnp.where(odd, -1.0, 1.0)
        same = one_hot(
            iota((2 * LANES, LANES), 0) % LANES // BAND == iota((2 * LANES, LANES), 1) // BAND
        )
        group_segs = max(1, min(seg_count, part_rows // (per_seg * rows)))
        for first in range(0, seg_count, group_segs):
            segs = min(group_segs, seg_count - first)
            lhs = trace[first * per_seg * rows : (first + segs) * per_seg * rows, :]
            for j in range(CHUNKS):
                acc = jnp.dot(
                    lhs, tab_ref[:, 4 * j * LANES : 4 * (j + 1) * LANES],
                    preferred_element_type=jnp.float32,
                )
                half = acc[:, : 2 * LANES] + acc[:, 2 * LANES :]
                spec = []
                for g in range(segs):
                    a = half[g * per_seg * rows : (g * per_seg + 1) * rows]
                    b = half[(g * per_seg + 1) * rows : (g * per_seg + 2) * rows]
                    spec.append(a + sign * b)
                spec = jnp.concatenate(spec, axis=0)
                re, im = spec[:, :LANES], spec[:, LANES:]
                power = re * re + im * im
                hi = power.astype(jnp.bfloat16)
                lo = (power - hi.astype(jnp.float32)).astype(jnp.bfloat16)
                total = jnp.dot(
                    jnp.concatenate([hi, lo], axis=1), same, preferred_element_type=jnp.float32
                )
                scale = lax.rsqrt(total * (1.0 / BAND) + whiten_eps)
                w_re = (re * scale).astype(jnp.bfloat16).astype(jnp.float32)
                w_im = (im * scale).astype(jnp.bfloat16).astype(jnp.float32)
                at = 2 * j * LANES
                for g in range(segs):
                    r, o = g * rows, (first + g) * ch
                    own[o : o + ch, at : at + LANES] = w_re[r : r + ch]
                    own[o : o + ch, at + LANES : at + 2 * LANES] = w_im[r : r + ch]
                    o = (first + g) * src_count
                    other[o : o + src_count, at : at + LANES] = w_re[r + ch : r + rows]
                    other[o : o + src_count, at + LANES : at + 2 * LANES] = w_im[r + ch : r + rows]

    block = cross.shape[1] // ch
    copies = []
    for i in range(count):
        start = pl.multiple_of((pl.program_id(0) * count + i) * block, 8)
        for j in range(CHUNKS):
            at = 2 * j * LANES
            a_re = [own[g * ch : (g + 1) * ch, at : at + LANES] for g in range(seg_count)]
            a_im = [own[g * ch : (g + 1) * ch, at + LANES : at + 2 * LANES] for g in range(seg_count)]
            for s in range(block):
                if s % 8 == 0:
                    tiles = [
                        other[
                            pl.ds(pl.multiple_of(g * src_count + start + s, 8), 8),
                            at : at + 2 * LANES,
                        ]
                        for g in range(seg_count)
                    ]
                re = im = None
                for g in range(seg_count):
                    b_re = tiles[g][s % 8 : s % 8 + 1, :LANES]
                    b_im = tiles[g][s % 8 : s % 8 + 1, LANES:]
                    p = a_re[g] * b_re + a_im[g] * b_im
                    q = a_im[g] * b_re - a_re[g] * b_im
                    re, im = (p, q) if re is None else (re + p, im + q)
                row = slice(s * ch, (s + 1) * ch)
                cross[i, row, at : at + LANES] = re.astype(jnp.bfloat16)
                cross[i, row, at + LANES : at + 2 * LANES] = im.astype(jnp.bfloat16)
        lags = sum(
            jnp.dot(
                cross[i, :, h * dec : (h + 1) * dec],
                tab_ref[:, d_cols + 2 * LAGH * h : d_cols + 2 * LAGH * (h + 1)],
                preferred_element_type=jnp.float32,
            )
            for h in range(per_seg)
        )
        result[i] = lags.reshape(result.shape[1:])
        copy = pltpu.make_async_copy(result.at[i], out_ref.at[pl.ds(start, block)], sems.at[i])
        copy.start()
        copies.append(copy)
    for copy in copies:
        copy.wait()


def whole(space=pltpu.VMEM):
    return pl.BlockSpec(memory_space=space)


def local(raw_strain, fir_taps, source_channels, live_counts):
    rows, raw_len = raw_strain.shape
    steps = lax.axis_size("tm")
    chan_count = lax.axis_size("chan")
    dec = raw_len // DECIM
    blocks = dec // LANES
    ch = rows // steps
    seg_count = steps * dec // SEG
    src_count = source_channels.shape[0]
    slots = 2 * SRC_DEV * steps
    span = raw_len // blocks
    total_rows = ch + src_count
    tile_rows = edge_tiles(total_rows) * ROWS
    height = blocks * total_rows + tile_rows
    head_len = -(-(fir_taps.shape[0] - 1) // DECIM)
    assert head_len < EDGE and ch == ROWS and src_count <= 256
    src = source_channels.reshape(1, src_count)
    taps = fir_taps.reshape(1, fir_taps.shape[0])
    part, picked = pl.pallas_call(
        functools.partial(filter_kernel, blocks),
        out_shape=[
            pltpu.VMEM((steps, (blocks + 1) * ch, LANES), jnp.bfloat16),
            pltpu.VMEM((slots, dec + LANES), jnp.bfloat16),
        ],
        in_specs=[whole(pl.ANY)] * 3,
        out_specs=[whole(), whole()],
        scratch_shapes=[
            pltpu.VMEM((blocks * rows, span + LANES), jnp.bfloat16),
            pltpu.VMEM((2 * LANES, span + LANES), jnp.bfloat16),
            pltpu.VMEM(src.shape, src.dtype),
            pltpu.VMEM(taps.shape, taps.dtype),
            pltpu.SemaphoreType.DMA((blocks + 2,)),
        ],
        compiler_params=pltpu.CompilerParams(vmem_limit_bytes=16 * MIB),
        name="fir",
    )(*(pltpu.with_memory_space_constraint(a, pltpu.HBM) for a in (src, taps, raw_strain)))
    order = list(range(steps))
    if steps % 8 == 0:
        order = [
            q * (steps // 4) + r for r in range(steps // 4) for q in (0, 2, 1, 3)
        ]
    gathered = lax.all_gather(picked, "chan", axis=0, tiled=True)
    outgoing = pl.pallas_call(
        functools.partial(arrange_kernel, src_count, blocks, order),
        out_shape=pltpu.HBM((steps, height, LANES), jnp.bfloat16),
        in_specs=[whole(), whole()],
        out_specs=whole(pl.ANY),
        scratch_shapes=[
            pltpu.VMEM((blocks * src_count, LANES), jnp.bfloat16),
            pltpu.VMEM((steps, tile_rows, LANES), jnp.bfloat16),
            pltpu.SemaphoreType.DMA((2 * steps + 1,)),
        ],
        compiler_params=pltpu.CompilerParams(vmem_limit_bytes=8 * MIB),
        name="arrange",
    )(*(pltpu.with_memory_space_constraint(a, pltpu.VMEM) for a in (gathered, part)))
    relaid = lax.all_to_all(outgoing, "tm", 0, 0, axis_index_groups=[order])
    block = math.gcd(src_count, 16)
    count = math.gcd(src_count // block, 2)
    state = seg_count * total_rows * SEG * 4
    table = np.concatenate([dft_table(dec), *lag_table(seg_count).reshape(SEG // dec, dec, -1)], axis=1)
    return pl.pallas_call(
        functools.partial(
            correlate_kernel, seg_count, src_count, dec, head_len, 1024, order, count
        ),
        grid=(src_count // (block * count),),
        out_shape=jax.ShapeDtypeStruct((src_count, ch, 2 * LAGH), jnp.float32),
        in_specs=[whole(pltpu.SMEM), whole(), whole()],
        out_specs=whole(pl.ANY),
        scratch_shapes=[
            pltpu.VMEM((steps * total_rows, dec), jnp.bfloat16),
            pltpu.VMEM((seg_count * ch, SEG), jnp.float32),
            pltpu.VMEM((seg_count * src_count, SEG), jnp.float32),
            pltpu.VMEM((count, block * ch, SEG), jnp.bfloat16),
            pltpu.VMEM((count, block, ch, 2 * LAGH), jnp.float32),
            pltpu.SemaphoreType.DMA((count,)),
        ],
        compiler_params=pltpu.CompilerParams(vmem_limit_bytes=16 * MIB + 2 * state),
        name="correlate",
    )(live_counts, relaid, jnp.asarray(table))


def solution(mesh):
    placed = (P("chan", "tm"), P(), P(), P(("chan", "tm")))
    return jax.shard_map(
        local, mesh=mesh, in_specs=placed, out_specs=P(None, ("chan", "tm"), None), check_vma=False
    )
```

```python
import functools
import math

import jax
import jax.numpy as jnp
import ml_dtypes
import numpy as np
from jax import lax
from jax.experimental import pallas as pl
from jax.experimental.pallas import tpu as pltpu
from jax.sharding import PartitionSpec as P

DECIM = 10
SEG = 1024
BAND = 64
LAGH = 192
SRC_DEV = 1
LANES = 128
HALF = SEG // 2
CHUNKS = HALF // LANES
EDGE = 14
PER_TILE = LANES // (3 * EDGE)
ROWS = 16
CORES = 2
MIB = 1024 * 1024

whiten_eps = 1e-06

NT = (((1,), (1,)), ((), ()))


def split_table(table):
    hi = table.astype(ml_dtypes.bfloat16)
    lo = (table - hi.astype(np.float64)).astype(ml_dtypes.bfloat16)
    return hi, lo


def dft_table(rows):
    phase = (np.arange(rows)[:, None] * np.arange(HALF)[None, :] % SEG) * (2.0 * np.pi / SEG)
    parts = []
    for j in range(CHUNKS):
        cut = slice(j * LANES, (j + 1) * LANES)
        hi, lo = split_table(np.concatenate([np.cos(phase[:, cut]), -np.sin(phase[:, cut])], 1))
        parts += [hi, lo]
    return np.concatenate(parts, axis=1)


def lag_table(seg_count):
    freq = np.arange(HALF)[:, None]
    phase = (freq * np.arange(-LAGH, LAGH)[None, :] % SEG) * (2.0 * np.pi / SEG)
    weight = np.where(freq == 0, 1.0, 2.0) * (math.sqrt(SEG / seg_count) / SEG)
    re = (weight * np.cos(phase)).reshape(CHUNKS, LANES, 2 * LAGH)
    im = (-weight * np.sin(phase)).reshape(CHUNKS, LANES, 2 * LAGH)
    return np.concatenate([re, im], axis=1).reshape(SEG, 2 * LAGH).astype(ml_dtypes.bfloat16)


def iota(shape, dim):
    return lax.broadcasted_iota(jnp.int32, shape, dim)


def one_hot(mask):
    return jnp.where(mask, 1.0, 0.0).astype(jnp.bfloat16)


def column(row):
    n = row.shape[1]
    return jnp.sum(jnp.where(iota((n, n), 0) == iota((n, n), 1), row, 0), axis=1, keepdims=True)


def tap_rows(taps):
    tap_count = taps.shape[1]
    width = 3 * LANES
    flip = one_hot(iota((tap_count, width), 0) + iota((tap_count, width), 1) == tap_count)
    hi = taps.astype(jnp.bfloat16)
    lo = (taps - hi.astype(jnp.float32)).astype(jnp.bfloat16)
    out = []
    for part in (hi, lo):
        base = jnp.dot(
            jnp.broadcast_to(part.astype(jnp.float32), (8, tap_count)).astype(jnp.bfloat16),
            flip,
            preferred_element_type=jnp.float32,
        )
        upper = pltpu.roll(base, 0, 1, stride=DECIM, stride_axis=0)
        out.append(jnp.concatenate([upper, pltpu.roll(upper, 8 * DECIM, 1)], axis=0))
    return out


def edge_tiles(count):
    return -(-count // (PER_TILE * ROWS))


def filter_kernel(
    blocks, src_hbm, taps_hbm, raw_ref, out_ref, slot_ref, ext, weight, src_ref, taps_ref, sems
):
    rows, raw_len = raw_ref.shape
    steps = out_ref.shape[0]
    ch = rows // steps
    span = raw_len // blocks
    wide = span + LANES
    copies = []
    for b in range(blocks):
        if b == 0:
            copy = pltpu.make_async_copy(
                raw_ref.at[:, pl.ds(0, span)],
                ext.at[pl.ds(0, rows), pl.ds(LANES, span)],
                sems.at[b],
            )
        else:
            copy = pltpu.make_async_copy(
                raw_ref.at[:, pl.ds(b * span - LANES, wide)],
                ext.at[pl.ds(b * rows, rows), :],
                sems.at[b],
            )
        copy.start()
        copies.append(copy)
    small = [
        pltpu.make_async_copy(taps_hbm, taps_ref, sems.at[blocks]),
        pltpu.make_async_copy(src_hbm, src_ref, sems.at[blocks + 1]),
    ]
    for copy in small:
        copy.start()
    ext[:rows, :LANES] = jnp.zeros((rows, LANES), ext.dtype)
    weight[...] = jnp.zeros_like(weight)
    for copy in small:
        copy.wait()
    for p, base in enumerate(tap_rows(taps_ref[...])):
        for i in range(LANES // 16):
            tile, lane = divmod(16 * DECIM * i, LANES)
            piece = pltpu.roll(base, lane, 1) if lane else base
            weight[p * LANES + 16 * i : p * LANES + 16 * (i + 1), tile * LANES : (tile + 3) * LANES] = (
                piece.astype(jnp.bfloat16)
            )
    src = src_ref[...]
    src_count = src.shape[1]
    slots = slot_ref.shape[0]
    group = src // rows
    group_col = column(group)
    src_col = column(src)
    rank = jnp.sum(
        jnp.where(
            (group_col == group)
            & (iota((src_count, src_count), 0) < iota((src_count, src_count), 1)),
            1,
            0,
        ),
        axis=0,
        keepdims=True,
    )
    mine = lax.axis_index("chan")
    to_slot = one_hot((iota((slots, src_count), 0) == rank) & (group == mine))
    to_row = one_hot(src_col - mine * rows == iota((src_count, rows), 1))
    pick = jnp.dot(to_slot, to_row, preferred_element_type=jnp.float32).astype(jnp.bfloat16)
    number = jnp.where(
        iota((src_count, LANES), 1) == LANES - 1, iota((src_count, LANES), 0) + 1, 0
    ).astype(jnp.float32).astype(jnp.bfloat16)
    number = jnp.dot(to_slot, number, preferred_element_type=jnp.float32)
    for copy in copies:
        copy.wait()
    acc = lax.dot_general(ext[...], weight[...], NT, preferred_element_type=jnp.float32)
    acc = acc[:, :LANES] + acc[:, LANES:]
    y = acc.astype(jnp.bfloat16)
    head = acc[:rows]
    head_lo = head - head.astype(jnp.bfloat16).astype(jnp.float32)
    tail = lax.dot_general(
        ext[(blocks - 1) * rows :, wide - LANES :], weight[:, :LANES], NT,
        preferred_element_type=jnp.float32,
    )
    tail = tail[:, :LANES] + tail[:, LANES:]
    tail_hi = tail.astype(jnp.bfloat16).astype(jnp.float32)
    lane = iota((rows, LANES), 1)
    edge = jnp.where(
        lane < EDGE,
        head_lo,
        jnp.where(
            lane < 2 * EDGE,
            pltpu.roll(tail_hi, EDGE, 1),
            jnp.where(lane < 3 * EDGE, pltpu.roll(tail - tail_hi, 2 * EDGE, 1), 0.0),
        ),
    ).astype(jnp.bfloat16)
    parts = [y[b * rows : (b + 1) * rows] for b in range(blocks)] + [edge]
    last = blocks * ch
    for t in range(steps):
        for b in range(blocks):
            out_ref[t, b * ch : (b + 1) * ch] = parts[b][t * ch : (t + 1) * ch]
        out_ref[t, last : last + ch] = edge[t * ch : (t + 1) * ch]
    for b, part in enumerate(parts):
        found = jnp.dot(pick, part, preferred_element_type=jnp.float32)
        if b == blocks:
            found += number
        slot_ref[:, b * LANES : (b + 1) * LANES] = found.astype(jnp.bfloat16)


def arrange_kernel(half, blocks, order, slots_ref, part_ref, out_ref, fill, packs, sems):
    steps, height, _ = out_ref.shape
    tile_rows = packs.shape[1]
    own_rows = part_ref.shape[1] - ROWS
    copies = [
        pltpu.make_async_copy(
            part_ref.at[t, pl.ds(0, own_rows)], out_ref.at[p, pl.ds(0, own_rows)], sems.at[p]
        )
        for p, t in enumerate(order)
    ]
    for copy in copies:
        copy.start()
    numbers = slots_ref[:, blocks * LANES :].astype(jnp.float32)
    total = numbers.shape[0]
    numbers = jnp.sum(
        jnp.where(iota((total, LANES), 1) == LANES - 1, numbers, 0.0), axis=1, keepdims=True
    ).astype(jnp.int32)
    first = lax.axis_index("chan") % CORES * half
    pick = one_hot(numbers == iota((total, half), 1) + 1 + first)
    found = lax.dot_general(
        pick, slots_ref[...], (((0,), (0,)), ((), ())), preferred_element_type=jnp.float32
    )
    for b in range(blocks):
        fill[b * half : (b + 1) * half] = found[:, b * LANES : (b + 1) * LANES].astype(
            jnp.bfloat16
        )
    fills = [
        pltpu.make_async_copy(
            fill, out_ref.at[p, pl.ds(own_rows, fill.shape[0])], sems.at[steps + p]
        )
        for p in range(steps)
    ]
    for copy in fills:
        copy.start()
    edges = jnp.where(
        iota((half, LANES), 1) < 3 * EDGE, found[:, blocks * LANES :], 0.0
    )
    added = [jnp.zeros((ROWS, LANES), jnp.float32) for _ in range(tile_rows // ROWS)]
    for i in range(half // ROWS):
        tile, place = divmod(i + 1, PER_TILE)
        piece = edges[i * ROWS : (i + 1) * ROWS]
        added[tile] += pltpu.roll(piece, 3 * EDGE * place, 1) if place else piece
    for p, t in enumerate(order):
        own = part_ref[t, own_rows:].astype(jnp.float32)
        packs[p, :ROWS] = (own + added[0]).astype(jnp.bfloat16)
        for tile in range(1, tile_rows // ROWS):
            packs[p, tile * ROWS : (tile + 1) * ROWS] = added[tile].astype(jnp.bfloat16)
    store = pltpu.make_async_copy(
        packs, out_ref.at[:, pl.ds(height - tile_rows, tile_rows)], sems.at[2 * steps]
    )
    store.start()
    for copy in [*copies, *fills, store]:
        copy.wait()


def correlate_kernel(
    seg_count, src_count, dec, head_len, part_rows, order, count,
    live_ref, near_ref, far_ref, tab_ref, out_ref,
    trace, own, other, cross, result, sems,
):
    steps, height, _ = near_ref.shape
    ch = out_ref.shape[1]
    half = src_count // CORES
    rows = ch + src_count
    per_seg = SEG // dec
    blocks = dec // LANES
    d_cols = 4 * HALF

    @pl.when(pl.program_id(0) == 0)
    def _():
        live = iota((ch, LANES), 0) < live_ref[0]
        before = jnp.zeros((rows, LANES), jnp.float32)
        is_head = iota((rows, LANES), 1) < head_len
        last = height - edge_tiles(ch + half) * ROWS
        low_core = lax.axis_index("chan") % CORES == 0

        def edge_groups(ref, p):
            out = []
            for i in range((ch + half) // ROWS):
                tile, place = divmod(i, PER_TILE)
                if place == 0:
                    pack = ref[p, last + tile * ROWS : last + (tile + 1) * ROWS].astype(jnp.float32)
                    out.append(pack)
                else:
                    out.append(pltpu.roll(pack, LANES - 3 * EDGE * place, 1))
            return out[0], jnp.concatenate(out[1:], axis=0)

        def in_order(near, far):
            return [jnp.where(low_core, near, far), jnp.where(low_core, far, near)]

        for t in range(steps):
            p = order.index(t)
            edge, near = edge_groups(near_ref, p)
            _, far = edge_groups(far_ref, p)
            edge = jnp.concatenate([jnp.where(live, edge, 0.0), *in_order(near, far)], axis=0)
            for b in range(blocks):
                mine = near_ref[p, b * ch : (b + 1) * ch]
                mine = jnp.where(live, mine, jnp.zeros_like(mine))
                at = blocks * ch + b * half
                both = jnp.concatenate(
                    [mine, *in_order(near_ref[p, at : at + half], far_ref[p, at : at + half])], axis=0
                )
                if b == 0:
                    tail = pltpu.roll(before, LANES - EDGE, 1) + pltpu.roll(before, LANES - 2 * EDGE, 1)
                    both = both.astype(jnp.float32)
                    both = jnp.where(is_head, both + edge + tail, both).astype(jnp.bfloat16)
                trace[t * rows : (t + 1) * rows, b * LANES : (b + 1) * LANES] = both
            before = edge
        odd = (iota((rows, 2 * LANES), 1) & 1) == 1
        sign = jnp.where(odd, -1.0, 1.0)
        same = one_hot(
            iota((2 * LANES, LANES), 0) % LANES // BAND == iota((2 * LANES, LANES), 1) // BAND
        )
        group_segs = max(1, min(seg_count, part_rows // (per_seg * rows)))
        for first in range(0, seg_count, group_segs):
            segs = min(group_segs, seg_count - first)
            lhs = trace[first * per_seg * rows : (first + segs) * per_seg * rows, :]
            for j in range(CHUNKS):
                acc = jnp.dot(
                    lhs, tab_ref[:, 4 * j * LANES : 4 * (j + 1) * LANES],
                    preferred_element_type=jnp.float32,
                )
                folded = acc[:, : 2 * LANES] + acc[:, 2 * LANES :]
                spec = []
                for g in range(segs):
                    a = folded[g * per_seg * rows : (g * per_seg + 1) * rows]
                    b = folded[(g * per_seg + 1) * rows : (g * per_seg + 2) * rows]
                    spec.append(a + sign * b)
                spec = jnp.concatenate(spec, axis=0)
                re, im = spec[:, :LANES], spec[:, LANES:]
                power = re * re + im * im
                hi = power.astype(jnp.bfloat16)
                lo = (power - hi.astype(jnp.float32)).astype(jnp.bfloat16)
                total = jnp.dot(
                    jnp.concatenate([hi, lo], axis=1), same, preferred_element_type=jnp.float32
                )
                scale = lax.rsqrt(total * (1.0 / BAND) + whiten_eps)
                w_re = (re * scale).astype(jnp.bfloat16).astype(jnp.float32)
                w_im = (im * scale).astype(jnp.bfloat16).astype(jnp.float32)
                at = 2 * j * LANES
                for g in range(segs):
                    r, o = g * rows, (first + g) * ch
                    own[o : o + ch, at : at + LANES] = w_re[r : r + ch]
                    own[o : o + ch, at + LANES : at + 2 * LANES] = w_im[r : r + ch]
                    o = (first + g) * src_count
                    other[o : o + src_count, at : at + LANES] = w_re[r + ch : r + rows]
                    other[o : o + src_count, at + LANES : at + 2 * LANES] = w_im[r + ch : r + rows]

    block = cross.shape[1] // ch
    copies = []
    for i in range(count):
        start = pl.multiple_of((pl.program_id(0) * count + i) * block, 8)
        for j in range(CHUNKS):
            at = 2 * j * LANES
            a_re = [own[g * ch : (g + 1) * ch, at : at + LANES] for g in range(seg_count)]
            a_im = [own[g * ch : (g + 1) * ch, at + LANES : at + 2 * LANES] for g in range(seg_count)]
            for s in range(block):
                if s % 8 == 0:
                    tiles = [
                        other[
                            pl.ds(pl.multiple_of(g * src_count + start + s, 8), 8),
                            at : at + 2 * LANES,
                        ]
                        for g in range(seg_count)
                    ]
                re = im = None
                for g in range(seg_count):
                    b_re = tiles[g][s % 8 : s % 8 + 1, :LANES]
                    b_im = tiles[g][s % 8 : s % 8 + 1, LANES:]
                    p = a_re[g] * b_re + a_im[g] * b_im
                    q = a_im[g] * b_re - a_re[g] * b_im
                    re, im = (p, q) if re is None else (re + p, im + q)
                row = slice(s * ch, (s + 1) * ch)
                cross[i, row, at : at + LANES] = re.astype(jnp.bfloat16)
                cross[i, row, at + LANES : at + 2 * LANES] = im.astype(jnp.bfloat16)
        lags = sum(
            jnp.dot(
                cross[i, :, h * dec : (h + 1) * dec],
                tab_ref[:, d_cols + 2 * LAGH * h : d_cols + 2 * LAGH * (h + 1)],
                preferred_element_type=jnp.float32,
            )
            for h in range(per_seg)
        )
        result[i] = lags.reshape(result.shape[1:])
        copy = pltpu.make_async_copy(result.at[i], out_ref.at[pl.ds(start, block)], sems.at[i])
        copy.start()
        copies.append(copy)
    for copy in copies:
        copy.wait()


def whole(space=pltpu.VMEM):
    return pl.BlockSpec(memory_space=space)


def local(raw_strain, fir_taps, source_channels, live_counts):
    rows, raw_len = raw_strain.shape
    steps = lax.axis_size("tm")
    chan_count = lax.axis_size("chan")
    dec = raw_len // DECIM
    blocks = dec // LANES
    ch = rows // steps
    seg_count = steps * dec // SEG
    src_count = source_channels.shape[0]
    slots = 2 * SRC_DEV * steps
    span = raw_len // blocks
    total_rows = ch + src_count
    half = src_count // CORES
    tile_rows = edge_tiles(ch + half) * ROWS
    height = blocks * (ch + half) + tile_rows
    head_len = -(-(fir_taps.shape[0] - 1) // DECIM)
    assert head_len < EDGE and ch == ROWS and src_count <= 256 and half % ROWS == 0
    src = source_channels.reshape(1, src_count)
    taps = fir_taps.reshape(1, fir_taps.shape[0])
    part, picked = pl.pallas_call(
        functools.partial(filter_kernel, blocks),
        out_shape=[
            pltpu.VMEM((steps, (blocks + 1) * ch, LANES), jnp.bfloat16),
            pltpu.VMEM((slots, dec + LANES), jnp.bfloat16),
        ],
        in_specs=[whole(pl.ANY)] * 3,
        out_specs=[whole(), whole()],
        scratch_shapes=[
            pltpu.VMEM((blocks * rows, span + LANES), jnp.bfloat16),
            pltpu.VMEM((2 * LANES, span + LANES), jnp.bfloat16),
            pltpu.VMEM(src.shape, src.dtype),
            pltpu.VMEM(taps.shape, taps.dtype),
            pltpu.SemaphoreType.DMA((blocks + 2,)),
        ],
        compiler_params=pltpu.CompilerParams(vmem_limit_bytes=16 * MIB),
        name="fir",
    )(*(pltpu.with_memory_space_constraint(a, pltpu.HBM) for a in (src, taps, raw_strain)))
    order = list(range(steps))
    if steps % 8 == 0:
        order = [
            q * (steps // 4) + r for r in range(steps // 4) for q in (2, 0, 3, 1)
        ]
    gathered = lax.all_gather(picked, "chan", axis=0, tiled=True)
    outgoing = pl.pallas_call(
        functools.partial(arrange_kernel, half, blocks, order),
        out_shape=pltpu.HBM((steps, height, LANES), jnp.bfloat16),
        in_specs=[whole(), whole()],
        out_specs=whole(pl.ANY),
        scratch_shapes=[
            pltpu.VMEM((blocks * half, LANES), jnp.bfloat16),
            pltpu.VMEM((steps, tile_rows, LANES), jnp.bfloat16),
            pltpu.SemaphoreType.DMA((2 * steps + 1,)),
        ],
        compiler_params=pltpu.CompilerParams(vmem_limit_bytes=8 * MIB),
        name="arrange",
    )(*(pltpu.with_memory_space_constraint(a, pltpu.VMEM) for a in (gathered, part)))
    relaid = lax.all_to_all(outgoing, "tm", 0, 0, axis_index_groups=[order])
    swapped = lax.ppermute(relaid, "chan", [(c, c ^ 1) for c in range(chan_count)])
    block = math.gcd(src_count, 16)
    count = math.gcd(src_count // block, 2)
    state = seg_count * total_rows * SEG * 4
    table = np.concatenate([dft_table(dec), *lag_table(seg_count).reshape(SEG // dec, dec, -1)], axis=1)
    return pl.pallas_call(
        functools.partial(
            correlate_kernel, seg_count, src_count, dec, head_len, 1024, order, count
        ),
        grid=(src_count // (block * count),),
        out_shape=jax.ShapeDtypeStruct((src_count, ch, 2 * LAGH), jnp.float32),
        in_specs=[whole(pltpu.SMEM)] + [whole()] * 3,
        out_specs=whole(pl.ANY),
        scratch_shapes=[
            pltpu.VMEM((steps * total_rows, dec), jnp.bfloat16),
            pltpu.VMEM((seg_count * ch, SEG), jnp.float32),
            pltpu.VMEM((seg_count * src_count, SEG), jnp.float32),
            pltpu.VMEM((count, block * ch, SEG), jnp.bfloat16),
            pltpu.VMEM((count, block, ch, 2 * LAGH), jnp.float32),
            pltpu.SemaphoreType.DMA((count,)),
        ],
        compiler_params=pltpu.CompilerParams(vmem_limit_bytes=16 * MIB + 2 * state),
        name="correlate",
    )(live_counts, relaid, swapped, jnp.asarray(table))


def solution(mesh):
    placed = (P("chan", "tm"), P(), P(), P(("chan", "tm")))
    return jax.shard_map(
        local, mesh=mesh, in_specs=placed, out_specs=P(None, ("chan", "tm"), None), check_vma=False
    )
```

```python
import functools
import math

import jax
import jax.numpy as jnp
import ml_dtypes
import numpy as np
from jax import lax
from jax.experimental import pallas as pl
from jax.experimental.pallas import tpu as pltpu
from jax.sharding import PartitionSpec as P

DECIM = 10
SEG = 1024
BAND = 64
LAGH = 192
SRC_DEV = 1
LANES = 128
HALF = SEG // 2
CHUNKS = HALF // LANES
EDGE = 14
PER_TILE = LANES // (3 * EDGE)
ROWS = 16
CORES = 2
MIB = 1024 * 1024

whiten_eps = 1e-06

NT = (((1,), (1,)), ((), ()))


def split_table(table):
    hi = table.astype(ml_dtypes.bfloat16)
    lo = (table - hi.astype(np.float64)).astype(ml_dtypes.bfloat16)
    return hi, lo


def dft_table(rows):
    phase = (np.arange(rows)[:, None] * np.arange(HALF)[None, :] % SEG) * (2.0 * np.pi / SEG)
    parts = []
    for j in range(CHUNKS):
        cut = slice(j * LANES, (j + 1) * LANES)
        hi, lo = split_table(np.concatenate([np.cos(phase[:, cut]), -np.sin(phase[:, cut])], 1))
        parts += [hi, lo]
    return np.concatenate(parts, axis=1)


def lag_table(seg_count):
    freq = np.arange(HALF)[:, None]
    phase = (freq * np.arange(-LAGH, LAGH)[None, :] % SEG) * (2.0 * np.pi / SEG)
    weight = np.where(freq == 0, 1.0, 2.0) * (math.sqrt(SEG / seg_count) / SEG)
    re = (weight * np.cos(phase)).reshape(CHUNKS, LANES, 2 * LAGH)
    im = (-weight * np.sin(phase)).reshape(CHUNKS, LANES, 2 * LAGH)
    return np.concatenate([re, im], axis=1).reshape(SEG, 2 * LAGH).astype(ml_dtypes.bfloat16)


def iota(shape, dim):
    return lax.broadcasted_iota(jnp.int32, shape, dim)


def one_hot(mask):
    return jnp.where(mask, 1.0, 0.0).astype(jnp.bfloat16)


def column(row):
    n = row.shape[1]
    return jnp.sum(jnp.where(iota((n, n), 0) == iota((n, n), 1), row, 0), axis=1, keepdims=True)


def tap_rows(taps):
    tap_count = taps.shape[1]
    width = 3 * LANES
    flip = one_hot(iota((tap_count, width), 0) + iota((tap_count, width), 1) == tap_count)
    hi = taps.astype(jnp.bfloat16)
    lo = (taps - hi.astype(jnp.float32)).astype(jnp.bfloat16)
    out = []
    for part in (hi, lo):
        base = jnp.dot(
            jnp.broadcast_to(part.astype(jnp.float32), (8, tap_count)).astype(jnp.bfloat16),
            flip,
            preferred_element_type=jnp.float32,
        )
        upper = pltpu.roll(base, 0, 1, stride=DECIM, stride_axis=0)
        out.append(jnp.concatenate([upper, pltpu.roll(upper, 8 * DECIM, 1)], axis=0))
    return out


def edge_tiles(count):
    return -(-count // (PER_TILE * ROWS))


def filter_kernel(
    blocks,
    src_hbm, taps_hbm, raw_ref, tab_hbm,
    out_ref, slot_ref, tab_ref,
    ext, weight, src_ref, taps_ref, sems,
):
    rows, raw_len = raw_ref.shape
    steps = out_ref.shape[0]
    ch = rows // steps
    span = raw_len // blocks
    wide = span + LANES
    copies = []
    for b in range(blocks):
        if b == 0:
            copy = pltpu.make_async_copy(
                raw_ref.at[:, pl.ds(0, span)],
                ext.at[pl.ds(0, rows), pl.ds(LANES, span)],
                sems.at[b],
            )
        else:
            copy = pltpu.make_async_copy(
                raw_ref.at[:, pl.ds(b * span - LANES, wide)],
                ext.at[pl.ds(b * rows, rows), :],
                sems.at[b],
            )
        copy.start()
        copies.append(copy)
    small = [
        pltpu.make_async_copy(taps_hbm, taps_ref, sems.at[blocks]),
        pltpu.make_async_copy(src_hbm, src_ref, sems.at[blocks + 1]),
    ]
    tables = pltpu.make_async_copy(tab_hbm, tab_ref, sems.at[blocks + 2])
    for copy in [*small, tables]:
        copy.start()
    ext[:rows, :LANES] = jnp.zeros((rows, LANES), ext.dtype)
    weight[...] = jnp.zeros_like(weight)
    for copy in small:
        copy.wait()
    for p, base in enumerate(tap_rows(taps_ref[...])):
        for i in range(LANES // 16):
            tile, lane = divmod(16 * DECIM * i, LANES)
            piece = pltpu.roll(base, lane, 1) if lane else base
            weight[p * LANES + 16 * i : p * LANES + 16 * (i + 1), tile * LANES : (tile + 3) * LANES] = (
                piece.astype(jnp.bfloat16)
            )
    src = src_ref[...]
    src_count = src.shape[1]
    slots = slot_ref.shape[0]
    group = src // rows
    group_col = column(group)
    src_col = column(src)
    rank = jnp.sum(
        jnp.where(
            (group_col == group)
            & (iota((src_count, src_count), 0) < iota((src_count, src_count), 1)),
            1,
            0,
        ),
        axis=0,
        keepdims=True,
    )
    mine = lax.axis_index("chan")
    to_slot = one_hot((iota((slots, src_count), 0) == rank) & (group == mine))
    to_row = one_hot(src_col - mine * rows == iota((src_count, rows), 1))
    pick = jnp.dot(to_slot, to_row, preferred_element_type=jnp.float32).astype(jnp.bfloat16)
    number = jnp.where(
        iota((src_count, LANES), 1) == LANES - 1, iota((src_count, LANES), 0) + 1, 0
    ).astype(jnp.float32).astype(jnp.bfloat16)
    number = jnp.dot(to_slot, number, preferred_element_type=jnp.float32)
    for copy in copies:
        copy.wait()
    acc = lax.dot_general(ext[...], weight[...], NT, preferred_element_type=jnp.float32)
    acc = acc[:, :LANES] + acc[:, LANES:]
    y = acc.astype(jnp.bfloat16)
    head = acc[:rows]
    head_lo = head - head.astype(jnp.bfloat16).astype(jnp.float32)
    tail = lax.dot_general(
        ext[(blocks - 1) * rows :, wide - LANES :], weight[:, :LANES], NT,
        preferred_element_type=jnp.float32,
    )
    tail = tail[:, :LANES] + tail[:, LANES:]
    tail_hi = tail.astype(jnp.bfloat16).astype(jnp.float32)
    lane = iota((rows, LANES), 1)
    edge = jnp.where(
        lane < EDGE,
        head_lo,
        jnp.where(
            lane < 2 * EDGE,
            pltpu.roll(tail_hi, EDGE, 1),
            jnp.where(lane < 3 * EDGE, pltpu.roll(tail - tail_hi, 2 * EDGE, 1), 0.0),
        ),
    ).astype(jnp.bfloat16)
    parts = [y[b * rows : (b + 1) * rows] for b in range(blocks)] + [edge]
    last = blocks * ch
    for t in range(steps):
        for b in range(blocks):
            out_ref[t, b * ch : (b + 1) * ch] = parts[b][t * ch : (t + 1) * ch]
        out_ref[t, last : last + ch] = edge[t * ch : (t + 1) * ch]
    for b, part in enumerate(parts):
        found = jnp.dot(pick, part, preferred_element_type=jnp.float32)
        if b == blocks:
            found += number
        slot_ref[:, b * LANES : (b + 1) * LANES] = found.astype(jnp.bfloat16)
    tables.wait()


def arrange_kernel(half, blocks, order, slots_ref, part_ref, out_ref, fill, packs, sems):
    steps, height, _ = out_ref.shape
    tile_rows = packs.shape[1]
    own_rows = part_ref.shape[1] - ROWS
    copies = [
        pltpu.make_async_copy(
            part_ref.at[t, pl.ds(0, own_rows)], out_ref.at[p, pl.ds(0, own_rows)], sems.at[p]
        )
        for p, t in enumerate(order)
    ]
    for copy in copies:
        copy.start()
    numbers = slots_ref[:, blocks * LANES :].astype(jnp.float32)
    total = numbers.shape[0]
    numbers = jnp.sum(
        jnp.where(iota((total, LANES), 1) == LANES - 1, numbers, 0.0), axis=1, keepdims=True
    ).astype(jnp.int32)
    first = lax.axis_index("chan") % CORES * half
    pick = one_hot(numbers == iota((total, half), 1) + 1 + first)
    found = lax.dot_general(
        pick, slots_ref[...], (((0,), (0,)), ((), ())), preferred_element_type=jnp.float32
    )
    for b in range(blocks):
        fill[b * half : (b + 1) * half] = found[:, b * LANES : (b + 1) * LANES].astype(
            jnp.bfloat16
        )
    fills = [
        pltpu.make_async_copy(
            fill, out_ref.at[p, pl.ds(own_rows, fill.shape[0])], sems.at[steps + p]
        )
        for p in range(steps)
    ]
    for copy in fills:
        copy.start()
    edges = jnp.where(
        iota((half, LANES), 1) < 3 * EDGE, found[:, blocks * LANES :], 0.0
    )
    added = [jnp.zeros((ROWS, LANES), jnp.float32) for _ in range(tile_rows // ROWS)]
    for i in range(half // ROWS):
        tile, place = divmod(i + 1, PER_TILE)
        piece = edges[i * ROWS : (i + 1) * ROWS]
        added[tile] += pltpu.roll(piece, 3 * EDGE * place, 1) if place else piece
    for p, t in enumerate(order):
        own = part_ref[t, own_rows:].astype(jnp.float32)
        packs[p, :ROWS] = (own + added[0]).astype(jnp.bfloat16)
        for tile in range(1, tile_rows // ROWS):
            packs[p, tile * ROWS : (tile + 1) * ROWS] = added[tile].astype(jnp.bfloat16)
    store = pltpu.make_async_copy(
        packs, out_ref.at[:, pl.ds(height - tile_rows, tile_rows)], sems.at[2 * steps]
    )
    store.start()
    for copy in [*copies, *fills, store]:
        copy.wait()


def correlate_kernel(
    seg_count, src_count, dec, head_len, part_rows, order, count,
    live_ref, near_ref, far_ref, tab_ref, out_ref,
    trace, own, other, cross, result, sems,
):
    steps, height, _ = near_ref.shape
    ch = out_ref.shape[1]
    half = src_count // CORES
    rows = ch + src_count
    per_seg = SEG // dec
    blocks = dec // LANES
    d_cols = 4 * HALF

    @pl.when(pl.program_id(0) == 0)
    def _():
        live = iota((ch, LANES), 0) < live_ref[0]
        before = jnp.zeros((rows, LANES), jnp.float32)
        is_head = iota((rows, LANES), 1) < head_len
        last = height - edge_tiles(ch + half) * ROWS
        low_core = lax.axis_index("chan") % CORES == 0

        def edge_groups(ref, p):
            out = []
            for i in range((ch + half) // ROWS):
                tile, place = divmod(i, PER_TILE)
                if place == 0:
                    pack = ref[p, last + tile * ROWS : last + (tile + 1) * ROWS].astype(jnp.float32)
                    out.append(pack)
                else:
                    out.append(pltpu.roll(pack, LANES - 3 * EDGE * place, 1))
            return out[0], jnp.concatenate(out[1:], axis=0)

        def in_order(near, far):
            return [jnp.where(low_core, near, far), jnp.where(low_core, far, near)]

        for t in range(steps):
            p = order.index(t)
            edge, near = edge_groups(near_ref, p)
            _, far = edge_groups(far_ref, p)
            edge = jnp.concatenate([jnp.where(live, edge, 0.0), *in_order(near, far)], axis=0)
            for b in range(blocks):
                mine = near_ref[p, b * ch : (b + 1) * ch]
                mine = jnp.where(live, mine, jnp.zeros_like(mine))
                at = blocks * ch + b * half
                both = jnp.concatenate(
                    [mine, *in_order(near_ref[p, at : at + half], far_ref[p, at : at + half])], axis=0
                )
                if b == 0:
                    tail = pltpu.roll(before, LANES - EDGE, 1) + pltpu.roll(before, LANES - 2 * EDGE, 1)
                    both = both.astype(jnp.float32)
                    both = jnp.where(is_head, both + edge + tail, both).astype(jnp.bfloat16)
                trace[t * rows : (t + 1) * rows, b * LANES : (b + 1) * LANES] = both
            before = edge
        odd = (iota((rows, 2 * LANES), 1) & 1) == 1
        sign = jnp.where(odd, -1.0, 1.0)
        same = one_hot(
            iota((2 * LANES, LANES), 0) % LANES // BAND == iota((2 * LANES, LANES), 1) // BAND
        )
        group_segs = max(1, min(seg_count, part_rows // (per_seg * rows)))
        for first in range(0, seg_count, group_segs):
            segs = min(group_segs, seg_count - first)
            lhs = trace[first * per_seg * rows : (first + segs) * per_seg * rows, :]
            for j in range(CHUNKS):
                acc = jnp.dot(
                    lhs, tab_ref[:, 4 * j * LANES : 4 * (j + 1) * LANES],
                    preferred_element_type=jnp.float32,
                )
                folded = acc[:, : 2 * LANES] + acc[:, 2 * LANES :]
                spec = []
                for g in range(segs):
                    a = folded[g * per_seg * rows : (g * per_seg + 1) * rows]
                    b = folded[(g * per_seg + 1) * rows : (g * per_seg + 2) * rows]
                    spec.append(a + sign * b)
                spec = jnp.concatenate(spec, axis=0)
                re, im = spec[:, :LANES], spec[:, LANES:]
                power = re * re + im * im
                hi = power.astype(jnp.bfloat16)
                lo = (power - hi.astype(jnp.float32)).astype(jnp.bfloat16)
                total = jnp.dot(
                    jnp.concatenate([hi, lo], axis=1), same, preferred_element_type=jnp.float32
                )
                scale = lax.rsqrt(total * (1.0 / BAND) + whiten_eps)
                w_re = (re * scale).astype(jnp.bfloat16).astype(jnp.float32)
                w_im = (im * scale).astype(jnp.bfloat16).astype(jnp.float32)
                at = 2 * j * LANES
                for g in range(segs):
                    r, o = g * rows, (first + g) * ch
                    own[o : o + ch, at : at + LANES] = w_re[r : r + ch]
                    own[o : o + ch, at + LANES : at + 2 * LANES] = w_im[r : r + ch]
                    o = (first + g) * src_count
                    other[o : o + src_count, at : at + LANES] = w_re[r + ch : r + rows]
                    other[o : o + src_count, at + LANES : at + 2 * LANES] = w_im[r + ch : r + rows]

    block = cross.shape[1] // ch
    copies = []
    for i in range(count):
        start = pl.multiple_of((pl.program_id(0) * count + i) * block, 8)
        for j in range(CHUNKS):
            at = 2 * j * LANES
            a_re = [own[g * ch : (g + 1) * ch, at : at + LANES] for g in range(seg_count)]
            a_im = [own[g * ch : (g + 1) * ch, at + LANES : at + 2 * LANES] for g in range(seg_count)]
            for s in range(block):
                if s % 8 == 0:
                    tiles = [
                        other[
                            pl.ds(pl.multiple_of(g * src_count + start + s, 8), 8),
                            at : at + 2 * LANES,
                        ]
                        for g in range(seg_count)
                    ]
                re = im = None
                for g in range(seg_count):
                    b_re = tiles[g][s % 8 : s % 8 + 1, :LANES]
                    b_im = tiles[g][s % 8 : s % 8 + 1, LANES:]
                    p = a_re[g] * b_re + a_im[g] * b_im
                    q = a_im[g] * b_re - a_re[g] * b_im
                    re, im = (p, q) if re is None else (re + p, im + q)
                row = slice(s * ch, (s + 1) * ch)
                cross[i, row, at : at + LANES] = re.astype(jnp.bfloat16)
                cross[i, row, at + LANES : at + 2 * LANES] = im.astype(jnp.bfloat16)
        lags = sum(
            jnp.dot(
                cross[i, :, h * dec : (h + 1) * dec],
                tab_ref[:, d_cols + 2 * LAGH * h : d_cols + 2 * LAGH * (h + 1)],
                preferred_element_type=jnp.float32,
            )
            for h in range(per_seg)
        )
        result[i] = lags.reshape(result.shape[1:])
        copy = pltpu.make_async_copy(result.at[i], out_ref.at[pl.ds(start, block)], sems.at[i])
        copy.start()
        copies.append(copy)
    for copy in copies:
        copy.wait()


def whole(space=pltpu.VMEM):
    return pl.BlockSpec(memory_space=space)


def local(raw_strain, fir_taps, source_channels, live_counts):
    rows, raw_len = raw_strain.shape
    steps = lax.axis_size("tm")
    chan_count = lax.axis_size("chan")
    dec = raw_len // DECIM
    blocks = dec // LANES
    ch = rows // steps
    seg_count = steps * dec // SEG
    src_count = source_channels.shape[0]
    slots = 2 * SRC_DEV * steps
    span = raw_len // blocks
    total_rows = ch + src_count
    half = src_count // CORES
    tile_rows = edge_tiles(ch + half) * ROWS
    height = blocks * (ch + half) + tile_rows
    head_len = -(-(fir_taps.shape[0] - 1) // DECIM)
    assert head_len < EDGE and ch == ROWS and src_count <= 256 and half % ROWS == 0
    src = source_channels.reshape(1, src_count)
    taps = fir_taps.reshape(1, fir_taps.shape[0])
    table = np.concatenate([dft_table(dec), *lag_table(seg_count).reshape(SEG // dec, dec, -1)], axis=1)
    inputs = (src, taps, raw_strain, jnp.asarray(table))
    part, picked, table = pl.pallas_call(
        functools.partial(filter_kernel, blocks),
        out_shape=[
            pltpu.VMEM((steps, (blocks + 1) * ch, LANES), jnp.bfloat16),
            pltpu.VMEM((slots, dec + LANES), jnp.bfloat16),
            pltpu.VMEM(table.shape, jnp.bfloat16),
        ],
        in_specs=[whole(pl.ANY)] * 4,
        out_specs=[whole(), whole(), whole(pl.ANY)],
        scratch_shapes=[
            pltpu.VMEM((blocks * rows, span + LANES), jnp.bfloat16),
            pltpu.VMEM((2 * LANES, span + LANES), jnp.bfloat16),
            pltpu.VMEM(src.shape, src.dtype),
            pltpu.VMEM(taps.shape, taps.dtype),
            pltpu.SemaphoreType.DMA((blocks + 3,)),
        ],
        compiler_params=pltpu.CompilerParams(vmem_limit_bytes=16 * MIB),
        name="fir",
    )(*(pltpu.with_memory_space_constraint(a, pltpu.HBM) for a in inputs))
    order = list(range(steps))
    if steps % 8 == 0:
        order = [
            q * (steps // 4) + r for r in range(steps // 4) for q in (2, 0, 3, 1)
        ]
    gathered = lax.all_gather(picked, "chan", axis=0, tiled=True)
    outgoing = pl.pallas_call(
        functools.partial(arrange_kernel, half, blocks, order),
        out_shape=pltpu.HBM((steps, height, LANES), jnp.bfloat16),
        in_specs=[whole(), whole()],
        out_specs=whole(pl.ANY),
        scratch_shapes=[
            pltpu.VMEM((blocks * half, LANES), jnp.bfloat16),
            pltpu.VMEM((steps, tile_rows, LANES), jnp.bfloat16),
            pltpu.SemaphoreType.DMA((2 * steps + 1,)),
        ],
        compiler_params=pltpu.CompilerParams(vmem_limit_bytes=8 * MIB),
        name="arrange",
    )(*(pltpu.with_memory_space_constraint(a, pltpu.VMEM) for a in (gathered, part)))
    relaid = lax.all_to_all(outgoing, "tm", 0, 0, axis_index_groups=[order])
    swapped = lax.ppermute(relaid, "chan", [(c, c ^ 1) for c in range(chan_count)])
    block = math.gcd(src_count, 16)
    count = math.gcd(src_count // block, 2)
    state = seg_count * total_rows * SEG * 4
    return pl.pallas_call(
        functools.partial(
            correlate_kernel, seg_count, src_count, dec, head_len, 1024, order, count
        ),
        grid=(src_count // (block * count),),
        out_shape=jax.ShapeDtypeStruct((src_count, ch, 2 * LAGH), jnp.float32),
        in_specs=[whole(pltpu.SMEM)] + [whole()] * 3,
        out_specs=whole(pl.ANY),
        scratch_shapes=[
            pltpu.VMEM((steps * total_rows, dec), jnp.bfloat16),
            pltpu.VMEM((seg_count * ch, SEG), jnp.float32),
            pltpu.VMEM((seg_count * src_count, SEG), jnp.float32),
            pltpu.VMEM((count, block * ch, SEG), jnp.bfloat16),
            pltpu.VMEM((count, block, ch, 2 * LAGH), jnp.float32),
            pltpu.SemaphoreType.DMA((count,)),
        ],
        compiler_params=pltpu.CompilerParams(vmem_limit_bytes=16 * MIB + 2 * state),
        name="correlate",
    )(live_counts, relaid, swapped, table)


def solution(mesh):
    placed = (P("chan", "tm"), P(), P(), P(("chan", "tm")))
    return jax.shard_map(
        local, mesh=mesh, in_specs=placed, out_specs=P(None, ("chan", "tm"), None), check_vma=False
    )
```

```python
import functools
import math

import jax
import jax.numpy as jnp
import ml_dtypes
import numpy as np
from jax import lax
from jax.experimental import pallas as pl
from jax.experimental.pallas import tpu as pltpu
from jax.sharding import PartitionSpec as P

DECIM = 10
SEG = 1024
BAND = 64
LAGH = 192
SRC_DEV = 1
LANES = 128
HALF = SEG // 2
CHUNKS = HALF // LANES
EDGE = 14
PER_TILE = LANES // (3 * EDGE)
ROWS = 16
CORES = 2
MIB = 1024 * 1024

whiten_eps = 1e-06

NT = (((1,), (1,)), ((), ()))


def split_table(table):
    hi = table.astype(ml_dtypes.bfloat16)
    lo = (table - hi.astype(np.float64)).astype(ml_dtypes.bfloat16)
    return hi, lo


def dft_table(rows):
    phase = (np.arange(rows)[:, None] * np.arange(HALF)[None, :] % SEG) * (2.0 * np.pi / SEG)
    parts = []
    for j in range(CHUNKS):
        cut = slice(j * LANES, (j + 1) * LANES)
        hi, lo = split_table(np.concatenate([np.cos(phase[:, cut]), -np.sin(phase[:, cut])], 1))
        parts += [hi, lo]
    return np.concatenate(parts, axis=1)


def lag_table(seg_count):
    freq = np.arange(HALF)[:, None]
    phase = (freq * np.arange(-LAGH, LAGH)[None, :] % SEG) * (2.0 * np.pi / SEG)
    weight = np.where(freq == 0, 1.0, 2.0) * (math.sqrt(SEG / seg_count) / SEG)
    re = (weight * np.cos(phase)).reshape(CHUNKS, LANES, 2 * LAGH)
    im = (-weight * np.sin(phase)).reshape(CHUNKS, LANES, 2 * LAGH)
    return np.concatenate([re, im], axis=1).reshape(SEG, 2 * LAGH).astype(ml_dtypes.bfloat16)


def iota(shape, dim):
    return lax.broadcasted_iota(jnp.int32, shape, dim)


def one_hot(mask):
    return jnp.where(mask, 1.0, 0.0).astype(jnp.bfloat16)


def column(row):
    n = row.shape[1]
    return jnp.sum(jnp.where(iota((n, n), 0) == iota((n, n), 1), row, 0), axis=1, keepdims=True)


def tap_rows(taps):
    tap_count = taps.shape[1]
    width = 3 * LANES
    flip = one_hot(iota((tap_count, width), 0) + iota((tap_count, width), 1) == tap_count)
    hi = taps.astype(jnp.bfloat16)
    lo = (taps - hi.astype(jnp.float32)).astype(jnp.bfloat16)
    out = []
    for part in (hi, lo):
        base = jnp.dot(
            jnp.broadcast_to(part.astype(jnp.float32), (8, tap_count)).astype(jnp.bfloat16),
            flip,
            preferred_element_type=jnp.float32,
        )
        upper = pltpu.roll(base, 0, 1, stride=DECIM, stride_axis=0)
        out.append(jnp.concatenate([upper, pltpu.roll(upper, 8 * DECIM, 1)], axis=0))
    return out


def edge_tiles(count):
    return -(-count // (PER_TILE * ROWS))


def filter_kernel(
    blocks,
    src_hbm, taps_hbm, raw_ref, tab_hbm,
    out_ref, slot_ref, tab_ref,
    ext, weight, src_ref, taps_ref, sems,
):
    rows, raw_len = raw_ref.shape
    steps = out_ref.shape[0]
    ch = rows // steps
    span = raw_len // blocks
    wide = span + LANES
    copies = []
    for b in range(blocks):
        if b == 0:
            copy = pltpu.make_async_copy(
                raw_ref.at[:, pl.ds(0, span)],
                ext.at[pl.ds(0, rows), pl.ds(LANES, span)],
                sems.at[b],
            )
        else:
            copy = pltpu.make_async_copy(
                raw_ref.at[:, pl.ds(b * span - LANES, wide)],
                ext.at[pl.ds(b * rows, rows), :],
                sems.at[b],
            )
        copy.start()
        copies.append(copy)
    small = [
        pltpu.make_async_copy(taps_hbm, taps_ref, sems.at[blocks]),
        pltpu.make_async_copy(src_hbm, src_ref, sems.at[blocks + 1]),
    ]
    tables = pltpu.make_async_copy(tab_hbm, tab_ref, sems.at[blocks + 2])
    for copy in [*small, tables]:
        copy.start()
    ext[:rows, :LANES] = jnp.zeros((rows, LANES), ext.dtype)
    weight[...] = jnp.zeros_like(weight)
    for copy in small:
        copy.wait()
    for p, base in enumerate(tap_rows(taps_ref[...])):
        for i in range(LANES // 16):
            tile, lane = divmod(16 * DECIM * i, LANES)
            piece = pltpu.roll(base, lane, 1) if lane else base
            weight[p * LANES + 16 * i : p * LANES + 16 * (i + 1), tile * LANES : (tile + 3) * LANES] = (
                piece.astype(jnp.bfloat16)
            )
    src = src_ref[...]
    src_count = src.shape[1]
    slots = slot_ref.shape[0]
    group = src // rows
    group_col = column(group)
    src_col = column(src)
    rank = jnp.sum(
        jnp.where(
            (group_col == group)
            & (iota((src_count, src_count), 0) < iota((src_count, src_count), 1)),
            1,
            0,
        ),
        axis=0,
        keepdims=True,
    )
    mine = lax.axis_index("chan")
    to_slot = one_hot((iota((slots, src_count), 0) == rank) & (group == mine))
    to_row = one_hot(src_col - mine * rows == iota((src_count, rows), 1))
    pick = jnp.dot(to_slot, to_row, preferred_element_type=jnp.float32).astype(jnp.bfloat16)
    number = jnp.where(
        iota((src_count, LANES), 1) == LANES - 1, iota((src_count, LANES), 0) + 1, 0
    ).astype(jnp.float32).astype(jnp.bfloat16)
    number = jnp.dot(to_slot, number, preferred_element_type=jnp.float32)
    for copy in copies:
        copy.wait()
    acc = lax.dot_general(ext[...], weight[...], NT, preferred_element_type=jnp.float32)
    acc = acc[:, :LANES] + acc[:, LANES:]
    y = acc.astype(jnp.bfloat16)
    head = acc[:rows]
    head_lo = head - head.astype(jnp.bfloat16).astype(jnp.float32)
    tail = lax.dot_general(
        ext[(blocks - 1) * rows :, wide - LANES :], weight[:, :LANES], NT,
        preferred_element_type=jnp.float32,
    )
    tail = tail[:, :LANES] + tail[:, LANES:]
    tail_hi = tail.astype(jnp.bfloat16).astype(jnp.float32)
    lane = iota((rows, LANES), 1)
    edge = jnp.where(
        lane < EDGE,
        head_lo,
        jnp.where(
            lane < 2 * EDGE,
            pltpu.roll(tail_hi, EDGE, 1),
            jnp.where(lane < 3 * EDGE, pltpu.roll(tail - tail_hi, 2 * EDGE, 1), 0.0),
        ),
    ).astype(jnp.bfloat16)
    parts = [y[b * rows : (b + 1) * rows] for b in range(blocks)] + [edge]
    last = blocks * ch
    for t in range(steps):
        for b in range(blocks):
            out_ref[t, b * ch : (b + 1) * ch] = parts[b][t * ch : (t + 1) * ch]
        out_ref[t, last : last + ch] = edge[t * ch : (t + 1) * ch]
    for b, part in enumerate(parts):
        found = jnp.dot(pick, part, preferred_element_type=jnp.float32)
        if b == blocks:
            found += number
        slot_ref[:, b * LANES : (b + 1) * LANES] = found.astype(jnp.bfloat16)
    tables.wait()


def arrange_kernel(half, blocks, order, slots_ref, part_ref, out_ref, fill, packs, sems):
    steps, height, _ = out_ref.shape
    tile_rows = packs.shape[1]
    own_rows = part_ref.shape[1] - ROWS
    copies = [
        pltpu.make_async_copy(
            part_ref.at[t, pl.ds(0, own_rows)], out_ref.at[p, pl.ds(0, own_rows)], sems.at[p]
        )
        for p, t in enumerate(order)
    ]
    for copy in copies:
        copy.start()
    numbers = slots_ref[:, blocks * LANES :].astype(jnp.float32)
    total = numbers.shape[0]
    numbers = jnp.sum(
        jnp.where(iota((total, LANES), 1) == LANES - 1, numbers, 0.0), axis=1, keepdims=True
    ).astype(jnp.int32)
    first = lax.axis_index("chan") % CORES * half
    pick = one_hot(numbers == iota((total, half), 1) + 1 + first)
    found = lax.dot_general(
        pick, slots_ref[...], (((0,), (0,)), ((), ())), preferred_element_type=jnp.float32
    )
    for b in range(blocks):
        fill[b * half : (b + 1) * half] = found[:, b * LANES : (b + 1) * LANES].astype(
            jnp.bfloat16
        )
    fills = [
        pltpu.make_async_copy(
            fill, out_ref.at[p, pl.ds(own_rows, fill.shape[0])], sems.at[steps + p]
        )
        for p in range(steps)
    ]
    for copy in fills:
        copy.start()
    edges = jnp.where(
        iota((half, LANES), 1) < 3 * EDGE, found[:, blocks * LANES :], 0.0
    )
    added = [jnp.zeros((ROWS, LANES), jnp.float32) for _ in range(tile_rows // ROWS)]
    for i in range(half // ROWS):
        tile, place = divmod(i + 1, PER_TILE)
        piece = edges[i * ROWS : (i + 1) * ROWS]
        added[tile] += pltpu.roll(piece, 3 * EDGE * place, 1) if place else piece
    for p, t in enumerate(order):
        own = part_ref[t, own_rows:].astype(jnp.float32)
        packs[p, :ROWS] = (own + added[0]).astype(jnp.bfloat16)
        for tile in range(1, tile_rows // ROWS):
            packs[p, tile * ROWS : (tile + 1) * ROWS] = added[tile].astype(jnp.bfloat16)
    store = pltpu.make_async_copy(
        packs, out_ref.at[:, pl.ds(height - tile_rows, tile_rows)], sems.at[2 * steps]
    )
    store.start()
    for copy in [*copies, *fills, store]:
        copy.wait()


def lay_traces(trace, ref, live, order, ch, half, blocks, head_len, with_own):
    steps, height, _ = ref.shape
    rows = half + (ch if with_own else 0)
    before = jnp.zeros((rows, LANES), jnp.float32)
    is_head = iota((rows, LANES), 1) < head_len
    last = height - edge_tiles(ch + half) * ROWS
    for t in range(steps):
        p = order.index(t)
        edge = []
        for i in range((ch + half) // ROWS):
            tile, place = divmod(i, PER_TILE)
            if place == 0:
                pack = ref[p, last + tile * ROWS : last + (tile + 1) * ROWS].astype(jnp.float32)
                edge.append(pack)
            else:
                edge.append(pltpu.roll(pack, LANES - 3 * EDGE * place, 1))
        if with_own:
            edge[0] = jnp.where(live, edge[0], 0.0)
        else:
            edge = edge[1:]
        edge = jnp.concatenate(edge, axis=0)
        for b in range(blocks):
            at = blocks * ch + b * half
            both = ref[p, at : at + half]
            if with_own:
                mine = ref[p, b * ch : (b + 1) * ch]
                mine = jnp.where(live, mine, jnp.zeros_like(mine))
                both = jnp.concatenate([mine, both], axis=0)
            if b == 0:
                tail = pltpu.roll(before, LANES - EDGE, 1) + pltpu.roll(before, LANES - 2 * EDGE, 1)
                both = both.astype(jnp.float32)
                both = jnp.where(is_head, both + edge + tail, both).astype(jnp.bfloat16)
            trace[t * rows : (t + 1) * rows, b * LANES : (b + 1) * LANES] = both
        before = edge


def whiten(trace, tab_ref, seg_count, rows, dec, part_rows, targets):
    per_seg = SEG // dec
    sign = jnp.where((iota((rows, 2 * LANES), 1) & 1) == 1, -1.0, 1.0)
    same = one_hot(
        iota((2 * LANES, LANES), 0) % LANES // BAND == iota((2 * LANES, LANES), 1) // BAND
    )
    group_segs = max(1, min(seg_count, part_rows // (per_seg * rows)))
    for first in range(0, seg_count, group_segs):
        segs = min(group_segs, seg_count - first)
        lhs = trace[first * per_seg * rows : (first + segs) * per_seg * rows, :]
        for j in range(CHUNKS):
            acc = jnp.dot(
                lhs, tab_ref[:, 4 * j * LANES : 4 * (j + 1) * LANES],
                preferred_element_type=jnp.float32,
            )
            folded = acc[:, : 2 * LANES] + acc[:, 2 * LANES :]
            spec = []
            for g in range(segs):
                a = folded[g * per_seg * rows : (g * per_seg + 1) * rows]
                b = folded[(g * per_seg + 1) * rows : (g * per_seg + 2) * rows]
                spec.append(a + sign * b)
            spec = jnp.concatenate(spec, axis=0)
            re, im = spec[:, :LANES], spec[:, LANES:]
            power = re * re + im * im
            hi = power.astype(jnp.bfloat16)
            lo = (power - hi.astype(jnp.float32)).astype(jnp.bfloat16)
            total = jnp.dot(
                jnp.concatenate([hi, lo], axis=1), same, preferred_element_type=jnp.float32
            )
            scale = lax.rsqrt(total * (1.0 / BAND) + whiten_eps)
            w_re = (re * scale).astype(jnp.bfloat16).astype(jnp.float32)
            w_im = (im * scale).astype(jnp.bfloat16).astype(jnp.float32)
            at = 2 * j * LANES
            for g in range(segs):
                r = g * rows
                for ref, n in targets:
                    o = (first + g) * n
                    ref[o : o + n, at : at + LANES] = w_re[r : r + n]
                    ref[o : o + n, at + LANES : at + 2 * LANES] = w_im[r : r + n]
                    r += n


def near_kernel(
    seg_count, dec, head_len, part_rows, order, ch,
    live_ref, near_ref, tab_ref, own, other,
    trace,
):
    half = other.shape[0] // seg_count
    live = iota((ch, LANES), 0) < live_ref[0]
    lay_traces(trace, near_ref, live, order, ch, half, dec // LANES, head_len, True)
    whiten(
        trace, tab_ref, seg_count, ch + half, dec, part_rows, [(own, ch), (other, half)]
    )


def correlate_kernel(
    seg_count, dec, head_len, part_rows, order, single,
    far_ref, tab_ref, own, near, out_ref,
    trace, far, cross, result, sems,
):
    ch = own.shape[0] // seg_count
    half = near.shape[0] // seg_count
    per_seg = SEG // dec
    d_cols = 4 * HALF

    def prepare():
        lay_traces(trace, far_ref, None, order, ch, half, dec // LANES, head_len, False)
        whiten(trace, tab_ref, seg_count, half, dec, part_rows, [(far, half)])

    if single:
        prepare()
    else:
        pl.when(pl.program_id(0) == 0)(prepare)

    core = lax.axis_index("chan") % CORES
    block = cross.shape[1] // ch
    start = pl.multiple_of(pl.program_id(0) * block, 8)
    if single:
        start = 0
    copies = []
    for i, (other, place) in enumerate([(near, core), (far, 1 - core)]):
        for j in range(CHUNKS):
            at = 2 * j * LANES
            a_re = [own[g * ch : (g + 1) * ch, at : at + LANES] for g in range(seg_count)]
            a_im = [own[g * ch : (g + 1) * ch, at + LANES : at + 2 * LANES] for g in range(seg_count)]
            for s in range(block):
                if s % 8 == 0:
                    tiles = [
                        other[
                            pl.ds(pl.multiple_of(g * half + start + s, 8), 8),
                            at : at + 2 * LANES,
                        ]
                        for g in range(seg_count)
                    ]
                re = im = None
                for g in range(seg_count):
                    b_re = tiles[g][s % 8 : s % 8 + 1, :LANES]
                    b_im = tiles[g][s % 8 : s % 8 + 1, LANES:]
                    p = a_re[g] * b_re + a_im[g] * b_im
                    q = a_im[g] * b_re - a_re[g] * b_im
                    re, im = (p, q) if re is None else (re + p, im + q)
                row = slice(s * ch, (s + 1) * ch)
                cross[i, row, at : at + LANES] = re.astype(jnp.bfloat16)
                cross[i, row, at + LANES : at + 2 * LANES] = im.astype(jnp.bfloat16)
        lags = sum(
            jnp.dot(
                cross[i, :, h * dec : (h + 1) * dec],
                tab_ref[:, d_cols + 2 * LAGH * h : d_cols + 2 * LAGH * (h + 1)],
                preferred_element_type=jnp.float32,
            )
            for h in range(per_seg)
        )
        result[i] = lags.reshape(result.shape[1:])
        copy = pltpu.make_async_copy(
            result.at[i], out_ref.at[pl.ds(place * half + start, block)], sems.at[i]
        )
        copy.start()
        copies.append(copy)
    for copy in copies:
        copy.wait()


def whole(space=pltpu.VMEM):
    return pl.BlockSpec(memory_space=space)


def local(raw_strain, fir_taps, source_channels, live_counts):
    rows, raw_len = raw_strain.shape
    steps = lax.axis_size("tm")
    chan_count = lax.axis_size("chan")
    dec = raw_len // DECIM
    blocks = dec // LANES
    ch = rows // steps
    seg_count = steps * dec // SEG
    src_count = source_channels.shape[0]
    slots = 2 * SRC_DEV * steps
    span = raw_len // blocks
    total_rows = ch + src_count
    half = src_count // CORES
    tile_rows = edge_tiles(ch + half) * ROWS
    height = blocks * (ch + half) + tile_rows
    head_len = -(-(fir_taps.shape[0] - 1) // DECIM)
    assert head_len < EDGE and ch == ROWS and src_count <= 256 and half % ROWS == 0
    src = source_channels.reshape(1, src_count)
    taps = fir_taps.reshape(1, fir_taps.shape[0])
    table = np.concatenate([dft_table(dec), *lag_table(seg_count).reshape(SEG // dec, dec, -1)], axis=1)
    inputs = (src, taps, raw_strain, jnp.asarray(table))
    part, picked, table = pl.pallas_call(
        functools.partial(filter_kernel, blocks),
        out_shape=[
            pltpu.VMEM((steps, (blocks + 1) * ch, LANES), jnp.bfloat16),
            pltpu.VMEM((slots, dec + LANES), jnp.bfloat16),
            pltpu.VMEM(table.shape, jnp.bfloat16),
        ],
        in_specs=[whole(pl.ANY)] * 4,
        out_specs=[whole(), whole(), whole(pl.ANY)],
        scratch_shapes=[
            pltpu.VMEM((blocks * rows, span + LANES), jnp.bfloat16),
            pltpu.VMEM((2 * LANES, span + LANES), jnp.bfloat16),
            pltpu.VMEM(src.shape, src.dtype),
            pltpu.VMEM(taps.shape, taps.dtype),
            pltpu.SemaphoreType.DMA((blocks + 3,)),
        ],
        compiler_params=pltpu.CompilerParams(vmem_limit_bytes=16 * MIB),
        name="fir",
    )(*(pltpu.with_memory_space_constraint(a, pltpu.HBM) for a in inputs))
    order = list(range(steps))
    if steps % 8 == 0:
        order = [
            q * (steps // 4) + r for r in range(steps // 4) for q in (2, 0, 3, 1)
        ]
    gathered = lax.all_gather(picked, "chan", axis=0, tiled=True)
    outgoing = pl.pallas_call(
        functools.partial(arrange_kernel, half, blocks, order),
        out_shape=pltpu.HBM((steps, height, LANES), jnp.bfloat16),
        in_specs=[whole(), whole()],
        out_specs=whole(pl.ANY),
        scratch_shapes=[
            pltpu.VMEM((blocks * half, LANES), jnp.bfloat16),
            pltpu.VMEM((steps, tile_rows, LANES), jnp.bfloat16),
            pltpu.SemaphoreType.DMA((2 * steps + 1,)),
        ],
        compiler_params=pltpu.CompilerParams(vmem_limit_bytes=8 * MIB),
        name="arrange",
    )(*(pltpu.with_memory_space_constraint(a, pltpu.VMEM) for a in (gathered, part)))
    relaid = lax.all_to_all(outgoing, "tm", 0, 0, axis_index_groups=[order])
    swapped = lax.ppermute(relaid, "chan", [(c, c ^ 1) for c in range(chan_count)])
    block = math.gcd(half, 16)
    state = seg_count * total_rows * SEG * 4
    shape = (seg_count, dec, head_len, 1024, order)
    limit = pltpu.CompilerParams(vmem_limit_bytes=14 * MIB + 2 * state)
    own, near = pl.pallas_call(
        functools.partial(near_kernel, *shape, ch),
        out_shape=[
            pltpu.VMEM((seg_count * ch, SEG), jnp.float32),
            pltpu.VMEM((seg_count * half, SEG), jnp.float32),
        ],
        in_specs=[whole(pltpu.SMEM), whole(), whole()],
        out_specs=[whole(), whole()],
        scratch_shapes=[pltpu.VMEM((steps * (ch + half), dec), jnp.bfloat16)],
        compiler_params=limit,
        cost_estimate=pl.CostEstimate(
            flops=16 * steps * (ch + half) * dec * HALF, bytes_accessed=2 * state, transcendentals=0
        ),
        name="near",
    )(live_counts, relaid, table)
    return pl.pallas_call(
        functools.partial(correlate_kernel, *shape, half == block),
        grid=(half // block,),
        out_shape=jax.ShapeDtypeStruct((src_count, ch, 2 * LAGH), jnp.float32),
        in_specs=[whole()] * 4,
        out_specs=whole(pl.ANY),
        scratch_shapes=[
            pltpu.VMEM((steps * half, dec), jnp.bfloat16),
            pltpu.VMEM((seg_count * half, SEG), jnp.float32),
            pltpu.VMEM((CORES, block * ch, SEG), jnp.bfloat16),
            pltpu.VMEM((CORES, block, ch, 2 * LAGH), jnp.float32),
            pltpu.SemaphoreType.DMA((CORES,)),
        ],
        compiler_params=limit,
        name="correlate",
    )(swapped, table, own, near)


def solution(mesh):
    placed = (P("chan", "tm"), P(), P(), P(("chan", "tm")))
    return jax.shard_map(
        local, mesh=mesh, in_specs=placed, out_specs=P(None, ("chan", "tm"), None), check_vma=False
    )
```

```python
import functools
import math

import jax
import jax.numpy as jnp
import ml_dtypes
import numpy as np
from jax import lax
from jax.experimental import pallas as pl
from jax.experimental.pallas import tpu as pltpu
from jax.sharding import PartitionSpec as P

DECIM = 10
SEG = 1024
BAND = 64
LAGH = 192
SRC_DEV = 1
LANES = 128
HALF = SEG // 2
CHUNKS = HALF // LANES
EDGE = 14
PER_TILE = LANES // (3 * EDGE)
ROWS = 16
CORES = 2
MIB = 1024 * 1024

whiten_eps = 1e-06

NT = (((1,), (1,)), ((), ()))


def split_table(table):
    hi = table.astype(ml_dtypes.bfloat16)
    lo = (table - hi.astype(np.float64)).astype(ml_dtypes.bfloat16)
    return hi, lo


def dft_table(rows):
    phase = (np.arange(rows)[:, None] * np.arange(HALF)[None, :] % SEG) * (2.0 * np.pi / SEG)
    parts = []
    for j in range(CHUNKS):
        cut = slice(j * LANES, (j + 1) * LANES)
        hi, lo = split_table(np.concatenate([np.cos(phase[:, cut]), -np.sin(phase[:, cut])], 1))
        parts += [hi, lo]
    return np.concatenate(parts, axis=1)


def lag_table(seg_count):
    freq = np.arange(HALF)[:, None]
    phase = (freq * np.arange(-LAGH, LAGH)[None, :] % SEG) * (2.0 * np.pi / SEG)
    weight = np.where(freq == 0, 1.0, 2.0) * (math.sqrt(SEG / seg_count) / SEG)
    re = (weight * np.cos(phase)).reshape(CHUNKS, LANES, 2 * LAGH)
    im = (-weight * np.sin(phase)).reshape(CHUNKS, LANES, 2 * LAGH)
    return np.concatenate([re, im], axis=1).reshape(SEG, 2 * LAGH).astype(ml_dtypes.bfloat16)


def iota(shape, dim):
    return lax.broadcasted_iota(jnp.int32, shape, dim)


def one_hot(mask):
    return jnp.where(mask, 1.0, 0.0).astype(jnp.bfloat16)


def column(row):
    n = row.shape[1]
    return jnp.sum(jnp.where(iota((n, n), 0) == iota((n, n), 1), row, 0), axis=1, keepdims=True)


def tap_rows(taps):
    tap_count = taps.shape[1]
    width = 3 * LANES
    flip = one_hot(iota((tap_count, width), 0) + iota((tap_count, width), 1) == tap_count)
    hi = taps.astype(jnp.bfloat16)
    lo = (taps - hi.astype(jnp.float32)).astype(jnp.bfloat16)
    out = []
    for part in (hi, lo):
        base = jnp.dot(
            jnp.broadcast_to(part.astype(jnp.float32), (8, tap_count)).astype(jnp.bfloat16),
            flip,
            preferred_element_type=jnp.float32,
        )
        upper = pltpu.roll(base, 0, 1, stride=DECIM, stride_axis=0)
        out.append(jnp.concatenate([upper, pltpu.roll(upper, 8 * DECIM, 1)], axis=0))
    return out


def edge_tiles(count):
    return -(-count // (PER_TILE * ROWS))


def filter_kernel(
    blocks,
    src_hbm, taps_hbm, raw_ref, tab_hbm,
    out_ref, slot_ref, tab_ref,
    ext, weight, src_ref, taps_ref, sems,
):
    rows, raw_len = raw_ref.shape
    steps = out_ref.shape[0]
    ch = rows // steps
    span = raw_len // blocks
    wide = span + LANES
    copies = []
    for b in range(blocks):
        if b == 0:
            copy = pltpu.make_async_copy(
                raw_ref.at[:, pl.ds(0, span)],
                ext.at[pl.ds(0, rows), pl.ds(LANES, span)],
                sems.at[b],
            )
        else:
            copy = pltpu.make_async_copy(
                raw_ref.at[:, pl.ds(b * span - LANES, wide)],
                ext.at[pl.ds(b * rows, rows), :],
                sems.at[b],
            )
        copy.start()
        copies.append(copy)
    small = [
        pltpu.make_async_copy(taps_hbm, taps_ref, sems.at[blocks]),
        pltpu.make_async_copy(src_hbm, src_ref, sems.at[blocks + 1]),
    ]
    tables = pltpu.make_async_copy(tab_hbm, tab_ref, sems.at[blocks + 2])
    for copy in [*small, tables]:
        copy.start()
    ext[:rows, :LANES] = jnp.zeros((rows, LANES), ext.dtype)
    weight[...] = jnp.zeros_like(weight)
    for copy in small:
        copy.wait()
    for p, base in enumerate(tap_rows(taps_ref[...])):
        for i in range(LANES // 16):
            tile, lane = divmod(16 * DECIM * i, LANES)
            piece = pltpu.roll(base, lane, 1) if lane else base
            weight[p * LANES + 16 * i : p * LANES + 16 * (i + 1), tile * LANES : (tile + 3) * LANES] = (
                piece.astype(jnp.bfloat16)
            )
    src = src_ref[...]
    src_count = src.shape[1]
    slots = slot_ref.shape[0]
    group = src // rows
    group_col = column(group)
    src_col = column(src)
    rank = jnp.sum(
        jnp.where(
            (group_col == group)
            & (iota((src_count, src_count), 0) < iota((src_count, src_count), 1)),
            1,
            0,
        ),
        axis=0,
        keepdims=True,
    )
    mine = lax.axis_index("chan")
    to_slot = one_hot((iota((slots, src_count), 0) == rank) & (group == mine))
    to_row = one_hot(src_col - mine * rows == iota((src_count, rows), 1))
    pick = jnp.dot(to_slot, to_row, preferred_element_type=jnp.float32).astype(jnp.bfloat16)
    number = jnp.where(
        iota((src_count, LANES), 1) == LANES - 1, iota((src_count, LANES), 0) + 1, 0
    ).astype(jnp.float32).astype(jnp.bfloat16)
    number = jnp.dot(to_slot, number, preferred_element_type=jnp.float32)
    for copy in copies:
        copy.wait()
    acc = lax.dot_general(ext[...], weight[...], NT, preferred_element_type=jnp.float32)
    acc = acc[:, :LANES] + acc[:, LANES:]
    y = acc.astype(jnp.bfloat16)
    head = acc[:rows]
    head_lo = head - head.astype(jnp.bfloat16).astype(jnp.float32)
    tail = lax.dot_general(
        ext[(blocks - 1) * rows :, wide - LANES :], weight[:, :LANES], NT,
        preferred_element_type=jnp.float32,
    )
    tail = tail[:, :LANES] + tail[:, LANES:]
    tail_hi = tail.astype(jnp.bfloat16).astype(jnp.float32)
    lane = iota((rows, LANES), 1)
    edge = jnp.where(
        lane < EDGE,
        head_lo,
        jnp.where(
            lane < 2 * EDGE,
            pltpu.roll(tail_hi, EDGE, 1),
            jnp.where(lane < 3 * EDGE, pltpu.roll(tail - tail_hi, 2 * EDGE, 1), 0.0),
        ),
    ).astype(jnp.bfloat16)
    parts = [y[b * rows : (b + 1) * rows] for b in range(blocks)] + [edge]
    last = blocks * ch
    for t in range(steps):
        for b in range(blocks):
            out_ref[t, b * ch : (b + 1) * ch] = parts[b][t * ch : (t + 1) * ch]
        out_ref[t, last : last + ch] = edge[t * ch : (t + 1) * ch]
    for b, part in enumerate(parts):
        found = jnp.dot(pick, part, preferred_element_type=jnp.float32)
        if b == blocks:
            found += number
        slot_ref[:, b * LANES : (b + 1) * LANES] = found.astype(jnp.bfloat16)
    tables.wait()


def arrange_kernel(half, blocks, order, *refs):
    *slot_refs, part_ref, out_ref, fill, packs, sems = refs
    slots = jnp.concatenate([ref[...] for ref in slot_refs], axis=0)
    steps, height, _ = out_ref.shape
    tile_rows = packs.shape[1]
    own_rows = part_ref.shape[1] - ROWS
    copies = [
        pltpu.make_async_copy(
            part_ref.at[t, pl.ds(0, own_rows)], out_ref.at[p, pl.ds(0, own_rows)], sems.at[p]
        )
        for p, t in enumerate(order)
    ]
    for copy in copies:
        copy.start()
    numbers = slots[:, blocks * LANES :].astype(jnp.float32)
    total = numbers.shape[0]
    numbers = jnp.sum(
        jnp.where(iota((total, LANES), 1) == LANES - 1, numbers, 0.0), axis=1, keepdims=True
    ).astype(jnp.int32)
    first = lax.axis_index("chan") % CORES * half
    pick = one_hot(numbers == iota((total, half), 1) + 1 + first)
    found = lax.dot_general(
        pick, slots, (((0,), (0,)), ((), ())), preferred_element_type=jnp.float32
    )
    for b in range(blocks):
        fill[b * half : (b + 1) * half] = found[:, b * LANES : (b + 1) * LANES].astype(
            jnp.bfloat16
        )
    fills = [
        pltpu.make_async_copy(
            fill, out_ref.at[p, pl.ds(own_rows, fill.shape[0])], sems.at[steps + p]
        )
        for p in range(steps)
    ]
    for copy in fills:
        copy.start()
    edges = jnp.where(
        iota((half, LANES), 1) < 3 * EDGE, found[:, blocks * LANES :], 0.0
    )
    added = [jnp.zeros((ROWS, LANES), jnp.float32) for _ in range(tile_rows // ROWS)]
    for i in range(half // ROWS):
        tile, place = divmod(i + 1, PER_TILE)
        piece = edges[i * ROWS : (i + 1) * ROWS]
        added[tile] += pltpu.roll(piece, 3 * EDGE * place, 1) if place else piece
    for p, t in enumerate(order):
        own = part_ref[t, own_rows:].astype(jnp.float32)
        packs[p, :ROWS] = (own + added[0]).astype(jnp.bfloat16)
        for tile in range(1, tile_rows // ROWS):
            packs[p, tile * ROWS : (tile + 1) * ROWS] = added[tile].astype(jnp.bfloat16)
    store = pltpu.make_async_copy(
        packs, out_ref.at[:, pl.ds(height - tile_rows, tile_rows)], sems.at[2 * steps]
    )
    store.start()
    for copy in [*copies, *fills, store]:
        copy.wait()


def correlate_kernel(
    seg_count, src_count, dec, head_len, part_rows, order, count,
    live_ref, near_ref, far_ref, tab_ref, out_ref,
    trace, own, other, cross, result, sems,
):
    steps, height, _ = near_ref.shape
    ch = out_ref.shape[1]
    half = src_count // CORES
    rows = ch + src_count
    per_seg = SEG // dec
    blocks = dec // LANES
    d_cols = 4 * HALF

    @pl.when(pl.program_id(0) == 0)
    def _():
        live = iota((ch, LANES), 0) < live_ref[0]
        before = jnp.zeros((rows, LANES), jnp.float32)
        is_head = iota((rows, LANES), 1) < head_len
        last = height - edge_tiles(ch + half) * ROWS
        low_core = lax.axis_index("chan") % CORES == 0

        def edge_groups(ref, p):
            out = []
            for i in range((ch + half) // ROWS):
                tile, place = divmod(i, PER_TILE)
                if place == 0:
                    pack = ref[p, last + tile * ROWS : last + (tile + 1) * ROWS].astype(jnp.float32)
                    out.append(pack)
                else:
                    out.append(pltpu.roll(pack, LANES - 3 * EDGE * place, 1))
            return out[0], jnp.concatenate(out[1:], axis=0)

        def in_order(near, far):
            return [jnp.where(low_core, near, far), jnp.where(low_core, far, near)]

        for t in range(steps):
            p = order.index(t)
            edge, near = edge_groups(near_ref, p)
            _, far = edge_groups(far_ref, p)
            edge = jnp.concatenate([jnp.where(live, edge, 0.0), *in_order(near, far)], axis=0)
            for b in range(blocks):
                mine = near_ref[p, b * ch : (b + 1) * ch]
                mine = jnp.where(live, mine, jnp.zeros_like(mine))
                at = blocks * ch + b * half
                both = jnp.concatenate(
                    [mine, *in_order(near_ref[p, at : at + half], far_ref[p, at : at + half])], axis=0
                )
                if b == 0:
                    tail = pltpu.roll(before, LANES - EDGE, 1) + pltpu.roll(before, LANES - 2 * EDGE, 1)
                    both = both.astype(jnp.float32)
                    both = jnp.where(is_head, both + edge + tail, both).astype(jnp.bfloat16)
                trace[t * rows : (t + 1) * rows, b * LANES : (b + 1) * LANES] = both
            before = edge
        odd = (iota((rows, 2 * LANES), 1) & 1) == 1
        sign = jnp.where(odd, -1.0, 1.0)
        same = one_hot(
            iota((2 * LANES, LANES), 0) % LANES // BAND == iota((2 * LANES, LANES), 1) // BAND
        )
        group_segs = max(1, min(seg_count, part_rows // (per_seg * rows)))
        for first in range(0, seg_count, group_segs):
            segs = min(group_segs, seg_count - first)
            lhs = trace[first * per_seg * rows : (first + segs) * per_seg * rows, :]
            for j in range(CHUNKS):
                acc = jnp.dot(
                    lhs, tab_ref[:, 4 * j * LANES : 4 * (j + 1) * LANES],
                    preferred_element_type=jnp.float32,
                )
                folded = acc[:, : 2 * LANES] + acc[:, 2 * LANES :]
                spec = []
                for g in range(segs):
                    a = folded[g * per_seg * rows : (g * per_seg + 1) * rows]
                    b = folded[(g * per_seg + 1) * rows : (g * per_seg + 2) * rows]
                    spec.append(a + sign * b)
                spec = jnp.concatenate(spec, axis=0)
                re, im = spec[:, :LANES], spec[:, LANES:]
                power = re * re + im * im
                hi = power.astype(jnp.bfloat16)
                lo = (power - hi.astype(jnp.float32)).astype(jnp.bfloat16)
                total = jnp.dot(
                    jnp.concatenate([hi, lo], axis=1), same, preferred_element_type=jnp.float32
                )
                scale = lax.rsqrt(total * (1.0 / BAND) + whiten_eps)
                w_re = (re * scale).astype(jnp.bfloat16).astype(jnp.float32)
                w_im = (im * scale).astype(jnp.bfloat16).astype(jnp.float32)
                at = 2 * j * LANES
                for g in range(segs):
                    r, o = g * rows, (first + g) * ch
                    own[o : o + ch, at : at + LANES] = w_re[r : r + ch]
                    own[o : o + ch, at + LANES : at + 2 * LANES] = w_im[r : r + ch]
                    o = (first + g) * src_count
                    other[o : o + src_count, at : at + LANES] = w_re[r + ch : r + rows]
                    other[o : o + src_count, at + LANES : at + 2 * LANES] = w_im[r + ch : r + rows]

    block = cross.shape[1] // ch
    copies = []
    for i in range(count):
        start = pl.multiple_of((pl.program_id(0) * count + i) * block, 8)
        for j in range(CHUNKS):
            at = 2 * j * LANES
            a_re = [own[g * ch : (g + 1) * ch, at : at + LANES] for g in range(seg_count)]
            a_im = [own[g * ch : (g + 1) * ch, at + LANES : at + 2 * LANES] for g in range(seg_count)]
            for s in range(block):
                if s % 8 == 0:
                    tiles = [
                        other[
                            pl.ds(pl.multiple_of(g * src_count + start + s, 8), 8),
                            at : at + 2 * LANES,
                        ]
                        for g in range(seg_count)
                    ]
                re = im = None
                for g in range(seg_count):
                    b_re = tiles[g][s % 8 : s % 8 + 1, :LANES]
                    b_im = tiles[g][s % 8 : s % 8 + 1, LANES:]
                    p = a_re[g] * b_re + a_im[g] * b_im
                    q = a_im[g] * b_re - a_re[g] * b_im
                    re, im = (p, q) if re is None else (re + p, im + q)
                row = slice(s * ch, (s + 1) * ch)
                cross[i, row, at : at + LANES] = re.astype(jnp.bfloat16)
                cross[i, row, at + LANES : at + 2 * LANES] = im.astype(jnp.bfloat16)
        lags = sum(
            jnp.dot(
                cross[i, :, h * dec : (h + 1) * dec],
                tab_ref[:, d_cols + 2 * LAGH * h : d_cols + 2 * LAGH * (h + 1)],
                preferred_element_type=jnp.float32,
            )
            for h in range(per_seg)
        )
        result[i] = lags.reshape(result.shape[1:])
        copy = pltpu.make_async_copy(result.at[i], out_ref.at[pl.ds(start, block)], sems.at[i])
        copy.start()
        copies.append(copy)
    for copy in copies:
        copy.wait()


def whole(space=pltpu.VMEM):
    return pl.BlockSpec(memory_space=space)


def local(raw_strain, fir_taps, source_channels, live_counts):
    rows, raw_len = raw_strain.shape
    steps = lax.axis_size("tm")
    chan_count = lax.axis_size("chan")
    dec = raw_len // DECIM
    blocks = dec // LANES
    ch = rows // steps
    seg_count = steps * dec // SEG
    src_count = source_channels.shape[0]
    slots = 2 * SRC_DEV * steps
    span = raw_len // blocks
    total_rows = ch + src_count
    half = src_count // CORES
    tile_rows = edge_tiles(ch + half) * ROWS
    height = blocks * (ch + half) + tile_rows
    head_len = -(-(fir_taps.shape[0] - 1) // DECIM)
    assert head_len < EDGE and ch == ROWS and src_count <= 256 and half % ROWS == 0
    src = source_channels.reshape(1, src_count)
    taps = fir_taps.reshape(1, fir_taps.shape[0])
    table = np.concatenate([dft_table(dec), *lag_table(seg_count).reshape(SEG // dec, dec, -1)], axis=1)
    inputs = (src, taps, raw_strain, jnp.asarray(table))
    part, picked, table = pl.pallas_call(
        functools.partial(filter_kernel, blocks),
        out_shape=[
            pltpu.VMEM((steps, (blocks + 1) * ch, LANES), jnp.bfloat16),
            pltpu.VMEM((slots, dec + LANES), jnp.bfloat16),
            pltpu.VMEM(table.shape, jnp.bfloat16),
        ],
        in_specs=[whole(pl.ANY)] * 4,
        out_specs=[whole(), whole(), whole(pl.ANY)],
        scratch_shapes=[
            pltpu.VMEM((blocks * rows, span + LANES), jnp.bfloat16),
            pltpu.VMEM((2 * LANES, span + LANES), jnp.bfloat16),
            pltpu.VMEM(src.shape, src.dtype),
            pltpu.VMEM(taps.shape, taps.dtype),
            pltpu.SemaphoreType.DMA((blocks + 3,)),
        ],
        compiler_params=pltpu.CompilerParams(vmem_limit_bytes=16 * MIB),
        name="fir",
    )(*(pltpu.with_memory_space_constraint(a, pltpu.HBM) for a in inputs))
    order = list(range(steps))
    if steps % 8 == 0:
        order = [q * (steps // 8) + r for r in range(steps // 8) for q in (5, 7, 3, 6, 4, 2, 1, 0)]
    pieces = [picked]
    bit = chan_count // 2
    while bit:
        swap = [(c, c ^ bit) for c in range(chan_count)]
        pieces += [lax.ppermute(piece, "chan", swap) for piece in pieces]
        bit //= 2
    outgoing = pl.pallas_call(
        functools.partial(arrange_kernel, half, blocks, order),
        out_shape=pltpu.HBM((steps, height, LANES), jnp.bfloat16),
        in_specs=[whole()] * (chan_count + 1),
        out_specs=whole(pl.ANY),
        scratch_shapes=[
            pltpu.VMEM((blocks * half, LANES), jnp.bfloat16),
            pltpu.VMEM((steps, tile_rows, LANES), jnp.bfloat16),
            pltpu.SemaphoreType.DMA((2 * steps + 1,)),
        ],
        compiler_params=pltpu.CompilerParams(vmem_limit_bytes=8 * MIB),
        name="arrange",
    )(*(pltpu.with_memory_space_constraint(a, pltpu.VMEM) for a in (*pieces, part)))
    relaid = lax.all_to_all(outgoing, "tm", 0, 0, axis_index_groups=[order])
    swapped = lax.ppermute(relaid, "chan", [(c, c ^ 1) for c in range(chan_count)])
    block = math.gcd(src_count, 16)
    count = math.gcd(src_count // block, 2)
    state = seg_count * total_rows * SEG * 4
    return pl.pallas_call(
        functools.partial(
            correlate_kernel, seg_count, src_count, dec, head_len, 1024, order, count
        ),
        grid=(src_count // (block * count),),
        out_shape=jax.ShapeDtypeStruct((src_count, ch, 2 * LAGH), jnp.float32),
        in_specs=[whole(pltpu.SMEM)] + [whole()] * 3,
        out_specs=whole(pl.ANY),
        scratch_shapes=[
            pltpu.VMEM((steps * total_rows, dec), jnp.bfloat16),
            pltpu.VMEM((seg_count * ch, SEG), jnp.float32),
            pltpu.VMEM((seg_count * src_count, SEG), jnp.float32),
            pltpu.VMEM((count, block * ch, SEG), jnp.bfloat16),
            pltpu.VMEM((count, block, ch, 2 * LAGH), jnp.float32),
            pltpu.SemaphoreType.DMA((count,)),
        ],
        compiler_params=pltpu.CompilerParams(vmem_limit_bytes=16 * MIB + 2 * state),
        name="correlate",
    )(live_counts, relaid, swapped, table)


def solution(mesh):
    placed = (P("chan", "tm"), P(), P(), P(("chan", "tm")))
    return jax.shard_map(
        local, mesh=mesh, in_specs=placed, out_specs=P(None, ("chan", "tm"), None), check_vma=False
    )
```

```python
import functools
import math

import jax
import jax.numpy as jnp
import ml_dtypes
import numpy as np
from jax import lax
from jax.experimental import pallas as pl
from jax.experimental.pallas import tpu as pltpu
from jax.sharding import PartitionSpec as P

DECIM = 10
SEG = 1024
BAND = 64
LAGH = 192
SRC_DEV = 1
LANES = 128
HALF = SEG // 2
CHUNKS = HALF // LANES
EDGE = 14
PER_TILE = LANES // (3 * EDGE)
ROWS = 16
MIB = 1024 * 1024

whiten_eps = 1e-06

NT = (((1,), (1,)), ((), ()))


def split_table(table):
    hi = table.astype(ml_dtypes.bfloat16)
    lo = (table - hi.astype(np.float64)).astype(ml_dtypes.bfloat16)
    return hi, lo


def dft_table(rows):
    phase = (np.arange(rows)[:, None] * np.arange(HALF)[None, :] % SEG) * (2.0 * np.pi / SEG)
    parts = []
    for j in range(CHUNKS):
        cut = slice(j * LANES, (j + 1) * LANES)
        hi, lo = split_table(np.concatenate([np.cos(phase[:, cut]), -np.sin(phase[:, cut])], 1))
        parts += [hi, lo]
    return np.concatenate(parts, axis=1)


def lag_table(seg_count):
    freq = np.arange(HALF)[:, None]
    phase = (freq * np.arange(-LAGH, LAGH)[None, :] % SEG) * (2.0 * np.pi / SEG)
    weight = np.where(freq == 0, 1.0, 2.0) * (math.sqrt(SEG / seg_count) / SEG)
    re = (weight * np.cos(phase)).reshape(CHUNKS, LANES, 2 * LAGH)
    im = (-weight * np.sin(phase)).reshape(CHUNKS, LANES, 2 * LAGH)
    return np.concatenate([re, im], axis=1).reshape(SEG, 2 * LAGH).astype(ml_dtypes.bfloat16)


def iota(shape, dim):
    return lax.broadcasted_iota(jnp.int32, shape, dim)


def one_hot(mask):
    return jnp.where(mask, 1.0, 0.0).astype(jnp.bfloat16)


def column(row):
    n = row.shape[1]
    return jnp.sum(jnp.where(iota((n, n), 0) == iota((n, n), 1), row, 0), axis=1, keepdims=True)


def tap_rows(taps):
    tap_count = taps.shape[1]
    width = 3 * LANES
    flip = one_hot(iota((tap_count, width), 0) + iota((tap_count, width), 1) == tap_count)
    hi = taps.astype(jnp.bfloat16)
    lo = (taps - hi.astype(jnp.float32)).astype(jnp.bfloat16)
    out = []
    for part in (hi, lo):
        base = jnp.dot(
            jnp.broadcast_to(part.astype(jnp.float32), (8, tap_count)).astype(jnp.bfloat16),
            flip,
            preferred_element_type=jnp.float32,
        )
        upper = pltpu.roll(base, 0, 1, stride=DECIM, stride_axis=0)
        out.append(jnp.concatenate([upper, pltpu.roll(upper, 8 * DECIM, 1)], axis=0))
    return out


def edge_tiles(count):
    return -(-count // (PER_TILE * ROWS))


def filter_kernel(
    blocks,
    src_hbm, taps_hbm, raw_ref, tab_hbm,
    out_ref, slot_ref, tab_ref,
    ext, weight, src_ref, taps_ref, sems,
):
    rows, raw_len = raw_ref.shape
    steps = out_ref.shape[0]
    ch = rows // steps
    span = raw_len // blocks
    wide = span + LANES
    copies = []
    for b in range(blocks):
        if b == 0:
            copy = pltpu.make_async_copy(
                raw_ref.at[:, pl.ds(0, span)],
                ext.at[pl.ds(0, rows), pl.ds(LANES, span)],
                sems.at[b],
            )
        else:
            copy = pltpu.make_async_copy(
                raw_ref.at[:, pl.ds(b * span - LANES, wide)],
                ext.at[pl.ds(b * rows, rows), :],
                sems.at[b],
            )
        copy.start()
        copies.append(copy)
    small = [
        pltpu.make_async_copy(taps_hbm, taps_ref, sems.at[blocks]),
        pltpu.make_async_copy(src_hbm, src_ref, sems.at[blocks + 1]),
    ]
    tables = pltpu.make_async_copy(tab_hbm, tab_ref, sems.at[blocks + 2])
    for copy in [*small, tables]:
        copy.start()
    ext[:rows, :LANES] = jnp.zeros((rows, LANES), ext.dtype)
    weight[...] = jnp.zeros_like(weight)
    for copy in small:
        copy.wait()
    for p, base in enumerate(tap_rows(taps_ref[...])):
        for i in range(LANES // 16):
            tile, lane = divmod(16 * DECIM * i, LANES)
            piece = pltpu.roll(base, lane, 1) if lane else base
            weight[p * LANES + 16 * i : p * LANES + 16 * (i + 1), tile * LANES : (tile + 3) * LANES] = (
                piece.astype(jnp.bfloat16)
            )
    src = src_ref[...]
    src_count = src.shape[1]
    slots = slot_ref.shape[0]
    group = src // rows
    group_col = column(group)
    src_col = column(src)
    rank = jnp.sum(
        jnp.where(
            (group_col == group)
            & (iota((src_count, src_count), 0) < iota((src_count, src_count), 1)),
            1,
            0,
        ),
        axis=0,
        keepdims=True,
    )
    mine = lax.axis_index("chan")
    to_slot = one_hot((iota((slots, src_count), 0) == rank) & (group == mine))
    to_row = one_hot(src_col - mine * rows == iota((src_count, rows), 1))
    pick = jnp.dot(to_slot, to_row, preferred_element_type=jnp.float32).astype(jnp.bfloat16)
    number = jnp.where(
        iota((src_count, LANES), 1) == LANES - 1, iota((src_count, LANES), 0) + 1, 0
    ).astype(jnp.float32).astype(jnp.bfloat16)
    number = jnp.dot(to_slot, number, preferred_element_type=jnp.float32)
    for copy in copies:
        copy.wait()
    acc = lax.dot_general(ext[...], weight[...], NT, preferred_element_type=jnp.float32)
    acc = acc[:, :LANES] + acc[:, LANES:]
    y = acc.astype(jnp.bfloat16)
    head = acc[:rows]
    head_lo = head - head.astype(jnp.bfloat16).astype(jnp.float32)
    tail = lax.dot_general(
        ext[(blocks - 1) * rows :, wide - LANES :], weight[:, :LANES], NT,
        preferred_element_type=jnp.float32,
    )
    tail = tail[:, :LANES] + tail[:, LANES:]
    tail_hi = tail.astype(jnp.bfloat16).astype(jnp.float32)
    lane = iota((rows, LANES), 1)
    edge = jnp.where(
        lane < EDGE,
        head_lo,
        jnp.where(
            lane < 2 * EDGE,
            pltpu.roll(tail_hi, EDGE, 1),
            jnp.where(lane < 3 * EDGE, pltpu.roll(tail - tail_hi, 2 * EDGE, 1), 0.0),
        ),
    ).astype(jnp.bfloat16)
    parts = [y[b * rows : (b + 1) * rows] for b in range(blocks)] + [edge]
    last = blocks * ch
    for t in range(steps):
        for b in range(blocks):
            out_ref[t, b * ch : (b + 1) * ch] = parts[b][t * ch : (t + 1) * ch]
        out_ref[t, last : last + ch] = edge[t * ch : (t + 1) * ch]
    for b, part in enumerate(parts):
        found = jnp.dot(pick, part, preferred_element_type=jnp.float32)
        if b == blocks:
            found += number
        slot_ref[:, b * LANES : (b + 1) * LANES] = found.astype(jnp.bfloat16)
    tables.wait()


def arrange_kernel(src_count, blocks, pieces, *refs):
    slots = jnp.concatenate([ref[...] for ref in refs[:pieces]], axis=0)
    part_ref, *out_refs = refs[pieces:]
    height = out_refs[0].shape[0]
    own_rows = part_ref.shape[1] - ROWS
    tile_rows = height - own_rows - blocks * src_count
    numbers = slots[:, blocks * LANES :].astype(jnp.float32)
    total = numbers.shape[0]
    numbers = jnp.sum(
        jnp.where(iota((total, LANES), 1) == LANES - 1, numbers, 0.0), axis=1, keepdims=True
    ).astype(jnp.int32)
    pick = one_hot(numbers == iota((total, src_count), 1) + 1)
    found = lax.dot_general(
        pick, slots, (((0,), (0,)), ((), ())), preferred_element_type=jnp.float32
    )
    fill = [found[:, b * LANES : (b + 1) * LANES].astype(jnp.bfloat16) for b in range(blocks)]
    edges = jnp.where(
        iota((src_count, LANES), 1) < 3 * EDGE, found[:, blocks * LANES :], 0.0
    )
    added = [jnp.zeros((ROWS, LANES), jnp.float32) for _ in range(tile_rows // ROWS)]
    for i in range(src_count // ROWS):
        tile, place = divmod(i + 1, PER_TILE)
        piece = edges[i * ROWS : (i + 1) * ROWS]
        added[tile] += pltpu.roll(piece, 3 * EDGE * place, 1) if place else piece
    me = lax.axis_index("tm")
    for k, out_ref in enumerate(out_refs):
        own = part_ref[me ^ k]
        out_ref[:own_rows] = own[:own_rows]
        for b in range(blocks):
            at = own_rows + b * src_count
            out_ref[at : at + src_count] = fill[b]
        own = own[own_rows:].astype(jnp.float32)
        for tile, extra in enumerate(added):
            at = height - tile_rows + tile * ROWS
            out_ref[at : at + ROWS] = (extra + own if tile == 0 else extra).astype(jnp.bfloat16)


def correlate_kernel(
    seg_count, src_count, dec, head_len, part_rows, count, steps, live_ref, tab_ref, *refs
):
    block_refs, out_ref = refs[:steps], refs[steps]
    x_ref, trace, own, other, cross, result, sems = refs[steps + 1 :]
    height = x_ref.shape[1]
    ch = out_ref.shape[1]
    rows = ch + src_count
    per_seg = SEG // dec
    blocks = dec // LANES
    d_cols = 4 * HALF

    @pl.when(pl.program_id(0) == 0)
    def _():
        me = lax.axis_index("tm")
        for k, block_ref in enumerate(block_refs):
            x_ref[me ^ k] = block_ref[...]
        live = iota((ch, LANES), 0) < live_ref[0]
        before = jnp.zeros((rows, LANES), jnp.float32)
        is_head = iota((rows, LANES), 1) < head_len
        last = height - edge_tiles(rows) * ROWS
        for t in range(steps):
            edge = []
            for i in range(rows // ROWS):
                tile, place = divmod(i, PER_TILE)
                if place == 0:
                    pack = x_ref[t, last + tile * ROWS : last + (tile + 1) * ROWS].astype(jnp.float32)
                    edge.append(pack)
                else:
                    edge.append(pltpu.roll(pack, LANES - 3 * EDGE * place, 1))
            edge[0] = jnp.where(live, edge[0], 0.0)
            edge = jnp.concatenate(edge, axis=0)
            for b in range(blocks):
                mine = x_ref[t, b * ch : (b + 1) * ch]
                mine = jnp.where(live, mine, jnp.zeros_like(mine))
                at = blocks * ch + b * src_count
                both = jnp.concatenate([mine, x_ref[t, at : at + src_count]], axis=0)
                if b == 0:
                    tail = pltpu.roll(before, LANES - EDGE, 1) + pltpu.roll(before, LANES - 2 * EDGE, 1)
                    both = both.astype(jnp.float32)
                    both = jnp.where(is_head, both + edge + tail, both).astype(jnp.bfloat16)
                trace[t * rows : (t + 1) * rows, b * LANES : (b + 1) * LANES] = both
            before = edge
        odd = (iota((rows, 2 * LANES), 1) & 1) == 1
        sign = jnp.where(odd, -1.0, 1.0)
        same = one_hot(
            iota((2 * LANES, LANES), 0) % LANES // BAND == iota((2 * LANES, LANES), 1) // BAND
        )
        group_segs = max(1, min(seg_count, part_rows // (per_seg * rows)))
        for first in range(0, seg_count, group_segs):
            segs = min(group_segs, seg_count - first)
            lhs = trace[first * per_seg * rows : (first + segs) * per_seg * rows, :]
            for j in range(CHUNKS):
                acc = jnp.dot(
                    lhs, tab_ref[:, 4 * j * LANES : 4 * (j + 1) * LANES],
                    preferred_element_type=jnp.float32,
                )
                half = acc[:, : 2 * LANES] + acc[:, 2 * LANES :]
                spec = []
                for g in range(segs):
                    a = half[g * per_seg * rows : (g * per_seg + 1) * rows]
                    b = half[(g * per_seg + 1) * rows : (g * per_seg + 2) * rows]
                    spec.append(a + sign * b)
                spec = jnp.concatenate(spec, axis=0)
                re, im = spec[:, :LANES], spec[:, LANES:]
                power = re * re + im * im
                hi = power.astype(jnp.bfloat16)
                lo = (power - hi.astype(jnp.float32)).astype(jnp.bfloat16)
                total = jnp.dot(
                    jnp.concatenate([hi, lo], axis=1), same, preferred_element_type=jnp.float32
                )
                scale = lax.rsqrt(total * (1.0 / BAND) + whiten_eps)
                w_re = (re * scale).astype(jnp.bfloat16).astype(jnp.float32)
                w_im = (im * scale).astype(jnp.bfloat16).astype(jnp.float32)
                at = 2 * j * LANES
                for g in range(segs):
                    r, o = g * rows, (first + g) * ch
                    own[o : o + ch, at : at + LANES] = w_re[r : r + ch]
                    own[o : o + ch, at + LANES : at + 2 * LANES] = w_im[r : r + ch]
                    o = (first + g) * src_count
                    other[o : o + src_count, at : at + LANES] = w_re[r + ch : r + rows]
                    other[o : o + src_count, at + LANES : at + 2 * LANES] = w_im[r + ch : r + rows]

    block = cross.shape[1] // ch
    copies = []
    for i in range(count):
        start = pl.multiple_of((pl.program_id(0) * count + i) * block, 8)
        for j in range(CHUNKS):
            at = 2 * j * LANES
            a_re = [own[g * ch : (g + 1) * ch, at : at + LANES] for g in range(seg_count)]
            a_im = [own[g * ch : (g + 1) * ch, at + LANES : at + 2 * LANES] for g in range(seg_count)]
            for s in range(block):
                if s % 8 == 0:
                    tiles = [
                        other[
                            pl.ds(pl.multiple_of(g * src_count + start + s, 8), 8),
                            at : at + 2 * LANES,
                        ]
                        for g in range(seg_count)
                    ]
                re = im = None
                for g in range(seg_count):
                    b_re = tiles[g][s % 8 : s % 8 + 1, :LANES]
                    b_im = tiles[g][s % 8 : s % 8 + 1, LANES:]
                    p = a_re[g] * b_re + a_im[g] * b_im
                    q = a_im[g] * b_re - a_re[g] * b_im
                    re, im = (p, q) if re is None else (re + p, im + q)
                row = slice(s * ch, (s + 1) * ch)
                cross[i, row, at : at + LANES] = re.astype(jnp.bfloat16)
                cross[i, row, at + LANES : at + 2 * LANES] = im.astype(jnp.bfloat16)
        lags = sum(
            jnp.dot(
                cross[i, :, h * dec : (h + 1) * dec],
                tab_ref[:, d_cols + 2 * LAGH * h : d_cols + 2 * LAGH * (h + 1)],
                preferred_element_type=jnp.float32,
            )
            for h in range(per_seg)
        )
        result[i] = lags.reshape(result.shape[1:])
        copy = pltpu.make_async_copy(result.at[i], out_ref.at[pl.ds(start, block)], sems.at[i])
        copy.start()
        copies.append(copy)
    for copy in copies:
        copy.wait()


def whole(space=pltpu.VMEM):
    return pl.BlockSpec(memory_space=space)


def local(raw_strain, fir_taps, source_channels, live_counts):
    rows, raw_len = raw_strain.shape
    steps = lax.axis_size("tm")
    chan_count = lax.axis_size("chan")
    dec = raw_len // DECIM
    blocks = dec // LANES
    ch = rows // steps
    seg_count = steps * dec // SEG
    src_count = source_channels.shape[0]
    slots = 2 * SRC_DEV * steps
    span = raw_len // blocks
    total_rows = ch + src_count
    tile_rows = edge_tiles(total_rows) * ROWS
    height = blocks * total_rows + tile_rows
    head_len = -(-(fir_taps.shape[0] - 1) // DECIM)
    assert head_len < EDGE and ch == ROWS and src_count <= 256
    assert steps & (steps - 1) == 0 and chan_count & (chan_count - 1) == 0 and src_count % ROWS == 0
    src = source_channels.reshape(1, src_count)
    taps = fir_taps.reshape(1, fir_taps.shape[0])
    table = np.concatenate([dft_table(dec), *lag_table(seg_count).reshape(SEG // dec, dec, -1)], axis=1)
    inputs = (src, taps, raw_strain, jnp.asarray(table))
    part, picked, table = pl.pallas_call(
        functools.partial(filter_kernel, blocks),
        out_shape=[
            pltpu.VMEM((steps, (blocks + 1) * ch, LANES), jnp.bfloat16),
            pltpu.VMEM((slots, dec + LANES), jnp.bfloat16),
            pltpu.VMEM(table.shape, jnp.bfloat16),
        ],
        in_specs=[whole(pl.ANY)] * 4,
        out_specs=[whole(), whole(), whole(pl.ANY)],
        scratch_shapes=[
            pltpu.VMEM((blocks * rows, span + LANES), jnp.bfloat16),
            pltpu.VMEM((2 * LANES, span + LANES), jnp.bfloat16),
            pltpu.VMEM(src.shape, src.dtype),
            pltpu.VMEM(taps.shape, taps.dtype),
            pltpu.SemaphoreType.DMA((blocks + 3,)),
        ],
        compiler_params=pltpu.CompilerParams(vmem_limit_bytes=16 * MIB),
        name="fir",
    )(*(pltpu.with_memory_space_constraint(a, pltpu.HBM) for a in inputs))
    pieces = [picked] + [
        lax.ppermute(picked, "chan", [(c, c ^ k) for c in range(chan_count)])
        for k in range(chan_count - 1, 0, -1)
    ]
    to_vmem = functools.partial(pltpu.with_memory_space_constraint, memory_space=pltpu.VMEM)
    outgoing = pl.pallas_call(
        functools.partial(arrange_kernel, src_count, blocks, chan_count),
        out_shape=[pltpu.VMEM((height, LANES), jnp.bfloat16)] * steps,
        in_specs=[whole()] * (chan_count + 1),
        out_specs=[whole()] * steps,
        compiler_params=pltpu.CompilerParams(vmem_limit_bytes=8 * MIB),
        name="arrange",
    )(*(to_vmem(a) for a in (*pieces, part)))
    arrived = [
        lax.ppermute(outgoing[k], "tm", [(t, t ^ k) for t in range(steps)])
        for k in range(steps - 1, 0, -1)
    ]
    arrived = [outgoing[0], *arrived[::-1]]
    block = math.gcd(src_count, 16)
    count = math.gcd(src_count // block, 2)
    state = seg_count * total_rows * SEG * 4
    return pl.pallas_call(
        functools.partial(
            correlate_kernel, seg_count, src_count, dec, head_len, 1024, count, steps
        ),
        grid=(src_count // (block * count),),
        out_shape=jax.ShapeDtypeStruct((src_count, ch, 2 * LAGH), jnp.float32),
        in_specs=[whole(pltpu.SMEM)] + [whole()] * (steps + 1),
        out_specs=whole(pl.ANY),
        scratch_shapes=[
            pltpu.VMEM((steps, height, LANES), jnp.bfloat16),
            pltpu.VMEM((steps * total_rows, dec), jnp.bfloat16),
            pltpu.VMEM((seg_count * ch, SEG), jnp.float32),
            pltpu.VMEM((seg_count * src_count, SEG), jnp.float32),
            pltpu.VMEM((count, block * ch, SEG), jnp.bfloat16),
            pltpu.VMEM((count, block, ch, 2 * LAGH), jnp.float32),
            pltpu.SemaphoreType.DMA((count,)),
        ],
        compiler_params=pltpu.CompilerParams(vmem_limit_bytes=16 * MIB + 2 * state),
        name="correlate",
    )(live_counts, table, *(to_vmem(a) for a in arrived))


def solution(mesh):
    placed = (P("chan", "tm"), P(), P(), P(("chan", "tm")))
    return jax.shard_map(
        local, mesh=mesh, in_specs=placed, out_specs=P(None, ("chan", "tm"), None), check_vma=False
    )
```

```python
import functools
import math

import jax
import jax.numpy as jnp
import ml_dtypes
import numpy as np
from jax import lax
from jax.experimental import pallas as pl
from jax.experimental.pallas import tpu as pltpu
from jax.sharding import PartitionSpec as P

DECIM = 10
SEG = 1024
BAND = 64
LAGH = 192
SRC_DEV = 1
LANES = 128
HALF = SEG // 2
CHUNKS = HALF // LANES
EDGE = 14
PER_TILE = LANES // (3 * EDGE)
ROWS = 16
CORES = 2
MIB = 1024 * 1024

whiten_eps = 1e-06

NT = (((1,), (1,)), ((), ()))


def split_table(table):
    hi = table.astype(ml_dtypes.bfloat16)
    lo = (table - hi.astype(np.float64)).astype(ml_dtypes.bfloat16)
    return hi, lo


def dft_table(rows):
    phase = (np.arange(rows)[:, None] * np.arange(HALF)[None, :] % SEG) * (2.0 * np.pi / SEG)
    parts = []
    for j in range(CHUNKS):
        cut = slice(j * LANES, (j + 1) * LANES)
        hi, lo = split_table(np.concatenate([np.cos(phase[:, cut]), -np.sin(phase[:, cut])], 1))
        parts += [hi, lo]
    return np.concatenate(parts, axis=1)


def lag_table(seg_count):
    freq = np.arange(HALF)[:, None]
    phase = (freq * np.arange(-LAGH, LAGH)[None, :] % SEG) * (2.0 * np.pi / SEG)
    weight = np.where(freq == 0, 1.0, 2.0) * (math.sqrt(SEG / seg_count) / SEG)
    re = (weight * np.cos(phase)).reshape(CHUNKS, LANES, 2 * LAGH)
    im = (-weight * np.sin(phase)).reshape(CHUNKS, LANES, 2 * LAGH)
    return np.concatenate([re, im], axis=1).reshape(SEG, 2 * LAGH).astype(ml_dtypes.bfloat16)


def iota(shape, dim):
    return lax.broadcasted_iota(jnp.int32, shape, dim)


def one_hot(mask):
    return jnp.where(mask, 1.0, 0.0).astype(jnp.bfloat16)


def column(row):
    n = row.shape[1]
    return jnp.sum(jnp.where(iota((n, n), 0) == iota((n, n), 1), row, 0), axis=1, keepdims=True)


def tap_rows(taps):
    tap_count = taps.shape[1]
    width = 3 * LANES
    flip = one_hot(iota((tap_count, width), 0) + iota((tap_count, width), 1) == tap_count)
    hi = taps.astype(jnp.bfloat16)
    lo = (taps - hi.astype(jnp.float32)).astype(jnp.bfloat16)
    out = []
    for part in (hi, lo):
        base = jnp.dot(
            jnp.broadcast_to(part.astype(jnp.float32), (8, tap_count)).astype(jnp.bfloat16),
            flip,
            preferred_element_type=jnp.float32,
        )
        upper = pltpu.roll(base, 0, 1, stride=DECIM, stride_axis=0)
        out.append(jnp.concatenate([upper, pltpu.roll(upper, 8 * DECIM, 1)], axis=0))
    return out


def edge_tiles(count):
    return -(-count // (PER_TILE * ROWS))


def filter_kernel(
    blocks,
    src_hbm, taps_hbm, raw_ref, tab_hbm,
    out_ref, slot_ref, tab_ref,
    ext, weight, src_ref, taps_ref, sems,
):
    rows, raw_len = raw_ref.shape
    steps = out_ref.shape[0]
    ch = rows // steps
    span = raw_len // blocks
    wide = span + LANES
    copies = []
    for b in range(blocks):
        if b == 0:
            copy = pltpu.make_async_copy(
                raw_ref.at[:, pl.ds(0, span)],
                ext.at[pl.ds(0, rows), pl.ds(LANES, span)],
                sems.at[b],
            )
        else:
            copy = pltpu.make_async_copy(
                raw_ref.at[:, pl.ds(b * span - LANES, wide)],
                ext.at[pl.ds(b * rows, rows), :],
                sems.at[b],
            )
        copy.start()
        copies.append(copy)
    small = [
        pltpu.make_async_copy(taps_hbm, taps_ref, sems.at[blocks]),
        pltpu.make_async_copy(src_hbm, src_ref, sems.at[blocks + 1]),
    ]
    tables = pltpu.make_async_copy(tab_hbm, tab_ref, sems.at[blocks + 2])
    for copy in [*small, tables]:
        copy.start()
    ext[:rows, :LANES] = jnp.zeros((rows, LANES), ext.dtype)
    weight[...] = jnp.zeros_like(weight)
    for copy in small:
        copy.wait()
    for p, base in enumerate(tap_rows(taps_ref[...])):
        for i in range(LANES // 16):
            tile, lane = divmod(16 * DECIM * i, LANES)
            piece = pltpu.roll(base, lane, 1) if lane else base
            weight[p * LANES + 16 * i : p * LANES + 16 * (i + 1), tile * LANES : (tile + 3) * LANES] = (
                piece.astype(jnp.bfloat16)
            )
    src = src_ref[...]
    src_count = src.shape[1]
    slots = slot_ref.shape[0]
    group = src // rows
    group_col = column(group)
    src_col = column(src)
    rank = jnp.sum(
        jnp.where(
            (group_col == group)
            & (iota((src_count, src_count), 0) < iota((src_count, src_count), 1)),
            1,
            0,
        ),
        axis=0,
        keepdims=True,
    )
    mine = lax.axis_index("chan")
    to_slot = one_hot((iota((slots, src_count), 0) == rank) & (group == mine))
    to_row = one_hot(src_col - mine * rows == iota((src_count, rows), 1))
    pick = jnp.dot(to_slot, to_row, preferred_element_type=jnp.float32).astype(jnp.bfloat16)
    number = jnp.where(
        iota((src_count, LANES), 1) == LANES - 1, iota((src_count, LANES), 0) + 1, 0
    ).astype(jnp.float32).astype(jnp.bfloat16)
    number = jnp.dot(to_slot, number, preferred_element_type=jnp.float32)
    for copy in copies:
        copy.wait()
    acc = lax.dot_general(ext[...], weight[...], NT, preferred_element_type=jnp.float32)
    acc = acc[:, :LANES] + acc[:, LANES:]
    y = acc.astype(jnp.bfloat16)
    head = acc[:rows]
    head_lo = head - head.astype(jnp.bfloat16).astype(jnp.float32)
    tail = lax.dot_general(
        ext[(blocks - 1) * rows :, wide - LANES :], weight[:, :LANES], NT,
        preferred_element_type=jnp.float32,
    )
    tail = tail[:, :LANES] + tail[:, LANES:]
    tail_hi = tail.astype(jnp.bfloat16).astype(jnp.float32)
    lane = iota((rows, LANES), 1)
    edge = jnp.where(
        lane < EDGE,
        head_lo,
        jnp.where(
            lane < 2 * EDGE,
            pltpu.roll(tail_hi, EDGE, 1),
            jnp.where(lane < 3 * EDGE, pltpu.roll(tail - tail_hi, 2 * EDGE, 1), 0.0),
        ),
    ).astype(jnp.bfloat16)
    parts = [y[b * rows : (b + 1) * rows] for b in range(blocks)] + [edge]
    last = blocks * ch
    for t in range(steps):
        for b in range(blocks):
            out_ref[t, b * ch : (b + 1) * ch] = parts[b][t * ch : (t + 1) * ch]
        out_ref[t, last : last + ch] = edge[t * ch : (t + 1) * ch]
    for b, part in enumerate(parts):
        found = jnp.dot(pick, part, preferred_element_type=jnp.float32)
        if b == blocks:
            found += number
        slot_ref[:, b * LANES : (b + 1) * LANES] = found.astype(jnp.bfloat16)
    tables.wait()


def arrange_kernel(half, blocks, pieces, *refs):
    slots = jnp.concatenate([ref[...] for ref in refs[:pieces]], axis=0)
    part_ref, *out_refs = refs[pieces:]
    height = out_refs[0].shape[0]
    own_rows = part_ref.shape[1] - ROWS
    tile_rows = height - own_rows - blocks * half
    numbers = slots[:, blocks * LANES :].astype(jnp.float32)
    total = numbers.shape[0]
    numbers = jnp.sum(
        jnp.where(iota((total, LANES), 1) == LANES - 1, numbers, 0.0), axis=1, keepdims=True
    ).astype(jnp.int32)
    first = lax.axis_index("chan") % CORES * half
    pick = one_hot(numbers == iota((total, half), 1) + 1 + first)
    found = lax.dot_general(
        pick, slots, (((0,), (0,)), ((), ())), preferred_element_type=jnp.float32
    )
    fill = [found[:, b * LANES : (b + 1) * LANES].astype(jnp.bfloat16) for b in range(blocks)]
    edges = jnp.where(
        iota((half, LANES), 1) < 3 * EDGE, found[:, blocks * LANES :], 0.0
    )
    added = [jnp.zeros((ROWS, LANES), jnp.float32) for _ in range(tile_rows // ROWS)]
    for i in range(half // ROWS):
        tile, place = divmod(i + 1, PER_TILE)
        piece = edges[i * ROWS : (i + 1) * ROWS]
        added[tile] += pltpu.roll(piece, 3 * EDGE * place, 1) if place else piece
    me = lax.axis_index("tm")
    for k, out_ref in enumerate(out_refs):
        own = part_ref[me ^ k]
        out_ref[:own_rows] = own[:own_rows]
        for b in range(blocks):
            at = own_rows + b * half
            out_ref[at : at + half] = fill[b]
        own = own[own_rows:].astype(jnp.float32)
        for tile, extra in enumerate(added):
            at = height - tile_rows + tile * ROWS
            out_ref[at : at + ROWS] = (extra + own if tile == 0 else extra).astype(jnp.bfloat16)


def collect_kernel(*refs):
    *block_refs, out_ref = refs
    me = lax.axis_index("tm")
    size = out_ref.shape[1]
    for k, ref in enumerate(block_refs):
        out_ref[me ^ k] = ref[ref.shape[0] - size :]


def correlate_kernel(
    seg_count, src_count, dec, head_len, part_rows, count, steps, live_ref, tab_ref, *refs
):
    block_refs, far_ref, out_ref = refs[:steps], refs[steps], refs[steps + 1]
    near_ref, trace, own, other, cross, result, sems = refs[steps + 2 :]
    ch = out_ref.shape[1]
    half = src_count // CORES
    rows = ch + src_count
    per_seg = SEG // dec
    blocks = dec // LANES
    d_cols = 4 * HALF

    @pl.when(pl.program_id(0) == 0)
    def _():
        me = lax.axis_index("tm")
        for k, block_ref in enumerate(block_refs):
            near_ref[me ^ k] = block_ref[...]
        live = iota((ch, LANES), 0) < live_ref[0]
        before = jnp.zeros((rows, LANES), jnp.float32)
        is_head = iota((rows, LANES), 1) < head_len
        tile_rows = edge_tiles(ch + half) * ROWS
        low_core = lax.axis_index("chan") % CORES == 0

        def edge_groups(ref, p):
            out = []
            last = ref.shape[1] - tile_rows
            for i in range((ch + half) // ROWS):
                tile, place = divmod(i, PER_TILE)
                if place == 0:
                    pack = ref[p, last + tile * ROWS : last + (tile + 1) * ROWS].astype(jnp.float32)
                    out.append(pack)
                else:
                    out.append(pltpu.roll(pack, LANES - 3 * EDGE * place, 1))
            return out[0], jnp.concatenate(out[1:], axis=0)

        def in_order(near, far):
            return [jnp.where(low_core, near, far), jnp.where(low_core, far, near)]

        for t in range(steps):
            edge, near = edge_groups(near_ref, t)
            _, far = edge_groups(far_ref, t)
            edge = jnp.concatenate([jnp.where(live, edge, 0.0), *in_order(near, far)], axis=0)
            for b in range(blocks):
                mine = near_ref[t, b * ch : (b + 1) * ch]
                mine = jnp.where(live, mine, jnp.zeros_like(mine))
                at = blocks * ch + b * half
                theirs = near_ref[t, at : at + half], far_ref[t, b * half : (b + 1) * half]
                both = jnp.concatenate([mine, *in_order(*theirs)], axis=0)
                if b == 0:
                    tail = pltpu.roll(before, LANES - EDGE, 1) + pltpu.roll(before, LANES - 2 * EDGE, 1)
                    both = both.astype(jnp.float32)
                    both = jnp.where(is_head, both + edge + tail, both).astype(jnp.bfloat16)
                trace[t * rows : (t + 1) * rows, b * LANES : (b + 1) * LANES] = both
            before = edge
        odd = (iota((rows, 2 * LANES), 1) & 1) == 1
        sign = jnp.where(odd, -1.0, 1.0)
        same = one_hot(
            iota((2 * LANES, LANES), 0) % LANES // BAND == iota((2 * LANES, LANES), 1) // BAND
        )
        group_segs = max(1, min(seg_count, part_rows // (per_seg * rows)))
        for first in range(0, seg_count, group_segs):
            segs = min(group_segs, seg_count - first)
            lhs = trace[first * per_seg * rows : (first + segs) * per_seg * rows, :]
            for j in range(CHUNKS):
                acc = jnp.dot(
                    lhs, tab_ref[:, 4 * j * LANES : 4 * (j + 1) * LANES],
                    preferred_element_type=jnp.float32,
                )
                folded = acc[:, : 2 * LANES] + acc[:, 2 * LANES :]
                spec = []
                for g in range(segs):
                    a = folded[g * per_seg * rows : (g * per_seg + 1) * rows]
                    b = folded[(g * per_seg + 1) * rows : (g * per_seg + 2) * rows]
                    spec.append(a + sign * b)
                spec = jnp.concatenate(spec, axis=0)
                re, im = spec[:, :LANES], spec[:, LANES:]
                power = re * re + im * im
                hi = power.astype(jnp.bfloat16)
                lo = (power - hi.astype(jnp.float32)).astype(jnp.bfloat16)
                total = jnp.dot(
                    jnp.concatenate([hi, lo], axis=1), same, preferred_element_type=jnp.float32
                )
                scale = lax.rsqrt(total * (1.0 / BAND) + whiten_eps)
                w_re = (re * scale).astype(jnp.bfloat16).astype(jnp.float32)
                w_im = (im * scale).astype(jnp.bfloat16).astype(jnp.float32)
                at = 2 * j * LANES
                for g in range(segs):
                    r, o = g * rows, (first + g) * ch
                    own[o : o + ch, at : at + LANES] = w_re[r : r + ch]
                    own[o : o + ch, at + LANES : at + 2 * LANES] = w_im[r : r + ch]
                    o = (first + g) * src_count
                    other[o : o + src_count, at : at + LANES] = w_re[r + ch : r + rows]
                    other[o : o + src_count, at + LANES : at + 2 * LANES] = w_im[r + ch : r + rows]

    block = cross.shape[1] // ch
    copies = []
    for i in range(count):
        start = pl.multiple_of((pl.program_id(0) * count + i) * block, 8)
        for j in range(CHUNKS):
            at = 2 * j * LANES
            a_re = [own[g * ch : (g + 1) * ch, at : at + LANES] for g in range(seg_count)]
            a_im = [own[g * ch : (g + 1) * ch, at + LANES : at + 2 * LANES] for g in range(seg_count)]
            for s in range(block):
                if s % 8 == 0:
                    tiles = [
                        other[
                            pl.ds(pl.multiple_of(g * src_count + start + s, 8), 8),
                            at : at + 2 * LANES,
                        ]
                        for g in range(seg_count)
                    ]
                re = im = None
                for g in range(seg_count):
                    b_re = tiles[g][s % 8 : s % 8 + 1, :LANES]
                    b_im = tiles[g][s % 8 : s % 8 + 1, LANES:]
                    p = a_re[g] * b_re + a_im[g] * b_im
                    q = a_im[g] * b_re - a_re[g] * b_im
                    re, im = (p, q) if re is None else (re + p, im + q)
                row = slice(s * ch, (s + 1) * ch)
                cross[i, row, at : at + LANES] = re.astype(jnp.bfloat16)
                cross[i, row, at + LANES : at + 2 * LANES] = im.astype(jnp.bfloat16)
        lags = sum(
            jnp.dot(
                cross[i, :, h * dec : (h + 1) * dec],
                tab_ref[:, d_cols + 2 * LAGH * h : d_cols + 2 * LAGH * (h + 1)],
                preferred_element_type=jnp.float32,
            )
            for h in range(per_seg)
        )
        result[i] = lags.reshape(result.shape[1:])
        copy = pltpu.make_async_copy(result.at[i], out_ref.at[pl.ds(start, block)], sems.at[i])
        copy.start()
        copies.append(copy)
    for copy in copies:
        copy.wait()


def whole(space=pltpu.VMEM):
    return pl.BlockSpec(memory_space=space)


def local(raw_strain, fir_taps, source_channels, live_counts):
    rows, raw_len = raw_strain.shape
    steps = lax.axis_size("tm")
    chan_count = lax.axis_size("chan")
    dec = raw_len // DECIM
    blocks = dec // LANES
    ch = rows // steps
    seg_count = steps * dec // SEG
    src_count = source_channels.shape[0]
    slots = 2 * SRC_DEV * steps
    span = raw_len // blocks
    total_rows = ch + src_count
    half = src_count // CORES
    tile_rows = edge_tiles(ch + half) * ROWS
    height = blocks * (ch + half) + tile_rows
    head_len = -(-(fir_taps.shape[0] - 1) // DECIM)
    assert head_len < EDGE and ch == ROWS and src_count <= 256
    assert steps & (steps - 1) == 0 and chan_count & (chan_count - 1) == 0 and half % ROWS == 0
    src = source_channels.reshape(1, src_count)
    taps = fir_taps.reshape(1, fir_taps.shape[0])
    table = np.concatenate([dft_table(dec), *lag_table(seg_count).reshape(SEG // dec, dec, -1)], axis=1)
    inputs = (src, taps, raw_strain, jnp.asarray(table))
    part, picked, table = pl.pallas_call(
        functools.partial(filter_kernel, blocks),
        out_shape=[
            pltpu.VMEM((steps, (blocks + 1) * ch, LANES), jnp.bfloat16),
            pltpu.VMEM((slots, dec + LANES), jnp.bfloat16),
            pltpu.VMEM(table.shape, jnp.bfloat16),
        ],
        in_specs=[whole(pl.ANY)] * 4,
        out_specs=[whole(), whole(), whole(pl.ANY)],
        scratch_shapes=[
            pltpu.VMEM((blocks * rows, span + LANES), jnp.bfloat16),
            pltpu.VMEM((2 * LANES, span + LANES), jnp.bfloat16),
            pltpu.VMEM(src.shape, src.dtype),
            pltpu.VMEM(taps.shape, taps.dtype),
            pltpu.SemaphoreType.DMA((blocks + 3,)),
        ],
        compiler_params=pltpu.CompilerParams(vmem_limit_bytes=16 * MIB),
        name="fir",
    )(*(pltpu.with_memory_space_constraint(a, pltpu.HBM) for a in inputs))
    pieces = [picked] + [
        lax.ppermute(picked, "chan", [(c, c ^ k) for c in range(chan_count)])
        for k in range(chan_count - 1, 0, -1)
    ]
    to_vmem = functools.partial(pltpu.with_memory_space_constraint, memory_space=pltpu.VMEM)
    outgoing = pl.pallas_call(
        functools.partial(arrange_kernel, half, blocks, chan_count),
        out_shape=[pltpu.VMEM((height, LANES), jnp.bfloat16)] * steps,
        in_specs=[whole()] * (chan_count + 1),
        out_specs=[whole()] * steps,
        compiler_params=pltpu.CompilerParams(vmem_limit_bytes=8 * MIB),
        name="arrange",
    )(*(to_vmem(a) for a in (*pieces, part)))
    arrived = [
        lax.ppermute(outgoing[k], "tm", [(t, t ^ k) for t in range(steps)])
        for k in range(steps - 1, 0, -1)
    ]
    arrived = [to_vmem(a) for a in (outgoing[0], *arrived[::-1])]
    given = pl.pallas_call(
        collect_kernel,
        out_shape=pltpu.VMEM((steps, blocks * half + tile_rows, LANES), jnp.bfloat16),
        in_specs=[whole()] * steps,
        out_specs=whole(),
        compiler_params=pltpu.CompilerParams(vmem_limit_bytes=8 * MIB),
        name="collect",
    )(*arrived)
    swapped = lax.ppermute(given, "chan", [(c, c ^ 1) for c in range(chan_count)])
    block = math.gcd(src_count, 16)
    count = math.gcd(src_count // block, 2)
    state = seg_count * total_rows * SEG * 4
    return pl.pallas_call(
        functools.partial(
            correlate_kernel, seg_count, src_count, dec, head_len, 1024, count, steps
        ),
        grid=(src_count // (block * count),),
        out_shape=jax.ShapeDtypeStruct((src_count, ch, 2 * LAGH), jnp.float32),
        in_specs=[whole(pltpu.SMEM)] + [whole()] * (steps + 2),
        out_specs=whole(pl.ANY),
        scratch_shapes=[
            pltpu.VMEM((steps, height, LANES), jnp.bfloat16),
            pltpu.VMEM((steps * total_rows, dec), jnp.bfloat16),
            pltpu.VMEM((seg_count * ch, SEG), jnp.float32),
            pltpu.VMEM((seg_count * src_count, SEG), jnp.float32),
            pltpu.VMEM((count, block * ch, SEG), jnp.bfloat16),
            pltpu.VMEM((count, block, ch, 2 * LAGH), jnp.float32),
            pltpu.SemaphoreType.DMA((count,)),
        ],
        compiler_params=pltpu.CompilerParams(vmem_limit_bytes=16 * MIB + 2 * state),
        name="correlate",
    )(live_counts, table, *arrived, to_vmem(swapped))


def solution(mesh):
    placed = (P("chan", "tm"), P(), P(), P(("chan", "tm")))
    return jax.shard_map(
        local, mesh=mesh, in_specs=placed, out_specs=P(None, ("chan", "tm"), None), check_vma=False
    )
```

```python
import functools
import math

import jax
import jax.numpy as jnp
import ml_dtypes
import numpy as np
from jax import lax
from jax.experimental import pallas as pl
from jax.experimental.pallas import tpu as pltpu
from jax.sharding import PartitionSpec as P

DECIM = 10
SEG = 1024
BAND = 64
LAGH = 192
SRC_DEV = 1
LANES = 128
HALF = SEG // 2
CHUNKS = HALF // LANES
EDGE = 14
PER_TILE = LANES // (3 * EDGE)
ROWS = 16
CORES = 2
MIB = 1024 * 1024

whiten_eps = 1e-06

NT = (((1,), (1,)), ((), ()))


def split_table(table):
    hi = table.astype(ml_dtypes.bfloat16)
    lo = (table - hi.astype(np.float64)).astype(ml_dtypes.bfloat16)
    return hi, lo


def dft_table(rows):
    phase = (np.arange(rows)[:, None] * np.arange(HALF)[None, :] % SEG) * (2.0 * np.pi / SEG)
    parts = []
    for j in range(CHUNKS):
        cut = slice(j * LANES, (j + 1) * LANES)
        hi, lo = split_table(np.concatenate([np.cos(phase[:, cut]), -np.sin(phase[:, cut])], 1))
        parts += [hi, lo]
    return np.concatenate(parts, axis=1)


def lag_table(seg_count):
    freq = np.arange(HALF)[:, None]
    phase = (freq * np.arange(-LAGH, LAGH)[None, :] % SEG) * (2.0 * np.pi / SEG)
    weight = np.where(freq == 0, 1.0, 2.0) * (math.sqrt(SEG / seg_count) / SEG)
    re = (weight * np.cos(phase)).reshape(CHUNKS, LANES, 2 * LAGH)
    im = (-weight * np.sin(phase)).reshape(CHUNKS, LANES, 2 * LAGH)
    return np.concatenate([re, im], axis=1).reshape(SEG, 2 * LAGH).astype(ml_dtypes.bfloat16)


def iota(shape, dim):
    return lax.broadcasted_iota(jnp.int32, shape, dim)


def one_hot(mask):
    return jnp.where(mask, 1.0, 0.0).astype(jnp.bfloat16)


def column(row):
    n = row.shape[1]
    return jnp.sum(jnp.where(iota((n, n), 0) == iota((n, n), 1), row, 0), axis=1, keepdims=True)


def tap_rows(taps):
    tap_count = taps.shape[1]
    width = 3 * LANES
    flip = one_hot(iota((tap_count, width), 0) + iota((tap_count, width), 1) == tap_count)
    hi = taps.astype(jnp.bfloat16)
    lo = (taps - hi.astype(jnp.float32)).astype(jnp.bfloat16)
    out = []
    for part in (hi, lo):
        base = jnp.dot(
            jnp.broadcast_to(part.astype(jnp.float32), (8, tap_count)).astype(jnp.bfloat16),
            flip,
            preferred_element_type=jnp.float32,
        )
        upper = pltpu.roll(base, 0, 1, stride=DECIM, stride_axis=0)
        out.append(jnp.concatenate([upper, pltpu.roll(upper, 8 * DECIM, 1)], axis=0))
    return out


def edge_tiles(count):
    return -(-count // (PER_TILE * ROWS))


def filter_kernel(
    blocks,
    src_hbm, taps_hbm, raw_ref, tab_hbm,
    out_ref, slot_ref, tab_ref,
    ext, weight, src_ref, taps_ref, sems,
):
    rows, raw_len = raw_ref.shape
    steps = out_ref.shape[0]
    ch = rows // steps
    span = raw_len // blocks
    wide = span + LANES
    copies = []
    for b in range(blocks):
        if b == 0:
            copy = pltpu.make_async_copy(
                raw_ref.at[:, pl.ds(0, span)],
                ext.at[pl.ds(0, rows), pl.ds(LANES, span)],
                sems.at[b],
            )
        else:
            copy = pltpu.make_async_copy(
                raw_ref.at[:, pl.ds(b * span - LANES, wide)],
                ext.at[pl.ds(b * rows, rows), :],
                sems.at[b],
            )
        copy.start()
        copies.append(copy)
    small = [
        pltpu.make_async_copy(taps_hbm, taps_ref, sems.at[blocks]),
        pltpu.make_async_copy(src_hbm, src_ref, sems.at[blocks + 1]),
    ]
    tables = pltpu.make_async_copy(tab_hbm, tab_ref, sems.at[blocks + 2])
    for copy in [*small, tables]:
        copy.start()
    ext[:rows, :LANES] = jnp.zeros((rows, LANES), ext.dtype)
    weight[...] = jnp.zeros_like(weight)
    for copy in small:
        copy.wait()
    for p, base in enumerate(tap_rows(taps_ref[...])):
        for i in range(LANES // 16):
            tile, lane = divmod(16 * DECIM * i, LANES)
            piece = pltpu.roll(base, lane, 1) if lane else base
            weight[p * LANES + 16 * i : p * LANES + 16 * (i + 1), tile * LANES : (tile + 3) * LANES] = (
                piece.astype(jnp.bfloat16)
            )
    src = src_ref[...]
    src_count = src.shape[1]
    slots = slot_ref.shape[0]
    group = src // rows
    group_col = column(group)
    src_col = column(src)
    rank = jnp.sum(
        jnp.where(
            (group_col == group)
            & (iota((src_count, src_count), 0) < iota((src_count, src_count), 1)),
            1,
            0,
        ),
        axis=0,
        keepdims=True,
    )
    mine = lax.axis_index("chan")
    to_slot = one_hot((iota((slots, src_count), 0) == rank) & (group == mine))
    to_row = one_hot(src_col - mine * rows == iota((src_count, rows), 1))
    pick = jnp.dot(to_slot, to_row, preferred_element_type=jnp.float32).astype(jnp.bfloat16)
    number = jnp.where(
        iota((src_count, LANES), 1) == LANES - 1, iota((src_count, LANES), 0) + 1, 0
    ).astype(jnp.float32).astype(jnp.bfloat16)
    number = jnp.dot(to_slot, number, preferred_element_type=jnp.float32)
    for copy in copies:
        copy.wait()
    acc = lax.dot_general(ext[...], weight[...], NT, preferred_element_type=jnp.float32)
    acc = acc[:, :LANES] + acc[:, LANES:]
    y = acc.astype(jnp.bfloat16)
    head = acc[:rows]
    head_lo = head - head.astype(jnp.bfloat16).astype(jnp.float32)
    tail = lax.dot_general(
        ext[(blocks - 1) * rows :, wide - LANES :], weight[:, :LANES], NT,
        preferred_element_type=jnp.float32,
    )
    tail = tail[:, :LANES] + tail[:, LANES:]
    tail_hi = tail.astype(jnp.bfloat16).astype(jnp.float32)
    lane = iota((rows, LANES), 1)
    edge = jnp.where(
        lane < EDGE,
        head_lo,
        jnp.where(
            lane < 2 * EDGE,
            pltpu.roll(tail_hi, EDGE, 1),
            jnp.where(lane < 3 * EDGE, pltpu.roll(tail - tail_hi, 2 * EDGE, 1), 0.0),
        ),
    ).astype(jnp.bfloat16)
    parts = [y[b * rows : (b + 1) * rows] for b in range(blocks)] + [edge]
    last = blocks * ch
    for t in range(steps):
        for b in range(blocks):
            out_ref[t, b * ch : (b + 1) * ch] = parts[b][t * ch : (t + 1) * ch]
        out_ref[t, last : last + ch] = edge[t * ch : (t + 1) * ch]
    for b, part in enumerate(parts):
        found = jnp.dot(pick, part, preferred_element_type=jnp.float32)
        if b == blocks:
            found += number
        slot_ref[:, b * LANES : (b + 1) * LANES] = found.astype(jnp.bfloat16)
    tables.wait()


def arrange_kernel(half, blocks, pieces, *refs):
    slots = jnp.concatenate([ref[...] for ref in refs[:pieces]], axis=0)
    part_ref, *out_refs = refs[pieces:]
    height = out_refs[0].shape[0]
    own_rows = part_ref.shape[1] - ROWS
    tile_rows = height - 2 * own_rows - blocks * half
    numbers = slots[:, blocks * LANES :].astype(jnp.float32)
    total = numbers.shape[0]
    numbers = jnp.sum(
        jnp.where(iota((total, LANES), 1) == LANES - 1, numbers, 0.0), axis=1, keepdims=True
    ).astype(jnp.int32)
    first = lax.axis_index("chan") % CORES * half
    pick = one_hot(numbers == iota((total, half), 1) + 1 + first)
    found = lax.dot_general(
        pick, slots, (((0,), (0,)), ((), ())), preferred_element_type=jnp.float32
    )
    fill = [found[:, b * LANES : (b + 1) * LANES].astype(jnp.bfloat16) for b in range(blocks)]
    edges = jnp.where(iota((half, LANES), 1) < 3 * EDGE, found[:, blocks * LANES :], 0.0)
    added = [jnp.zeros((ROWS, LANES), jnp.float32) for _ in range(tile_rows // ROWS)]
    for i in range(half // ROWS):
        tile, place = divmod(i + 2, PER_TILE)
        piece = edges[i * ROWS : (i + 1) * ROWS]
        added[tile] += pltpu.roll(piece, 3 * EDGE * place, 1) if place else piece
    me = lax.axis_index("tm")
    for k, out_ref in enumerate(out_refs):
        same = part_ref[me ^ (2 * k)]
        other = part_ref[me ^ (2 * k) ^ 1]
        out_ref[:own_rows] = same[:own_rows]
        out_ref[own_rows : 2 * own_rows] = other[:own_rows]
        for b in range(blocks):
            at = 2 * own_rows + b * half
            out_ref[at : at + half] = fill[b]
        mixed = same[own_rows:].astype(jnp.float32) + pltpu.roll(
            other[own_rows:].astype(jnp.float32), 3 * EDGE, 1
        )
        for tile, extra in enumerate(added):
            at = height - tile_rows + tile * ROWS
            out_ref[at : at + ROWS] = (extra + mixed if tile == 0 else extra).astype(jnp.bfloat16)


def forward_kernel(own_rows, *refs):
    *block_refs, out_ref = refs
    high = lax.axis_index("tm") // 2
    for k, ref in enumerate(block_refs):
        out_ref[high ^ k] = ref[own_rows:]


def collect_kernel(own_rows, *refs):
    *block_refs, passed_ref, out_ref = refs
    me = lax.axis_index("tm")
    for k, ref in enumerate(block_refs):
        out_ref[me ^ (2 * k)] = ref[2 * own_rows :]
    for high in range(passed_ref.shape[0]):
        out_ref[2 * high + (1 - me % 2)] = passed_ref[high, own_rows:]


def correlate_kernel(
    seg_count, src_count, dec, head_len, part_rows, count, steps, live_ref, tab_ref, *refs
):
    count_high = steps // 2
    block_refs, passed_ref, given_ref = refs[:count_high], refs[count_high], refs[count_high + 1]
    far_ref, out_ref = refs[count_high + 2 : count_high + 4]
    mine_ref, mine_edge, trace, own, other, cross, result, sems = refs[count_high + 4 :]
    ch = out_ref.shape[1]
    own_rows = mine_ref.shape[1]
    half = src_count // CORES
    rows = ch + src_count
    per_seg = SEG // dec
    blocks = dec // LANES
    d_cols = 4 * HALF

    @pl.when(pl.program_id(0) == 0)
    def _():
        me = lax.axis_index("tm")
        last = block_refs[0].shape[0] - edge_tiles(2 * ch + half) * ROWS
        for k, ref in enumerate(block_refs):
            mine_ref[me ^ (2 * k)] = ref[:own_rows]
            mine_edge[me ^ (2 * k)] = ref[last : last + ROWS].astype(jnp.float32)
        for high in range(count_high):
            t = 2 * high + (1 - me % 2)
            mine_ref[t] = passed_ref[high, :own_rows]
            pack = passed_ref[high, last - own_rows : last - own_rows + ROWS].astype(jnp.float32)
            mine_edge[t] = pltpu.roll(pack, LANES - 3 * EDGE, 1)
        live = iota((ch, LANES), 0) < live_ref[0]
        before = jnp.zeros((rows, LANES), jnp.float32)
        is_head = iota((rows, LANES), 1) < head_len
        tile_rows = edge_tiles(2 * ch + half) * ROWS
        low_core = lax.axis_index("chan") % CORES == 0

        def edge_groups(ref, t):
            out = []
            last = ref.shape[1] - tile_rows
            for i in range(2, 2 + half // ROWS):
                tile, place = divmod(i, PER_TILE)
                pack = ref[t, last + tile * ROWS : last + (tile + 1) * ROWS].astype(jnp.float32)
                out.append(pltpu.roll(pack, LANES - 3 * EDGE * place, 1) if place else pack)
            return jnp.concatenate(out, axis=0)

        def in_order(near, far):
            return [jnp.where(low_core, near, far), jnp.where(low_core, far, near)]

        for t in range(steps):
            edge = jnp.where(live, mine_edge[t], 0.0)
            theirs = edge_groups(given_ref, t), edge_groups(far_ref, t)
            edge = jnp.concatenate([edge, *in_order(*theirs)], axis=0)
            for b in range(blocks):
                mine = mine_ref[t, b * ch : (b + 1) * ch]
                mine = jnp.where(live, mine, jnp.zeros_like(mine))
                rows_b = slice(b * half, (b + 1) * half)
                theirs = given_ref[t, rows_b], far_ref[t, rows_b]
                both = jnp.concatenate([mine, *in_order(*theirs)], axis=0)
                if b == 0:
                    tail = pltpu.roll(before, LANES - EDGE, 1) + pltpu.roll(before, LANES - 2 * EDGE, 1)
                    both = both.astype(jnp.float32)
                    both = jnp.where(is_head, both + edge + tail, both).astype(jnp.bfloat16)
                trace[t * rows : (t + 1) * rows, b * LANES : (b + 1) * LANES] = both
            before = edge
        odd = (iota((rows, 2 * LANES), 1) & 1) == 1
        sign = jnp.where(odd, -1.0, 1.0)
        same = one_hot(
            iota((2 * LANES, LANES), 0) % LANES // BAND == iota((2 * LANES, LANES), 1) // BAND
        )
        group_segs = max(1, min(seg_count, part_rows // (per_seg * rows)))
        for first in range(0, seg_count, group_segs):
            segs = min(group_segs, seg_count - first)
            lhs = trace[first * per_seg * rows : (first + segs) * per_seg * rows, :]
            for j in range(CHUNKS):
                acc = jnp.dot(
                    lhs, tab_ref[:, 4 * j * LANES : 4 * (j + 1) * LANES],
                    preferred_element_type=jnp.float32,
                )
                folded = acc[:, : 2 * LANES] + acc[:, 2 * LANES :]
                spec = []
                for g in range(segs):
                    a = folded[g * per_seg * rows : (g * per_seg + 1) * rows]
                    b = folded[(g * per_seg + 1) * rows : (g * per_seg + 2) * rows]
                    spec.append(a + sign * b)
                spec = jnp.concatenate(spec, axis=0)
                re, im = spec[:, :LANES], spec[:, LANES:]
                power = re * re + im * im
                hi = power.astype(jnp.bfloat16)
                lo = (power - hi.astype(jnp.float32)).astype(jnp.bfloat16)
                total = jnp.dot(
                    jnp.concatenate([hi, lo], axis=1), same, preferred_element_type=jnp.float32
                )
                scale = lax.rsqrt(total * (1.0 / BAND) + whiten_eps)
                w_re = (re * scale).astype(jnp.bfloat16).astype(jnp.float32)
                w_im = (im * scale).astype(jnp.bfloat16).astype(jnp.float32)
                at = 2 * j * LANES
                for g in range(segs):
                    r, o = g * rows, (first + g) * ch
                    own[o : o + ch, at : at + LANES] = w_re[r : r + ch]
                    own[o : o + ch, at + LANES : at + 2 * LANES] = w_im[r : r + ch]
                    o = (first + g) * src_count
                    other[o : o + src_count, at : at + LANES] = w_re[r + ch : r + rows]
                    other[o : o + src_count, at + LANES : at + 2 * LANES] = w_im[r + ch : r + rows]

    block = cross.shape[1] // ch
    copies = []
    for i in range(count):
        start = pl.multiple_of((pl.program_id(0) * count + i) * block, 8)
        for j in range(CHUNKS):
            at = 2 * j * LANES
            a_re = [own[g * ch : (g + 1) * ch, at : at + LANES] for g in range(seg_count)]
            a_im = [own[g * ch : (g + 1) * ch, at + LANES : at + 2 * LANES] for g in range(seg_count)]
            for s in range(block):
                if s % 8 == 0:
                    tiles = [
                        other[
                            pl.ds(pl.multiple_of(g * src_count + start + s, 8), 8),
                            at : at + 2 * LANES,
                        ]
                        for g in range(seg_count)
                    ]
                re = im = None
                for g in range(seg_count):
                    b_re = tiles[g][s % 8 : s % 8 + 1, :LANES]
                    b_im = tiles[g][s % 8 : s % 8 + 1, LANES:]
                    p = a_re[g] * b_re + a_im[g] * b_im
                    q = a_im[g] * b_re - a_re[g] * b_im
                    re, im = (p, q) if re is None else (re + p, im + q)
                row = slice(s * ch, (s + 1) * ch)
                cross[i, row, at : at + LANES] = re.astype(jnp.bfloat16)
                cross[i, row, at + LANES : at + 2 * LANES] = im.astype(jnp.bfloat16)
        lags = sum(
            jnp.dot(
                cross[i, :, h * dec : (h + 1) * dec],
                tab_ref[:, d_cols + 2 * LAGH * h : d_cols + 2 * LAGH * (h + 1)],
                preferred_element_type=jnp.float32,
            )
            for h in range(per_seg)
        )
        result[i] = lags.reshape(result.shape[1:])
        copy = pltpu.make_async_copy(result.at[i], out_ref.at[pl.ds(start, block)], sems.at[i])
        copy.start()
        copies.append(copy)
    for copy in copies:
        copy.wait()


def whole(space=pltpu.VMEM):
    return pl.BlockSpec(memory_space=space)


def local(raw_strain, fir_taps, source_channels, live_counts):
    rows, raw_len = raw_strain.shape
    steps = lax.axis_size("tm")
    chan_count = lax.axis_size("chan")
    dec = raw_len // DECIM
    blocks = dec // LANES
    ch = rows // steps
    seg_count = steps * dec // SEG
    src_count = source_channels.shape[0]
    slots = 2 * SRC_DEV * steps
    span = raw_len // blocks
    total_rows = ch + src_count
    half = src_count // CORES
    highs = steps // 2
    own_rows = blocks * ch
    given_rows = blocks * half + edge_tiles(2 * ch + half) * ROWS
    height = 2 * own_rows + given_rows
    head_len = -(-(fir_taps.shape[0] - 1) // DECIM)
    assert head_len < EDGE and ch == ROWS and src_count <= 256
    assert steps & (steps - 1) == 0 and chan_count & (chan_count - 1) == 0 and half % ROWS == 0
    src = source_channels.reshape(1, src_count)
    taps = fir_taps.reshape(1, fir_taps.shape[0])
    table = np.concatenate([dft_table(dec), *lag_table(seg_count).reshape(SEG // dec, dec, -1)], axis=1)
    inputs = (src, taps, raw_strain, jnp.asarray(table))
    part, picked, table = pl.pallas_call(
        functools.partial(filter_kernel, blocks),
        out_shape=[
            pltpu.VMEM((steps, (blocks + 1) * ch, LANES), jnp.bfloat16),
            pltpu.VMEM((slots, dec + LANES), jnp.bfloat16),
            pltpu.VMEM(table.shape, jnp.bfloat16),
        ],
        in_specs=[whole(pl.ANY)] * 4,
        out_specs=[whole(), whole(), whole(pl.ANY)],
        scratch_shapes=[
            pltpu.VMEM((blocks * rows, span + LANES), jnp.bfloat16),
            pltpu.VMEM((2 * LANES, span + LANES), jnp.bfloat16),
            pltpu.VMEM(src.shape, src.dtype),
            pltpu.VMEM(taps.shape, taps.dtype),
            pltpu.SemaphoreType.DMA((blocks + 3,)),
        ],
        compiler_params=pltpu.CompilerParams(vmem_limit_bytes=16 * MIB),
        name="fir",
    )(*(pltpu.with_memory_space_constraint(a, pltpu.HBM) for a in inputs))
    pieces = [picked] + [
        lax.ppermute(picked, "chan", [(c, c ^ k) for c in range(chan_count)])
        for k in range(chan_count - 1, 0, -1)
    ]
    to_vmem = functools.partial(pltpu.with_memory_space_constraint, memory_space=pltpu.VMEM)
    outgoing = pl.pallas_call(
        functools.partial(arrange_kernel, half, blocks, chan_count),
        out_shape=[pltpu.VMEM((height, LANES), jnp.bfloat16)] * highs,
        in_specs=[whole()] * (chan_count + 1),
        out_specs=[whole()] * highs,
        compiler_params=pltpu.CompilerParams(vmem_limit_bytes=8 * MIB),
        name="arrange",
    )(*(to_vmem(a) for a in (*pieces, part)))
    arrived = [
        lax.ppermute(outgoing[k], "tm", [(t, t ^ (2 * k)) for t in range(steps)])
        for k in range(highs - 1, 0, -1)
    ]
    arrived = [to_vmem(a) for a in (outgoing[0], *arrived[::-1])]
    small = pltpu.CompilerParams(vmem_limit_bytes=8 * MIB)
    forward = pl.pallas_call(
        functools.partial(forward_kernel, own_rows),
        out_shape=pltpu.VMEM((highs, own_rows + given_rows, LANES), jnp.bfloat16),
        in_specs=[whole()] * highs,
        out_specs=whole(),
        compiler_params=small,
        name="forward",
    )(*arrived)
    passed = to_vmem(lax.ppermute(forward, "tm", [(t, t ^ 1) for t in range(steps)]))
    given = pl.pallas_call(
        functools.partial(collect_kernel, own_rows),
        out_shape=pltpu.VMEM((steps, given_rows, LANES), jnp.bfloat16),
        in_specs=[whole()] * (highs + 1),
        out_specs=whole(),
        compiler_params=small,
        name="collect",
    )(*arrived, passed)
    swapped = lax.ppermute(given, "chan", [(c, c ^ 1) for c in range(chan_count)])
    block = math.gcd(src_count, 16)
    count = math.gcd(src_count // block, 2)
    state = seg_count * total_rows * SEG * 4
    return pl.pallas_call(
        functools.partial(
            correlate_kernel, seg_count, src_count, dec, head_len, 1024, count, steps
        ),
        grid=(src_count // (block * count),),
        out_shape=jax.ShapeDtypeStruct((src_count, ch, 2 * LAGH), jnp.float32),
        in_specs=[whole(pltpu.SMEM)] + [whole()] * (highs + 4),
        out_specs=whole(pl.ANY),
        scratch_shapes=[
            pltpu.VMEM((steps, own_rows, LANES), jnp.bfloat16),
            pltpu.VMEM((steps, ROWS, LANES), jnp.float32),
            pltpu.VMEM((steps * total_rows, dec), jnp.bfloat16),
            pltpu.VMEM((seg_count * ch, SEG), jnp.float32),
            pltpu.VMEM((seg_count * src_count, SEG), jnp.float32),
            pltpu.VMEM((count, block * ch, SEG), jnp.bfloat16),
            pltpu.VMEM((count, block, ch, 2 * LAGH), jnp.float32),
            pltpu.SemaphoreType.DMA((count,)),
        ],
        compiler_params=pltpu.CompilerParams(vmem_limit_bytes=16 * MIB + 2 * state),
        name="correlate",
    )(live_counts, table, *arrived, passed, to_vmem(given), to_vmem(swapped))


def solution(mesh):
    placed = (P("chan", "tm"), P(), P(), P(("chan", "tm")))
    return jax.shard_map(
        local, mesh=mesh, in_specs=placed, out_specs=P(None, ("chan", "tm"), None), check_vma=False
    )
```

```python
import functools
import math

import jax
import jax.numpy as jnp
import ml_dtypes
import numpy as np
from jax import lax
from jax.experimental import pallas as pl
from jax.experimental.pallas import tpu as pltpu
from jax.sharding import PartitionSpec as P

DECIM = 10
SEG = 1024
BAND = 64
LAGH = 192
SRC_DEV = 1
LANES = 128
HALF = SEG // 2
CHUNKS = HALF // LANES
EDGE = 14
PER_TILE = LANES // (3 * EDGE)
ROWS = 16
CORES = 2
MIB = 1024 * 1024

whiten_eps = 1e-06

NT = (((1,), (1,)), ((), ()))


def split_table(table):
    hi = table.astype(ml_dtypes.bfloat16)
    lo = (table - hi.astype(np.float64)).astype(ml_dtypes.bfloat16)
    return hi, lo


def dft_table(rows):
    phase = (np.arange(rows)[:, None] * np.arange(HALF)[None, :] % SEG) * (2.0 * np.pi / SEG)
    parts = []
    for j in range(CHUNKS):
        cut = slice(j * LANES, (j + 1) * LANES)
        hi, lo = split_table(np.concatenate([np.cos(phase[:, cut]), -np.sin(phase[:, cut])], 1))
        parts += [hi, lo]
    return np.concatenate(parts, axis=1)


def lag_table(seg_count):
    freq = np.arange(HALF)[:, None]
    phase = (freq * np.arange(-LAGH, LAGH)[None, :] % SEG) * (2.0 * np.pi / SEG)
    weight = np.where(freq == 0, 1.0, 2.0) * (math.sqrt(SEG / seg_count) / SEG)
    re = (weight * np.cos(phase)).reshape(CHUNKS, LANES, 2 * LAGH)
    im = (-weight * np.sin(phase)).reshape(CHUNKS, LANES, 2 * LAGH)
    return np.concatenate([re, im], axis=1).reshape(SEG, 2 * LAGH).astype(ml_dtypes.bfloat16)


def iota(shape, dim):
    return lax.broadcasted_iota(jnp.int32, shape, dim)


def one_hot(mask):
    return jnp.where(mask, 1.0, 0.0).astype(jnp.bfloat16)


def column(row):
    n = row.shape[1]
    return jnp.sum(jnp.where(iota((n, n), 0) == iota((n, n), 1), row, 0), axis=1, keepdims=True)


def tap_rows(taps):
    tap_count = taps.shape[1]
    width = 3 * LANES
    flip = one_hot(iota((tap_count, width), 0) + iota((tap_count, width), 1) == tap_count)
    hi = taps.astype(jnp.bfloat16)
    lo = (taps - hi.astype(jnp.float32)).astype(jnp.bfloat16)
    out = []
    for part in (hi, lo):
        base = jnp.dot(
            jnp.broadcast_to(part.astype(jnp.float32), (8, tap_count)).astype(jnp.bfloat16),
            flip,
            preferred_element_type=jnp.float32,
        )
        upper = pltpu.roll(base, 0, 1, stride=DECIM, stride_axis=0)
        out.append(jnp.concatenate([upper, pltpu.roll(upper, 8 * DECIM, 1)], axis=0))
    return out


def edge_tiles(count):
    return -(-count // (PER_TILE * ROWS))


def filter_kernel(
    blocks,
    src_hbm, taps_hbm, raw_ref, tab_hbm,
    out_ref, slot_ref, tab_ref,
    ext, weight, src_ref, taps_ref, sems,
):
    rows, raw_len = raw_ref.shape
    steps = out_ref.shape[0]
    ch = rows // steps
    span = raw_len // blocks
    wide = span + LANES
    copies = []
    for b in range(blocks):
        if b == 0:
            copy = pltpu.make_async_copy(
                raw_ref.at[:, pl.ds(0, span)],
                ext.at[pl.ds(0, rows), pl.ds(LANES, span)],
                sems.at[b],
            )
        else:
            copy = pltpu.make_async_copy(
                raw_ref.at[:, pl.ds(b * span - LANES, wide)],
                ext.at[pl.ds(b * rows, rows), :],
                sems.at[b],
            )
        copy.start()
        copies.append(copy)
    small = [
        pltpu.make_async_copy(taps_hbm, taps_ref, sems.at[blocks]),
        pltpu.make_async_copy(src_hbm, src_ref, sems.at[blocks + 1]),
    ]
    tables = pltpu.make_async_copy(tab_hbm, tab_ref, sems.at[blocks + 2])
    for copy in [*small, tables]:
        copy.start()
    ext[:rows, :LANES] = jnp.zeros((rows, LANES), ext.dtype)
    weight[...] = jnp.zeros_like(weight)
    for copy in small:
        copy.wait()
    for p, base in enumerate(tap_rows(taps_ref[...])):
        for i in range(LANES // 16):
            tile, lane = divmod(16 * DECIM * i, LANES)
            piece = pltpu.roll(base, lane, 1) if lane else base
            weight[p * LANES + 16 * i : p * LANES + 16 * (i + 1), tile * LANES : (tile + 3) * LANES] = (
                piece.astype(jnp.bfloat16)
            )
    src = src_ref[...]
    src_count = src.shape[1]
    slots = slot_ref.shape[0]
    group = src // rows
    group_col = column(group)
    src_col = column(src)
    rank = jnp.sum(
        jnp.where(
            (group_col == group)
            & (iota((src_count, src_count), 0) < iota((src_count, src_count), 1)),
            1,
            0,
        ),
        axis=0,
        keepdims=True,
    )
    mine = lax.axis_index("chan")
    to_slot = one_hot((iota((slots, src_count), 0) == rank) & (group == mine))
    to_row = one_hot(src_col - mine * rows == iota((src_count, rows), 1))
    pick = jnp.dot(to_slot, to_row, preferred_element_type=jnp.float32).astype(jnp.bfloat16)
    number = jnp.where(
        iota((src_count, LANES), 1) == LANES - 1, iota((src_count, LANES), 0) + 1, 0
    ).astype(jnp.float32).astype(jnp.bfloat16)
    number = jnp.dot(to_slot, number, preferred_element_type=jnp.float32)
    for copy in copies:
        copy.wait()
    acc = lax.dot_general(ext[...], weight[...], NT, preferred_element_type=jnp.float32)
    acc = acc[:, :LANES] + acc[:, LANES:]
    y = acc.astype(jnp.bfloat16)
    head = acc[:rows]
    head_lo = head - head.astype(jnp.bfloat16).astype(jnp.float32)
    tail = lax.dot_general(
        ext[(blocks - 1) * rows :, wide - LANES :], weight[:, :LANES], NT,
        preferred_element_type=jnp.float32,
    )
    tail = tail[:, :LANES] + tail[:, LANES:]
    tail_hi = tail.astype(jnp.bfloat16).astype(jnp.float32)
    lane = iota((rows, LANES), 1)
    edge = jnp.where(
        lane < EDGE,
        head_lo,
        jnp.where(
            lane < 2 * EDGE,
            pltpu.roll(tail_hi, EDGE, 1),
            jnp.where(lane < 3 * EDGE, pltpu.roll(tail - tail_hi, 2 * EDGE, 1), 0.0),
        ),
    ).astype(jnp.bfloat16)
    parts = [y[b * rows : (b + 1) * rows] for b in range(blocks)] + [edge]
    last = blocks * ch
    for t in range(steps):
        for b in range(blocks):
            out_ref[t, b * ch : (b + 1) * ch] = parts[b][t * ch : (t + 1) * ch]
        out_ref[t, last : last + ch] = edge[t * ch : (t + 1) * ch]
    for b, part in enumerate(parts):
        found = jnp.dot(pick, part, preferred_element_type=jnp.float32)
        if b == blocks:
            found += number
        slot_ref[:, b * LANES : (b + 1) * LANES] = found.astype(jnp.bfloat16)
    tables.wait()


def arrange_kernel(half, blocks, pieces, *refs):
    slots = jnp.concatenate([ref[...] for ref in refs[:pieces]], axis=0)
    part_ref, *out_refs = refs[pieces:]
    height = out_refs[0].shape[0]
    own_rows = part_ref.shape[1] - ROWS
    tile_rows = height - 2 * own_rows - blocks * half
    numbers = slots[:, blocks * LANES :].astype(jnp.float32)
    total = numbers.shape[0]
    numbers = jnp.sum(
        jnp.where(iota((total, LANES), 1) == LANES - 1, numbers, 0.0), axis=1, keepdims=True
    ).astype(jnp.int32)
    first = lax.axis_index("chan") % CORES * half
    pick = one_hot(numbers == iota((total, half), 1) + 1 + first)
    found = lax.dot_general(
        pick, slots, (((0,), (0,)), ((), ())), preferred_element_type=jnp.float32
    )
    fill = [found[:, b * LANES : (b + 1) * LANES].astype(jnp.bfloat16) for b in range(blocks)]
    edges = jnp.where(iota((half, LANES), 1) < 3 * EDGE, found[:, blocks * LANES :], 0.0)
    added = [jnp.zeros((ROWS, LANES), jnp.float32) for _ in range(tile_rows // ROWS)]
    for i in range(half // ROWS):
        tile, place = divmod(i + 2, PER_TILE)
        piece = edges[i * ROWS : (i + 1) * ROWS]
        added[tile] += pltpu.roll(piece, 3 * EDGE * place, 1) if place else piece
    me = lax.axis_index("tm")
    for k, out_ref in enumerate(out_refs):
        same = part_ref[me ^ (2 * k)]
        other = part_ref[me ^ (2 * k) ^ 1]
        out_ref[:own_rows] = same[:own_rows]
        out_ref[own_rows : 2 * own_rows] = other[:own_rows]
        for b in range(blocks):
            at = 2 * own_rows + b * half
            out_ref[at : at + half] = fill[b]
        mixed = same[own_rows:].astype(jnp.float32) + pltpu.roll(
            other[own_rows:].astype(jnp.float32), 3 * EDGE, 1
        )
        for tile, extra in enumerate(added):
            at = height - tile_rows + tile * ROWS
            out_ref[at : at + ROWS] = (extra + mixed if tile == 0 else extra).astype(jnp.bfloat16)


def forward_kernel(own_rows, block_ref, out_ref):
    out_ref[...] = block_ref[own_rows:]


def collect_kernel(own_rows, *refs):
    *block_refs, out_ref = refs
    highs = len(block_refs) // 2
    me = lax.axis_index("tm")
    for k in range(highs):
        out_ref[me ^ (2 * k)] = block_refs[k][2 * own_rows :]
        out_ref[me ^ (2 * k) ^ 1] = block_refs[highs + k][own_rows:]


def correlate_kernel(
    seg_count, src_count, dec, head_len, part_rows, count, steps, live_ref, tab_ref, *refs
):
    count_high = steps // 2
    block_refs, passed_refs = refs[:count_high], refs[count_high:steps]
    given_ref, far_ref, out_ref = refs[steps : steps + 3]
    mine_ref, mine_edge, trace, own, other, cross, result, sems = refs[steps + 3 :]
    ch = out_ref.shape[1]
    own_rows = mine_ref.shape[1]
    half = src_count // CORES
    rows = ch + src_count
    per_seg = SEG // dec
    blocks = dec // LANES
    d_cols = 4 * HALF

    @pl.when(pl.program_id(0) == 0)
    def _():
        me = lax.axis_index("tm")
        last = block_refs[0].shape[0] - edge_tiles(2 * ch + half) * ROWS
        for k, ref in enumerate(block_refs):
            mine_ref[me ^ (2 * k)] = ref[:own_rows]
            mine_edge[me ^ (2 * k)] = ref[last : last + ROWS].astype(jnp.float32)
        for k, ref in enumerate(passed_refs):
            mine_ref[me ^ (2 * k) ^ 1] = ref[:own_rows]
            pack = ref[last - own_rows : last - own_rows + ROWS].astype(jnp.float32)
            mine_edge[me ^ (2 * k) ^ 1] = pltpu.roll(pack, LANES - 3 * EDGE, 1)
        live = iota((ch, LANES), 0) < live_ref[0]
        before = jnp.zeros((rows, LANES), jnp.float32)
        is_head = iota((rows, LANES), 1) < head_len
        tile_rows = edge_tiles(2 * ch + half) * ROWS
        low_core = lax.axis_index("chan") % CORES == 0

        def edge_groups(ref, t):
            out = []
            last = ref.shape[1] - tile_rows
            for i in range(2, 2 + half // ROWS):
                tile, place = divmod(i, PER_TILE)
                pack = ref[t, last + tile * ROWS : last + (tile + 1) * ROWS].astype(jnp.float32)
                out.append(pltpu.roll(pack, LANES - 3 * EDGE * place, 1) if place else pack)
            return jnp.concatenate(out, axis=0)

        def in_order(near, far):
            return [jnp.where(low_core, near, far), jnp.where(low_core, far, near)]

        for t in range(steps):
            edge = jnp.where(live, mine_edge[t], 0.0)
            theirs = edge_groups(given_ref, t), edge_groups(far_ref, t)
            edge = jnp.concatenate([edge, *in_order(*theirs)], axis=0)
            for b in range(blocks):
                mine = mine_ref[t, b * ch : (b + 1) * ch]
                mine = jnp.where(live, mine, jnp.zeros_like(mine))
                rows_b = slice(b * half, (b + 1) * half)
                theirs = given_ref[t, rows_b], far_ref[t, rows_b]
                both = jnp.concatenate([mine, *in_order(*theirs)], axis=0)
                if b == 0:
                    tail = pltpu.roll(before, LANES - EDGE, 1) + pltpu.roll(before, LANES - 2 * EDGE, 1)
                    both = both.astype(jnp.float32)
                    both = jnp.where(is_head, both + edge + tail, both).astype(jnp.bfloat16)
                trace[t * rows : (t + 1) * rows, b * LANES : (b + 1) * LANES] = both
            before = edge
        odd = (iota((rows, 2 * LANES), 1) & 1) == 1
        sign = jnp.where(odd, -1.0, 1.0)
        same = one_hot(
            iota((2 * LANES, LANES), 0) % LANES // BAND == iota((2 * LANES, LANES), 1) // BAND
        )
        group_segs = max(1, min(seg_count, part_rows // (per_seg * rows)))
        for first in range(0, seg_count, group_segs):
            segs = min(group_segs, seg_count - first)
            lhs = trace[first * per_seg * rows : (first + segs) * per_seg * rows, :]
            for j in range(CHUNKS):
                acc = jnp.dot(
                    lhs, tab_ref[:, 4 * j * LANES : 4 * (j + 1) * LANES],
                    preferred_element_type=jnp.float32,
                )
                folded = acc[:, : 2 * LANES] + acc[:, 2 * LANES :]
                spec = []
                for g in range(segs):
                    a = folded[g * per_seg * rows : (g * per_seg + 1) * rows]
                    b = folded[(g * per_seg + 1) * rows : (g * per_seg + 2) * rows]
                    spec.append(a + sign * b)
                spec = jnp.concatenate(spec, axis=0)
                re, im = spec[:, :LANES], spec[:, LANES:]
                power = re * re + im * im
                hi = power.astype(jnp.bfloat16)
                lo = (power - hi.astype(jnp.float32)).astype(jnp.bfloat16)
                total = jnp.dot(
                    jnp.concatenate([hi, lo], axis=1), same, preferred_element_type=jnp.float32
                )
                scale = lax.rsqrt(total * (1.0 / BAND) + whiten_eps)
                w_re = (re * scale).astype(jnp.bfloat16).astype(jnp.float32)
                w_im = (im * scale).astype(jnp.bfloat16).astype(jnp.float32)
                at = 2 * j * LANES
                for g in range(segs):
                    r, o = g * rows, (first + g) * ch
                    own[o : o + ch, at : at + LANES] = w_re[r : r + ch]
                    own[o : o + ch, at + LANES : at + 2 * LANES] = w_im[r : r + ch]
                    o = (first + g) * src_count
                    other[o : o + src_count, at : at + LANES] = w_re[r + ch : r + rows]
                    other[o : o + src_count, at + LANES : at + 2 * LANES] = w_im[r + ch : r + rows]

    block = cross.shape[1] // ch
    copies = []
    for i in range(count):
        start = pl.multiple_of((pl.program_id(0) * count + i) * block, 8)
        for j in range(CHUNKS):
            at = 2 * j * LANES
            a_re = [own[g * ch : (g + 1) * ch, at : at + LANES] for g in range(seg_count)]
            a_im = [own[g * ch : (g + 1) * ch, at + LANES : at + 2 * LANES] for g in range(seg_count)]
            for s in range(block):
                if s % 8 == 0:
                    tiles = [
                        other[
                            pl.ds(pl.multiple_of(g * src_count + start + s, 8), 8),
                            at : at + 2 * LANES,
                        ]
                        for g in range(seg_count)
                    ]
                re = im = None
                for g in range(seg_count):
                    b_re = tiles[g][s % 8 : s % 8 + 1, :LANES]
                    b_im = tiles[g][s % 8 : s % 8 + 1, LANES:]
                    p = a_re[g] * b_re + a_im[g] * b_im
                    q = a_im[g] * b_re - a_re[g] * b_im
                    re, im = (p, q) if re is None else (re + p, im + q)
                row = slice(s * ch, (s + 1) * ch)
                cross[i, row, at : at + LANES] = re.astype(jnp.bfloat16)
                cross[i, row, at + LANES : at + 2 * LANES] = im.astype(jnp.bfloat16)
        lags = sum(
            jnp.dot(
                cross[i, :, h * dec : (h + 1) * dec],
                tab_ref[:, d_cols + 2 * LAGH * h : d_cols + 2 * LAGH * (h + 1)],
                preferred_element_type=jnp.float32,
            )
            for h in range(per_seg)
        )
        result[i] = lags.reshape(result.shape[1:])
        copy = pltpu.make_async_copy(result.at[i], out_ref.at[pl.ds(start, block)], sems.at[i])
        copy.start()
        copies.append(copy)
    for copy in copies:
        copy.wait()


def whole(space=pltpu.VMEM):
    return pl.BlockSpec(memory_space=space)


def local(raw_strain, fir_taps, source_channels, live_counts):
    rows, raw_len = raw_strain.shape
    steps = lax.axis_size("tm")
    chan_count = lax.axis_size("chan")
    dec = raw_len // DECIM
    blocks = dec // LANES
    ch = rows // steps
    seg_count = steps * dec // SEG
    src_count = source_channels.shape[0]
    slots = 2 * SRC_DEV * steps
    span = raw_len // blocks
    total_rows = ch + src_count
    half = src_count // CORES
    highs = steps // 2
    own_rows = blocks * ch
    given_rows = blocks * half + edge_tiles(2 * ch + half) * ROWS
    height = 2 * own_rows + given_rows
    head_len = -(-(fir_taps.shape[0] - 1) // DECIM)
    assert head_len < EDGE and ch == ROWS and src_count <= 256
    assert steps & (steps - 1) == 0 and chan_count & (chan_count - 1) == 0 and half % ROWS == 0
    src = source_channels.reshape(1, src_count)
    taps = fir_taps.reshape(1, fir_taps.shape[0])
    table = np.concatenate([dft_table(dec), *lag_table(seg_count).reshape(SEG // dec, dec, -1)], axis=1)
    inputs = (src, taps, raw_strain, jnp.asarray(table))
    part, picked, table = pl.pallas_call(
        functools.partial(filter_kernel, blocks),
        out_shape=[
            pltpu.VMEM((steps, (blocks + 1) * ch, LANES), jnp.bfloat16),
            pltpu.VMEM((slots, dec + LANES), jnp.bfloat16),
            pltpu.VMEM(table.shape, jnp.bfloat16),
        ],
        in_specs=[whole(pl.ANY)] * 4,
        out_specs=[whole(), whole(), whole(pl.ANY)],
        scratch_shapes=[
            pltpu.VMEM((blocks * rows, span + LANES), jnp.bfloat16),
            pltpu.VMEM((2 * LANES, span + LANES), jnp.bfloat16),
            pltpu.VMEM(src.shape, src.dtype),
            pltpu.VMEM(taps.shape, taps.dtype),
            pltpu.SemaphoreType.DMA((blocks + 3,)),
        ],
        compiler_params=pltpu.CompilerParams(vmem_limit_bytes=16 * MIB),
        name="fir",
    )(*(pltpu.with_memory_space_constraint(a, pltpu.HBM) for a in inputs))
    pieces = [picked] + [
        lax.ppermute(picked, "chan", [(c, c ^ k) for c in range(chan_count)])
        for k in range(chan_count - 1, 0, -1)
    ]
    to_vmem = functools.partial(pltpu.with_memory_space_constraint, memory_space=pltpu.VMEM)
    outgoing = pl.pallas_call(
        functools.partial(arrange_kernel, half, blocks, chan_count),
        out_shape=[pltpu.VMEM((height, LANES), jnp.bfloat16)] * highs,
        in_specs=[whole()] * (chan_count + 1),
        out_specs=[whole()] * highs,
        compiler_params=pltpu.CompilerParams(vmem_limit_bytes=8 * MIB),
        name="arrange",
    )(*(to_vmem(a) for a in (*pieces, part)))
    arrived = [
        lax.ppermute(outgoing[k], "tm", [(t, t ^ (2 * k)) for t in range(steps)])
        for k in range(highs - 1, 0, -1)
    ]
    arrived = [to_vmem(a) for a in (outgoing[0], *arrived[::-1])]
    small = pltpu.CompilerParams(vmem_limit_bytes=8 * MIB)
    passed = [None] * highs
    for k in [0, *range(highs - 1, 0, -1)]:
        forward = pl.pallas_call(
            functools.partial(forward_kernel, own_rows),
            out_shape=pltpu.VMEM((own_rows + given_rows, LANES), jnp.bfloat16),
            in_specs=[whole()],
            out_specs=whole(),
            compiler_params=small,
            name="forward",
        )(arrived[k])
        passed[k] = to_vmem(lax.ppermute(forward, "tm", [(t, t ^ 1) for t in range(steps)]))
    given = pl.pallas_call(
        functools.partial(collect_kernel, own_rows),
        out_shape=pltpu.VMEM((steps, given_rows, LANES), jnp.bfloat16),
        in_specs=[whole()] * steps,
        out_specs=whole(),
        compiler_params=small,
        name="collect",
    )(*arrived, *passed)
    swapped = lax.ppermute(given, "chan", [(c, c ^ 1) for c in range(chan_count)])
    block = math.gcd(src_count, 16)
    count = math.gcd(src_count // block, 2)
    state = seg_count * total_rows * SEG * 4
    return pl.pallas_call(
        functools.partial(
            correlate_kernel, seg_count, src_count, dec, head_len, 1024, count, steps
        ),
        grid=(src_count // (block * count),),
        out_shape=jax.ShapeDtypeStruct((src_count, ch, 2 * LAGH), jnp.float32),
        in_specs=[whole(pltpu.SMEM)] + [whole()] * (steps + 3),
        out_specs=whole(pl.ANY),
        scratch_shapes=[
            pltpu.VMEM((steps, own_rows, LANES), jnp.bfloat16),
            pltpu.VMEM((steps, ROWS, LANES), jnp.float32),
            pltpu.VMEM((steps * total_rows, dec), jnp.bfloat16),
            pltpu.VMEM((seg_count * ch, SEG), jnp.float32),
            pltpu.VMEM((seg_count * src_count, SEG), jnp.float32),
            pltpu.VMEM((count, block * ch, SEG), jnp.bfloat16),
            pltpu.VMEM((count, block, ch, 2 * LAGH), jnp.float32),
            pltpu.SemaphoreType.DMA((count,)),
        ],
        compiler_params=pltpu.CompilerParams(vmem_limit_bytes=16 * MIB + 2 * state),
        name="correlate",
    )(live_counts, table, *arrived, *passed, to_vmem(given), to_vmem(swapped))


def solution(mesh):
    placed = (P("chan", "tm"), P(), P(), P(("chan", "tm")))
    return jax.shard_map(
        local, mesh=mesh, in_specs=placed, out_specs=P(None, ("chan", "tm"), None), check_vma=False
    )
```

```python
import functools
import math

import jax
import jax.numpy as jnp
import ml_dtypes
import numpy as np
from jax import lax
from jax.experimental import pallas as pl
from jax.experimental.pallas import tpu as pltpu
from jax.sharding import PartitionSpec as P

DECIM = 10
SEG = 1024
BAND = 64
LAGH = 192
SRC_DEV = 1
LANES = 128
HALF = SEG // 2
CHUNKS = HALF // LANES
EDGE = 14
PER_TILE = LANES // (3 * EDGE)
ROWS = 16
CORES = 2
MIB = 1024 * 1024

whiten_eps = 1e-06

NT = (((1,), (1,)), ((), ()))


def split_table(table):
    hi = table.astype(ml_dtypes.bfloat16)
    lo = (table - hi.astype(np.float64)).astype(ml_dtypes.bfloat16)
    return hi, lo


def dft_table(rows):
    phase = (np.arange(rows)[:, None] * np.arange(HALF)[None, :] % SEG) * (2.0 * np.pi / SEG)
    parts = []
    for j in range(CHUNKS):
        cut = slice(j * LANES, (j + 1) * LANES)
        hi, lo = split_table(np.concatenate([np.cos(phase[:, cut]), -np.sin(phase[:, cut])], 1))
        parts += [hi, lo]
    return np.concatenate(parts, axis=1)


def lag_table(seg_count):
    freq = np.arange(HALF)[:, None]
    phase = (freq * np.arange(-LAGH, LAGH)[None, :] % SEG) * (2.0 * np.pi / SEG)
    weight = np.where(freq == 0, 1.0, 2.0) * (math.sqrt(SEG / seg_count) / SEG)
    re = (weight * np.cos(phase)).reshape(CHUNKS, LANES, 2 * LAGH)
    im = (-weight * np.sin(phase)).reshape(CHUNKS, LANES, 2 * LAGH)
    return np.concatenate([re, im], axis=1).reshape(SEG, 2 * LAGH).astype(ml_dtypes.bfloat16)


def iota(shape, dim):
    return lax.broadcasted_iota(jnp.int32, shape, dim)


def one_hot(mask):
    return jnp.where(mask, 1.0, 0.0).astype(jnp.bfloat16)


def column(row):
    n = row.shape[1]
    return jnp.sum(jnp.where(iota((n, n), 0) == iota((n, n), 1), row, 0), axis=1, keepdims=True)


def tap_rows(taps):
    tap_count = taps.shape[1]
    width = 3 * LANES
    flip = one_hot(iota((tap_count, width), 0) + iota((tap_count, width), 1) == tap_count)
    hi = taps.astype(jnp.bfloat16)
    lo = (taps - hi.astype(jnp.float32)).astype(jnp.bfloat16)
    out = []
    for part in (hi, lo):
        base = jnp.dot(
            jnp.broadcast_to(part.astype(jnp.float32), (8, tap_count)).astype(jnp.bfloat16),
            flip,
            preferred_element_type=jnp.float32,
        )
        upper = pltpu.roll(base, 0, 1, stride=DECIM, stride_axis=0)
        out.append(jnp.concatenate([upper, pltpu.roll(upper, 8 * DECIM, 1)], axis=0))
    return out


def edge_tiles(count):
    return -(-count // (PER_TILE * ROWS))


def filter_kernel(
    blocks,
    src_hbm, taps_hbm, raw_ref, tab_hbm,
    out_ref, slot_ref, tab_ref,
    ext, weight, src_ref, taps_ref, sems,
):
    rows, raw_len = raw_ref.shape
    steps = out_ref.shape[0]
    ch = rows // steps
    span = raw_len // blocks
    wide = span + LANES
    copies = []
    for b in range(blocks):
        if b == 0:
            copy = pltpu.make_async_copy(
                raw_ref.at[:, pl.ds(0, span)],
                ext.at[pl.ds(0, rows), pl.ds(LANES, span)],
                sems.at[b],
            )
        else:
            copy = pltpu.make_async_copy(
                raw_ref.at[:, pl.ds(b * span - LANES, wide)],
                ext.at[pl.ds(b * rows, rows), :],
                sems.at[b],
            )
        copy.start()
        copies.append(copy)
    small = [
        pltpu.make_async_copy(taps_hbm, taps_ref, sems.at[blocks]),
        pltpu.make_async_copy(src_hbm, src_ref, sems.at[blocks + 1]),
    ]
    tables = pltpu.make_async_copy(tab_hbm, tab_ref, sems.at[blocks + 2])
    for copy in [*small, tables]:
        copy.start()
    ext[:rows, :LANES] = jnp.zeros((rows, LANES), ext.dtype)
    weight[...] = jnp.zeros_like(weight)
    for copy in small:
        copy.wait()
    for p, base in enumerate(tap_rows(taps_ref[...])):
        for i in range(LANES // 16):
            tile, lane = divmod(16 * DECIM * i, LANES)
            piece = pltpu.roll(base, lane, 1) if lane else base
            weight[p * LANES + 16 * i : p * LANES + 16 * (i + 1), tile * LANES : (tile + 3) * LANES] = (
                piece.astype(jnp.bfloat16)
            )
    src = src_ref[...]
    src_count = src.shape[1]
    slots = slot_ref.shape[0]
    group = src // rows
    group_col = column(group)
    src_col = column(src)
    rank = jnp.sum(
        jnp.where(
            (group_col == group)
            & (iota((src_count, src_count), 0) < iota((src_count, src_count), 1)),
            1,
            0,
        ),
        axis=0,
        keepdims=True,
    )
    mine = lax.axis_index("chan")
    to_slot = one_hot((iota((slots, src_count), 0) == rank) & (group == mine))
    to_row = one_hot(src_col - mine * rows == iota((src_count, rows), 1))
    pick = jnp.dot(to_slot, to_row, preferred_element_type=jnp.float32).astype(jnp.bfloat16)
    number = jnp.where(
        iota((src_count, LANES), 1) == LANES - 1, iota((src_count, LANES), 0) + 1, 0
    ).astype(jnp.float32).astype(jnp.bfloat16)
    number = jnp.dot(to_slot, number, preferred_element_type=jnp.float32)
    for copy in copies:
        copy.wait()
    acc = lax.dot_general(ext[...], weight[...], NT, preferred_element_type=jnp.float32)
    acc = acc[:, :LANES] + acc[:, LANES:]
    y = acc.astype(jnp.bfloat16)
    head = acc[:rows]
    head_lo = head - head.astype(jnp.bfloat16).astype(jnp.float32)
    tail = lax.dot_general(
        ext[(blocks - 1) * rows :, wide - LANES :], weight[:, :LANES], NT,
        preferred_element_type=jnp.float32,
    )
    tail = tail[:, :LANES] + tail[:, LANES:]
    tail_hi = tail.astype(jnp.bfloat16).astype(jnp.float32)
    lane = iota((rows, LANES), 1)
    edge = jnp.where(
        lane < EDGE,
        head_lo,
        jnp.where(
            lane < 2 * EDGE,
            pltpu.roll(tail_hi, EDGE, 1),
            jnp.where(lane < 3 * EDGE, pltpu.roll(tail - tail_hi, 2 * EDGE, 1), 0.0),
        ),
    ).astype(jnp.bfloat16)
    parts = [y[b * rows : (b + 1) * rows] for b in range(blocks)] + [edge]
    last = blocks * ch
    for t in range(steps):
        for b in range(blocks):
            out_ref[t, b * ch : (b + 1) * ch] = parts[b][t * ch : (t + 1) * ch]
        out_ref[t, last : last + ch] = edge[t * ch : (t + 1) * ch]
    for b, part in enumerate(parts):
        found = jnp.dot(pick, part, preferred_element_type=jnp.float32)
        if b == blocks:
            found += number
        slot_ref[:, b * LANES : (b + 1) * LANES] = found.astype(jnp.bfloat16)
    tables.wait()


def arrange_kernel(half, blocks, pieces, *refs):
    slots = jnp.concatenate([ref[...] for ref in refs[:pieces]], axis=0)
    part_ref, *out_refs = refs[pieces:]
    height = out_refs[0].shape[0]
    own_rows = part_ref.shape[1] - ROWS
    tile_rows = height - 2 * own_rows - blocks * half
    numbers = slots[:, blocks * LANES :].astype(jnp.float32)
    total = numbers.shape[0]
    numbers = jnp.sum(
        jnp.where(iota((total, LANES), 1) == LANES - 1, numbers, 0.0), axis=1, keepdims=True
    ).astype(jnp.int32)
    first = lax.axis_index("chan") % CORES * half
    pick = one_hot(numbers == iota((total, half), 1) + 1 + first)
    found = lax.dot_general(
        pick, slots, (((0,), (0,)), ((), ())), preferred_element_type=jnp.float32
    )
    fill = [found[:, b * LANES : (b + 1) * LANES].astype(jnp.bfloat16) for b in range(blocks)]
    edges = jnp.where(iota((half, LANES), 1) < 3 * EDGE, found[:, blocks * LANES :], 0.0)
    added = [jnp.zeros((ROWS, LANES), jnp.float32) for _ in range(tile_rows // ROWS)]
    for i in range(half // ROWS):
        tile, place = divmod(i + 2, PER_TILE)
        piece = edges[i * ROWS : (i + 1) * ROWS]
        added[tile] += pltpu.roll(piece, 3 * EDGE * place, 1) if place else piece
    me = lax.axis_index("tm")
    for k, out_ref in enumerate(out_refs):
        same = part_ref[me ^ (2 * k)]
        other = part_ref[me ^ (2 * k) ^ 1]
        out_ref[:own_rows] = same[:own_rows]
        out_ref[own_rows : 2 * own_rows] = other[:own_rows]
        for b in range(blocks):
            at = 2 * own_rows + b * half
            out_ref[at : at + half] = fill[b]
        mixed = same[own_rows:].astype(jnp.float32) + pltpu.roll(
            other[own_rows:].astype(jnp.float32), 3 * EDGE, 1
        )
        for tile, extra in enumerate(added):
            at = height - tile_rows + tile * ROWS
            out_ref[at : at + ROWS] = (extra + mixed if tile == 0 else extra).astype(jnp.bfloat16)


def forward_kernel(own_rows, block_ref, out_ref):
    out_ref[...] = block_ref[own_rows:]


def forward_live_kernel(own_rows, live_ref, block_ref, out_ref, spread_ref):
    out_ref[...] = block_ref[own_rows:]
    spread_ref[...] = jnp.full(spread_ref.shape, live_ref[0], jnp.int32)


def collect_kernel(own_rows, *refs):
    *block_refs, out_ref = refs
    highs = len(block_refs) // 2
    me = lax.axis_index("tm")
    for k in range(highs):
        out_ref[me ^ (2 * k)] = block_refs[k][2 * own_rows :]
        out_ref[me ^ (2 * k) ^ 1] = block_refs[highs + k][own_rows:]


def correlate_kernel(
    seg_count, src_count, dec, head_len, part_rows, count, steps, live_ref, tab_ref, *refs
):
    count_high = steps // 2
    block_refs, passed_refs = refs[:count_high], refs[count_high:steps]
    given_ref, far_ref, out_ref = refs[steps : steps + 3]
    mine_ref, mine_edge, trace, own, other, cross, result, sems = refs[steps + 3 :]
    ch = out_ref.shape[1]
    own_rows = mine_ref.shape[1]
    half = src_count // CORES
    rows = ch + src_count
    per_seg = SEG // dec
    blocks = dec // LANES
    d_cols = 4 * HALF

    @pl.when(pl.program_id(0) == 0)
    def _():
        me = lax.axis_index("tm")
        last = block_refs[0].shape[0] - edge_tiles(2 * ch + half) * ROWS
        for k, ref in enumerate(block_refs):
            mine_ref[me ^ (2 * k)] = ref[:own_rows]
            mine_edge[me ^ (2 * k)] = ref[last : last + ROWS].astype(jnp.float32)
        for k, ref in enumerate(passed_refs):
            mine_ref[me ^ (2 * k) ^ 1] = ref[:own_rows]
            pack = ref[last - own_rows : last - own_rows + ROWS].astype(jnp.float32)
            mine_edge[me ^ (2 * k) ^ 1] = pltpu.roll(pack, LANES - 3 * EDGE, 1)
        live = iota((ch, LANES), 0) < live_ref[...]
        before = jnp.zeros((rows, LANES), jnp.float32)
        is_head = iota((rows, LANES), 1) < head_len
        tile_rows = edge_tiles(2 * ch + half) * ROWS
        low_core = lax.axis_index("chan") % CORES == 0

        def edge_groups(ref, t):
            out = []
            last = ref.shape[1] - tile_rows
            for i in range(2, 2 + half // ROWS):
                tile, place = divmod(i, PER_TILE)
                pack = ref[t, last + tile * ROWS : last + (tile + 1) * ROWS].astype(jnp.float32)
                out.append(pltpu.roll(pack, LANES - 3 * EDGE * place, 1) if place else pack)
            return jnp.concatenate(out, axis=0)

        def in_order(near, far):
            return [jnp.where(low_core, near, far), jnp.where(low_core, far, near)]

        for t in range(steps):
            edge = jnp.where(live, mine_edge[t], 0.0)
            theirs = edge_groups(given_ref, t), edge_groups(far_ref, t)
            edge = jnp.concatenate([edge, *in_order(*theirs)], axis=0)
            for b in range(blocks):
                mine = mine_ref[t, b * ch : (b + 1) * ch]
                mine = jnp.where(live, mine, jnp.zeros_like(mine))
                rows_b = slice(b * half, (b + 1) * half)
                theirs = given_ref[t, rows_b], far_ref[t, rows_b]
                both = jnp.concatenate([mine, *in_order(*theirs)], axis=0)
                if b == 0:
                    tail = pltpu.roll(before, LANES - EDGE, 1) + pltpu.roll(before, LANES - 2 * EDGE, 1)
                    both = both.astype(jnp.float32)
                    both = jnp.where(is_head, both + edge + tail, both).astype(jnp.bfloat16)
                trace[t * rows : (t + 1) * rows, b * LANES : (b + 1) * LANES] = both
            before = edge
        odd = (iota((rows, 2 * LANES), 1) & 1) == 1
        sign = jnp.where(odd, -1.0, 1.0)
        same = one_hot(
            iota((2 * LANES, LANES), 0) % LANES // BAND == iota((2 * LANES, LANES), 1) // BAND
        )
        group_segs = max(1, min(seg_count, part_rows // (per_seg * rows)))
        for first in range(0, seg_count, group_segs):
            segs = min(group_segs, seg_count - first)
            lhs = trace[first * per_seg * rows : (first + segs) * per_seg * rows, :]
            for j in range(CHUNKS):
                acc = jnp.dot(
                    lhs, tab_ref[:, 4 * j * LANES : 4 * (j + 1) * LANES],
                    preferred_element_type=jnp.float32,
                )
                folded = acc[:, : 2 * LANES] + acc[:, 2 * LANES :]
                spec = []
                for g in range(segs):
                    a = folded[g * per_seg * rows : (g * per_seg + 1) * rows]
                    b = folded[(g * per_seg + 1) * rows : (g * per_seg + 2) * rows]
                    spec.append(a + sign * b)
                spec = jnp.concatenate(spec, axis=0)
                re, im = spec[:, :LANES], spec[:, LANES:]
                power = re * re + im * im
                hi = power.astype(jnp.bfloat16)
                lo = (power - hi.astype(jnp.float32)).astype(jnp.bfloat16)
                total = jnp.dot(
                    jnp.concatenate([hi, lo], axis=1), same, preferred_element_type=jnp.float32
                )
                scale = lax.rsqrt(total * (1.0 / BAND) + whiten_eps)
                w_re = (re * scale).astype(jnp.bfloat16).astype(jnp.float32)
                w_im = (im * scale).astype(jnp.bfloat16).astype(jnp.float32)
                at = 2 * j * LANES
                for g in range(segs):
                    r, o = g * rows, (first + g) * ch
                    own[o : o + ch, at : at + LANES] = w_re[r : r + ch]
                    own[o : o + ch, at + LANES : at + 2 * LANES] = w_im[r : r + ch]
                    o = (first + g) * src_count
                    other[o : o + src_count, at : at + LANES] = w_re[r + ch : r + rows]
                    other[o : o + src_count, at + LANES : at + 2 * LANES] = w_im[r + ch : r + rows]

    block = cross.shape[1] // ch
    copies = []
    for i in range(count):
        start = pl.multiple_of((pl.program_id(0) * count + i) * block, 8)
        for j in range(CHUNKS):
            at = 2 * j * LANES
            a_re = [own[g * ch : (g + 1) * ch, at : at + LANES] for g in range(seg_count)]
            a_im = [own[g * ch : (g + 1) * ch, at + LANES : at + 2 * LANES] for g in range(seg_count)]
            for s in range(block):
                if s % 8 == 0:
                    tiles = [
                        other[
                            pl.ds(pl.multiple_of(g * src_count + start + s, 8), 8),
                            at : at + 2 * LANES,
                        ]
                        for g in range(seg_count)
                    ]
                re = im = None
                for g in range(seg_count):
                    b_re = tiles[g][s % 8 : s % 8 + 1, :LANES]
                    b_im = tiles[g][s % 8 : s % 8 + 1, LANES:]
                    p = a_re[g] * b_re + a_im[g] * b_im
                    q = a_im[g] * b_re - a_re[g] * b_im
                    re, im = (p, q) if re is None else (re + p, im + q)
                row = slice(s * ch, (s + 1) * ch)
                cross[i, row, at : at + LANES] = re.astype(jnp.bfloat16)
                cross[i, row, at + LANES : at + 2 * LANES] = im.astype(jnp.bfloat16)
        lags = sum(
            jnp.dot(
                cross[i, :, h * dec : (h + 1) * dec],
                tab_ref[:, d_cols + 2 * LAGH * h : d_cols + 2 * LAGH * (h + 1)],
                preferred_element_type=jnp.float32,
            )
            for h in range(per_seg)
        )
        result[i] = lags.reshape(result.shape[1:])
        copy = pltpu.make_async_copy(result.at[i], out_ref.at[pl.ds(start, block)], sems.at[i])
        copy.start()
        copies.append(copy)
    for copy in copies:
        copy.wait()


def whole(space=pltpu.VMEM):
    return pl.BlockSpec(memory_space=space)


def local(raw_strain, fir_taps, source_channels, live_counts):
    rows, raw_len = raw_strain.shape
    steps = lax.axis_size("tm")
    chan_count = lax.axis_size("chan")
    dec = raw_len // DECIM
    blocks = dec // LANES
    ch = rows // steps
    seg_count = steps * dec // SEG
    src_count = source_channels.shape[0]
    slots = 2 * SRC_DEV * steps
    span = raw_len // blocks
    total_rows = ch + src_count
    half = src_count // CORES
    highs = steps // 2
    own_rows = blocks * ch
    given_rows = blocks * half + edge_tiles(2 * ch + half) * ROWS
    height = 2 * own_rows + given_rows
    head_len = -(-(fir_taps.shape[0] - 1) // DECIM)
    assert head_len < EDGE and ch == ROWS and src_count <= 256
    assert steps & (steps - 1) == 0 and chan_count & (chan_count - 1) == 0 and half % ROWS == 0
    src = source_channels.reshape(1, src_count)
    taps = fir_taps.reshape(1, fir_taps.shape[0])
    table = np.concatenate([dft_table(dec), *lag_table(seg_count).reshape(SEG // dec, dec, -1)], axis=1)
    inputs = (src, taps, raw_strain, jnp.asarray(table))
    part, picked, table = pl.pallas_call(
        functools.partial(filter_kernel, blocks),
        out_shape=[
            pltpu.VMEM((steps, (blocks + 1) * ch, LANES), jnp.bfloat16),
            pltpu.VMEM((slots, dec + LANES), jnp.bfloat16),
            pltpu.VMEM(table.shape, jnp.bfloat16),
        ],
        in_specs=[whole(pl.ANY)] * 4,
        out_specs=[whole(), whole(), whole(pl.ANY)],
        scratch_shapes=[
            pltpu.VMEM((blocks * rows, span + LANES), jnp.bfloat16),
            pltpu.VMEM((2 * LANES, span + LANES), jnp.bfloat16),
            pltpu.VMEM(src.shape, src.dtype),
            pltpu.VMEM(taps.shape, taps.dtype),
            pltpu.SemaphoreType.DMA((blocks + 3,)),
        ],
        compiler_params=pltpu.CompilerParams(vmem_limit_bytes=16 * MIB),
        name="fir",
    )(*(pltpu.with_memory_space_constraint(a, pltpu.HBM) for a in inputs))
    pieces = [picked] + [
        lax.ppermute(picked, "chan", [(c, c ^ k) for c in range(chan_count)])
        for k in range(1, chan_count)
    ]
    to_vmem = functools.partial(pltpu.with_memory_space_constraint, memory_space=pltpu.VMEM)
    outgoing = pl.pallas_call(
        functools.partial(arrange_kernel, half, blocks, chan_count),
        out_shape=[pltpu.VMEM((height, LANES), jnp.bfloat16)] * highs,
        in_specs=[whole()] * (chan_count + 1),
        out_specs=[whole()] * highs,
        compiler_params=pltpu.CompilerParams(vmem_limit_bytes=8 * MIB),
        name="arrange",
    )(*(to_vmem(a) for a in (*pieces, part)))
    arrived = [
        lax.ppermute(outgoing[k], "tm", [(t, t ^ (2 * k)) for t in range(steps)])
        for k in range(highs - 1, 0, -1)
    ]
    arrived = [to_vmem(a) for a in (outgoing[0], *arrived[::-1])]
    small = pltpu.CompilerParams(vmem_limit_bytes=8 * MIB)
    passed = [None] * highs
    cut = pltpu.VMEM((own_rows + given_rows, LANES), jnp.bfloat16)
    for k in [0, *range(highs - 1, 0, -1)]:
        if k == highs - 1:
            forward, live = pl.pallas_call(
                functools.partial(forward_live_kernel, own_rows),
                out_shape=[cut, pltpu.VMEM((ch, LANES), jnp.int32)],
                in_specs=[whole(pltpu.SMEM), whole()],
                out_specs=[whole(), whole()],
                compiler_params=small,
                name="forward_live",
            )(live_counts, arrived[k])
        else:
            forward = pl.pallas_call(
                functools.partial(forward_kernel, own_rows),
                out_shape=cut,
                in_specs=[whole()],
                out_specs=whole(),
                compiler_params=small,
                name="forward",
            )(arrived[k])
        passed[k] = to_vmem(lax.ppermute(forward, "tm", [(t, t ^ 1) for t in range(steps)]))
    given = pl.pallas_call(
        functools.partial(collect_kernel, own_rows),
        out_shape=pltpu.VMEM((steps, given_rows, LANES), jnp.bfloat16),
        in_specs=[whole()] * steps,
        out_specs=whole(),
        compiler_params=small,
        name="collect",
    )(*arrived, *passed)
    swapped = lax.ppermute(given, "chan", [(c, c ^ 1) for c in range(chan_count)])
    block = math.gcd(src_count, 16)
    count = math.gcd(src_count // block, 2)
    state = seg_count * total_rows * SEG * 4
    return pl.pallas_call(
        functools.partial(
            correlate_kernel, seg_count, src_count, dec, head_len, 1024, count, steps
        ),
        grid=(src_count // (block * count),),
        out_shape=jax.ShapeDtypeStruct((src_count, ch, 2 * LAGH), jnp.float32),
        in_specs=[whole()] * (steps + 4),
        out_specs=whole(pl.ANY),
        scratch_shapes=[
            pltpu.VMEM((steps, own_rows, LANES), jnp.bfloat16),
            pltpu.VMEM((steps, ROWS, LANES), jnp.float32),
            pltpu.VMEM((steps * total_rows, dec), jnp.bfloat16),
            pltpu.VMEM((seg_count * ch, SEG), jnp.float32),
            pltpu.VMEM((seg_count * src_count, SEG), jnp.float32),
            pltpu.VMEM((count, block * ch, SEG), jnp.bfloat16),
            pltpu.VMEM((count, block, ch, 2 * LAGH), jnp.float32),
            pltpu.SemaphoreType.DMA((count,)),
        ],
        compiler_params=pltpu.CompilerParams(vmem_limit_bytes=16 * MIB + 2 * state),
        name="correlate",
    )(live, table, *arrived, *passed, to_vmem(given), to_vmem(swapped))


def solution(mesh):
    placed = (P("chan", "tm"), P(), P(), P(("chan", "tm")))
    return jax.shard_map(
        local, mesh=mesh, in_specs=placed, out_specs=P(None, ("chan", "tm"), None), check_vma=False
    )
```

```python
import functools
import math

import jax
import jax.numpy as jnp
import ml_dtypes
import numpy as np
from jax import lax
from jax.experimental import pallas as pl
from jax.experimental.pallas import tpu as pltpu
from jax.sharding import PartitionSpec as P

DECIM = 10
SEG = 1024
BAND = 64
LAGH = 192
SRC_DEV = 1
LANES = 128
HALF = SEG // 2
CHUNKS = HALF // LANES
EDGE = 14
PER_TILE = LANES // (3 * EDGE)
ROWS = 16
CORES = 2
MIB = 1024 * 1024

whiten_eps = 1e-06

NT = (((1,), (1,)), ((), ()))


def split_table(table):
    hi = table.astype(ml_dtypes.bfloat16)
    lo = (table - hi.astype(np.float64)).astype(ml_dtypes.bfloat16)
    return hi, lo


def dft_table(rows):
    phase = (np.arange(rows)[:, None] * np.arange(HALF)[None, :] % SEG) * (2.0 * np.pi / SEG)
    parts = []
    for j in range(CHUNKS):
        cut = slice(j * LANES, (j + 1) * LANES)
        hi, lo = split_table(np.concatenate([np.cos(phase[:, cut]), -np.sin(phase[:, cut])], 1))
        parts += [hi, lo]
    return np.concatenate(parts, axis=1)


def lag_table(seg_count):
    freq = np.arange(HALF)[:, None]
    phase = (freq * np.arange(-LAGH, LAGH)[None, :] % SEG) * (2.0 * np.pi / SEG)
    weight = np.where(freq == 0, 1.0, 2.0) * (math.sqrt(SEG / seg_count) / SEG)
    re = (weight * np.cos(phase)).reshape(CHUNKS, LANES, 2 * LAGH)
    im = (-weight * np.sin(phase)).reshape(CHUNKS, LANES, 2 * LAGH)
    return np.concatenate([re, im], axis=1).reshape(SEG, 2 * LAGH).astype(ml_dtypes.bfloat16)


def iota(shape, dim):
    return lax.broadcasted_iota(jnp.int32, shape, dim)


def one_hot(mask):
    return jnp.where(mask, 1.0, 0.0).astype(jnp.bfloat16)


def column(row):
    n = row.shape[1]
    return jnp.sum(jnp.where(iota((n, n), 0) == iota((n, n), 1), row, 0), axis=1, keepdims=True)


def tap_rows(taps):
    tap_count = taps.shape[1]
    width = 3 * LANES
    flip = one_hot(iota((tap_count, width), 0) + iota((tap_count, width), 1) == tap_count)
    hi = taps.astype(jnp.bfloat16)
    lo = (taps - hi.astype(jnp.float32)).astype(jnp.bfloat16)
    out = []
    for part in (hi, lo):
        base = jnp.dot(
            jnp.broadcast_to(part.astype(jnp.float32), (8, tap_count)).astype(jnp.bfloat16),
            flip,
            preferred_element_type=jnp.float32,
        )
        upper = pltpu.roll(base, 0, 1, stride=DECIM, stride_axis=0)
        out.append(jnp.concatenate([upper, pltpu.roll(upper, 8 * DECIM, 1)], axis=0))
    return out


def edge_tiles(count):
    return -(-count // (PER_TILE * ROWS))


def filter_kernel(
    blocks,
    src_hbm, taps_hbm, raw_ref, tab_hbm,
    out_ref, slot_ref, tab_ref,
    ext, weight, src_ref, taps_ref, sems,
):
    rows, raw_len = raw_ref.shape
    steps = out_ref.shape[0]
    ch = rows // steps
    span = raw_len // blocks
    wide = span + LANES
    copies = []
    for b in range(blocks):
        if b == 0:
            copy = pltpu.make_async_copy(
                raw_ref.at[:, pl.ds(0, span)],
                ext.at[pl.ds(0, rows), pl.ds(LANES, span)],
                sems.at[b],
            )
        else:
            copy = pltpu.make_async_copy(
                raw_ref.at[:, pl.ds(b * span - LANES, wide)],
                ext.at[pl.ds(b * rows, rows), :],
                sems.at[b],
            )
        copy.start()
        copies.append(copy)
    small = [
        pltpu.make_async_copy(taps_hbm, taps_ref, sems.at[blocks]),
        pltpu.make_async_copy(src_hbm, src_ref, sems.at[blocks + 1]),
    ]
    tables = pltpu.make_async_copy(tab_hbm, tab_ref, sems.at[blocks + 2])
    for copy in [*small, tables]:
        copy.start()
    ext[:rows, :LANES] = jnp.zeros((rows, LANES), ext.dtype)
    weight[...] = jnp.zeros_like(weight)
    for copy in small:
        copy.wait()
    for p, base in enumerate(tap_rows(taps_ref[...])):
        for i in range(LANES // 16):
            tile, lane = divmod(16 * DECIM * i, LANES)
            piece = pltpu.roll(base, lane, 1) if lane else base
            weight[p * LANES + 16 * i : p * LANES + 16 * (i + 1), tile * LANES : (tile + 3) * LANES] = (
                piece.astype(jnp.bfloat16)
            )
    src = src_ref[...]
    src_count = src.shape[1]
    slots = slot_ref.shape[0]
    group = src // rows
    group_col = column(group)
    src_col = column(src)
    rank = jnp.sum(
        jnp.where(
            (group_col == group)
            & (iota((src_count, src_count), 0) < iota((src_count, src_count), 1)),
            1,
            0,
        ),
        axis=0,
        keepdims=True,
    )
    mine = lax.axis_index("chan")
    to_slot = one_hot((iota((slots, src_count), 0) == rank) & (group == mine))
    to_row = one_hot(src_col - mine * rows == iota((src_count, rows), 1))
    pick = jnp.dot(to_slot, to_row, preferred_element_type=jnp.float32).astype(jnp.bfloat16)
    number = jnp.where(
        iota((src_count, LANES), 1) == LANES - 1, iota((src_count, LANES), 0) + 1, 0
    ).astype(jnp.float32).astype(jnp.bfloat16)
    number = jnp.dot(to_slot, number, preferred_element_type=jnp.float32)
    for copy in copies:
        copy.wait()
    acc = lax.dot_general(ext[...], weight[...], NT, preferred_element_type=jnp.float32)
    acc = acc[:, :LANES] + acc[:, LANES:]
    y = acc.astype(jnp.bfloat16)
    head = acc[:rows]
    head_lo = head - head.astype(jnp.bfloat16).astype(jnp.float32)
    tail = lax.dot_general(
        ext[(blocks - 1) * rows :, wide - LANES :], weight[:, :LANES], NT,
        preferred_element_type=jnp.float32,
    )
    tail = tail[:, :LANES] + tail[:, LANES:]
    tail_hi = tail.astype(jnp.bfloat16).astype(jnp.float32)
    lane = iota((rows, LANES), 1)
    edge = jnp.where(
        lane < EDGE,
        head_lo,
        jnp.where(
            lane < 2 * EDGE,
            pltpu.roll(tail_hi, EDGE, 1),
            jnp.where(lane < 3 * EDGE, pltpu.roll(tail - tail_hi, 2 * EDGE, 1), 0.0),
        ),
    ).astype(jnp.bfloat16)
    parts = [y[b * rows : (b + 1) * rows] for b in range(blocks)] + [edge]
    last = blocks * ch
    for t in range(steps):
        for b in range(blocks):
            out_ref[t, b * ch : (b + 1) * ch] = parts[b][t * ch : (t + 1) * ch]
        out_ref[t, last : last + ch] = edge[t * ch : (t + 1) * ch]
    for b, part in enumerate(parts):
        found = jnp.dot(pick, part, preferred_element_type=jnp.float32)
        if b == blocks:
            found += number
        slot_ref[:, b * LANES : (b + 1) * LANES] = found.astype(jnp.bfloat16)
    tables.wait()


def arrange_kernel(half, blocks, pieces, *refs):
    slots = jnp.concatenate([ref[...] for ref in refs[:pieces]], axis=0)
    part_ref, *out_refs = refs[pieces:]
    height = out_refs[0].shape[0]
    own_rows = part_ref.shape[1] - ROWS
    tile_rows = height - 2 * own_rows - blocks * half
    numbers = slots[:, blocks * LANES :].astype(jnp.float32)
    total = numbers.shape[0]
    numbers = jnp.sum(
        jnp.where(iota((total, LANES), 1) == LANES - 1, numbers, 0.0), axis=1, keepdims=True
    ).astype(jnp.int32)
    first = lax.axis_index("chan") % CORES * half
    pick = one_hot(numbers == iota((total, half), 1) + 1 + first)
    found = lax.dot_general(
        pick, slots, (((0,), (0,)), ((), ())), preferred_element_type=jnp.float32
    )
    fill = [found[:, b * LANES : (b + 1) * LANES].astype(jnp.bfloat16) for b in range(blocks)]
    edges = jnp.where(iota((half, LANES), 1) < 3 * EDGE, found[:, blocks * LANES :], 0.0)
    added = [jnp.zeros((ROWS, LANES), jnp.float32) for _ in range(tile_rows // ROWS)]
    for i in range(half // ROWS):
        tile, place = divmod(i + 2, PER_TILE)
        piece = edges[i * ROWS : (i + 1) * ROWS]
        added[tile] += pltpu.roll(piece, 3 * EDGE * place, 1) if place else piece
    me = lax.axis_index("tm")
    for k, out_ref in enumerate(out_refs):
        same = part_ref[me ^ (2 * k)]
        other = part_ref[me ^ (2 * k) ^ 1]
        out_ref[:own_rows] = same[:own_rows]
        out_ref[own_rows : 2 * own_rows] = other[:own_rows]
        for b in range(blocks):
            at = 2 * own_rows + b * half
            out_ref[at : at + half] = fill[b]
        mixed = same[own_rows:].astype(jnp.float32) + pltpu.roll(
            other[own_rows:].astype(jnp.float32), 3 * EDGE, 1
        )
        for tile, extra in enumerate(added):
            at = height - tile_rows + tile * ROWS
            out_ref[at : at + ROWS] = (extra + mixed if tile == 0 else extra).astype(jnp.bfloat16)


def forward_kernel(own_rows, block_ref, out_ref):
    out_ref[...] = block_ref[own_rows:]


def collect_kernel(own_rows, *refs):
    *block_refs, out_ref = refs
    highs = len(block_refs) // 2
    me = lax.axis_index("tm")
    for k in range(highs):
        out_ref[me ^ (2 * k)] = block_refs[k][2 * own_rows :]
        out_ref[me ^ (2 * k) ^ 1] = block_refs[highs + k][own_rows:]


def correlate_kernel(
    seg_count, src_count, dec, head_len, part_rows, count, steps, live_ref, tab_ref, *refs
):
    count_high = steps // 2
    block_refs, passed_refs = refs[:count_high], refs[count_high:steps]
    given_ref, far_ref, out_ref = refs[steps : steps + 3]
    mine_ref, mine_edge, trace, own, other, cross, result, sems = refs[steps + 3 :]
    ch = out_ref.shape[1]
    own_rows = mine_ref.shape[1]
    half = src_count // CORES
    rows = ch + src_count
    per_seg = SEG // dec
    blocks = dec // LANES
    d_cols = 4 * HALF

    @pl.when(pl.program_id(0) == 0)
    def _():
        me = lax.axis_index("tm")
        last = block_refs[0].shape[0] - edge_tiles(2 * ch + half) * ROWS
        for k, ref in enumerate(block_refs):
            mine_ref[me ^ (2 * k)] = ref[:own_rows]
            mine_edge[me ^ (2 * k)] = ref[last : last + ROWS].astype(jnp.float32)
        for k, ref in enumerate(passed_refs):
            mine_ref[me ^ (2 * k) ^ 1] = ref[:own_rows]
            pack = ref[last - own_rows : last - own_rows + ROWS].astype(jnp.float32)
            mine_edge[me ^ (2 * k) ^ 1] = pltpu.roll(pack, LANES - 3 * EDGE, 1)
        live = iota((ch, LANES), 0) < live_ref[0]
        before = jnp.zeros((rows, LANES), jnp.float32)
        is_head = iota((rows, LANES), 1) < head_len
        tile_rows = edge_tiles(2 * ch + half) * ROWS
        low_core = lax.axis_index("chan") % CORES == 0

        def edge_groups(ref, t):
            out = []
            last = ref.shape[1] - tile_rows
            for i in range(2, 2 + half // ROWS):
                tile, place = divmod(i, PER_TILE)
                pack = ref[t, last + tile * ROWS : last + (tile + 1) * ROWS].astype(jnp.float32)
                out.append(pltpu.roll(pack, LANES - 3 * EDGE * place, 1) if place else pack)
            return jnp.concatenate(out, axis=0)

        def in_order(near, far):
            return [jnp.where(low_core, near, far), jnp.where(low_core, far, near)]

        for t in range(steps):
            edge = jnp.where(live, mine_edge[t], 0.0)
            theirs = edge_groups(given_ref, t), edge_groups(far_ref, t)
            edge = jnp.concatenate([edge, *in_order(*theirs)], axis=0)
            for b in range(blocks):
                mine = mine_ref[t, b * ch : (b + 1) * ch]
                mine = jnp.where(live, mine, jnp.zeros_like(mine))
                rows_b = slice(b * half, (b + 1) * half)
                theirs = given_ref[t, rows_b], far_ref[t, rows_b]
                both = jnp.concatenate([mine, *in_order(*theirs)], axis=0)
                if b == 0:
                    tail = pltpu.roll(before, LANES - EDGE, 1) + pltpu.roll(before, LANES - 2 * EDGE, 1)
                    both = both.astype(jnp.float32)
                    both = jnp.where(is_head, both + edge + tail, both).astype(jnp.bfloat16)
                trace[t * rows : (t + 1) * rows, b * LANES : (b + 1) * LANES] = both
            before = edge
        odd = (iota((rows, 2 * LANES), 1) & 1) == 1
        sign = jnp.where(odd, -1.0, 1.0)
        same = one_hot(
            iota((2 * LANES, LANES), 0) % LANES // BAND == iota((2 * LANES, LANES), 1) // BAND
        )
        group_segs = max(1, min(seg_count, part_rows // (per_seg * rows)))
        for first in range(0, seg_count, group_segs):
            segs = min(group_segs, seg_count - first)
            lhs = trace[first * per_seg * rows : (first + segs) * per_seg * rows, :]
            for j in range(CHUNKS):
                acc = jnp.dot(
                    lhs, tab_ref[:, 4 * j * LANES : 4 * (j + 1) * LANES],
                    preferred_element_type=jnp.float32,
                )
                folded = acc[:, : 2 * LANES] + acc[:, 2 * LANES :]
                spec = []
                for g in range(segs):
                    a = folded[g * per_seg * rows : (g * per_seg + 1) * rows]
                    b = folded[(g * per_seg + 1) * rows : (g * per_seg + 2) * rows]
                    spec.append(a + sign * b)
                spec = jnp.concatenate(spec, axis=0)
                re, im = spec[:, :LANES], spec[:, LANES:]
                power = re * re + im * im
                hi = power.astype(jnp.bfloat16)
                lo = (power - hi.astype(jnp.float32)).astype(jnp.bfloat16)
                total = jnp.dot(
                    jnp.concatenate([hi, lo], axis=1), same, preferred_element_type=jnp.float32
                )
                scale = lax.rsqrt(total * (1.0 / BAND) + whiten_eps)
                w_re = (re * scale).astype(jnp.bfloat16).astype(jnp.float32)
                w_im = (im * scale).astype(jnp.bfloat16).astype(jnp.float32)
                at = 2 * j * LANES
                for g in range(segs):
                    r, o = g * rows, (first + g) * ch
                    own[o : o + ch, at : at + LANES] = w_re[r : r + ch]
                    own[o : o + ch, at + LANES : at + 2 * LANES] = w_im[r : r + ch]
                    o = (first + g) * src_count
                    other[o : o + src_count, at : at + LANES] = w_re[r + ch : r + rows]
                    other[o : o + src_count, at + LANES : at + 2 * LANES] = w_im[r + ch : r + rows]

    block = cross.shape[1] // ch
    copies = []
    for i in range(count):
        start = pl.multiple_of((pl.program_id(0) * count + i) * block, 8)
        for j in range(CHUNKS):
            at = 2 * j * LANES
            a_re = [own[g * ch : (g + 1) * ch, at : at + LANES] for g in range(seg_count)]
            a_im = [own[g * ch : (g + 1) * ch, at + LANES : at + 2 * LANES] for g in range(seg_count)]
            for s in range(block):
                if s % 8 == 0:
                    tiles = [
                        other[
                            pl.ds(pl.multiple_of(g * src_count + start + s, 8), 8),
                            at : at + 2 * LANES,
                        ]
                        for g in range(seg_count)
                    ]
                re = im = None
                for g in range(seg_count):
                    b_re = tiles[g][s % 8 : s % 8 + 1, :LANES]
                    b_im = tiles[g][s % 8 : s % 8 + 1, LANES:]
                    p = a_re[g] * b_re + a_im[g] * b_im
                    q = a_im[g] * b_re - a_re[g] * b_im
                    re, im = (p, q) if re is None else (re + p, im + q)
                row = slice(s * ch, (s + 1) * ch)
                cross[i, row, at : at + LANES] = re.astype(jnp.bfloat16)
                cross[i, row, at + LANES : at + 2 * LANES] = im.astype(jnp.bfloat16)
        lags = sum(
            jnp.dot(
                cross[i, :, h * dec : (h + 1) * dec],
                tab_ref[:, d_cols + 2 * LAGH * h : d_cols + 2 * LAGH * (h + 1)],
                preferred_element_type=jnp.float32,
            )
            for h in range(per_seg)
        )
        result[i] = lags.reshape(result.shape[1:])
        copy = pltpu.make_async_copy(result.at[i], out_ref.at[pl.ds(start, block)], sems.at[i])
        copy.start()
        copies.append(copy)
    for copy in copies:
        copy.wait()


def whole(space=pltpu.VMEM):
    return pl.BlockSpec(memory_space=space)


def local(raw_strain, fir_taps, source_channels, live_counts):
    rows, raw_len = raw_strain.shape
    steps = lax.axis_size("tm")
    chan_count = lax.axis_size("chan")
    dec = raw_len // DECIM
    blocks = dec // LANES
    ch = rows // steps
    seg_count = steps * dec // SEG
    src_count = source_channels.shape[0]
    slots = 2 * SRC_DEV * steps
    span = raw_len // blocks
    total_rows = ch + src_count
    half = src_count // CORES
    highs = steps // 2
    own_rows = blocks * ch
    given_rows = blocks * half + edge_tiles(2 * ch + half) * ROWS
    height = 2 * own_rows + given_rows
    head_len = -(-(fir_taps.shape[0] - 1) // DECIM)
    assert head_len < EDGE and ch == ROWS and src_count <= 256
    assert steps & (steps - 1) == 0 and chan_count & (chan_count - 1) == 0 and half % ROWS == 0
    src = source_channels.reshape(1, src_count)
    taps = fir_taps.reshape(1, fir_taps.shape[0])
    table = np.concatenate([dft_table(dec), *lag_table(seg_count).reshape(SEG // dec, dec, -1)], axis=1)
    inputs = (src, taps, raw_strain, jnp.asarray(table))
    part, picked, table = pl.pallas_call(
        functools.partial(filter_kernel, blocks),
        out_shape=[
            pltpu.VMEM((steps, (blocks + 1) * ch, LANES), jnp.bfloat16),
            pltpu.VMEM((slots, dec + LANES), jnp.bfloat16),
            pltpu.VMEM(table.shape, jnp.bfloat16),
        ],
        in_specs=[whole(pl.ANY)] * 4,
        out_specs=[whole(), whole(), whole(pl.ANY)],
        scratch_shapes=[
            pltpu.VMEM((blocks * rows, span + LANES), jnp.bfloat16),
            pltpu.VMEM((2 * LANES, span + LANES), jnp.bfloat16),
            pltpu.VMEM(src.shape, src.dtype),
            pltpu.VMEM(taps.shape, taps.dtype),
            pltpu.SemaphoreType.DMA((blocks + 3,)),
        ],
        compiler_params=pltpu.CompilerParams(vmem_limit_bytes=16 * MIB),
        name="fir",
    )(*(pltpu.with_memory_space_constraint(a, pltpu.HBM) for a in inputs))
    pieces = [picked] + [
        lax.ppermute(picked, "chan", [(c, c ^ k) for c in range(chan_count)])
        for k in range(1, chan_count)
    ]
    to_vmem = functools.partial(pltpu.with_memory_space_constraint, memory_space=pltpu.VMEM)
    outgoing = pl.pallas_call(
        functools.partial(arrange_kernel, half, blocks, chan_count),
        out_shape=[pltpu.VMEM((height, LANES), jnp.bfloat16)] * highs,
        in_specs=[whole()] * (chan_count + 1),
        out_specs=[whole()] * highs,
        compiler_params=pltpu.CompilerParams(vmem_limit_bytes=8 * MIB),
        name="arrange",
    )(*(to_vmem(a) for a in (*pieces, part)))
    arrived = [
        lax.ppermute(outgoing[k], "tm", [(t, t ^ (2 * k)) for t in range(steps)])
        for k in range(highs - 1, 0, -1)
    ]
    arrived = [to_vmem(a) for a in (outgoing[0], *arrived[::-1])]
    small = pltpu.CompilerParams(vmem_limit_bytes=8 * MIB)
    passed = [None] * highs
    for k in [1, 0, *range(highs - 1, 1, -1)]:
        direct = k == 1
        forward = pl.pallas_call(
            functools.partial(forward_kernel, own_rows),
            out_shape=pltpu.VMEM((own_rows + given_rows, LANES), jnp.bfloat16),
            in_specs=[whole()],
            out_specs=whole(),
            compiler_params=small,
            name="forward",
        )(to_vmem(outgoing[1]) if direct else arrived[k])
        to = [(t, t ^ (3 if direct else 1)) for t in range(steps)]
        passed[k] = to_vmem(lax.ppermute(forward, "tm", to))
    given = pl.pallas_call(
        functools.partial(collect_kernel, own_rows),
        out_shape=pltpu.VMEM((steps, given_rows, LANES), jnp.bfloat16),
        in_specs=[whole()] * steps,
        out_specs=whole(),
        compiler_params=small,
        name="collect",
    )(*arrived, *passed)
    swapped = lax.ppermute(given, "chan", [(c, c ^ 1) for c in range(chan_count)])
    block = math.gcd(src_count, 16)
    count = math.gcd(src_count // block, 2)
    state = seg_count * total_rows * SEG * 4
    return pl.pallas_call(
        functools.partial(
            correlate_kernel, seg_count, src_count, dec, head_len, 1024, count, steps
        ),
        grid=(src_count // (block * count),),
        out_shape=jax.ShapeDtypeStruct((src_count, ch, 2 * LAGH), jnp.float32),
        in_specs=[whole(pltpu.SMEM)] + [whole()] * (steps + 3),
        out_specs=whole(pl.ANY),
        scratch_shapes=[
            pltpu.VMEM((steps, own_rows, LANES), jnp.bfloat16),
            pltpu.VMEM((steps, ROWS, LANES), jnp.float32),
            pltpu.VMEM((steps * total_rows, dec), jnp.bfloat16),
            pltpu.VMEM((seg_count * ch, SEG), jnp.float32),
            pltpu.VMEM((seg_count * src_count, SEG), jnp.float32),
            pltpu.VMEM((count, block * ch, SEG), jnp.bfloat16),
            pltpu.VMEM((count, block, ch, 2 * LAGH), jnp.float32),
            pltpu.SemaphoreType.DMA((count,)),
        ],
        compiler_params=pltpu.CompilerParams(vmem_limit_bytes=16 * MIB + 2 * state),
        name="correlate",
    )(live_counts, table, *arrived, *passed, to_vmem(given), to_vmem(swapped))


def solution(mesh):
    placed = (P("chan", "tm"), P(), P(), P(("chan", "tm")))
    return jax.shard_map(
        local, mesh=mesh, in_specs=placed, out_specs=P(None, ("chan", "tm"), None), check_vma=False
    )
```

```python
import functools
import math

import jax
import jax.numpy as jnp
import ml_dtypes
import numpy as np
from jax import lax
from jax.experimental import pallas as pl
from jax.experimental.pallas import tpu as pltpu
from jax.sharding import PartitionSpec as P

DECIM = 10
SEG = 1024
BAND = 64
LAGH = 192
SRC_DEV = 1
LANES = 128
HALF = SEG // 2
CHUNKS = HALF // LANES
EDGE = 14
PER_TILE = LANES // (3 * EDGE)
ROWS = 16
CORES = 2
MIB = 1024 * 1024

whiten_eps = 1e-06

NT = (((1,), (1,)), ((), ()))


def split_table(table):
    hi = table.astype(ml_dtypes.bfloat16)
    lo = (table - hi.astype(np.float64)).astype(ml_dtypes.bfloat16)
    return hi, lo


def dft_table(rows):
    phase = (np.arange(rows)[:, None] * np.arange(HALF)[None, :] % SEG) * (2.0 * np.pi / SEG)
    parts = []
    for j in range(CHUNKS):
        cut = slice(j * LANES, (j + 1) * LANES)
        hi, lo = split_table(np.concatenate([np.cos(phase[:, cut]), -np.sin(phase[:, cut])], 1))
        parts += [hi, lo]
    return np.concatenate(parts, axis=1)


def lag_table(seg_count):
    freq = np.arange(HALF)[:, None]
    phase = (freq * np.arange(-LAGH, LAGH)[None, :] % SEG) * (2.0 * np.pi / SEG)
    weight = np.where(freq == 0, 1.0, 2.0) * (math.sqrt(SEG / seg_count) / SEG)
    re = (weight * np.cos(phase)).reshape(CHUNKS, LANES, 2 * LAGH)
    im = (-weight * np.sin(phase)).reshape(CHUNKS, LANES, 2 * LAGH)
    return np.concatenate([re, im], axis=1).reshape(SEG, 2 * LAGH).astype(ml_dtypes.bfloat16)


def iota(shape, dim):
    return lax.broadcasted_iota(jnp.int32, shape, dim)


def one_hot(mask):
    return jnp.where(mask, 1.0, 0.0).astype(jnp.bfloat16)


def column(row):
    n = row.shape[1]
    return jnp.sum(jnp.where(iota((n, n), 0) == iota((n, n), 1), row, 0), axis=1, keepdims=True)


def tap_rows(taps):
    tap_count = taps.shape[1]
    width = 3 * LANES
    flip = one_hot(iota((tap_count, width), 0) + iota((tap_count, width), 1) == tap_count)
    hi = taps.astype(jnp.bfloat16)
    lo = (taps - hi.astype(jnp.float32)).astype(jnp.bfloat16)
    out = []
    for part in (hi, lo):
        base = jnp.dot(
            jnp.broadcast_to(part.astype(jnp.float32), (8, tap_count)).astype(jnp.bfloat16),
            flip,
            preferred_element_type=jnp.float32,
        )
        upper = pltpu.roll(base, 0, 1, stride=DECIM, stride_axis=0)
        out.append(jnp.concatenate([upper, pltpu.roll(upper, 8 * DECIM, 1)], axis=0))
    return out


def edge_tiles(count):
    return -(-count // (PER_TILE * ROWS))


def filter_kernel(
    blocks,
    src_hbm, taps_hbm, raw_ref, tab_hbm,
    out_ref, slot_ref, tab_ref,
    ext, weight, src_ref, taps_ref, sems,
):
    rows, raw_len = raw_ref.shape
    steps = out_ref.shape[0]
    ch = rows // steps
    span = raw_len // blocks
    wide = span + LANES
    copies = []
    for b in range(blocks):
        if b == 0:
            copy = pltpu.make_async_copy(
                raw_ref.at[:, pl.ds(0, span)],
                ext.at[pl.ds(0, rows), pl.ds(LANES, span)],
                sems.at[b],
            )
        else:
            copy = pltpu.make_async_copy(
                raw_ref.at[:, pl.ds(b * span - LANES, wide)],
                ext.at[pl.ds(b * rows, rows), :],
                sems.at[b],
            )
        copy.start()
        copies.append(copy)
    small = [
        pltpu.make_async_copy(taps_hbm, taps_ref, sems.at[blocks]),
        pltpu.make_async_copy(src_hbm, src_ref, sems.at[blocks + 1]),
    ]
    tables = pltpu.make_async_copy(tab_hbm, tab_ref, sems.at[blocks + 2])
    for copy in [*small, tables]:
        copy.start()
    ext[:rows, :LANES] = jnp.zeros((rows, LANES), ext.dtype)
    weight[...] = jnp.zeros_like(weight)
    for copy in small:
        copy.wait()
    for p, base in enumerate(tap_rows(taps_ref[...])):
        for i in range(LANES // 16):
            tile, lane = divmod(16 * DECIM * i, LANES)
            piece = pltpu.roll(base, lane, 1) if lane else base
            weight[p * LANES + 16 * i : p * LANES + 16 * (i + 1), tile * LANES : (tile + 3) * LANES] = (
                piece.astype(jnp.bfloat16)
            )
    src = src_ref[...]
    src_count = src.shape[1]
    slots = slot_ref.shape[0]
    group = src // rows
    group_col = column(group)
    src_col = column(src)
    rank = jnp.sum(
        jnp.where(
            (group_col == group)
            & (iota((src_count, src_count), 0) < iota((src_count, src_count), 1)),
            1,
            0,
        ),
        axis=0,
        keepdims=True,
    )
    mine = lax.axis_index("chan")
    to_slot = one_hot((iota((slots, src_count), 0) == rank) & (group == mine))
    to_row = one_hot(src_col - mine * rows == iota((src_count, rows), 1))
    pick = jnp.dot(to_slot, to_row, preferred_element_type=jnp.float32).astype(jnp.bfloat16)
    number = jnp.where(
        iota((src_count, LANES), 1) == LANES - 1, iota((src_count, LANES), 0) + 1, 0
    ).astype(jnp.float32).astype(jnp.bfloat16)
    number = jnp.dot(to_slot, number, preferred_element_type=jnp.float32)
    for copy in copies:
        copy.wait()
    acc = lax.dot_general(ext[...], weight[...], NT, preferred_element_type=jnp.float32)
    acc = acc[:, :LANES] + acc[:, LANES:]
    y = acc.astype(jnp.bfloat16)
    head = acc[:rows]
    head_lo = head - head.astype(jnp.bfloat16).astype(jnp.float32)
    tail = lax.dot_general(
        ext[(blocks - 1) * rows :, wide - LANES :], weight[:, :LANES], NT,
        preferred_element_type=jnp.float32,
    )
    tail = tail[:, :LANES] + tail[:, LANES:]
    tail_hi = tail.astype(jnp.bfloat16).astype(jnp.float32)
    lane = iota((rows, LANES), 1)
    edge = jnp.where(
        lane < EDGE,
        head_lo,
        jnp.where(
            lane < 2 * EDGE,
            pltpu.roll(tail_hi, EDGE, 1),
            jnp.where(lane < 3 * EDGE, pltpu.roll(tail - tail_hi, 2 * EDGE, 1), 0.0),
        ),
    ).astype(jnp.bfloat16)
    parts = [y[b * rows : (b + 1) * rows] for b in range(blocks)] + [edge]
    last = blocks * ch
    for t in range(steps):
        for b in range(blocks):
            out_ref[t, b * ch : (b + 1) * ch] = parts[b][t * ch : (t + 1) * ch]
        out_ref[t, last : last + ch] = edge[t * ch : (t + 1) * ch]
    for b, part in enumerate(parts):
        found = jnp.dot(pick, part, preferred_element_type=jnp.float32)
        if b == blocks:
            found += number
        slot_ref[:, b * LANES : (b + 1) * LANES] = found.astype(jnp.bfloat16)
    tables.wait()


def arrange_kernel(half, blocks, pieces, *refs):
    slots = jnp.concatenate([ref[...] for ref in refs[:pieces]], axis=0)
    part_ref, *out_refs = refs[pieces:]
    height = out_refs[0].shape[0]
    own_rows = part_ref.shape[1] - ROWS
    tile_rows = height - 2 * own_rows - blocks * half
    numbers = slots[:, blocks * LANES :].astype(jnp.float32)
    total = numbers.shape[0]
    numbers = jnp.sum(
        jnp.where(iota((total, LANES), 1) == LANES - 1, numbers, 0.0), axis=1, keepdims=True
    ).astype(jnp.int32)
    first = lax.axis_index("chan") % CORES * half
    pick = one_hot(numbers == iota((total, half), 1) + 1 + first)
    found = lax.dot_general(
        pick, slots, (((0,), (0,)), ((), ())), preferred_element_type=jnp.float32
    )
    fill = [found[:, b * LANES : (b + 1) * LANES].astype(jnp.bfloat16) for b in range(blocks)]
    edges = jnp.where(iota((half, LANES), 1) < 3 * EDGE, found[:, blocks * LANES :], 0.0)
    added = [jnp.zeros((ROWS, LANES), jnp.float32) for _ in range(tile_rows // ROWS)]
    for i in range(half // ROWS):
        tile, place = divmod(i + 2, PER_TILE)
        piece = edges[i * ROWS : (i + 1) * ROWS]
        added[tile] += pltpu.roll(piece, 3 * EDGE * place, 1) if place else piece
    me = lax.axis_index("tm")
    for k, out_ref in enumerate(out_refs):
        same = part_ref[me ^ (2 * k)]
        other = part_ref[me ^ (2 * k) ^ 1]
        out_ref[:own_rows] = same[:own_rows]
        out_ref[own_rows : 2 * own_rows] = other[:own_rows]
        for b in range(blocks):
            at = 2 * own_rows + b * half
            out_ref[at : at + half] = fill[b]
        mixed = same[own_rows:].astype(jnp.float32) + pltpu.roll(
            other[own_rows:].astype(jnp.float32), 3 * EDGE, 1
        )
        for tile, extra in enumerate(added):
            at = height - tile_rows + tile * ROWS
            out_ref[at : at + ROWS] = (extra + mixed if tile == 0 else extra).astype(jnp.bfloat16)


def forward_kernel(own_rows, *refs):
    *block_refs, out_ref = refs
    for i, ref in enumerate(block_refs):
        out_ref[i] = ref[own_rows:]


def by_high_bits(passed_refs):
    ends, *rest = passed_refs
    return [ends.at[0], *(ref.at[0] for ref in rest), ends.at[1]]


def collect_kernel(own_rows, highs, *refs):
    *block_refs, out_ref = refs
    passed_refs = by_high_bits(block_refs[highs:])
    me = lax.axis_index("tm")
    for k in range(highs):
        out_ref[me ^ (2 * k)] = block_refs[k][2 * own_rows :]
        out_ref[me ^ (2 * k) ^ 1] = passed_refs[k][own_rows:]


def correlate_kernel(
    seg_count, src_count, dec, head_len, part_rows, count, steps, live_ref, tab_ref, *refs
):
    count_high = steps // 2
    block_refs, passed_refs = refs[:count_high], by_high_bits(refs[count_high : steps - 1])
    given_ref, far_ref, out_ref = refs[steps - 1 : steps + 2]
    mine_ref, mine_edge, trace, own, other, cross, result, sems = refs[steps + 2 :]
    ch = out_ref.shape[1]
    own_rows = mine_ref.shape[1]
    half = src_count // CORES
    rows = ch + src_count
    per_seg = SEG // dec
    blocks = dec // LANES
    d_cols = 4 * HALF

    @pl.when(pl.program_id(0) == 0)
    def _():
        me = lax.axis_index("tm")
        last = block_refs[0].shape[0] - edge_tiles(2 * ch + half) * ROWS
        for k, ref in enumerate(block_refs):
            mine_ref[me ^ (2 * k)] = ref[:own_rows]
            mine_edge[me ^ (2 * k)] = ref[last : last + ROWS].astype(jnp.float32)
        for k, ref in enumerate(passed_refs):
            mine_ref[me ^ (2 * k) ^ 1] = ref[:own_rows]
            pack = ref[last - own_rows : last - own_rows + ROWS].astype(jnp.float32)
            mine_edge[me ^ (2 * k) ^ 1] = pltpu.roll(pack, LANES - 3 * EDGE, 1)
        live = iota((ch, LANES), 0) < live_ref[0]
        before = jnp.zeros((rows, LANES), jnp.float32)
        is_head = iota((rows, LANES), 1) < head_len
        tile_rows = edge_tiles(2 * ch + half) * ROWS
        low_core = lax.axis_index("chan") % CORES == 0

        def edge_groups(ref, t):
            out = []
            last = ref.shape[1] - tile_rows
            for i in range(2, 2 + half // ROWS):
                tile, place = divmod(i, PER_TILE)
                pack = ref[t, last + tile * ROWS : last + (tile + 1) * ROWS].astype(jnp.float32)
                out.append(pltpu.roll(pack, LANES - 3 * EDGE * place, 1) if place else pack)
            return jnp.concatenate(out, axis=0)

        def in_order(near, far):
            return [jnp.where(low_core, near, far), jnp.where(low_core, far, near)]

        for t in range(steps):
            edge = jnp.where(live, mine_edge[t], 0.0)
            theirs = edge_groups(given_ref, t), edge_groups(far_ref, t)
            edge = jnp.concatenate([edge, *in_order(*theirs)], axis=0)
            for b in range(blocks):
                mine = mine_ref[t, b * ch : (b + 1) * ch]
                mine = jnp.where(live, mine, jnp.zeros_like(mine))
                rows_b = slice(b * half, (b + 1) * half)
                theirs = given_ref[t, rows_b], far_ref[t, rows_b]
                both = jnp.concatenate([mine, *in_order(*theirs)], axis=0)
                if b == 0:
                    tail = pltpu.roll(before, LANES - EDGE, 1) + pltpu.roll(before, LANES - 2 * EDGE, 1)
                    both = both.astype(jnp.float32)
                    both = jnp.where(is_head, both + edge + tail, both).astype(jnp.bfloat16)
                trace[t * rows : (t + 1) * rows, b * LANES : (b + 1) * LANES] = both
            before = edge
        odd = (iota((rows, 2 * LANES), 1) & 1) == 1
        sign = jnp.where(odd, -1.0, 1.0)
        same = one_hot(
            iota((2 * LANES, LANES), 0) % LANES // BAND == iota((2 * LANES, LANES), 1) // BAND
        )
        group_segs = max(1, min(seg_count, part_rows // (per_seg * rows)))
        for first in range(0, seg_count, group_segs):
            segs = min(group_segs, seg_count - first)
            lhs = trace[first * per_seg * rows : (first + segs) * per_seg * rows, :]
            for j in range(CHUNKS):
                acc = jnp.dot(
                    lhs, tab_ref[:, 4 * j * LANES : 4 * (j + 1) * LANES],
                    preferred_element_type=jnp.float32,
                )
                folded = acc[:, : 2 * LANES] + acc[:, 2 * LANES :]
                spec = []
                for g in range(segs):
                    a = folded[g * per_seg * rows : (g * per_seg + 1) * rows]
                    b = folded[(g * per_seg + 1) * rows : (g * per_seg + 2) * rows]
                    spec.append(a + sign * b)
                spec = jnp.concatenate(spec, axis=0)
                re, im = spec[:, :LANES], spec[:, LANES:]
                power = re * re + im * im
                hi = power.astype(jnp.bfloat16)
                lo = (power - hi.astype(jnp.float32)).astype(jnp.bfloat16)
                total = jnp.dot(
                    jnp.concatenate([hi, lo], axis=1), same, preferred_element_type=jnp.float32
                )
                scale = lax.rsqrt(total * (1.0 / BAND) + whiten_eps)
                w_re = (re * scale).astype(jnp.bfloat16).astype(jnp.float32)
                w_im = (im * scale).astype(jnp.bfloat16).astype(jnp.float32)
                at = 2 * j * LANES
                for g in range(segs):
                    r, o = g * rows, (first + g) * ch
                    own[o : o + ch, at : at + LANES] = w_re[r : r + ch]
                    own[o : o + ch, at + LANES : at + 2 * LANES] = w_im[r : r + ch]
                    o = (first + g) * src_count
                    other[o : o + src_count, at : at + LANES] = w_re[r + ch : r + rows]
                    other[o : o + src_count, at + LANES : at + 2 * LANES] = w_im[r + ch : r + rows]

    block = cross.shape[1] // ch
    copies = []
    for i in range(count):
        start = pl.multiple_of((pl.program_id(0) * count + i) * block, 8)
        for j in range(CHUNKS):
            at = 2 * j * LANES
            a_re = [own[g * ch : (g + 1) * ch, at : at + LANES] for g in range(seg_count)]
            a_im = [own[g * ch : (g + 1) * ch, at + LANES : at + 2 * LANES] for g in range(seg_count)]
            for s in range(block):
                if s % 8 == 0:
                    tiles = [
                        other[
                            pl.ds(pl.multiple_of(g * src_count + start + s, 8), 8),
                            at : at + 2 * LANES,
                        ]
                        for g in range(seg_count)
                    ]
                re = im = None
                for g in range(seg_count):
                    b_re = tiles[g][s % 8 : s % 8 + 1, :LANES]
                    b_im = tiles[g][s % 8 : s % 8 + 1, LANES:]
                    p = a_re[g] * b_re + a_im[g] * b_im
                    q = a_im[g] * b_re - a_re[g] * b_im
                    re, im = (p, q) if re is None else (re + p, im + q)
                row = slice(s * ch, (s + 1) * ch)
                cross[i, row, at : at + LANES] = re.astype(jnp.bfloat16)
                cross[i, row, at + LANES : at + 2 * LANES] = im.astype(jnp.bfloat16)
        lags = sum(
            jnp.dot(
                cross[i, :, h * dec : (h + 1) * dec],
                tab_ref[:, d_cols + 2 * LAGH * h : d_cols + 2 * LAGH * (h + 1)],
                preferred_element_type=jnp.float32,
            )
            for h in range(per_seg)
        )
        result[i] = lags.reshape(result.shape[1:])
        copy = pltpu.make_async_copy(result.at[i], out_ref.at[pl.ds(start, block)], sems.at[i])
        copy.start()
        copies.append(copy)
    for copy in copies:
        copy.wait()


def whole(space=pltpu.VMEM):
    return pl.BlockSpec(memory_space=space)


def local(raw_strain, fir_taps, source_channels, live_counts):
    rows, raw_len = raw_strain.shape
    steps = lax.axis_size("tm")
    chan_count = lax.axis_size("chan")
    dec = raw_len // DECIM
    blocks = dec // LANES
    ch = rows // steps
    seg_count = steps * dec // SEG
    src_count = source_channels.shape[0]
    slots = 2 * SRC_DEV * steps
    span = raw_len // blocks
    total_rows = ch + src_count
    half = src_count // CORES
    highs = steps // 2
    own_rows = blocks * ch
    given_rows = blocks * half + edge_tiles(2 * ch + half) * ROWS
    height = 2 * own_rows + given_rows
    head_len = -(-(fir_taps.shape[0] - 1) // DECIM)
    assert head_len < EDGE and ch == ROWS and src_count <= 256
    assert steps >= 8 and steps & (steps - 1) == 0 and chan_count & (chan_count - 1) == 0 and half % ROWS == 0
    src = source_channels.reshape(1, src_count)
    taps = fir_taps.reshape(1, fir_taps.shape[0])
    table = np.concatenate([dft_table(dec), *lag_table(seg_count).reshape(SEG // dec, dec, -1)], axis=1)
    inputs = (src, taps, raw_strain, jnp.asarray(table))
    part, picked, table = pl.pallas_call(
        functools.partial(filter_kernel, blocks),
        out_shape=[
            pltpu.VMEM((steps, (blocks + 1) * ch, LANES), jnp.bfloat16),
            pltpu.VMEM((slots, dec + LANES), jnp.bfloat16),
            pltpu.VMEM(table.shape, jnp.bfloat16),
        ],
        in_specs=[whole(pl.ANY)] * 4,
        out_specs=[whole(), whole(), whole(pl.ANY)],
        scratch_shapes=[
            pltpu.VMEM((blocks * rows, span + LANES), jnp.bfloat16),
            pltpu.VMEM((2 * LANES, span + LANES), jnp.bfloat16),
            pltpu.VMEM(src.shape, src.dtype),
            pltpu.VMEM(taps.shape, taps.dtype),
            pltpu.SemaphoreType.DMA((blocks + 3,)),
        ],
        compiler_params=pltpu.CompilerParams(vmem_limit_bytes=16 * MIB),
        name="fir",
    )(*(pltpu.with_memory_space_constraint(a, pltpu.HBM) for a in inputs))
    pieces = [picked] + [
        lax.ppermute(picked, "chan", [(c, c ^ k) for c in range(chan_count)])
        for k in range(1, chan_count)
    ]
    to_vmem = functools.partial(pltpu.with_memory_space_constraint, memory_space=pltpu.VMEM)
    outgoing = pl.pallas_call(
        functools.partial(arrange_kernel, half, blocks, chan_count),
        out_shape=[pltpu.VMEM((height, LANES), jnp.bfloat16)] * highs,
        in_specs=[whole()] * (chan_count + 1),
        out_specs=[whole()] * highs,
        compiler_params=pltpu.CompilerParams(vmem_limit_bytes=8 * MIB),
        name="arrange",
    )(*(to_vmem(a) for a in (*pieces, part)))
    arrived = [
        lax.ppermute(outgoing[k], "tm", [(t, t ^ (2 * k)) for t in range(steps)])
        for k in range(highs - 1, 0, -1)
    ]
    arrived = [to_vmem(a) for a in (outgoing[0], *arrived[::-1])]
    small = pltpu.CompilerParams(vmem_limit_bytes=8 * MIB)
    passed = []
    for ks in [(0, highs - 1), *((k,) for k in range(1, highs - 1))]:
        direct = ks == (1,)
        forward = pl.pallas_call(
            functools.partial(forward_kernel, own_rows),
            out_shape=pltpu.VMEM((len(ks), own_rows + given_rows, LANES), jnp.bfloat16),
            in_specs=[whole()] * len(ks),
            out_specs=whole(),
            compiler_params=small,
            name="forward",
        )(*(to_vmem(outgoing[k]) if direct else arrived[k] for k in ks))
        to = [(t, t ^ (3 if direct else 1)) for t in range(steps)]
        passed.append(to_vmem(lax.ppermute(forward, "tm", to)))
    given = pl.pallas_call(
        functools.partial(collect_kernel, own_rows, highs),
        out_shape=pltpu.VMEM((steps, given_rows, LANES), jnp.bfloat16),
        in_specs=[whole()] * (steps - 1),
        out_specs=whole(),
        compiler_params=small,
        name="collect",
    )(*arrived, *passed)
    swapped = lax.ppermute(given, "chan", [(c, c ^ 1) for c in range(chan_count)])
    block = math.gcd(src_count, 16)
    count = math.gcd(src_count // block, 2)
    state = seg_count * total_rows * SEG * 4
    return pl.pallas_call(
        functools.partial(
            correlate_kernel, seg_count, src_count, dec, head_len, 1024, count, steps
        ),
        grid=(src_count // (block * count),),
        out_shape=jax.ShapeDtypeStruct((src_count, ch, 2 * LAGH), jnp.float32),
        in_specs=[whole(pltpu.SMEM)] + [whole()] * (steps + 2),
        out_specs=whole(pl.ANY),
        scratch_shapes=[
            pltpu.VMEM((steps, own_rows, LANES), jnp.bfloat16),
            pltpu.VMEM((steps, ROWS, LANES), jnp.float32),
            pltpu.VMEM((steps * total_rows, dec), jnp.bfloat16),
            pltpu.VMEM((seg_count * ch, SEG), jnp.float32),
            pltpu.VMEM((seg_count * src_count, SEG), jnp.float32),
            pltpu.VMEM((count, block * ch, SEG), jnp.bfloat16),
            pltpu.VMEM((count, block, ch, 2 * LAGH), jnp.float32),
            pltpu.SemaphoreType.DMA((count,)),
        ],
        compiler_params=pltpu.CompilerParams(vmem_limit_bytes=16 * MIB + 2 * state),
        name="correlate",
    )(live_counts, table, *arrived, *passed, to_vmem(given), to_vmem(swapped))


def solution(mesh):
    placed = (P("chan", "tm"), P(), P(), P(("chan", "tm")))
    return jax.shard_map(
        local, mesh=mesh, in_specs=placed, out_specs=P(None, ("chan", "tm"), None), check_vma=False
    )
```

```python
import functools
import math

import jax
import jax.numpy as jnp
import ml_dtypes
import numpy as np
from jax import lax
from jax.experimental import pallas as pl
from jax.experimental.pallas import tpu as pltpu
from jax.sharding import PartitionSpec as P

DECIM = 10
SEG = 1024
BAND = 64
LAGH = 192
SRC_DEV = 1
LANES = 128
HALF = SEG // 2
CHUNKS = HALF // LANES
EDGE = 14
PER_TILE = LANES // (3 * EDGE)
ROWS = 16
CORES = 2
MIB = 1024 * 1024

whiten_eps = 1e-06

NT = (((1,), (1,)), ((), ()))


def split_table(table):
    hi = table.astype(ml_dtypes.bfloat16)
    lo = (table - hi.astype(np.float64)).astype(ml_dtypes.bfloat16)
    return hi, lo


def dft_table(rows):
    phase = (np.arange(rows)[:, None] * np.arange(HALF)[None, :] % SEG) * (2.0 * np.pi / SEG)
    parts = []
    for j in range(CHUNKS):
        cut = slice(j * LANES, (j + 1) * LANES)
        hi, lo = split_table(np.concatenate([np.cos(phase[:, cut]), -np.sin(phase[:, cut])], 1))
        parts += [hi, lo]
    return np.concatenate(parts, axis=1)


def lag_table(seg_count):
    freq = np.arange(HALF)[:, None]
    phase = (freq * np.arange(-LAGH, LAGH)[None, :] % SEG) * (2.0 * np.pi / SEG)
    weight = np.where(freq == 0, 1.0, 2.0) * (math.sqrt(SEG / seg_count) / SEG)
    re = (weight * np.cos(phase)).reshape(CHUNKS, LANES, 2 * LAGH)
    im = (-weight * np.sin(phase)).reshape(CHUNKS, LANES, 2 * LAGH)
    return np.concatenate([re, im], axis=1).reshape(SEG, 2 * LAGH).astype(ml_dtypes.bfloat16)


def iota(shape, dim):
    return lax.broadcasted_iota(jnp.int32, shape, dim)


def one_hot(mask):
    return jnp.where(mask, 1.0, 0.0).astype(jnp.bfloat16)


def column(row):
    n = row.shape[1]
    return jnp.sum(jnp.where(iota((n, n), 0) == iota((n, n), 1), row, 0), axis=1, keepdims=True)


def tap_rows(taps):
    tap_count = taps.shape[1]
    width = 3 * LANES
    flip = one_hot(iota((tap_count, width), 0) + iota((tap_count, width), 1) == tap_count)
    hi = taps.astype(jnp.bfloat16)
    lo = (taps - hi.astype(jnp.float32)).astype(jnp.bfloat16)
    out = []
    for part in (hi, lo):
        base = jnp.dot(
            jnp.broadcast_to(part.astype(jnp.float32), (8, tap_count)).astype(jnp.bfloat16),
            flip,
            preferred_element_type=jnp.float32,
        )
        upper = pltpu.roll(base, 0, 1, stride=DECIM, stride_axis=0)
        out.append(jnp.concatenate([upper, pltpu.roll(upper, 8 * DECIM, 1)], axis=0))
    return out


def edge_tiles(count):
    return -(-count // (PER_TILE * ROWS))


def filter_kernel(
    blocks,
    src_hbm, taps_hbm, raw_ref, tab_hbm,
    out_ref, slot_ref, tab_ref,
    ext, weight, src_ref, taps_ref, sems,
):
    rows, raw_len = raw_ref.shape
    steps = out_ref.shape[0]
    ch = rows // steps
    span = raw_len // blocks
    wide = span + LANES
    copies = []
    for b in range(blocks):
        if b == 0:
            copy = pltpu.make_async_copy(
                raw_ref.at[:, pl.ds(0, span)],
                ext.at[pl.ds(0, rows), pl.ds(LANES, span)],
                sems.at[b],
            )
        else:
            copy = pltpu.make_async_copy(
                raw_ref.at[:, pl.ds(b * span - LANES, wide)],
                ext.at[pl.ds(b * rows, rows), :],
                sems.at[b],
            )
        copy.start()
        copies.append(copy)
    small = [
        pltpu.make_async_copy(taps_hbm, taps_ref, sems.at[blocks]),
        pltpu.make_async_copy(src_hbm, src_ref, sems.at[blocks + 1]),
    ]
    tables = pltpu.make_async_copy(tab_hbm, tab_ref, sems.at[blocks + 2])
    for copy in [*small, tables]:
        copy.start()
    ext[:rows, :LANES] = jnp.zeros((rows, LANES), ext.dtype)
    weight[...] = jnp.zeros_like(weight)
    for copy in small:
        copy.wait()
    for p, base in enumerate(tap_rows(taps_ref[...])):
        for i in range(LANES // 16):
            tile, lane = divmod(16 * DECIM * i, LANES)
            piece = pltpu.roll(base, lane, 1) if lane else base
            weight[p * LANES + 16 * i : p * LANES + 16 * (i + 1), tile * LANES : (tile + 3) * LANES] = (
                piece.astype(jnp.bfloat16)
            )
    src = src_ref[...]
    src_count = src.shape[1]
    slots = slot_ref.shape[0]
    group = src // rows
    group_col = column(group)
    src_col = column(src)
    rank = jnp.sum(
        jnp.where(
            (group_col == group)
            & (iota((src_count, src_count), 0) < iota((src_count, src_count), 1)),
            1,
            0,
        ),
        axis=0,
        keepdims=True,
    )
    mine = lax.axis_index("chan")
    to_slot = one_hot((iota((slots, src_count), 0) == rank) & (group == mine))
    to_row = one_hot(src_col - mine * rows == iota((src_count, rows), 1))
    pick = jnp.dot(to_slot, to_row, preferred_element_type=jnp.float32).astype(jnp.bfloat16)
    number = jnp.where(
        iota((src_count, LANES), 1) == LANES - 1, iota((src_count, LANES), 0) + 1, 0
    ).astype(jnp.float32).astype(jnp.bfloat16)
    number = jnp.dot(to_slot, number, preferred_element_type=jnp.float32)
    for copy in copies:
        copy.wait()
    acc = lax.dot_general(ext[...], weight[...], NT, preferred_element_type=jnp.float32)
    acc = acc[:, :LANES] + acc[:, LANES:]
    y = acc.astype(jnp.bfloat16)
    head = acc[:rows]
    head_lo = head - head.astype(jnp.bfloat16).astype(jnp.float32)
    tail = lax.dot_general(
        ext[(blocks - 1) * rows :, wide - LANES :], weight[:, :LANES], NT,
        preferred_element_type=jnp.float32,
    )
    tail = tail[:, :LANES] + tail[:, LANES:]
    tail_hi = tail.astype(jnp.bfloat16).astype(jnp.float32)
    lane = iota((rows, LANES), 1)
    edge = jnp.where(
        lane < EDGE,
        head_lo,
        jnp.where(
            lane < 2 * EDGE,
            pltpu.roll(tail_hi, EDGE, 1),
            jnp.where(lane < 3 * EDGE, pltpu.roll(tail - tail_hi, 2 * EDGE, 1), 0.0),
        ),
    ).astype(jnp.bfloat16)
    parts = [y[b * rows : (b + 1) * rows] for b in range(blocks)] + [edge]
    last = blocks * ch
    for t in range(steps):
        for b in range(blocks):
            out_ref[t, b * ch : (b + 1) * ch] = parts[b][t * ch : (t + 1) * ch]
        out_ref[t, last : last + ch] = edge[t * ch : (t + 1) * ch]
    for b, part in enumerate(parts):
        found = jnp.dot(pick, part, preferred_element_type=jnp.float32)
        if b == blocks:
            found += number
        slot_ref[:, b * LANES : (b + 1) * LANES] = found.astype(jnp.bfloat16)
    tables.wait()


def arrange_kernel(half, blocks, pieces, *refs):
    slots = jnp.concatenate([ref[...] for ref in refs[:pieces]], axis=0)
    part_ref, *out_refs = refs[pieces:]
    height = out_refs[0].shape[0]
    own_rows = part_ref.shape[1] - ROWS
    tile_rows = height - 2 * own_rows - blocks * half
    numbers = slots[:, blocks * LANES :].astype(jnp.float32)
    total = numbers.shape[0]
    numbers = jnp.sum(
        jnp.where(iota((total, LANES), 1) == LANES - 1, numbers, 0.0), axis=1, keepdims=True
    ).astype(jnp.int32)
    first = lax.axis_index("chan") % CORES * half
    pick = one_hot(numbers == iota((total, half), 1) + 1 + first)
    found = lax.dot_general(
        pick, slots, (((0,), (0,)), ((), ())), preferred_element_type=jnp.float32
    )
    fill = [found[:, b * LANES : (b + 1) * LANES].astype(jnp.bfloat16) for b in range(blocks)]
    edges = jnp.where(iota((half, LANES), 1) < 3 * EDGE, found[:, blocks * LANES :], 0.0)
    added = [jnp.zeros((ROWS, LANES), jnp.float32) for _ in range(tile_rows // ROWS)]
    for i in range(half // ROWS):
        tile, place = divmod(i + 2, PER_TILE)
        piece = edges[i * ROWS : (i + 1) * ROWS]
        added[tile] += pltpu.roll(piece, 3 * EDGE * place, 1) if place else piece
    me = lax.axis_index("tm")
    for k, out_ref in enumerate(out_refs):
        same = part_ref[me ^ (2 * k)]
        other = part_ref[me ^ (2 * k) ^ 1]
        out_ref[:own_rows] = same[:own_rows]
        out_ref[own_rows : 2 * own_rows] = other[:own_rows]
        for b in range(blocks):
            at = 2 * own_rows + b * half
            out_ref[at : at + half] = fill[b]
        mixed = same[own_rows:].astype(jnp.float32) + pltpu.roll(
            other[own_rows:].astype(jnp.float32), 3 * EDGE, 1
        )
        for tile, extra in enumerate(added):
            at = height - tile_rows + tile * ROWS
            out_ref[at : at + ROWS] = (extra + mixed if tile == 0 else extra).astype(jnp.bfloat16)


def forward_kernel(own_rows, block_ref, out_ref):
    out_ref[...] = block_ref[own_rows:]


def collect_kernel(own_rows, *refs):
    *block_refs, out_ref = refs
    highs = len(block_refs) // 2
    me = lax.axis_index("tm")
    for k in range(highs):
        out_ref[me ^ (2 * k)] = block_refs[k][2 * own_rows :]
        out_ref[me ^ (2 * k) ^ 1] = block_refs[highs + k][own_rows:]


def correlate_kernel(
    seg_count, src_count, dec, head_len, part_rows, count, steps, live_ref, tab_ref, *refs
):
    count_high = steps // 2
    block_refs, passed_refs = refs[:count_high], refs[count_high:steps]
    given_ref, far_ref, out_ref = refs[steps : steps + 3]
    mine_ref, mine_edge, trace, own, other, cross, result, sems = refs[steps + 3 :]
    ch = out_ref.shape[1]
    own_rows = mine_ref.shape[1]
    half = src_count // CORES
    rows = ch + src_count
    per_seg = SEG // dec
    blocks = dec // LANES
    d_cols = 4 * HALF

    @pl.when(pl.program_id(0) == 0)
    def _():
        me = lax.axis_index("tm")
        last = block_refs[0].shape[0] - edge_tiles(2 * ch + half) * ROWS
        for k, ref in enumerate(block_refs):
            mine_ref[me ^ (2 * k)] = ref[:own_rows]
            mine_edge[me ^ (2 * k)] = ref[last : last + ROWS].astype(jnp.float32)
        for k, ref in enumerate(passed_refs):
            mine_ref[me ^ (2 * k) ^ 1] = ref[:own_rows]
            pack = ref[last - own_rows : last - own_rows + ROWS].astype(jnp.float32)
            mine_edge[me ^ (2 * k) ^ 1] = pltpu.roll(pack, LANES - 3 * EDGE, 1)
        live = iota((ch, LANES), 0) < live_ref[0]
        before = jnp.zeros((rows, LANES), jnp.float32)
        is_head = iota((rows, LANES), 1) < head_len
        tile_rows = edge_tiles(2 * ch + half) * ROWS
        low_core = lax.axis_index("chan") % CORES == 0

        def edge_groups(ref, t):
            out = []
            last = ref.shape[1] - tile_rows
            for i in range(2, 2 + half // ROWS):
                tile, place = divmod(i, PER_TILE)
                pack = ref[t, last + tile * ROWS : last + (tile + 1) * ROWS].astype(jnp.float32)
                out.append(pltpu.roll(pack, LANES - 3 * EDGE * place, 1) if place else pack)
            return jnp.concatenate(out, axis=0)

        def in_order(near, far):
            return [jnp.where(low_core, near, far), jnp.where(low_core, far, near)]

        for t in range(steps):
            edge = jnp.where(live, mine_edge[t], 0.0)
            theirs = edge_groups(given_ref, t), edge_groups(far_ref, t)
            edge = jnp.concatenate([edge, *in_order(*theirs)], axis=0)
            for b in range(blocks):
                mine = mine_ref[t, b * ch : (b + 1) * ch]
                mine = jnp.where(live, mine, jnp.zeros_like(mine))
                rows_b = slice(b * half, (b + 1) * half)
                theirs = given_ref[t, rows_b], far_ref[t, rows_b]
                both = jnp.concatenate([mine, *in_order(*theirs)], axis=0)
                if b == 0:
                    tail = pltpu.roll(before, LANES - EDGE, 1) + pltpu.roll(before, LANES - 2 * EDGE, 1)
                    both = both.astype(jnp.float32)
                    both = jnp.where(is_head, both + edge + tail, both).astype(jnp.bfloat16)
                trace[t * rows : (t + 1) * rows, b * LANES : (b + 1) * LANES] = both
            before = edge
        odd = (iota((rows, 2 * LANES), 1) & 1) == 1
        sign = jnp.where(odd, -1.0, 1.0)
        same = one_hot(
            iota((2 * LANES, LANES), 0) % LANES // BAND == iota((2 * LANES, LANES), 1) // BAND
        )
        group_segs = max(1, min(seg_count, part_rows // (per_seg * rows)))
        for first in range(0, seg_count, group_segs):
            segs = min(group_segs, seg_count - first)
            lhs = trace[first * per_seg * rows : (first + segs) * per_seg * rows, :]
            for j in range(CHUNKS):
                acc = jnp.dot(
                    lhs, tab_ref[:, 4 * j * LANES : 4 * (j + 1) * LANES],
                    preferred_element_type=jnp.float32,
                )
                folded = acc[:, : 2 * LANES] + acc[:, 2 * LANES :]
                spec = []
                for g in range(segs):
                    a = folded[g * per_seg * rows : (g * per_seg + 1) * rows]
                    b = folded[(g * per_seg + 1) * rows : (g * per_seg + 2) * rows]
                    spec.append(a + sign * b)
                spec = jnp.concatenate(spec, axis=0)
                re, im = spec[:, :LANES], spec[:, LANES:]
                power = re * re + im * im
                hi = power.astype(jnp.bfloat16)
                lo = (power - hi.astype(jnp.float32)).astype(jnp.bfloat16)
                total = jnp.dot(
                    jnp.concatenate([hi, lo], axis=1), same, preferred_element_type=jnp.float32
                )
                scale = lax.rsqrt(total * (1.0 / BAND) + whiten_eps)
                w_re = (re * scale).astype(jnp.bfloat16).astype(jnp.float32)
                w_im = (im * scale).astype(jnp.bfloat16).astype(jnp.float32)
                at = 2 * j * LANES
                for g in range(segs):
                    r, o = g * rows, (first + g) * ch
                    own[o : o + ch, at : at + LANES] = w_re[r : r + ch]
                    own[o : o + ch, at + LANES : at + 2 * LANES] = w_im[r : r + ch]
                    o = (first + g) * src_count
                    other[o : o + src_count, at : at + LANES] = w_re[r + ch : r + rows]
                    other[o : o + src_count, at + LANES : at + 2 * LANES] = w_im[r + ch : r + rows]

    block = cross.shape[1] // ch
    copies = []
    for i in range(count):
        start = pl.multiple_of((pl.program_id(0) * count + i) * block, 8)
        for j in range(CHUNKS):
            at = 2 * j * LANES
            a_re = [own[g * ch : (g + 1) * ch, at : at + LANES] for g in range(seg_count)]
            a_im = [own[g * ch : (g + 1) * ch, at + LANES : at + 2 * LANES] for g in range(seg_count)]
            for s in range(block):
                if s % 8 == 0:
                    tiles = [
                        other[
                            pl.ds(pl.multiple_of(g * src_count + start + s, 8), 8),
                            at : at + 2 * LANES,
                        ]
                        for g in range(seg_count)
                    ]
                re = im = None
                for g in range(seg_count):
                    b_re = tiles[g][s % 8 : s % 8 + 1, :LANES]
                    b_im = tiles[g][s % 8 : s % 8 + 1, LANES:]
                    p = a_re[g] * b_re + a_im[g] * b_im
                    q = a_im[g] * b_re - a_re[g] * b_im
                    re, im = (p, q) if re is None else (re + p, im + q)
                row = slice(s * ch, (s + 1) * ch)
                cross[i, row, at : at + LANES] = re.astype(jnp.bfloat16)
                cross[i, row, at + LANES : at + 2 * LANES] = im.astype(jnp.bfloat16)
        lags = sum(
            jnp.dot(
                cross[i, :, h * dec : (h + 1) * dec],
                tab_ref[:, d_cols + 2 * LAGH * h : d_cols + 2 * LAGH * (h + 1)],
                preferred_element_type=jnp.float32,
            )
            for h in range(per_seg)
        )
        result[i] = lags.reshape(result.shape[1:])
        copy = pltpu.make_async_copy(result.at[i], out_ref.at[pl.ds(start, block)], sems.at[i])
        copy.start()
        copies.append(copy)
    for copy in copies:
        copy.wait()


def whole(space=pltpu.VMEM):
    return pl.BlockSpec(memory_space=space)


def local(raw_strain, fir_taps, source_channels, live_counts):
    rows, raw_len = raw_strain.shape
    steps = lax.axis_size("tm")
    chan_count = lax.axis_size("chan")
    dec = raw_len // DECIM
    blocks = dec // LANES
    ch = rows // steps
    seg_count = steps * dec // SEG
    src_count = source_channels.shape[0]
    slots = 2 * SRC_DEV * steps
    span = raw_len // blocks
    total_rows = ch + src_count
    half = src_count // CORES
    highs = steps // 2
    own_rows = blocks * ch
    given_rows = blocks * half + edge_tiles(2 * ch + half) * ROWS
    height = 2 * own_rows + given_rows
    head_len = -(-(fir_taps.shape[0] - 1) // DECIM)
    assert head_len < EDGE and ch == ROWS and src_count <= 256
    assert steps & (steps - 1) == 0 and chan_count & (chan_count - 1) == 0 and half % ROWS == 0
    src = source_channels.reshape(1, src_count)
    taps = fir_taps.reshape(1, fir_taps.shape[0])
    table = np.concatenate([dft_table(dec), *lag_table(seg_count).reshape(SEG // dec, dec, -1)], axis=1)
    inputs = (src, taps, raw_strain, jnp.asarray(table))
    part, picked, table = pl.pallas_call(
        functools.partial(filter_kernel, blocks),
        out_shape=[
            pltpu.VMEM((steps, (blocks + 1) * ch, LANES), jnp.bfloat16),
            pltpu.VMEM((slots, dec + LANES), jnp.bfloat16),
            pltpu.VMEM(table.shape, jnp.bfloat16),
        ],
        in_specs=[whole(pl.ANY)] * 4,
        out_specs=[whole(), whole(), whole(pl.ANY)],
        scratch_shapes=[
            pltpu.VMEM((blocks * rows, span + LANES), jnp.bfloat16),
            pltpu.VMEM((2 * LANES, span + LANES), jnp.bfloat16),
            pltpu.VMEM(src.shape, src.dtype),
            pltpu.VMEM(taps.shape, taps.dtype),
            pltpu.SemaphoreType.DMA((blocks + 3,)),
        ],
        compiler_params=pltpu.CompilerParams(vmem_limit_bytes=16 * MIB),
        name="fir",
    )(*(pltpu.with_memory_space_constraint(a, pltpu.HBM) for a in inputs))
    pieces = [picked] + [
        lax.ppermute(picked, "chan", [(c, c ^ k) for c in range(chan_count)])
        for k in range(1, chan_count)
    ]
    to_vmem = functools.partial(pltpu.with_memory_space_constraint, memory_space=pltpu.VMEM)
    outgoing = pl.pallas_call(
        functools.partial(arrange_kernel, half, blocks, chan_count),
        out_shape=[pltpu.VMEM((height, LANES), jnp.bfloat16)] * highs,
        in_specs=[whole()] * (chan_count + 1),
        out_specs=[whole()] * highs,
        compiler_params=pltpu.CompilerParams(vmem_limit_bytes=8 * MIB),
        name="arrange",
    )(*(to_vmem(a) for a in (*pieces, part)))
    arrived = [
        lax.ppermute(outgoing[k], "tm", [(t, t ^ (2 * k)) for t in range(steps)])
        for k in range(highs - 1, 0, -1)
    ]
    arrived = [to_vmem(a) for a in (outgoing[0], *arrived[::-1])]
    small = pltpu.CompilerParams(vmem_limit_bytes=8 * MIB)
    passed = [None] * highs
    for k in [0, 1, *range(highs - 1, 1, -1)]:
        direct = k == 1
        forward = pl.pallas_call(
            functools.partial(forward_kernel, own_rows),
            out_shape=pltpu.VMEM((own_rows + given_rows, LANES), jnp.bfloat16),
            in_specs=[whole()],
            out_specs=whole(),
            compiler_params=small,
            name="forward",
        )(to_vmem(outgoing[1]) if direct else arrived[k])
        to = [(t, t ^ (3 if direct else 1)) for t in range(steps)]
        passed[k] = to_vmem(lax.ppermute(forward, "tm", to))
    given = pl.pallas_call(
        functools.partial(collect_kernel, own_rows),
        out_shape=pltpu.VMEM((steps, given_rows, LANES), jnp.bfloat16),
        in_specs=[whole()] * steps,
        out_specs=whole(),
        compiler_params=small,
        name="collect",
    )(*arrived, *passed)
    swapped = lax.ppermute(given, "chan", [(c, c ^ 1) for c in range(chan_count)])
    block = math.gcd(src_count, 16)
    count = math.gcd(src_count // block, 2)
    state = seg_count * total_rows * SEG * 4
    return pl.pallas_call(
        functools.partial(
            correlate_kernel, seg_count, src_count, dec, head_len, 1024, count, steps
        ),
        grid=(src_count // (block * count),),
        out_shape=jax.ShapeDtypeStruct((src_count, ch, 2 * LAGH), jnp.float32),
        in_specs=[whole(pltpu.SMEM)] + [whole()] * (steps + 3),
        out_specs=whole(pl.ANY),
        scratch_shapes=[
            pltpu.VMEM((steps, own_rows, LANES), jnp.bfloat16),
            pltpu.VMEM((steps, ROWS, LANES), jnp.float32),
            pltpu.VMEM((steps * total_rows, dec), jnp.bfloat16),
            pltpu.VMEM((seg_count * ch, SEG), jnp.float32),
            pltpu.VMEM((seg_count * src_count, SEG), jnp.float32),
            pltpu.VMEM((count, block * ch, SEG), jnp.bfloat16),
            pltpu.VMEM((count, block, ch, 2 * LAGH), jnp.float32),
            pltpu.SemaphoreType.DMA((count,)),
        ],
        compiler_params=pltpu.CompilerParams(vmem_limit_bytes=16 * MIB + 2 * state),
        name="correlate",
    )(live_counts, table, *arrived, *passed, to_vmem(given), to_vmem(swapped))


def solution(mesh):
    placed = (P("chan", "tm"), P(), P(), P(("chan", "tm")))
    return jax.shard_map(
        local, mesh=mesh, in_specs=placed, out_specs=P(None, ("chan", "tm"), None), check_vma=False
    )
```

```python
import functools
import math

import jax
import jax.numpy as jnp
import ml_dtypes
import numpy as np
from jax import lax
from jax.experimental import pallas as pl
from jax.experimental.pallas import tpu as pltpu
from jax.sharding import PartitionSpec as P

DECIM = 10
SEG = 1024
BAND = 64
LAGH = 192
SRC_DEV = 1
LANES = 128
HALF = SEG // 2
CHUNKS = HALF // LANES
EDGE = 14
PER_TILE = LANES // (3 * EDGE)
ROWS = 16
CORES = 2
MIB = 1024 * 1024

whiten_eps = 1e-06

NT = (((1,), (1,)), ((), ()))


def split_table(table):
    hi = table.astype(ml_dtypes.bfloat16)
    lo = (table - hi.astype(np.float64)).astype(ml_dtypes.bfloat16)
    return hi, lo


def dft_table(rows):
    phase = (np.arange(rows)[:, None] * np.arange(HALF)[None, :] % SEG) * (2.0 * np.pi / SEG)
    parts = []
    for j in range(CHUNKS):
        cut = slice(j * LANES, (j + 1) * LANES)
        hi, lo = split_table(np.concatenate([np.cos(phase[:, cut]), -np.sin(phase[:, cut])], 1))
        parts += [hi, lo]
    return np.concatenate(parts, axis=1)


def lag_table(seg_count):
    freq = np.arange(HALF)[:, None]
    phase = (freq * np.arange(-LAGH, LAGH)[None, :] % SEG) * (2.0 * np.pi / SEG)
    weight = np.where(freq == 0, 1.0, 2.0) * (math.sqrt(SEG / seg_count) / SEG)
    re = (weight * np.cos(phase)).reshape(CHUNKS, LANES, 2 * LAGH)
    im = (-weight * np.sin(phase)).reshape(CHUNKS, LANES, 2 * LAGH)
    return np.concatenate([re, im], axis=1).reshape(SEG, 2 * LAGH).astype(ml_dtypes.bfloat16)


def iota(shape, dim):
    return lax.broadcasted_iota(jnp.int32, shape, dim)


def one_hot(mask):
    return jnp.where(mask, 1.0, 0.0).astype(jnp.bfloat16)


def column(row):
    n = row.shape[1]
    return jnp.sum(jnp.where(iota((n, n), 0) == iota((n, n), 1), row, 0), axis=1, keepdims=True)


def tap_rows(taps):
    tap_count = taps.shape[1]
    width = 3 * LANES
    flip = one_hot(iota((tap_count, width), 0) + iota((tap_count, width), 1) == tap_count)
    hi = taps.astype(jnp.bfloat16)
    lo = (taps - hi.astype(jnp.float32)).astype(jnp.bfloat16)
    out = []
    for part in (hi, lo):
        base = jnp.dot(
            jnp.broadcast_to(part.astype(jnp.float32), (8, tap_count)).astype(jnp.bfloat16),
            flip,
            preferred_element_type=jnp.float32,
        )
        upper = pltpu.roll(base, 0, 1, stride=DECIM, stride_axis=0)
        out.append(jnp.concatenate([upper, pltpu.roll(upper, 8 * DECIM, 1)], axis=0))
    return out


def edge_tiles(count):
    return -(-count // (PER_TILE * ROWS))


def filter_kernel(
    blocks,
    src_hbm, taps_hbm, raw_ref, tab_hbm,
    out_ref, slot_ref, tab_ref,
    ext, weight, src_ref, taps_ref, sems,
):
    rows, raw_len = raw_ref.shape
    steps = out_ref.shape[0]
    ch = rows // steps
    span = raw_len // blocks
    wide = span + LANES
    copies = []
    for b in range(blocks):
        if b == 0:
            copy = pltpu.make_async_copy(
                raw_ref.at[:, pl.ds(0, span)],
                ext.at[pl.ds(0, rows), pl.ds(LANES, span)],
                sems.at[b],
            )
        else:
            copy = pltpu.make_async_copy(
                raw_ref.at[:, pl.ds(b * span - LANES, wide)],
                ext.at[pl.ds(b * rows, rows), :],
                sems.at[b],
            )
        copy.start()
        copies.append(copy)
    small = [
        pltpu.make_async_copy(taps_hbm, taps_ref, sems.at[blocks]),
        pltpu.make_async_copy(src_hbm, src_ref, sems.at[blocks + 1]),
    ]
    tables = pltpu.make_async_copy(tab_hbm, tab_ref, sems.at[blocks + 2])
    for copy in [*small, tables]:
        copy.start()
    ext[:rows, :LANES] = jnp.zeros((rows, LANES), ext.dtype)
    weight[...] = jnp.zeros_like(weight)
    for copy in small:
        copy.wait()
    for p, base in enumerate(tap_rows(taps_ref[...])):
        for i in range(LANES // 16):
            tile, lane = divmod(16 * DECIM * i, LANES)
            piece = pltpu.roll(base, lane, 1) if lane else base
            weight[p * LANES + 16 * i : p * LANES + 16 * (i + 1), tile * LANES : (tile + 3) * LANES] = (
                piece.astype(jnp.bfloat16)
            )
    src = src_ref[...]
    src_count = src.shape[1]
    slots = slot_ref.shape[0]
    group = src // rows
    group_col = column(group)
    src_col = column(src)
    rank = jnp.sum(
        jnp.where(
            (group_col == group)
            & (iota((src_count, src_count), 0) < iota((src_count, src_count), 1)),
            1,
            0,
        ),
        axis=0,
        keepdims=True,
    )
    mine = lax.axis_index("chan")
    to_slot = one_hot((iota((slots, src_count), 0) == rank) & (group == mine))
    to_row = one_hot(src_col - mine * rows == iota((src_count, rows), 1))
    pick = jnp.dot(to_slot, to_row, preferred_element_type=jnp.float32).astype(jnp.bfloat16)
    number = jnp.where(
        iota((src_count, LANES), 1) == LANES - 1, iota((src_count, LANES), 0) + 1, 0
    ).astype(jnp.float32).astype(jnp.bfloat16)
    number = jnp.dot(to_slot, number, preferred_element_type=jnp.float32)
    for copy in copies:
        copy.wait()
    acc = lax.dot_general(ext[...], weight[...], NT, preferred_element_type=jnp.float32)
    acc = acc[:, :LANES] + acc[:, LANES:]
    y = acc.astype(jnp.bfloat16)
    head = acc[:rows]
    head_lo = head - head.astype(jnp.bfloat16).astype(jnp.float32)
    tail = lax.dot_general(
        ext[(blocks - 1) * rows :, wide - LANES :], weight[:, :LANES], NT,
        preferred_element_type=jnp.float32,
    )
    tail = tail[:, :LANES] + tail[:, LANES:]
    tail_hi = tail.astype(jnp.bfloat16).astype(jnp.float32)
    lane = iota((rows, LANES), 1)
    edge = jnp.where(
        lane < EDGE,
        head_lo,
        jnp.where(
            lane < 2 * EDGE,
            pltpu.roll(tail_hi, EDGE, 1),
            jnp.where(lane < 3 * EDGE, pltpu.roll(tail - tail_hi, 2 * EDGE, 1), 0.0),
        ),
    ).astype(jnp.bfloat16)
    parts = [y[b * rows : (b + 1) * rows] for b in range(blocks)] + [edge]
    last = blocks * ch
    for t in range(steps):
        for b in range(blocks):
            out_ref[t, b * ch : (b + 1) * ch] = parts[b][t * ch : (t + 1) * ch]
        out_ref[t, last : last + ch] = edge[t * ch : (t + 1) * ch]
    for b, part in enumerate(parts):
        found = jnp.dot(pick, part, preferred_element_type=jnp.float32)
        if b == blocks:
            found += number
        slot_ref[:, b * LANES : (b + 1) * LANES] = found.astype(jnp.bfloat16)
    tables.wait()


def arrange_kernel(half, blocks, pieces, *refs):
    slots = jnp.concatenate([ref[...] for ref in refs[:pieces]], axis=0)
    part_ref, *out_refs = refs[pieces:]
    height = out_refs[0].shape[0]
    own_rows = part_ref.shape[1] - ROWS
    tile_rows = height - 2 * own_rows - blocks * half
    numbers = slots[:, blocks * LANES :].astype(jnp.float32)
    total = numbers.shape[0]
    numbers = jnp.sum(
        jnp.where(iota((total, LANES), 1) == LANES - 1, numbers, 0.0), axis=1, keepdims=True
    ).astype(jnp.int32)
    first = lax.axis_index("chan") % CORES * half
    pick = one_hot(numbers == iota((total, half), 1) + 1 + first)
    found = lax.dot_general(
        pick, slots, (((0,), (0,)), ((), ())), preferred_element_type=jnp.float32
    )
    fill = [found[:, b * LANES : (b + 1) * LANES].astype(jnp.bfloat16) for b in range(blocks)]
    edges = jnp.where(iota((half, LANES), 1) < 3 * EDGE, found[:, blocks * LANES :], 0.0)
    added = [jnp.zeros((ROWS, LANES), jnp.float32) for _ in range(tile_rows // ROWS)]
    for i in range(half // ROWS):
        tile, place = divmod(i + 2, PER_TILE)
        piece = edges[i * ROWS : (i + 1) * ROWS]
        added[tile] += pltpu.roll(piece, 3 * EDGE * place, 1) if place else piece
    me = lax.axis_index("tm")
    *out_refs, direct_ref = out_refs
    for k, out_ref in enumerate(out_refs):
        same = part_ref[me ^ (2 * k)]
        other = part_ref[me ^ (2 * k) ^ 1]
        mixed = same[own_rows:].astype(jnp.float32) + pltpu.roll(
            other[own_rows:].astype(jnp.float32), 3 * EDGE, 1
        )
        if k == 1:
            writes = [(out_ref, [same]), (direct_ref, [other])]
        else:
            writes = [(out_ref, [same, other])]
        for ref, owners in writes:
            at = 0
            for owner in owners:
                ref[at : at + own_rows] = owner[:own_rows]
                at += own_rows
            for piece in fill:
                ref[at : at + half] = piece
                at += half
            for tile, extra in enumerate(added):
                ref[at : at + ROWS] = (extra + mixed if tile == 0 else extra).astype(jnp.bfloat16)
                at += ROWS


def forward_kernel(own_rows, block_ref, out_ref):
    out_ref[...] = block_ref[own_rows:]


def direct_first(refs):
    return [refs[1], refs[0], *refs[2:]]


def collect_kernel(own_rows, *refs):
    *block_refs, out_ref = refs
    highs = len(block_refs) // 2
    passed_refs = direct_first(block_refs[highs:])
    me = lax.axis_index("tm")
    for k in range(highs):
        out_ref[me ^ (2 * k)] = block_refs[k][block_refs[k].shape[0] - out_ref.shape[1] :]
        out_ref[me ^ (2 * k) ^ 1] = passed_refs[k][own_rows:]


def correlate_kernel(
    seg_count, src_count, dec, head_len, part_rows, count, steps, live_ref, tab_ref, *refs
):
    count_high = steps // 2
    block_refs, passed_refs = refs[:count_high], direct_first(refs[count_high:steps])
    given_ref, far_ref, out_ref = refs[steps : steps + 3]
    mine_ref, mine_edge, trace, own, other, cross, result, sems = refs[steps + 3 :]
    ch = out_ref.shape[1]
    own_rows = mine_ref.shape[1]
    half = src_count // CORES
    rows = ch + src_count
    per_seg = SEG // dec
    blocks = dec // LANES
    d_cols = 4 * HALF

    @pl.when(pl.program_id(0) == 0)
    def _():
        me = lax.axis_index("tm")
        last = block_refs[0].shape[0] - edge_tiles(2 * ch + half) * ROWS
        for k, ref in enumerate(block_refs):
            mine_ref[me ^ (2 * k)] = ref[:own_rows]
            at = ref.shape[0] - (block_refs[0].shape[0] - last)
            mine_edge[me ^ (2 * k)] = ref[at : at + ROWS].astype(jnp.float32)
        for k, ref in enumerate(passed_refs):
            mine_ref[me ^ (2 * k) ^ 1] = ref[:own_rows]
            pack = ref[last - own_rows : last - own_rows + ROWS].astype(jnp.float32)
            mine_edge[me ^ (2 * k) ^ 1] = pltpu.roll(pack, LANES - 3 * EDGE, 1)
        live = iota((ch, LANES), 0) < live_ref[0]
        before = jnp.zeros((rows, LANES), jnp.float32)
        is_head = iota((rows, LANES), 1) < head_len
        tile_rows = edge_tiles(2 * ch + half) * ROWS
        low_core = lax.axis_index("chan") % CORES == 0

        def edge_groups(ref, t):
            out = []
            last = ref.shape[1] - tile_rows
            for i in range(2, 2 + half // ROWS):
                tile, place = divmod(i, PER_TILE)
                pack = ref[t, last + tile * ROWS : last + (tile + 1) * ROWS].astype(jnp.float32)
                out.append(pltpu.roll(pack, LANES - 3 * EDGE * place, 1) if place else pack)
            return jnp.concatenate(out, axis=0)

        def in_order(near, far):
            return [jnp.where(low_core, near, far), jnp.where(low_core, far, near)]

        for t in range(steps):
            edge = jnp.where(live, mine_edge[t], 0.0)
            theirs = edge_groups(given_ref, t), edge_groups(far_ref, t)
            edge = jnp.concatenate([edge, *in_order(*theirs)], axis=0)
            for b in range(blocks):
                mine = mine_ref[t, b * ch : (b + 1) * ch]
                mine = jnp.where(live, mine, jnp.zeros_like(mine))
                rows_b = slice(b * half, (b + 1) * half)
                theirs = given_ref[t, rows_b], far_ref[t, rows_b]
                both = jnp.concatenate([mine, *in_order(*theirs)], axis=0)
                if b == 0:
                    tail = pltpu.roll(before, LANES - EDGE, 1) + pltpu.roll(before, LANES - 2 * EDGE, 1)
                    both = both.astype(jnp.float32)
                    both = jnp.where(is_head, both + edge + tail, both).astype(jnp.bfloat16)
                trace[t * rows : (t + 1) * rows, b * LANES : (b + 1) * LANES] = both
            before = edge
        odd = (iota((rows, 2 * LANES), 1) & 1) == 1
        sign = jnp.where(odd, -1.0, 1.0)
        same = one_hot(
            iota((2 * LANES, LANES), 0) % LANES // BAND == iota((2 * LANES, LANES), 1) // BAND
        )
        group_segs = max(1, min(seg_count, part_rows // (per_seg * rows)))
        for first in range(0, seg_count, group_segs):
            segs = min(group_segs, seg_count - first)
            lhs = trace[first * per_seg * rows : (first + segs) * per_seg * rows, :]
            for j in range(CHUNKS):
                acc = jnp.dot(
                    lhs, tab_ref[:, 4 * j * LANES : 4 * (j + 1) * LANES],
                    preferred_element_type=jnp.float32,
                )
                folded = acc[:, : 2 * LANES] + acc[:, 2 * LANES :]
                spec = []
                for g in range(segs):
                    a = folded[g * per_seg * rows : (g * per_seg + 1) * rows]
                    b = folded[(g * per_seg + 1) * rows : (g * per_seg + 2) * rows]
                    spec.append(a + sign * b)
                spec = jnp.concatenate(spec, axis=0)
                re, im = spec[:, :LANES], spec[:, LANES:]
                power = re * re + im * im
                hi = power.astype(jnp.bfloat16)
                lo = (power - hi.astype(jnp.float32)).astype(jnp.bfloat16)
                total = jnp.dot(
                    jnp.concatenate([hi, lo], axis=1), same, preferred_element_type=jnp.float32
                )
                scale = lax.rsqrt(total * (1.0 / BAND) + whiten_eps)
                w_re = (re * scale).astype(jnp.bfloat16).astype(jnp.float32)
                w_im = (im * scale).astype(jnp.bfloat16).astype(jnp.float32)
                at = 2 * j * LANES
                for g in range(segs):
                    r, o = g * rows, (first + g) * ch
                    own[o : o + ch, at : at + LANES] = w_re[r : r + ch]
                    own[o : o + ch, at + LANES : at + 2 * LANES] = w_im[r : r + ch]
                    o = (first + g) * src_count
                    other[o : o + src_count, at : at + LANES] = w_re[r + ch : r + rows]
                    other[o : o + src_count, at + LANES : at + 2 * LANES] = w_im[r + ch : r + rows]

    block = cross.shape[1] // ch
    copies = []
    for i in range(count):
        start = pl.multiple_of((pl.program_id(0) * count + i) * block, 8)
        for j in range(CHUNKS):
            at = 2 * j * LANES
            a_re = [own[g * ch : (g + 1) * ch, at : at + LANES] for g in range(seg_count)]
            a_im = [own[g * ch : (g + 1) * ch, at + LANES : at + 2 * LANES] for g in range(seg_count)]
            for s in range(block):
                if s % 8 == 0:
                    tiles = [
                        other[
                            pl.ds(pl.multiple_of(g * src_count + start + s, 8), 8),
                            at : at + 2 * LANES,
                        ]
                        for g in range(seg_count)
                    ]
                re = im = None
                for g in range(seg_count):
                    b_re = tiles[g][s % 8 : s % 8 + 1, :LANES]
                    b_im = tiles[g][s % 8 : s % 8 + 1, LANES:]
                    p = a_re[g] * b_re + a_im[g] * b_im
                    q = a_im[g] * b_re - a_re[g] * b_im
                    re, im = (p, q) if re is None else (re + p, im + q)
                row = slice(s * ch, (s + 1) * ch)
                cross[i, row, at : at + LANES] = re.astype(jnp.bfloat16)
                cross[i, row, at + LANES : at + 2 * LANES] = im.astype(jnp.bfloat16)
        lags = sum(
            jnp.dot(
                cross[i, :, h * dec : (h + 1) * dec],
                tab_ref[:, d_cols + 2 * LAGH * h : d_cols + 2 * LAGH * (h + 1)],
                preferred_element_type=jnp.float32,
            )
            for h in range(per_seg)
        )
        result[i] = lags.reshape(result.shape[1:])
        copy = pltpu.make_async_copy(result.at[i], out_ref.at[pl.ds(start, block)], sems.at[i])
        copy.start()
        copies.append(copy)
    for copy in copies:
        copy.wait()


def whole(space=pltpu.VMEM):
    return pl.BlockSpec(memory_space=space)


def local(raw_strain, fir_taps, source_channels, live_counts):
    rows, raw_len = raw_strain.shape
    steps = lax.axis_size("tm")
    chan_count = lax.axis_size("chan")
    dec = raw_len // DECIM
    blocks = dec // LANES
    ch = rows // steps
    seg_count = steps * dec // SEG
    src_count = source_channels.shape[0]
    slots = 2 * SRC_DEV * steps
    span = raw_len // blocks
    total_rows = ch + src_count
    half = src_count // CORES
    highs = steps // 2
    own_rows = blocks * ch
    given_rows = blocks * half + edge_tiles(2 * ch + half) * ROWS
    height = 2 * own_rows + given_rows
    head_len = -(-(fir_taps.shape[0] - 1) // DECIM)
    assert head_len < EDGE and ch == ROWS and src_count <= 256
    assert steps >= 8 and steps & (steps - 1) == 0 and chan_count & (chan_count - 1) == 0 and half % ROWS == 0
    src = source_channels.reshape(1, src_count)
    taps = fir_taps.reshape(1, fir_taps.shape[0])
    table = np.concatenate([dft_table(dec), *lag_table(seg_count).reshape(SEG // dec, dec, -1)], axis=1)
    inputs = (src, taps, raw_strain, jnp.asarray(table))
    part, picked, table = pl.pallas_call(
        functools.partial(filter_kernel, blocks),
        out_shape=[
            pltpu.VMEM((steps, (blocks + 1) * ch, LANES), jnp.bfloat16),
            pltpu.VMEM((slots, dec + LANES), jnp.bfloat16),
            pltpu.VMEM(table.shape, jnp.bfloat16),
        ],
        in_specs=[whole(pl.ANY)] * 4,
        out_specs=[whole(), whole(), whole(pl.ANY)],
        scratch_shapes=[
            pltpu.VMEM((blocks * rows, span + LANES), jnp.bfloat16),
            pltpu.VMEM((2 * LANES, span + LANES), jnp.bfloat16),
            pltpu.VMEM(src.shape, src.dtype),
            pltpu.VMEM(taps.shape, taps.dtype),
            pltpu.SemaphoreType.DMA((blocks + 3,)),
        ],
        compiler_params=pltpu.CompilerParams(vmem_limit_bytes=16 * MIB),
        name="fir",
    )(*(pltpu.with_memory_space_constraint(a, pltpu.HBM) for a in inputs))
    pieces = [picked] + [
        lax.ppermute(picked, "chan", [(c, c ^ k) for c in range(chan_count)])
        for k in range(1, chan_count)
    ]
    to_vmem = functools.partial(pltpu.with_memory_space_constraint, memory_space=pltpu.VMEM)
    outgoing = pl.pallas_call(
        functools.partial(arrange_kernel, half, blocks, chan_count),
        out_shape=[
            pltpu.VMEM((rows_k, LANES), jnp.bfloat16)
            for rows_k in [height, height - own_rows, *[height] * (highs - 2), height - own_rows]
        ],
        in_specs=[whole()] * (chan_count + 1),
        out_specs=[whole()] * (highs + 1),
        compiler_params=pltpu.CompilerParams(vmem_limit_bytes=8 * MIB),
        name="arrange",
    )(*(to_vmem(a) for a in (*pieces, part)))
    arrived = [
        lax.ppermute(outgoing[k], "tm", [(t, t ^ (2 * k)) for t in range(steps)])
        for k in range(highs - 1, 0, -1)
    ]
    arrived = [to_vmem(a) for a in (outgoing[0], *arrived[::-1])]
    small = pltpu.CompilerParams(vmem_limit_bytes=8 * MIB)
    passed = [None] * highs
    for k in [1, 0, *range(highs - 1, 1, -1)]:
        if k == 1:
            forward, by = outgoing[highs], 3
        else:
            by = 1
            forward = pl.pallas_call(
                functools.partial(forward_kernel, own_rows),
                out_shape=pltpu.VMEM((own_rows + given_rows, LANES), jnp.bfloat16),
                in_specs=[whole()],
                out_specs=whole(),
                compiler_params=small,
                name="forward",
            )(arrived[k])
        passed[k] = to_vmem(lax.ppermute(forward, "tm", [(t, t ^ by) for t in range(steps)]))
    passed = direct_first(passed)
    given = pl.pallas_call(
        functools.partial(collect_kernel, own_rows),
        out_shape=pltpu.VMEM((steps, given_rows, LANES), jnp.bfloat16),
        in_specs=[whole()] * steps,
        out_specs=whole(),
        compiler_params=small,
        name="collect",
    )(*arrived, *passed)
    swapped = lax.ppermute(given, "chan", [(c, c ^ 1) for c in range(chan_count)])
    block = math.gcd(src_count, 16)
    count = math.gcd(src_count // block, 2)
    state = seg_count * total_rows * SEG * 4
    return pl.pallas_call(
        functools.partial(
            correlate_kernel, seg_count, src_count, dec, head_len, 1024, count, steps
        ),
        grid=(src_count // (block * count),),
        out_shape=jax.ShapeDtypeStruct((src_count, ch, 2 * LAGH), jnp.float32),
        in_specs=[whole(pltpu.SMEM)] + [whole()] * (steps + 3),
        out_specs=whole(pl.ANY),
        scratch_shapes=[
            pltpu.VMEM((steps, own_rows, LANES), jnp.bfloat16),
            pltpu.VMEM((steps, ROWS, LANES), jnp.float32),
            pltpu.VMEM((steps * total_rows, dec), jnp.bfloat16),
            pltpu.VMEM((seg_count * ch, SEG), jnp.float32),
            pltpu.VMEM((seg_count * src_count, SEG), jnp.float32),
            pltpu.VMEM((count, block * ch, SEG), jnp.bfloat16),
            pltpu.VMEM((count, block, ch, 2 * LAGH), jnp.float32),
            pltpu.SemaphoreType.DMA((count,)),
        ],
        compiler_params=pltpu.CompilerParams(vmem_limit_bytes=16 * MIB + 2 * state),
        name="correlate",
    )(live_counts, table, *arrived, *passed, to_vmem(given), to_vmem(swapped))


def solution(mesh):
    placed = (P("chan", "tm"), P(), P(), P(("chan", "tm")))
    return jax.shard_map(
        local, mesh=mesh, in_specs=placed, out_specs=P(None, ("chan", "tm"), None), check_vma=False
    )
```

```python
import functools
import math

import jax
import jax.numpy as jnp
import ml_dtypes
import numpy as np
from jax import lax
from jax.experimental import pallas as pl
from jax.experimental.pallas import tpu as pltpu
from jax.sharding import PartitionSpec as P

DECIM = 10
SEG = 1024
BAND = 64
LAGH = 192
SRC_DEV = 1
LANES = 128
HALF = SEG // 2
CHUNKS = HALF // LANES
EDGE = 14
PER_TILE = LANES // (3 * EDGE)
ROWS = 16
CORES = 2
MIB = 1024 * 1024

whiten_eps = 1e-06

NT = (((1,), (1,)), ((), ()))


def split_table(table):
    hi = table.astype(ml_dtypes.bfloat16)
    lo = (table - hi.astype(np.float64)).astype(ml_dtypes.bfloat16)
    return hi, lo


def dft_table(rows):
    phase = (np.arange(rows)[:, None] * np.arange(HALF)[None, :] % SEG) * (2.0 * np.pi / SEG)
    parts = []
    for j in range(CHUNKS):
        cut = slice(j * LANES, (j + 1) * LANES)
        hi, lo = split_table(np.concatenate([np.cos(phase[:, cut]), -np.sin(phase[:, cut])], 1))
        parts += [hi, lo]
    return np.concatenate(parts, axis=1)


def lag_table(seg_count):
    freq = np.arange(HALF)[:, None]
    phase = (freq * np.arange(-LAGH, LAGH)[None, :] % SEG) * (2.0 * np.pi / SEG)
    weight = np.where(freq == 0, 1.0, 2.0) * (math.sqrt(SEG / seg_count) / SEG)
    re = (weight * np.cos(phase)).reshape(CHUNKS, LANES, 2 * LAGH)
    im = (-weight * np.sin(phase)).reshape(CHUNKS, LANES, 2 * LAGH)
    return np.concatenate([re, im], axis=1).reshape(SEG, 2 * LAGH).astype(ml_dtypes.bfloat16)


def iota(shape, dim):
    return lax.broadcasted_iota(jnp.int32, shape, dim)


def one_hot(mask):
    return jnp.where(mask, 1.0, 0.0).astype(jnp.bfloat16)


def column(row):
    n = row.shape[1]
    return jnp.sum(jnp.where(iota((n, n), 0) == iota((n, n), 1), row, 0), axis=1, keepdims=True)


def tap_rows(taps):
    tap_count = taps.shape[1]
    width = 3 * LANES
    flip = one_hot(iota((tap_count, width), 0) + iota((tap_count, width), 1) == tap_count)
    hi = taps.astype(jnp.bfloat16)
    lo = (taps - hi.astype(jnp.float32)).astype(jnp.bfloat16)
    out = []
    for part in (hi, lo):
        base = jnp.dot(
            jnp.broadcast_to(part.astype(jnp.float32), (8, tap_count)).astype(jnp.bfloat16),
            flip,
            preferred_element_type=jnp.float32,
        )
        upper = pltpu.roll(base, 0, 1, stride=DECIM, stride_axis=0)
        out.append(jnp.concatenate([upper, pltpu.roll(upper, 8 * DECIM, 1)], axis=0))
    return out


def edge_tiles(count):
    return -(-count // (PER_TILE * ROWS))


def filter_kernel(
    blocks,
    src_hbm, taps_hbm, raw_ref, tab_hbm,
    out_ref, slot_ref, tab_ref,
    ext, weight, src_ref, taps_ref, sems,
):
    rows, raw_len = raw_ref.shape
    steps = out_ref.shape[0]
    ch = rows // steps
    span = raw_len // blocks
    wide = span + LANES
    small = [
        pltpu.make_async_copy(taps_hbm, taps_ref, sems.at[blocks]),
        pltpu.make_async_copy(src_hbm, src_ref, sems.at[blocks + 1]),
    ]
    for copy in small:
        copy.start()
    copies = []
    for b in range(blocks):
        if b == 0:
            copy = pltpu.make_async_copy(
                raw_ref.at[:, pl.ds(0, span)],
                ext.at[pl.ds(0, rows), pl.ds(LANES, span)],
                sems.at[b],
            )
        else:
            copy = pltpu.make_async_copy(
                raw_ref.at[:, pl.ds(b * span - LANES, wide)],
                ext.at[pl.ds(b * rows, rows), :],
                sems.at[b],
            )
        copy.start()
        copies.append(copy)
    tables = pltpu.make_async_copy(tab_hbm, tab_ref, sems.at[blocks + 2])
    tables.start()
    ext[:rows, :LANES] = jnp.zeros((rows, LANES), ext.dtype)
    weight[...] = jnp.zeros_like(weight)
    for copy in small:
        copy.wait()
    for p, base in enumerate(tap_rows(taps_ref[...])):
        for i in range(LANES // 16):
            tile, lane = divmod(16 * DECIM * i, LANES)
            piece = pltpu.roll(base, lane, 1) if lane else base
            weight[p * LANES + 16 * i : p * LANES + 16 * (i + 1), tile * LANES : (tile + 3) * LANES] = (
                piece.astype(jnp.bfloat16)
            )
    src = src_ref[...]
    src_count = src.shape[1]
    slots = slot_ref.shape[0]
    group = src // rows
    group_col = column(group)
    src_col = column(src)
    rank = jnp.sum(
        jnp.where(
            (group_col == group)
            & (iota((src_count, src_count), 0) < iota((src_count, src_count), 1)),
            1,
            0,
        ),
        axis=0,
        keepdims=True,
    )
    mine = lax.axis_index("chan")
    to_slot = one_hot((iota((slots, src_count), 0) == rank) & (group == mine))
    to_row = one_hot(src_col - mine * rows == iota((src_count, rows), 1))
    pick = jnp.dot(to_slot, to_row, preferred_element_type=jnp.float32).astype(jnp.bfloat16)
    number = jnp.where(
        iota((src_count, LANES), 1) == LANES - 1, iota((src_count, LANES), 0) + 1, 0
    ).astype(jnp.float32).astype(jnp.bfloat16)
    number = jnp.dot(to_slot, number, preferred_element_type=jnp.float32)
    for copy in copies:
        copy.wait()
    acc = lax.dot_general(ext[...], weight[...], NT, preferred_element_type=jnp.float32)
    acc = acc[:, :LANES] + acc[:, LANES:]
    y = acc.astype(jnp.bfloat16)
    head = acc[:rows]
    head_lo = head - head.astype(jnp.bfloat16).astype(jnp.float32)
    tail = lax.dot_general(
        ext[(blocks - 1) * rows :, wide - LANES :], weight[:, :LANES], NT,
        preferred_element_type=jnp.float32,
    )
    tail = tail[:, :LANES] + tail[:, LANES:]
    tail_hi = tail.astype(jnp.bfloat16).astype(jnp.float32)
    lane = iota((rows, LANES), 1)
    edge = jnp.where(
        lane < EDGE,
        head_lo,
        jnp.where(
            lane < 2 * EDGE,
            pltpu.roll(tail_hi, EDGE, 1),
            jnp.where(lane < 3 * EDGE, pltpu.roll(tail - tail_hi, 2 * EDGE, 1), 0.0),
        ),
    ).astype(jnp.bfloat16)
    parts = [y[b * rows : (b + 1) * rows] for b in range(blocks)] + [edge]
    last = blocks * ch
    for t in range(steps):
        for b in range(blocks):
            out_ref[t, b * ch : (b + 1) * ch] = parts[b][t * ch : (t + 1) * ch]
        out_ref[t, last : last + ch] = edge[t * ch : (t + 1) * ch]
    for b, part in enumerate(parts):
        found = jnp.dot(pick, part, preferred_element_type=jnp.float32)
        if b == blocks:
            found += number
        slot_ref[:, b * LANES : (b + 1) * LANES] = found.astype(jnp.bfloat16)
    tables.wait()


def arrange_kernel(half, blocks, pieces, *refs):
    slots = jnp.concatenate([ref[...] for ref in refs[:pieces]], axis=0)
    part_ref, *out_refs = refs[pieces:]
    height = out_refs[0].shape[0]
    own_rows = part_ref.shape[1] - ROWS
    tile_rows = height - 2 * own_rows - blocks * half
    numbers = slots[:, blocks * LANES :].astype(jnp.float32)
    total = numbers.shape[0]
    numbers = jnp.sum(
        jnp.where(iota((total, LANES), 1) == LANES - 1, numbers, 0.0), axis=1, keepdims=True
    ).astype(jnp.int32)
    first = lax.axis_index("chan") % CORES * half
    pick = one_hot(numbers == iota((total, half), 1) + 1 + first)
    found = lax.dot_general(
        pick, slots, (((0,), (0,)), ((), ())), preferred_element_type=jnp.float32
    )
    fill = [found[:, b * LANES : (b + 1) * LANES].astype(jnp.bfloat16) for b in range(blocks)]
    edges = jnp.where(iota((half, LANES), 1) < 3 * EDGE, found[:, blocks * LANES :], 0.0)
    added = [jnp.zeros((ROWS, LANES), jnp.float32) for _ in range(tile_rows // ROWS)]
    for i in range(half // ROWS):
        tile, place = divmod(i + 2, PER_TILE)
        piece = edges[i * ROWS : (i + 1) * ROWS]
        added[tile] += pltpu.roll(piece, 3 * EDGE * place, 1) if place else piece
    me = lax.axis_index("tm")
    *out_refs, direct_ref = out_refs
    for k, out_ref in enumerate(out_refs):
        same = part_ref[me ^ (2 * k)]
        other = part_ref[me ^ (2 * k) ^ 1]
        mixed = same[own_rows:].astype(jnp.float32) + pltpu.roll(
            other[own_rows:].astype(jnp.float32), 3 * EDGE, 1
        )
        if k == 1:
            writes = [(out_ref, [same]), (direct_ref, [other])]
        else:
            writes = [(out_ref, [same, other])]
        for ref, owners in writes:
            at = 0
            for owner in owners:
                ref[at : at + own_rows] = owner[:own_rows]
                at += own_rows
            for piece in fill:
                ref[at : at + half] = piece
                at += half
            for tile, extra in enumerate(added):
                ref[at : at + ROWS] = (extra + mixed if tile == 0 else extra).astype(jnp.bfloat16)
                at += ROWS


def forward_kernel(own_rows, block_ref, out_ref):
    out_ref[...] = block_ref[own_rows:]


def direct_first(refs):
    return [refs[1], refs[0], *refs[2:]]


def collect_kernel(own_rows, *refs):
    *block_refs, out_ref = refs
    highs = len(block_refs) // 2
    passed_refs = direct_first(block_refs[highs:])
    me = lax.axis_index("tm")
    for k in range(highs):
        out_ref[me ^ (2 * k)] = block_refs[k][block_refs[k].shape[0] - out_ref.shape[1] :]
        out_ref[me ^ (2 * k) ^ 1] = passed_refs[k][own_rows:]


def correlate_kernel(
    seg_count, src_count, dec, head_len, part_rows, count, steps, live_ref, tab_ref, *refs
):
    count_high = steps // 2
    block_refs, passed_refs = refs[:count_high], direct_first(refs[count_high:steps])
    given_ref, far_ref, out_ref = refs[steps : steps + 3]
    mine_ref, mine_edge, trace, own, other, cross, result, sems = refs[steps + 3 :]
    ch = out_ref.shape[1]
    own_rows = mine_ref.shape[1]
    half = src_count // CORES
    rows = ch + src_count
    per_seg = SEG // dec
    blocks = dec // LANES
    d_cols = 4 * HALF

    @pl.when(pl.program_id(0) == 0)
    def _():
        me = lax.axis_index("tm")
        last = block_refs[0].shape[0] - edge_tiles(2 * ch + half) * ROWS
        for k, ref in enumerate(block_refs):
            mine_ref[me ^ (2 * k)] = ref[:own_rows]
            at = ref.shape[0] - (block_refs[0].shape[0] - last)
            mine_edge[me ^ (2 * k)] = ref[at : at + ROWS].astype(jnp.float32)
        for k, ref in enumerate(passed_refs):
            mine_ref[me ^ (2 * k) ^ 1] = ref[:own_rows]
            pack = ref[last - own_rows : last - own_rows + ROWS].astype(jnp.float32)
            mine_edge[me ^ (2 * k) ^ 1] = pltpu.roll(pack, LANES - 3 * EDGE, 1)
        live = iota((ch, LANES), 0) < live_ref[0]
        before = jnp.zeros((rows, LANES), jnp.float32)
        is_head = iota((rows, LANES), 1) < head_len
        tile_rows = edge_tiles(2 * ch + half) * ROWS
        low_core = lax.axis_index("chan") % CORES == 0

        def edge_groups(ref, t):
            out = []
            last = ref.shape[1] - tile_rows
            for i in range(2, 2 + half // ROWS):
                tile, place = divmod(i, PER_TILE)
                pack = ref[t, last + tile * ROWS : last + (tile + 1) * ROWS].astype(jnp.float32)
                out.append(pltpu.roll(pack, LANES - 3 * EDGE * place, 1) if place else pack)
            return jnp.concatenate(out, axis=0)

        def in_order(near, far):
            return [jnp.where(low_core, near, far), jnp.where(low_core, far, near)]

        for t in range(steps):
            edge = jnp.where(live, mine_edge[t], 0.0)
            theirs = edge_groups(given_ref, t), edge_groups(far_ref, t)
            edge = jnp.concatenate([edge, *in_order(*theirs)], axis=0)
            for b in range(blocks):
                mine = mine_ref[t, b * ch : (b + 1) * ch]
                mine = jnp.where(live, mine, jnp.zeros_like(mine))
                rows_b = slice(b * half, (b + 1) * half)
                theirs = given_ref[t, rows_b], far_ref[t, rows_b]
                both = jnp.concatenate([mine, *in_order(*theirs)], axis=0)
                if b == 0:
                    tail = pltpu.roll(before, LANES - EDGE, 1) + pltpu.roll(before, LANES - 2 * EDGE, 1)
                    both = both.astype(jnp.float32)
                    both = jnp.where(is_head, both + edge + tail, both).astype(jnp.bfloat16)
                trace[t * rows : (t + 1) * rows, b * LANES : (b + 1) * LANES] = both
            before = edge
        odd = (iota((rows, 2 * LANES), 1) & 1) == 1
        sign = jnp.where(odd, -1.0, 1.0)
        same = one_hot(
            iota((2 * LANES, LANES), 0) % LANES // BAND == iota((2 * LANES, LANES), 1) // BAND
        )
        group_segs = max(1, min(seg_count, part_rows // (per_seg * rows)))
        for first in range(0, seg_count, group_segs):
            segs = min(group_segs, seg_count - first)
            lhs = trace[first * per_seg * rows : (first + segs) * per_seg * rows, :]
            for j in range(CHUNKS):
                acc = jnp.dot(
                    lhs, tab_ref[:, 4 * j * LANES : 4 * (j + 1) * LANES],
                    preferred_element_type=jnp.float32,
                )
                folded = acc[:, : 2 * LANES] + acc[:, 2 * LANES :]
                spec = []
                for g in range(segs):
                    a = folded[g * per_seg * rows : (g * per_seg + 1) * rows]
                    b = folded[(g * per_seg + 1) * rows : (g * per_seg + 2) * rows]
                    spec.append(a + sign * b)
                spec = jnp.concatenate(spec, axis=0)
                re, im = spec[:, :LANES], spec[:, LANES:]
                power = re * re + im * im
                hi = power.astype(jnp.bfloat16)
                lo = (power - hi.astype(jnp.float32)).astype(jnp.bfloat16)
                total = jnp.dot(
                    jnp.concatenate([hi, lo], axis=1), same, preferred_element_type=jnp.float32
                )
                scale = lax.rsqrt(total * (1.0 / BAND) + whiten_eps)
                w_re = (re * scale).astype(jnp.bfloat16).astype(jnp.float32)
                w_im = (im * scale).astype(jnp.bfloat16).astype(jnp.float32)
                at = 2 * j * LANES
                for g in range(segs):
                    r, o = g * rows, (first + g) * ch
                    own[o : o + ch, at : at + LANES] = w_re[r : r + ch]
                    own[o : o + ch, at + LANES : at + 2 * LANES] = w_im[r : r + ch]
                    o = (first + g) * src_count
                    other[o : o + src_count, at : at + LANES] = w_re[r + ch : r + rows]
                    other[o : o + src_count, at + LANES : at + 2 * LANES] = w_im[r + ch : r + rows]

    block = cross.shape[1] // ch
    copies = []
    for i in range(count):
        start = pl.multiple_of((pl.program_id(0) * count + i) * block, 8)
        for j in range(CHUNKS):
            at = 2 * j * LANES
            a_re = [own[g * ch : (g + 1) * ch, at : at + LANES] for g in range(seg_count)]
            a_im = [own[g * ch : (g + 1) * ch, at + LANES : at + 2 * LANES] for g in range(seg_count)]
            for s in range(block):
                if s % 8 == 0:
                    tiles = [
                        other[
                            pl.ds(pl.multiple_of(g * src_count + start + s, 8), 8),
                            at : at + 2 * LANES,
                        ]
                        for g in range(seg_count)
                    ]
                re = im = None
                for g in range(seg_count):
                    b_re = tiles[g][s % 8 : s % 8 + 1, :LANES]
                    b_im = tiles[g][s % 8 : s % 8 + 1, LANES:]
                    p = a_re[g] * b_re + a_im[g] * b_im
                    q = a_im[g] * b_re - a_re[g] * b_im
                    re, im = (p, q) if re is None else (re + p, im + q)
                row = slice(s * ch, (s + 1) * ch)
                cross[i, row, at : at + LANES] = re.astype(jnp.bfloat16)
                cross[i, row, at + LANES : at + 2 * LANES] = im.astype(jnp.bfloat16)
        lags = sum(
            jnp.dot(
                cross[i, :, h * dec : (h + 1) * dec],
                tab_ref[:, d_cols + 2 * LAGH * h : d_cols + 2 * LAGH * (h + 1)],
                preferred_element_type=jnp.float32,
            )
            for h in range(per_seg)
        )
        result[i] = lags.reshape(result.shape[1:])
        copy = pltpu.make_async_copy(result.at[i], out_ref.at[pl.ds(start, block)], sems.at[i])
        copy.start()
        copies.append(copy)
    for copy in copies:
        copy.wait()


def whole(space=pltpu.VMEM):
    return pl.BlockSpec(memory_space=space)


def local(raw_strain, fir_taps, source_channels, live_counts):
    rows, raw_len = raw_strain.shape
    steps = lax.axis_size("tm")
    chan_count = lax.axis_size("chan")
    dec = raw_len // DECIM
    blocks = dec // LANES
    ch = rows // steps
    seg_count = steps * dec // SEG
    src_count = source_channels.shape[0]
    slots = 2 * SRC_DEV * steps
    span = raw_len // blocks
    total_rows = ch + src_count
    half = src_count // CORES
    highs = steps // 2
    own_rows = blocks * ch
    given_rows = blocks * half + edge_tiles(2 * ch + half) * ROWS
    height = 2 * own_rows + given_rows
    head_len = -(-(fir_taps.shape[0] - 1) // DECIM)
    assert head_len < EDGE and ch == ROWS and src_count <= 256
    assert steps >= 8 and steps & (steps - 1) == 0 and chan_count & (chan_count - 1) == 0 and half % ROWS == 0
    src = source_channels.reshape(1, src_count)
    taps = fir_taps.reshape(1, fir_taps.shape[0])
    table = np.concatenate([dft_table(dec), *lag_table(seg_count).reshape(SEG // dec, dec, -1)], axis=1)
    inputs = (src, taps, raw_strain, jnp.asarray(table))
    part, picked, table = pl.pallas_call(
        functools.partial(filter_kernel, blocks),
        out_shape=[
            pltpu.VMEM((steps, (blocks + 1) * ch, LANES), jnp.bfloat16),
            pltpu.VMEM((slots, dec + LANES), jnp.bfloat16),
            pltpu.VMEM(table.shape, jnp.bfloat16),
        ],
        in_specs=[whole(pl.ANY)] * 4,
        out_specs=[whole(), whole(), whole(pl.ANY)],
        scratch_shapes=[
            pltpu.VMEM((blocks * rows, span + LANES), jnp.bfloat16),
            pltpu.VMEM((2 * LANES, span + LANES), jnp.bfloat16),
            pltpu.VMEM(src.shape, src.dtype),
            pltpu.VMEM(taps.shape, taps.dtype),
            pltpu.SemaphoreType.DMA((blocks + 3,)),
        ],
        compiler_params=pltpu.CompilerParams(vmem_limit_bytes=16 * MIB),
        name="fir",
    )(*(pltpu.with_memory_space_constraint(a, pltpu.HBM) for a in inputs))
    pieces = [picked] + [
        lax.ppermute(picked, "chan", [(c, c ^ k) for c in range(chan_count)])
        for k in range(1, chan_count)
    ]
    to_vmem = functools.partial(pltpu.with_memory_space_constraint, memory_space=pltpu.VMEM)
    outgoing = pl.pallas_call(
        functools.partial(arrange_kernel, half, blocks, chan_count),
        out_shape=[
            pltpu.VMEM((rows_k, LANES), jnp.bfloat16)
            for rows_k in [height, height - own_rows, *[height] * (highs - 2), height - own_rows]
        ],
        in_specs=[whole()] * (chan_count + 1),
        out_specs=[whole()] * (highs + 1),
        compiler_params=pltpu.CompilerParams(vmem_limit_bytes=8 * MIB),
        name="arrange",
    )(*(to_vmem(a) for a in (*pieces, part)))
    arrived = [
        lax.ppermute(outgoing[k], "tm", [(t, t ^ (2 * k)) for t in range(steps)])
        for k in range(highs - 1, 0, -1)
    ]
    arrived = [to_vmem(a) for a in (outgoing[0], *arrived[::-1])]
    small = pltpu.CompilerParams(vmem_limit_bytes=8 * MIB)
    passed = [None] * highs
    for k in [1, 0, *range(highs - 1, 1, -1)]:
        if k == 1:
            forward, by = outgoing[highs], 3
        else:
            by = 1
            forward = pl.pallas_call(
                functools.partial(forward_kernel, own_rows),
                out_shape=pltpu.VMEM((own_rows + given_rows, LANES), jnp.bfloat16),
                in_specs=[whole()],
                out_specs=whole(),
                compiler_params=small,
                name="forward",
            )(arrived[k])
        passed[k] = to_vmem(lax.ppermute(forward, "tm", [(t, t ^ by) for t in range(steps)]))
    passed = direct_first(passed)
    given = pl.pallas_call(
        functools.partial(collect_kernel, own_rows),
        out_shape=pltpu.VMEM((steps, given_rows, LANES), jnp.bfloat16),
        in_specs=[whole()] * steps,
        out_specs=whole(),
        compiler_params=small,
        name="collect",
    )(*arrived, *passed)
    swapped = lax.ppermute(given, "chan", [(c, c ^ 1) for c in range(chan_count)])
    block = math.gcd(src_count, 8)
    count = math.gcd(src_count // block, 4)
    state = seg_count * total_rows * SEG * 4
    return pl.pallas_call(
        functools.partial(
            correlate_kernel, seg_count, src_count, dec, head_len, 1024, count, steps
        ),
        grid=(src_count // (block * count),),
        out_shape=jax.ShapeDtypeStruct((src_count, ch, 2 * LAGH), jnp.float32),
        in_specs=[whole(pltpu.SMEM)] + [whole()] * (steps + 3),
        out_specs=whole(pl.ANY),
        scratch_shapes=[
            pltpu.VMEM((steps, own_rows, LANES), jnp.bfloat16),
            pltpu.VMEM((steps, ROWS, LANES), jnp.float32),
            pltpu.VMEM((steps * total_rows, dec), jnp.bfloat16),
            pltpu.VMEM((seg_count * ch, SEG), jnp.float32),
            pltpu.VMEM((seg_count * src_count, SEG), jnp.float32),
            pltpu.VMEM((count, block * ch, SEG), jnp.bfloat16),
            pltpu.VMEM((count, block, ch, 2 * LAGH), jnp.float32),
            pltpu.SemaphoreType.DMA((count,)),
        ],
        compiler_params=pltpu.CompilerParams(vmem_limit_bytes=16 * MIB + 2 * state),
        name="correlate",
    )(live_counts, table, *arrived, *passed, to_vmem(given), to_vmem(swapped))


def solution(mesh):
    placed = (P("chan", "tm"), P(), P(), P(("chan", "tm")))
    return jax.shard_map(
        local, mesh=mesh, in_specs=placed, out_specs=P(None, ("chan", "tm"), None), check_vma=False
    )
```

```python
import functools
import math

import jax
import jax.numpy as jnp
import ml_dtypes
import numpy as np
from jax import lax
from jax.experimental import pallas as pl
from jax.experimental.pallas import tpu as pltpu
from jax.sharding import PartitionSpec as P

DECIM = 10
SEG = 1024
BAND = 64
LAGH = 192
SRC_DEV = 1
LANES = 128
HALF = SEG // 2
CHUNKS = HALF // LANES
EDGE = 14
PER_TILE = LANES // (3 * EDGE)
ROWS = 16
CORES = 2
MIB = 1024 * 1024

whiten_eps = 1e-06

NT = (((1,), (1,)), ((), ()))


def split_table(table):
    hi = table.astype(ml_dtypes.bfloat16)
    lo = (table - hi.astype(np.float64)).astype(ml_dtypes.bfloat16)
    return hi, lo


def dft_table(rows):
    phase = (np.arange(rows)[:, None] * np.arange(HALF)[None, :] % SEG) * (2.0 * np.pi / SEG)
    parts = []
    for j in range(CHUNKS):
        cut = slice(j * LANES, (j + 1) * LANES)
        hi, lo = split_table(np.concatenate([np.cos(phase[:, cut]), -np.sin(phase[:, cut])], 1))
        parts += [hi, lo]
    return np.concatenate(parts, axis=1)


def lag_table(seg_count):
    freq = np.arange(HALF)[:, None]
    phase = (freq * np.arange(-LAGH, LAGH)[None, :] % SEG) * (2.0 * np.pi / SEG)
    weight = np.where(freq == 0, 1.0, 2.0) * (math.sqrt(SEG / seg_count) / SEG)
    re = (weight * np.cos(phase)).reshape(CHUNKS, LANES, 2 * LAGH)
    im = (-weight * np.sin(phase)).reshape(CHUNKS, LANES, 2 * LAGH)
    return np.concatenate([re, im], axis=1).reshape(SEG, 2 * LAGH).astype(ml_dtypes.bfloat16)


def iota(shape, dim):
    return lax.broadcasted_iota(jnp.int32, shape, dim)


def one_hot(mask):
    return jnp.where(mask, 1.0, 0.0).astype(jnp.bfloat16)


def column(row):
    n = row.shape[1]
    return jnp.sum(jnp.where(iota((n, n), 0) == iota((n, n), 1), row, 0), axis=1, keepdims=True)


def tap_rows(taps):
    tap_count = taps.shape[1]
    width = 3 * LANES
    flip = one_hot(iota((tap_count, width), 0) + iota((tap_count, width), 1) == tap_count)
    hi = taps.astype(jnp.bfloat16)
    lo = (taps - hi.astype(jnp.float32)).astype(jnp.bfloat16)
    out = []
    for part in (hi, lo):
        base = jnp.dot(
            jnp.broadcast_to(part.astype(jnp.float32), (8, tap_count)).astype(jnp.bfloat16),
            flip,
            preferred_element_type=jnp.float32,
        )
        upper = pltpu.roll(base, 0, 1, stride=DECIM, stride_axis=0)
        out.append(jnp.concatenate([upper, pltpu.roll(upper, 8 * DECIM, 1)], axis=0))
    return out


def edge_tiles(count):
    return -(-count // (PER_TILE * ROWS))


def filter_kernel(
    blocks,
    src_hbm, taps_hbm, raw_ref, tab_hbm,
    out_ref, slot_ref, tab_ref,
    ext, weight, src_ref, taps_ref, sems,
):
    rows, raw_len = raw_ref.shape
    steps = out_ref.shape[0]
    ch = rows // steps
    span = raw_len // blocks
    wide = span + LANES
    small = [
        pltpu.make_async_copy(taps_hbm, taps_ref, sems.at[blocks]),
        pltpu.make_async_copy(src_hbm, src_ref, sems.at[blocks + 1]),
    ]
    for copy in small:
        copy.start()
    copies = []
    for b in range(blocks):
        if b == 0:
            copy = pltpu.make_async_copy(
                raw_ref.at[:, pl.ds(0, span)],
                ext.at[pl.ds(0, rows), pl.ds(LANES, span)],
                sems.at[b],
            )
        else:
            copy = pltpu.make_async_copy(
                raw_ref.at[:, pl.ds(b * span - LANES, wide)],
                ext.at[pl.ds(b * rows, rows), :],
                sems.at[b],
            )
        copy.start()
        copies.append(copy)
    tables = pltpu.make_async_copy(tab_hbm, tab_ref, sems.at[blocks + 2])
    tables.start()
    ext[:rows, :LANES] = jnp.zeros((rows, LANES), ext.dtype)
    weight[...] = jnp.zeros_like(weight)
    for copy in small:
        copy.wait()
    for p, base in enumerate(tap_rows(taps_ref[...])):
        for i in range(LANES // 16):
            tile, lane = divmod(16 * DECIM * i, LANES)
            piece = pltpu.roll(base, lane, 1) if lane else base
            weight[p * LANES + 16 * i : p * LANES + 16 * (i + 1), tile * LANES : (tile + 3) * LANES] = (
                piece.astype(jnp.bfloat16)
            )
    src = src_ref[...]
    src_count = src.shape[1]
    slots = slot_ref.shape[0]
    group = src // rows
    group_col = column(group)
    src_col = column(src)
    rank = jnp.sum(
        jnp.where(
            (group_col == group)
            & (iota((src_count, src_count), 0) < iota((src_count, src_count), 1)),
            1,
            0,
        ),
        axis=0,
        keepdims=True,
    )
    mine = lax.axis_index("chan")
    to_slot = one_hot((iota((slots, src_count), 0) == rank) & (group == mine))
    to_row = one_hot(src_col - mine * rows == iota((src_count, rows), 1))
    pick = jnp.dot(to_slot, to_row, preferred_element_type=jnp.float32).astype(jnp.bfloat16)
    number = jnp.where(
        iota((src_count, LANES), 1) == LANES - 1, iota((src_count, LANES), 0) + 1, 0
    ).astype(jnp.float32).astype(jnp.bfloat16)
    number = jnp.dot(to_slot, number, preferred_element_type=jnp.float32)
    for copy in copies:
        copy.wait()
    acc = lax.dot_general(ext[...], weight[...], NT, preferred_element_type=jnp.float32)
    acc = acc[:, :LANES] + acc[:, LANES:]
    y = acc.astype(jnp.bfloat16)
    head = acc[:rows]
    head_lo = head - head.astype(jnp.bfloat16).astype(jnp.float32)
    tail = lax.dot_general(
        ext[(blocks - 1) * rows :, wide - LANES :], weight[:, :LANES], NT,
        preferred_element_type=jnp.float32,
    )
    tail = tail[:, :LANES] + tail[:, LANES:]
    tail_hi = tail.astype(jnp.bfloat16).astype(jnp.float32)
    lane = iota((rows, LANES), 1)
    edge = jnp.where(
        lane < EDGE,
        head_lo,
        jnp.where(
            lane < 2 * EDGE,
            pltpu.roll(tail_hi, EDGE, 1),
            jnp.where(lane < 3 * EDGE, pltpu.roll(tail - tail_hi, 2 * EDGE, 1), 0.0),
        ),
    ).astype(jnp.bfloat16)
    parts = [y[b * rows : (b + 1) * rows] for b in range(blocks)] + [edge]
    last = blocks * ch
    for t in range(steps):
        for b in range(blocks):
            out_ref[t, b * ch : (b + 1) * ch] = parts[b][t * ch : (t + 1) * ch]
        out_ref[t, last : last + ch] = edge[t * ch : (t + 1) * ch]
    for b, part in enumerate(parts):
        found = jnp.dot(pick, part, preferred_element_type=jnp.float32)
        if b == blocks:
            found += number
        slot_ref[:, b * LANES : (b + 1) * LANES] = found.astype(jnp.bfloat16)
    tables.wait()


def arrange_kernel(half, blocks, pieces, *refs):
    slots = jnp.concatenate([ref[...] for ref in refs[:pieces]], axis=0)
    part_ref, *out_refs = refs[pieces:]
    height = out_refs[0].shape[0]
    own_rows = part_ref.shape[1] - ROWS
    tile_rows = height - 2 * own_rows - blocks * half
    numbers = slots[:, blocks * LANES :].astype(jnp.float32)
    total = numbers.shape[0]
    numbers = jnp.sum(
        jnp.where(iota((total, LANES), 1) == LANES - 1, numbers, 0.0), axis=1, keepdims=True
    ).astype(jnp.int32)
    first = lax.axis_index("chan") % CORES * half
    pick = one_hot(numbers == iota((total, half), 1) + 1 + first)
    found = lax.dot_general(
        pick, slots, (((0,), (0,)), ((), ())), preferred_element_type=jnp.float32
    )
    fill = [found[:, b * LANES : (b + 1) * LANES].astype(jnp.bfloat16) for b in range(blocks)]
    edges = jnp.where(iota((half, LANES), 1) < 3 * EDGE, found[:, blocks * LANES :], 0.0)
    added = [jnp.zeros((ROWS, LANES), jnp.float32) for _ in range(tile_rows // ROWS)]
    for i in range(half // ROWS):
        tile, place = divmod(i + 2, PER_TILE)
        piece = edges[i * ROWS : (i + 1) * ROWS]
        added[tile] += pltpu.roll(piece, 3 * EDGE * place, 1) if place else piece
    me = lax.axis_index("tm")
    *out_refs, direct_ref = out_refs
    for k, out_ref in enumerate(out_refs):
        same = part_ref[me ^ (2 * k)]
        other = part_ref[me ^ (2 * k) ^ 1]
        mixed = same[own_rows:].astype(jnp.float32) + pltpu.roll(
            other[own_rows:].astype(jnp.float32), 3 * EDGE, 1
        )
        if k == 1:
            writes = [(out_ref, [same]), (direct_ref, [other])]
        else:
            writes = [(out_ref, [same, other])]
        for ref, owners in writes:
            at = 0
            for owner in owners:
                ref[at : at + own_rows] = owner[:own_rows]
                at += own_rows
            for piece in fill:
                ref[at : at + half] = piece
                at += half
            for tile, extra in enumerate(added):
                ref[at : at + ROWS] = (extra + mixed if tile == 0 else extra).astype(jnp.bfloat16)
                at += ROWS


def forward_kernel(own_rows, block_ref, out_ref):
    out_ref[...] = block_ref[own_rows:]


def direct_first(refs):
    return [refs[1], refs[0], *refs[2:]]


def collect_kernel(own_rows, *refs):
    *block_refs, out_ref = refs
    highs = len(block_refs) // 2
    passed_refs = direct_first(block_refs[highs:])
    me = lax.axis_index("tm")
    for k in range(highs):
        out_ref[me ^ (2 * k)] = block_refs[k][block_refs[k].shape[0] - out_ref.shape[1] :]
        out_ref[me ^ (2 * k) ^ 1] = passed_refs[k][own_rows:]


def correlate_kernel(
    seg_count, src_count, dec, head_len, part_rows, count, steps, live_ref, tab_ref, *refs
):
    count_high = steps // 2
    block_refs, passed_refs = refs[:count_high], direct_first(refs[count_high:steps])
    given_ref, far_ref, out_ref = refs[steps : steps + 3]
    mine_ref, mine_edge, trace, own, other, cross, result, sems = refs[steps + 3 :]
    ch = out_ref.shape[1]
    own_rows = mine_ref.shape[1]
    half = src_count // CORES
    rows = ch + src_count
    per_seg = SEG // dec
    blocks = dec // LANES
    d_cols = 4 * HALF

    @pl.when(pl.program_id(0) == 0)
    def _():
        me = lax.axis_index("tm")
        last = block_refs[0].shape[0] - edge_tiles(2 * ch + half) * ROWS
        for k, ref in enumerate(block_refs):
            mine_ref[me ^ (2 * k)] = ref[:own_rows]
            at = ref.shape[0] - (block_refs[0].shape[0] - last)
            mine_edge[me ^ (2 * k)] = ref[at : at + ROWS].astype(jnp.float32)
        for k, ref in enumerate(passed_refs):
            mine_ref[me ^ (2 * k) ^ 1] = ref[:own_rows]
            pack = ref[last - own_rows : last - own_rows + ROWS].astype(jnp.float32)
            mine_edge[me ^ (2 * k) ^ 1] = pltpu.roll(pack, LANES - 3 * EDGE, 1)
        live = iota((ch, LANES), 0) < live_ref[0]
        before = jnp.zeros((rows, LANES), jnp.float32)
        is_head = iota((rows, LANES), 1) < head_len
        tile_rows = edge_tiles(2 * ch + half) * ROWS
        low_core = lax.axis_index("chan") % CORES == 0

        def edge_groups(ref, t):
            out = []
            last = ref.shape[1] - tile_rows
            for i in range(2, 2 + half // ROWS):
                tile, place = divmod(i, PER_TILE)
                pack = ref[t, last + tile * ROWS : last + (tile + 1) * ROWS].astype(jnp.float32)
                out.append(pltpu.roll(pack, LANES - 3 * EDGE * place, 1) if place else pack)
            return jnp.concatenate(out, axis=0)

        def in_order(near, far):
            return [jnp.where(low_core, near, far), jnp.where(low_core, far, near)]

        for t in range(steps):
            edge = jnp.where(live, mine_edge[t], 0.0)
            theirs = edge_groups(given_ref, t), edge_groups(far_ref, t)
            edge = jnp.concatenate([edge, *in_order(*theirs)], axis=0)
            for b in range(blocks):
                mine = mine_ref[t, b * ch : (b + 1) * ch]
                mine = jnp.where(live, mine, jnp.zeros_like(mine))
                rows_b = slice(b * half, (b + 1) * half)
                theirs = given_ref[t, rows_b], far_ref[t, rows_b]
                both = jnp.concatenate([mine, *in_order(*theirs)], axis=0)
                if b == 0:
                    tail = pltpu.roll(before, LANES - EDGE, 1) + pltpu.roll(before, LANES - 2 * EDGE, 1)
                    both = both.astype(jnp.float32)
                    both = jnp.where(is_head, both + edge + tail, both).astype(jnp.bfloat16)
                trace[t * rows : (t + 1) * rows, b * LANES : (b + 1) * LANES] = both
            before = edge
        odd = (iota((rows, 2 * LANES), 1) & 1) == 1
        sign = jnp.where(odd, -1.0, 1.0)
        same = one_hot(
            iota((2 * LANES, LANES), 0) % LANES // BAND == iota((2 * LANES, LANES), 1) // BAND
        )
        group_segs = max(1, min(seg_count, part_rows // (per_seg * rows)))
        for first in range(0, seg_count, group_segs):
            segs = min(group_segs, seg_count - first)
            lhs = trace[first * per_seg * rows : (first + segs) * per_seg * rows, :]
            for j in range(CHUNKS):
                acc = jnp.dot(
                    lhs, tab_ref[:, 4 * j * LANES : 4 * (j + 1) * LANES],
                    preferred_element_type=jnp.float32,
                )
                folded = acc[:, : 2 * LANES] + acc[:, 2 * LANES :]
                spec = []
                for g in range(segs):
                    a = folded[g * per_seg * rows : (g * per_seg + 1) * rows]
                    b = folded[(g * per_seg + 1) * rows : (g * per_seg + 2) * rows]
                    spec.append(a + sign * b)
                spec = jnp.concatenate(spec, axis=0)
                re, im = spec[:, :LANES], spec[:, LANES:]
                power = re * re + im * im
                hi = power.astype(jnp.bfloat16)
                lo = (power - hi.astype(jnp.float32)).astype(jnp.bfloat16)
                total = jnp.dot(
                    jnp.concatenate([hi, lo], axis=1), same, preferred_element_type=jnp.float32
                )
                scale = lax.rsqrt(total * (1.0 / BAND) + whiten_eps)
                w_re = (re * scale).astype(jnp.bfloat16).astype(jnp.float32)
                w_im = (im * scale).astype(jnp.bfloat16).astype(jnp.float32)
                at = 2 * j * LANES
                for g in range(segs):
                    r, o = g * rows, (first + g) * ch
                    own[o : o + ch, at : at + LANES] = w_re[r : r + ch]
                    own[o : o + ch, at + LANES : at + 2 * LANES] = w_im[r : r + ch]
                    o = (first + g) * src_count
                    other[o : o + src_count, at : at + LANES] = w_re[r + ch : r + rows]
                    other[o : o + src_count, at + LANES : at + 2 * LANES] = w_im[r + ch : r + rows]

    block = cross.shape[1] // ch
    copies = []
    for i in range(count):
        start = pl.multiple_of((pl.program_id(0) * count + i) * block, 8)
        for j in range(CHUNKS):
            at = 2 * j * LANES
            a_re = [own[g * ch : (g + 1) * ch, at : at + LANES] for g in range(seg_count)]
            a_im = [own[g * ch : (g + 1) * ch, at + LANES : at + 2 * LANES] for g in range(seg_count)]
            for s in range(block):
                if s % 8 == 0:
                    tiles = [
                        other[
                            pl.ds(pl.multiple_of(g * src_count + start + s, 8), 8),
                            at : at + 2 * LANES,
                        ]
                        for g in range(seg_count)
                    ]
                re = im = None
                for g in range(seg_count):
                    b_re = tiles[g][s % 8 : s % 8 + 1, :LANES]
                    b_im = tiles[g][s % 8 : s % 8 + 1, LANES:]
                    p = a_re[g] * b_re + a_im[g] * b_im
                    q = a_im[g] * b_re - a_re[g] * b_im
                    re, im = (p, q) if re is None else (re + p, im + q)
                row = slice(s * ch, (s + 1) * ch)
                cross[i, row, at : at + LANES] = re.astype(jnp.bfloat16)
                cross[i, row, at + LANES : at + 2 * LANES] = im.astype(jnp.bfloat16)
        lags = sum(
            jnp.dot(
                cross[i, :, h * dec : (h + 1) * dec],
                tab_ref[:, d_cols + 2 * LAGH * h : d_cols + 2 * LAGH * (h + 1)],
                preferred_element_type=jnp.float32,
            )
            for h in range(per_seg)
        )
        result[i] = lags.reshape(result.shape[1:])
        copy = pltpu.make_async_copy(result.at[i], out_ref.at[pl.ds(start, block)], sems.at[i])
        copy.start()
        copies.append(copy)
    for copy in copies:
        copy.wait()


def whole(space=pltpu.VMEM):
    return pl.BlockSpec(memory_space=space)


def local(raw_strain, fir_taps, source_channels, live_counts):
    rows, raw_len = raw_strain.shape
    steps = lax.axis_size("tm")
    chan_count = lax.axis_size("chan")
    dec = raw_len // DECIM
    blocks = dec // LANES
    ch = rows // steps
    seg_count = steps * dec // SEG
    src_count = source_channels.shape[0]
    slots = 2 * SRC_DEV * steps
    span = raw_len // blocks
    total_rows = ch + src_count
    half = src_count // CORES
    highs = steps // 2
    own_rows = blocks * ch
    given_rows = blocks * half + edge_tiles(2 * ch + half) * ROWS
    height = 2 * own_rows + given_rows
    head_len = -(-(fir_taps.shape[0] - 1) // DECIM)
    assert head_len < EDGE and ch == ROWS and src_count <= 256
    assert steps >= 8 and steps & (steps - 1) == 0 and chan_count & (chan_count - 1) == 0 and half % ROWS == 0
    src = source_channels.reshape(1, src_count)
    taps = fir_taps.reshape(1, fir_taps.shape[0])
    table = np.concatenate([dft_table(dec), *lag_table(seg_count).reshape(SEG // dec, dec, -1)], axis=1)
    inputs = (src, taps, raw_strain, jnp.asarray(table))
    part, picked, table = pl.pallas_call(
        functools.partial(filter_kernel, blocks),
        out_shape=[
            pltpu.VMEM((steps, (blocks + 1) * ch, LANES), jnp.bfloat16),
            pltpu.VMEM((slots, dec + LANES), jnp.bfloat16),
            pltpu.VMEM(table.shape, jnp.bfloat16),
        ],
        in_specs=[whole(pl.ANY)] * 4,
        out_specs=[whole(), whole(), whole(pl.ANY)],
        scratch_shapes=[
            pltpu.VMEM((blocks * rows, span + LANES), jnp.bfloat16),
            pltpu.VMEM((2 * LANES, span + LANES), jnp.bfloat16),
            pltpu.VMEM(src.shape, src.dtype),
            pltpu.VMEM(taps.shape, taps.dtype),
            pltpu.SemaphoreType.DMA((blocks + 3,)),
        ],
        compiler_params=pltpu.CompilerParams(vmem_limit_bytes=16 * MIB),
        name="fir",
    )(*(pltpu.with_memory_space_constraint(a, pltpu.HBM) for a in inputs))
    pieces = [picked] + [
        lax.ppermute(picked, "chan", [(c, c ^ k) for c in range(chan_count)])
        for k in range(1, chan_count)
    ]
    to_vmem = functools.partial(pltpu.with_memory_space_constraint, memory_space=pltpu.VMEM)
    outgoing = pl.pallas_call(
        functools.partial(arrange_kernel, half, blocks, chan_count),
        out_shape=[
            pltpu.VMEM((rows_k, LANES), jnp.bfloat16)
            for rows_k in [height, height - own_rows, *[height] * (highs - 2), height - own_rows]
        ],
        in_specs=[whole()] * (chan_count + 1),
        out_specs=[whole()] * (highs + 1),
        compiler_params=pltpu.CompilerParams(vmem_limit_bytes=8 * MIB),
        name="arrange",
    )(*(to_vmem(a) for a in (*pieces, part)))
    arrived = [
        lax.ppermute(outgoing[k], "tm", [(t, t ^ (2 * k)) for t in range(steps)])
        for k in range(1, highs)
    ]
    arrived = [to_vmem(a) for a in (outgoing[0], *arrived)]
    small = pltpu.CompilerParams(vmem_limit_bytes=8 * MIB)
    passed = [None] * highs
    for k in [1, 0, *range(highs - 1, 1, -1)]:
        if k == 1:
            forward, by = outgoing[highs], 3
        else:
            by = 1
            forward = pl.pallas_call(
                functools.partial(forward_kernel, own_rows),
                out_shape=pltpu.VMEM((own_rows + given_rows, LANES), jnp.bfloat16),
                in_specs=[whole()],
                out_specs=whole(),
                compiler_params=small,
                name="forward",
            )(arrived[k])
        passed[k] = to_vmem(lax.ppermute(forward, "tm", [(t, t ^ by) for t in range(steps)]))
    passed = direct_first(passed)
    given = pl.pallas_call(
        functools.partial(collect_kernel, own_rows),
        out_shape=pltpu.VMEM((steps, given_rows, LANES), jnp.bfloat16),
        in_specs=[whole()] * steps,
        out_specs=whole(),
        compiler_params=small,
        name="collect",
    )(*arrived, *passed)
    swapped = lax.ppermute(given, "chan", [(c, c ^ 1) for c in range(chan_count)])
    block = math.gcd(src_count, 8)
    count = math.gcd(src_count // block, 4)
    state = seg_count * total_rows * SEG * 4
    return pl.pallas_call(
        functools.partial(
            correlate_kernel, seg_count, src_count, dec, head_len, 1024, count, steps
        ),
        grid=(src_count // (block * count),),
        out_shape=jax.ShapeDtypeStruct((src_count, ch, 2 * LAGH), jnp.float32),
        in_specs=[whole(pltpu.SMEM)] + [whole()] * (steps + 3),
        out_specs=whole(pl.ANY),
        scratch_shapes=[
            pltpu.VMEM((steps, own_rows, LANES), jnp.bfloat16),
            pltpu.VMEM((steps, ROWS, LANES), jnp.float32),
            pltpu.VMEM((steps * total_rows, dec), jnp.bfloat16),
            pltpu.VMEM((seg_count * ch, SEG), jnp.float32),
            pltpu.VMEM((seg_count * src_count, SEG), jnp.float32),
            pltpu.VMEM((count, block * ch, SEG), jnp.bfloat16),
            pltpu.VMEM((count, block, ch, 2 * LAGH), jnp.float32),
            pltpu.SemaphoreType.DMA((count,)),
        ],
        compiler_params=pltpu.CompilerParams(vmem_limit_bytes=16 * MIB + 2 * state),
        name="correlate",
    )(live_counts, table, *arrived, *passed, to_vmem(given), to_vmem(swapped))


def solution(mesh):
    placed = (P("chan", "tm"), P(), P(), P(("chan", "tm")))
    return jax.shard_map(
        local, mesh=mesh, in_specs=placed, out_specs=P(None, ("chan", "tm"), None), check_vma=False
    )
```
